128 devices in a mesh: seq: 32 (over x, z, core), clips: 4 (over y).
Axes of the slice: x: 4, y: 4, z: 4, core: 2. Of those that a mesh axis runs over, the one named last changes fastest.
Arguments:
- inputs: float32 [8, 380, 8192], P('clips', None, 'seq'), may hold values from -6 to 6
- lengths: int32 [8], P('clips'), may hold values from 2048 to 8192, as said below
- window: int32 [2, 380, 2], replicated, may hold values from 0 to 8192, as said below
- gabor_params: float32 [2, 3, 4, 32], replicated, may hold values from -1024 to 1024, as said below
- hidden_w: float32 [2, 2, 32, 32], replicated, may hold values from -1 to 1
- hidden_b: float32 [2, 2, 32], replicated, may hold values from -4 to 4
- out_w: float32 [2, 380, 32], replicated, may hold values from -1 to 1
- out_b: float32 [2, 380], replicated, may hold values from -0.75 to 0.75
- bn_gain: float32 [2, 380], replicated, may hold values from 0.25 to 1.75
- bn_bias: float32 [2, 380], replicated, may hold values from -4 to 4
- mix_w: bfloat16 [2, 380, 380], replicated, may hold values from -0.3125 to 0.3125
- mix_b: float32 [2, 380], replicated, may hold values from -4 to 4
- cotangent: float32 [8, 380, 8192], P('clips', None, 'seq'), may hold values from -6 to 6
Outputs:
- outputs: float32 [8, 380, 8192], P('clips', None, 'seq')
- input_grad: float32 [8, 380, 8192], P('clips', None, 'seq')
- gabor_grad: float32 [2, 3, 4, 32], replicated
- hidden_w_grad: float32 [2, 2, 32, 32], replicated
- hidden_b_grad: float32 [2, 2, 32], replicated
- out_w_grad: float32 [2, 380, 32], replicated
- out_b_grad: float32 [2, 380], replicated
- bn_gain_grad: float32 [2, 380], replicated
- bn_bias_grad: float32 [2, 380], replicated
- mix_w_grad: float32 [2, 380, 380], replicated
- mix_b_grad: float32 [2, 380], replicated
The draws below stay inside these ranges and needn't reach their ends.
Inputs may be any that keep to these rules, and one draw needn't show every extreme that they name: `lengths`: in every aligned block of 2 clips one clip has length 8192. window[l, c, 0] is below 1024, window[l, c, 1] is at least 4096; in each block some channel has window[l, c, 1] = 8192. `gabor_params`: sharpness 1 to 8, centre -1 to 1, frequency magnitude 1 to 1024 with either sign, phase -pi to pi.
All inputs are finite; a program needn't handle non-finite values.
Results may differ from the reference program's by a relative error of at most 0.0089.
Values may be sent and summed in bfloat16 or wider, within the bound.
No kernel may reach another device: no remote copies, remote signals or barrier semaphores. Data moves between devices by JAX's collectives and lax.ppermute only.
A program may use at most 128 MiB of HBM per device.

```python
import math
import jax
import jax.numpy as jnp
from jax import lax

C = 380
H = 32
CLIP_DEV = 2
CLIPS = 8
SAMPLES = 8192


def draw_lengths(key, part):
    key = jax.random.fold_in(key, 11)
    first_key, second_key = jax.random.split(key)
    spans = jax.random.randint(first_key, (CLIPS,), SAMPLES // 4, SAMPLES + 1)
    chosen = jax.random.randint(second_key, (CLIPS // CLIP_DEV, 1), 0, CLIP_DEV)
    slot_ids = jnp.arange(CLIP_DEV, dtype=jnp.int32)[None, :]
    full_clip = (slot_ids == chosen).reshape(CLIPS)
    return jnp.where(full_clip, SAMPLES, spans).astype(jnp.int32)


def draw_window(key, part):
    key = jax.random.fold_in(key, 23)
    first_key, second_key, third_key = jax.random.split(key, 3)
    lower_edge = jax.random.randint(first_key, (2, C), 0, SAMPLES // 8)
    upper_edge = jax.random.randint(second_key, (2, C), SAMPLES // 2, SAMPLES + 1)
    chosen = jax.random.randint(third_key, (2, 1), 0, C)
    channel_ids = jnp.arange(C, dtype=jnp.int32)[None, :]
    upper_edge = jnp.where(channel_ids == chosen, SAMPLES, upper_edge)
    return jnp.stack([lower_edge, upper_edge], axis=-1).astype(jnp.int32)


def draw_gabor_params(key, part):
    key = jax.random.fold_in(key, 37)
    keys = jax.random.split(key, 5)
    sharpness = jnp.exp(jax.random.uniform(keys[0], (2, 3, H), jnp.float32, 0.0, math.log(8.0)))
    centre = jax.random.uniform(keys[1], (2, 3, H), jnp.float32, -1.0, 1.0)
    magnitude = jnp.exp(jax.random.uniform(keys[2], (2, 3, H), jnp.float32, 0.0, math.log(SAMPLES / 8.0)))
    signs = jnp.where(jax.random.uniform(keys[3], (2, 3, H), jnp.float32) < 0.5, -1.0, 1.0)
    phase_shift = jax.random.uniform(keys[4], (2, 3, H), jnp.float32, -math.pi, math.pi)
    return jnp.stack([sharpness, centre, magnitude * signs, phase_shift], axis=2).astype(jnp.float32)


def steps_of(rng, dims, cuts, least, high):
    loudness = 1.0
    for position, shards_of in cuts:
        steps = jax.random.uniform(jax.random.fold_in(jax.random.fold_in(rng, 6), position), (shards_of,), jnp.float32, least / len(cuts), high / len(cuts))
        loudness = loudness * jnp.repeat(jnp.exp(steps), dims[position] // shards_of).reshape((-1,) + (1,) * (len(dims) - 1 - position))
    return loudness


def noise(own_key, dims, deviation, most, cuts=(), kind=jnp.bfloat16):
    factor_of = steps_of(own_key, dims, cuts, -0.22, 0.18) if cuts else 1.0
    array = jax.random.normal(own_key, dims, jnp.float32) * deviation * factor_of
    return jnp.minimum(jnp.maximum(array, -most), most).astype(kind)


def setup_inputs(seed: int = 0) -> dict:
    key_of = jax.random.split(jax.random.key(seed), 14)
    return {
        "inputs": noise(key_of[0], (CLIPS, C, SAMPLES), 1.0, 6.0, ((0, 4), (2, 32)), jnp.float32),
        "lengths": draw_lengths(jax.random.fold_in(key_of[13], 71), 0),
        "window": draw_window(jax.random.fold_in(key_of[13], 71), 0),
        "gabor_params": draw_gabor_params(jax.random.fold_in(key_of[13], 71), 0),
        "hidden_w": noise(key_of[4], (2, 2, H, H), H ** -0.5, 1.0, (), jnp.float32),
        "hidden_b": noise(key_of[5], (2, 2, H), 0.3, 4.0, (), jnp.float32),
        "out_w": noise(key_of[6], (2, C, H), H ** -0.5, 1.0, (), jnp.float32),
        "out_b": noise(key_of[7], (2, C), 0.05, 0.75, (), jnp.float32),
        "bn_gain": jnp.clip(1.0 + 0.15 * jax.random.normal(key_of[8], (2, C), jnp.float32), 0.25, 1.75),
        "bn_bias": noise(key_of[9], (2, C), 0.3, 4.0, (), jnp.float32),
        "mix_w": noise(key_of[10], (2, C, C), C ** -0.5, 0.3125),
        "mix_b": noise(key_of[11], (2, C), 0.3, 4.0, (), jnp.float32),
        "cotangent": noise(key_of[12], (CLIPS, C, SAMPLES), 1.0, 6.0, ((0, 4), (2, 32)), jnp.float32),
    }


exactness = lax.Precision.HIGHEST
epsilon = 1e-05

@jax.custom_vjp
def low(v):
    return lax.optimization_barrier(v.astype(jnp.bfloat16)).astype(jnp.float32)

@jax.custom_vjp
def low_back(v):
    return v

def low_keep(v):
    return (low(v), None)

def low_pass(kept, grad):
    return (grad,)

def back_keep(v):
    return (v, None)

def back_low(kept, grad):
    return (low(grad),)
low.defvjp(low_keep, low_pass)
low_back.defvjp(back_keep, back_low)

def gabor_net(places, gabor_one, hidden_w_one, hidden_b_one, out_w_one, out_b_one):

    def filters(level_index):
        sharpness = gabor_one[level_index, 0][:, None]
        centre = gabor_one[level_index, 1][:, None]
        frequency = gabor_one[level_index, 2][:, None]
        phase_shift = gabor_one[level_index, 3][:, None]
        spread = sharpness * (places[None, :] - centre)
        return jnp.exp(-0.5 * spread * spread) * jnp.sin(frequency * places[None, :] + phase_shift)
    hidden_state = filters(0)
    for level_index in range(2):
        hidden_state = (jnp.dot(hidden_w_one[level_index], hidden_state, precision=exactness) + hidden_b_one[level_index][:, None]) * filters(level_index + 1)
    return jnp.dot(out_w_one, hidden_state, precision=exactness) + out_b_one[:, None]

def envelope(sample_ids, bounds):
    lower_edge = bounds[:, 0][:, None]
    upper_edge = bounds[:, 1][:, None]
    inside = (sample_ids[None, :] >= lower_edge) & (sample_ids[None, :] < upper_edge)
    breadth = 0.5 * (upper_edge - lower_edge).astype(jnp.float32)
    offset = (sample_ids[None, :] - lower_edge).astype(jnp.float32) / breadth
    return jnp.where(inside, jnp.exp(-0.5 * offset * offset), 0.0)

def kernel_of(places, sample_ids, bounds, gabor_one, hidden_w_one, hidden_b_one, out_w_one, out_b_one):
    return gabor_net(places, gabor_one, hidden_w_one, hidden_b_one, out_w_one, out_b_one) * envelope(sample_ids, bounds)

def causal(source, kernel):
    full_len = 2 * SAMPLES
    source_hat = jnp.fft.rfft(source, n=full_len, axis=-1)
    kernel_hat = jnp.fft.rfft(kernel, n=full_len, axis=-1)
    return jnp.fft.irfft(source_hat * kernel_hat[None], n=full_len, axis=-1)[..., :SAMPLES]

def reference(inputs, lengths, window, gabor_params, hidden_w, hidden_b, out_w, out_b, bn_gain, bn_bias, mix_w, mix_b, cotangent):
    sample_ids = jnp.arange(SAMPLES, dtype=jnp.int32)
    valid_rows = (sample_ids[None, :] < lengths[:, None]).astype(jnp.float32)[:, None, :]
    places = -1.0 + 2.0 * sample_ids.astype(jnp.float32) / (SAMPLES - 1)
    valid_count = jnp.sum(valid_rows)

    def forward(inputs, gabor_params, hidden_w, hidden_b, out_w, out_b, bn_gain, bn_bias, mix_w, mix_b):
        current = inputs
        for layer_index in range(2):
            kernel = low(kernel_of(places, sample_ids, window[layer_index], gabor_params[layer_index], hidden_w[layer_index], hidden_b[layer_index], out_w[layer_index], out_b[layer_index]))
            source = low(current * valid_rows)
            convolved = low_back(causal(source, kernel))
            chan_mean = lax.optimization_barrier(jnp.sum(convolved * valid_rows, axis=(0, 2))) / valid_count
            centred = convolved - chan_mean[None, :, None]
            chan_var = lax.optimization_barrier(jnp.sum(centred * centred * valid_rows, axis=(0, 2))) / valid_count
            normed = centred * lax.rsqrt(chan_var + epsilon)[None, :, None]
            pre_act = normed * bn_gain[layer_index][None, :, None] + bn_bias[layer_index][None, :, None]
            activation = low(jax.nn.gelu(pre_act, approximate=False))
            mixed = low_back(jnp.einsum('oc,bct->bot', mix_w[layer_index], activation, precision=exactness) + mix_b[layer_index][None, :, None])
            current = current + mixed * valid_rows
        return current
    mix_float = mix_w.astype(jnp.float32)
    outputs, pullback = jax.vjp(forward, inputs, gabor_params, hidden_w, hidden_b, out_w, out_b, bn_gain, bn_bias, mix_float, mix_b)
    gradients = pullback(cotangent)
    return (outputs, gradients[0], gradients[1], gradients[2], gradients[3], gradients[4], gradients[5], gradients[6], gradients[7], gradients[8], gradients[9])
```

```python
import math

import jax
import jax.numpy as jnp
import ml_dtypes
import numpy as np
from jax import lax
from jax.experimental import pallas as pl
from jax.experimental.pallas import tpu as pltpu
from jax.sharding import PartitionSpec as P

F32 = jnp.float32
BF16 = jnp.bfloat16
AXES = ("seq", "clips")
DEVICES = 128
OWN = 3
CHANNELS = 380
PADDED = DEVICES * OWN
SAMPLES = 8192
PIECE = 256
HIDDEN = 32
LANES = 128
SIGNALS = 12
PERIOD = 2 * SAMPLES
EPSILON = 1e-05
VMEM_LIMIT = 40 * 1024 * 1024
EXACT = lax.Precision.HIGHEST
SPOT = 2 * DEVICES + 126


def halves(table):
    high = table.astype(ml_dtypes.bfloat16)
    low = (table - high.astype(np.float64)).astype(ml_dtypes.bfloat16)
    return high, low


def tables():
    order = np.array([2 * j + r for r in range(2) for j in range(32)])
    k = np.arange(LANES)
    turn = 2 * np.pi * ((k[:, None] * order[None, :]) % LANES) / LANES
    c_high, c_low = halves(np.cos(turn))
    s_high, s_low = halves(np.sin(turn))
    first = np.concatenate(
        [
            np.concatenate([c_high, c_low, s_high, s_low], axis=1),
            np.concatenate([-s_high, -s_low, c_high, c_low], axis=1),
        ],
        axis=0,
    )
    turn = 2 * np.pi * ((k[:, None] * k[None, :]) % LANES) / LANES
    cosine, sine = np.cos(turn), np.sin(turn)
    second = halves(np.block([[cosine, -sine], [sine, cosine]]))
    second_back = halves(np.block([[cosine, sine], [-sine, cosine]]))
    turn = 2 * np.pi * ((order[:, None] * k[None, :]) % LANES) / LANES
    cosine, sine = np.cos(turn) / PERIOD, np.sin(turn) / PERIOD
    last = halves(np.block([[cosine, -sine], [sine, cosine]]))
    turn = 2 * np.pi * (k[:, None] * k[None, :]) / PERIOD
    twiddle = np.stack([np.cos(turn), np.sin(turn)]).astype(np.float32)
    times = (128 * order[:, None] + k[None, :]).astype(np.float32)
    places = (-1.0 + 2.0 * times / np.float32(SAMPLES - 1)).astype(np.float32)
    lookup = np.zeros((PADDED, PADDED), ml_dtypes.bfloat16)
    for part in range(OWN):
        for owner in range(DEVICES):
            lookup[part * DEVICES + owner, OWN * owner + part] = 1
    return dict(
        first=first,
        second=np.stack(second),
        second_back=np.stack(second_back),
        last=np.stack(last),
        twiddle=twiddle,
        times=np.concatenate([times, times], axis=0),
        time_row=times.reshape(1, SAMPLES),
        place_row=places.reshape(1, SAMPLES),
        lookup=lookup,
    )


TABLES = tables()


def run(body, outs, args, scratch, name, smem=()):
    return pl.pallas_call(
        body,
        out_shape=[jax.ShapeDtypeStruct(shape, kind) for shape, kind in outs],
        in_specs=[
            pl.BlockSpec(memory_space=pltpu.SMEM if i in smem else pltpu.VMEM) for i in range(len(args))
        ],
        out_specs=[pl.BlockSpec(memory_space=pltpu.VMEM)] * len(outs),
        scratch_shapes=[pltpu.VMEM(shape, kind) for shape, kind in scratch],
        compiler_params=pltpu.CompilerParams(vmem_limit_bytes=VMEM_LIMIT),
        name=name,
    )(*args)


def dot(a, b):
    return jnp.dot(a, b, preferred_element_type=F32)


def dot_rows(a, b, precision=None):
    return lax.dot_general(a, b, (((1,), (1,)), ((), ())), precision=precision, preferred_element_type=F32)


def dot_columns(a, b, precision=None):
    return lax.dot_general(a, b, (((0,), (0,)), ((), ())), precision=precision, preferred_element_type=F32)


def triple(a_high, a_low, b_high, b_low):
    return dot(a_high, b_high) + dot(a_low, b_high) + dot(a_high, b_low)


def put_halves(high_ref, low_ref, rows, columns, value):
    high = value.astype(BF16)
    high_ref[rows, columns] = high
    low_ref[rows, columns] = (value - high.astype(F32)).astype(BF16)


def block(i, size=LANES):
    return slice(i * size, (i + 1) * size)


RE, IM = slice(0, LANES), slice(LANES, 2 * LANES)


def signal_row(b, part, r):
    return b * 6 + part * 2 + r


def spread(message):
    return message.astype(F32).reshape(-1, LANES)


def transform(x_ref, high_ref, low_ref, first, second, twiddle, count):
    part_a = dot(first[...], x_ref[:, : count * LANES])
    cosine, sine = twiddle[0], twiddle[1]
    for s in range(count):
        real, imag = part_a[:LANES, block(s)], part_a[LANES:, block(s)]
        put_halves(high_ref, low_ref, block(s), RE, real * cosine + imag * sine)
        put_halves(high_ref, low_ref, block(s), IM, imag * cosine - real * sine)
    rows = slice(0, count * LANES)
    return triple(high_ref[rows, :], low_ref[rows, :], second[0], second[1])


def transform_back(high_ref, low_ref, e_high, e_low, second_back, last, twiddle, count):
    rows = slice(0, count * LANES)
    part_d = triple(high_ref[rows, :], low_ref[rows, :], second_back[0], second_back[1])
    cosine, sine = twiddle[0], twiddle[1]
    for s in range(count):
        real, imag = part_d[block(s), RE], part_d[block(s), IM]
        put_halves(e_high, e_low, RE, block(s), real * cosine - imag * sine)
        put_halves(e_high, e_low, IM, block(s), real * sine + imag * cosine)
    return triple(last[0], last[1], e_high[:, rows], e_low[:, rows])


def erf_parts(value):
    cdf = 0.5 * (1.0 + lax.erf(value * math.sqrt(0.5)))
    return cdf, jnp.exp(-0.5 * value * value) * (1.0 / math.sqrt(2.0 * math.pi))


def total(value):
    return jnp.sum(jnp.sum(value, axis=0, keepdims=True), axis=1, keepdims=True)


def valid_of(times, len_ref):
    columns = []
    for y in range(4):
        upper = times[0:64, :] < len_ref[2 * y : 2 * y + 1, :]
        lower = times[64:128, :] < len_ref[2 * y + 1 : 2 * y + 2, :]
        columns.append(jnp.concatenate([upper, lower], axis=0).astype(F32))
    return jnp.concatenate(columns, axis=1)


def tally_of(len_ref):
    return jnp.sum(len_ref[:, 0:1], axis=0, keepdims=True)


def load_signals(message, step, x_ref):
    for part in range(OWN):
        for y in range(4):
            lanes = block(part * 4 + y)
            for b in range(2):
                for r in range(2):
                    start = y * step + signal_row(b, part, r)
                    piece = message[pl.ds(start, 32, stride=4 * step), :].astype(BF16)
                    x_ref[b * 128 + r * 32 : b * 128 + r * 32 + 32, lanes] = piece
                    x_ref[b * 128 + r * 32 + 64 : b * 128 + r * 32 + 96, lanes] = piece


def store_signals(out, step, base, get):
    for part in range(OWN):
        for y in range(4):
            value = get(part, y)
            for b in range(2):
                for r in range(2):
                    start = y * step + base + signal_row(b, part, r)
                    out[pl.ds(start, 32, stride=4 * step), :] = value[b * 64 + r * 32 : b * 64 + r * 32 + 32, :]


def convolve(x_ref, spec_ref, kernel_spec, high, low, e_high, e_low, consts, y_ref):
    first, second, second_back, last, twiddle = consts
    spec_ref[...] = transform(x_ref, high, low, first, second, twiddle, SIGNALS)
    for part in range(OWN):
        k_re, k_im = kernel_spec[block(part), RE], kernel_spec[block(part), IM]
        for y in range(4):
            rows = block(part * 4 + y)
            s_re, s_im = spec_ref[rows, RE], spec_ref[rows, IM]
            put_halves(high, low, rows, RE, s_re * k_re - s_im * k_im)
            put_halves(high, low, rows, IM, s_re * k_im + s_im * k_re)
    y_ref[...] = transform_back(high, low, e_high, e_low, second_back, last, twiddle, SIGNALS)


def normalise(y_ref, own, valid, tally, part):
    value = y_ref[:, block(part, 512)]
    mean = total(valid * value) / tally
    centred = value - mean
    var = total(valid * centred * centred) / tally
    inv_std = lax.rsqrt(var + EPSILON)
    normed = centred * inv_std
    pre_act = normed * own[part : part + 1, 35:36] + own[part : part + 1, 36:37]
    cdf, density = erf_parts(pre_act)
    return normed, inv_std, pre_act * cdf, cdf + pre_act * density


def conv_backward(
    message, step, base, normed_of, slope_of, inv_of, own, valid, tally, spec_ref, kernel_spec, x_ref, high, low,
    e_high, e_low, consts, grad_ref,
):
    first, second, second_back, last, twiddle = consts
    sums = []
    for part in range(OWN):
        columns = []
        for y in range(4):
            pieces = []
            for b in range(2):
                for r in range(2):
                    start = y * step + base + signal_row(b, part, r)
                    pieces.append(message[pl.ds(start, 32, stride=4 * step), :])
            columns.append(jnp.concatenate(pieces, axis=0))
        act_grad = jnp.concatenate(columns, axis=1)
        normed = normed_of(part)
        pre_grad = act_grad * slope_of(part)
        bias_total = total(pre_grad)
        gain_total = total(pre_grad * normed)
        gain = own[part : part + 1, 35:36]
        conv_grad = inv_of(part) * (
            gain * pre_grad - valid * (gain * bias_total + normed * (gain * gain_total)) / tally
        )
        conv_low = conv_grad.astype(BF16)
        for b in range(2):
            piece = conv_low[b * 64 : b * 64 + 64, :]
            x_ref[b * 128 : b * 128 + 64, block(part, 512)] = piece
            x_ref[b * 128 + 64 : b * 128 + 128, block(part, 512)] = piece
        sums.append((gain_total, bias_total))
    grad_ref[...] = transform(x_ref, high, low, first, second, twiddle, SIGNALS)
    for part in range(OWN):
        k_re, k_im = kernel_spec[block(part), RE], kernel_spec[block(part), IM]
        corr_re, corr_im = None, None
        for y in range(4):
            rows = block(part * 4 + y)
            g_re, g_im = grad_ref[rows, RE], grad_ref[rows, IM]
            s_re, s_im = spec_ref[rows, RE], spec_ref[rows, IM]
            put_halves(high, low, rows, RE, k_re * g_re + k_im * g_im)
            put_halves(high, low, rows, IM, k_re * g_im - k_im * g_re)
            now_re, now_im = s_re * g_re + s_im * g_im, s_re * g_im - s_im * g_re
            corr_re = now_re if corr_re is None else corr_re + now_re
            corr_im = now_im if corr_im is None else corr_im + now_im
        put_halves(high, low, block(SIGNALS + part), RE, corr_re)
        put_halves(high, low, block(SIGNALS + part), IM, corr_im)
    returned = transform_back(high, low, e_high, e_low, second_back, last, twiddle, SIGNALS + OWN)
    return returned, sums


def sin_cos(angle):
    turns = jnp.floor(angle * (2.0 / math.pi) + 0.5)
    rest = angle - turns * 1.5703125
    rest = rest - turns * 4.837512969970703125e-4
    rest = rest - turns * 7.549789948768648e-8
    square = rest * rest
    sine = rest + rest * square * (
        -1.6666654611e-1 + square * (8.3321608736e-3 + square * -1.9515295891e-4)
    )
    cosine = 1.0 - 0.5 * square + square * square * (
        4.166664568298827e-2 + square * (-1.388731625493765e-3 + square * 2.443315711809948e-5)
    )
    half = jnp.floor(turns * 0.5)
    odd = turns - 2.0 * half
    sign = 1.0 - 2.0 * (half - 2.0 * jnp.floor(half * 0.5))
    is_odd = odd > 0.5
    return sign * jnp.where(is_odd, cosine, sine), sign * jnp.where(is_odd, -sine, cosine)


CHUNK = 1024


def envelope_of(times, own):
    lower, upper = own[:, 33:34], own[:, 34:35]
    inside = (times >= lower) & (times < upper)
    offset = (times - lower) / (0.5 * (upper - lower))
    return jnp.where(inside, jnp.exp(-0.5 * offset * offset), 0.0)


def generate(columns, hidden_w, own, place_row, time_row, first, second, twiddle, tab, spec, rows, pieces, x_ref, high, low):
    def step(i, carry):
        span = pl.ds(pl.multiple_of(i * CHUNK, CHUNK), CHUNK)
        places = place_row[:, span]

        def level(j):
            sharpness, centre = columns[:, 4 * j : 4 * j + 1], columns[:, 4 * j + 1 : 4 * j + 2]
            frequency, phase = columns[:, 4 * j + 2 : 4 * j + 3], columns[:, 4 * j + 3 : 4 * j + 4]
            width = sharpness * (places - centre)
            bell = jnp.exp(-0.5 * width * width)
            sine, cosine = sin_cos(frequency * places + phase)
            return bell * sine, bell * cosine

        f_0, c_0 = level(0)
        tab[0, :, span] = f_0
        tab[1, :, span] = c_0
        u_1 = jnp.dot(hidden_w[0], f_0, precision=EXACT, preferred_element_type=F32) + columns[:, 12:13]
        f_1, c_1 = level(1)
        z_1 = u_1 * f_1
        tab[2, :, span] = z_1
        tab[3, :, span] = u_1 * c_1
        tab[4, :, span] = f_1
        u_2 = jnp.dot(hidden_w[1], z_1, precision=EXACT, preferred_element_type=F32) + columns[:, 13:14]
        f_2, c_2 = level(2)
        z_2 = u_2 * f_2
        tab[5, :, span] = z_2
        tab[6, :, span] = u_2 * c_2
        tab[7, :, span] = f_2
        raw = jnp.dot(own[:, 0:32], z_2, precision=EXACT, preferred_element_type=F32) + own[:, 32:33]
        rows[:, span] = raw * envelope_of(time_row[:, span], own)
        return carry

    lax.fori_loop(0, SAMPLES // CHUNK, step, 0)
    for n in range(64):
        for part in range(OWN):
            pieces[part * 64 + n : part * 64 + n + 1, :] = rows[part : part + 1, block(n)]
    for part in range(OWN):
        piece = pieces[block(part, 64), :].astype(BF16)
        x_ref[0:64, block(part)] = piece
        x_ref[64:128, block(part)] = piece
        x_ref[128:256, block(part)] = jnp.zeros((128, LANES), BF16)
    spec[...] = transform(x_ref, high, low, first, second, twiddle, OWN)


def generate_back(kernel_grad, columns, hidden_w, own, place_row, time_row, tab, rows, sums, mats):
    rows[...] = jnp.zeros(rows.shape, F32)
    for part in range(OWN):
        grad = kernel_grad(part)
        for n in range(64):
            rows[part : part + 1, block(n)] = grad[n : n + 1, :]
    sums[...] = jnp.zeros(sums.shape, F32)
    mats[...] = jnp.zeros(mats.shape, F32)
    turned = jnp.transpose(jnp.concatenate([own[:, 0:128], jnp.zeros((120, 128), F32)], axis=0))
    weight = [turned[0:32, part : part + 1] for part in range(OWN)]

    def add(k, value):
        acc = value[:, block(0)]
        for i in range(1, CHUNK // LANES):
            acc = acc + value[:, block(i)]
        sums[block(k, 32), :] += acc

    def step(i, carry):
        span = pl.ds(pl.multiple_of(i * CHUNK, CHUNK), CHUNK)
        places = place_row[:, span]
        draw = rows[:, span] * envelope_of(time_row[:, span], own)
        dz_2 = weight[0] * draw[0:1, :] + weight[1] * draw[1:2, :] + weight[2] * draw[2:3, :]

        def level(j, e_value, g_value):
            centre = columns[:, 4 * j + 1 : 4 * j + 2]
            offset = places - centre
            moment = e_value * offset
            add(4 * j, moment * offset)
            add(4 * j + 1, moment)
            add(4 * j + 2, g_value * places)
            add(4 * j + 3, g_value)

        z_2 = tab[5, :, span]
        level(2, dz_2 * z_2, dz_2 * tab[6, :, span])
        du_2 = dz_2 * tab[7, :, span]
        add(13, du_2)
        dz_1 = dot_columns(hidden_w[1], du_2, EXACT)
        z_1 = tab[2, :, span]
        level(1, dz_1 * z_1, dz_1 * tab[3, :, span])
        du_1 = dz_1 * tab[4, :, span]
        add(12, du_1)
        dz_0 = dot_columns(hidden_w[0], du_1, EXACT)
        z_0 = tab[0, :, span]
        level(0, dz_0 * z_0, dz_0 * tab[1, :, span])
        left = jnp.concatenate([du_1, du_2, draw], axis=0)
        right = jnp.concatenate([z_0, z_1, z_2, jnp.zeros_like(z_0)], axis=0)
        mats[...] += dot_rows(left, right, EXACT)
        return carry

    lax.fori_loop(0, SAMPLES // CHUNK, step, 0)
    lane = lax.broadcasted_iota(jnp.int32, (32, LANES), 1)
    hidden = jnp.where(lane < 32, mats[0:32, :], jnp.where(lane < 64, mats[32:64, :], 0.0))

    def column(k):
        return jnp.sum(sums[block(k, 32), :], axis=1, keepdims=True)

    hidden = jnp.where(lane == 64, column(12), hidden)
    hidden = jnp.where(lane == 65, column(13), hidden)
    for j in range(3):
        sharpness = columns[:, 4 * j : 4 * j + 1]
        hidden = jnp.where(lane == 66 + 4 * j, -sharpness * column(4 * j), hidden)
        hidden = jnp.where(lane == 67 + 4 * j, sharpness * sharpness * column(4 * j + 1), hidden)
        hidden = jnp.where(lane == 68 + 4 * j, column(4 * j + 2), hidden)
        hidden = jnp.where(lane == 69 + 4 * j, column(4 * j + 3), hidden)
    lane8 = lax.broadcasted_iota(jnp.int32, (8, LANES), 1)
    outer = pltpu.roll(mats[64:72, :], LANES - 64, 1)
    raw_total = None
    for i in range(SAMPLES // CHUNK):
        span = slice(i * CHUNK, (i + 1) * CHUNK)
        draw = rows[:, span] * envelope_of(time_row[:, span], own)
        now = jnp.sum(draw, axis=1, keepdims=True)
        raw_total = now if raw_total is None else raw_total + now
    outer = jnp.where(lane8 < 32, outer, 0.0)
    outer = jnp.where(lane8 == 32, raw_total, outer)
    return hidden, outer


def with_norm_sums(outer, sums):
    row = lax.broadcasted_iota(jnp.int32, (8, LANES), 0)
    lane = lax.broadcasted_iota(jnp.int32, (8, LANES), 1)
    for part in range(OWN):
        gain_total, bias_total = sums[part]
        outer = jnp.where((row == part) & (lane == 33), gain_total, outer)
        outer = jnp.where((row == part) & (lane == 34), bias_total, outer)
    return outer


def one_row(outer):
    lane = lax.broadcasted_iota(jnp.int32, (1, LANES), 1)
    result = jnp.zeros((1, LANES), F32)
    for part in range(OWN):
        row = outer[part : part + 1, :]
        moved = pltpu.roll(row, 32 * part, 1) if part else row
        result = jnp.where((lane >= 32 * part) & (lane < 32 * part + 32), moved, result)
        moved = pltpu.roll(row, 64 + 3 * part, 1)
        result = jnp.where((lane >= 96 + 3 * part) & (lane < 99 + 3 * part), moved, result)
    return result


def packed_hidden(hidden):
    lane16 = lax.broadcasted_iota(jnp.int32, (16, LANES), 1)
    upper = jnp.where(lane16 < 64, hidden[0:16, :], pltpu.roll(hidden[16:32, :], 64, 1))
    lane4 = lax.broadcasted_iota(jnp.int32, (4, LANES), 1)
    lower = jnp.zeros((4, LANES), F32)
    for g in range(8):
        moved = pltpu.roll(hidden, (64 + 16 * g) % LANES, 1)[4 * g : 4 * g + 4, :]
        lower = jnp.where((lane4 >= 16 * g) & (lane4 < 16 * g + 16), moved, lower)
    return upper, lower


def unpacked_hidden(upper, lower):
    lane16 = lax.broadcasted_iota(jnp.int32, (16, LANES), 1)
    lane32 = lax.broadcasted_iota(jnp.int32, (32, LANES), 1)
    top = jnp.concatenate([upper, pltpu.roll(upper, 64, 1)], axis=0)
    tiled = jnp.concatenate([lower] * 8, axis=0)
    row32 = lax.broadcasted_iota(jnp.int32, (32, LANES), 0)
    rest = jnp.zeros((32, LANES), F32)
    for g in range(8):
        moved = pltpu.roll(tiled, (64 - 16 * g) % LANES, 1)
        rest = jnp.where((row32 >= 4 * g) & (row32 < 4 * g + 4), moved, rest)
    return jnp.where(lane32 < 64, top, rest)


def high_low(value):
    high = value.astype(BF16).astype(F32)
    return high, value - high


def valid_row(meta, b, r):
    lane = lax.broadcasted_iota(jnp.int32, (1, LANES), 1)
    return (meta[2] * PIECE + r * LANES + lane < meta[b]).astype(F32)


def natural_to_message(natural, out, step, base):
    for b in range(2):
        for r in range(2):
            for part in range(OWN):
                out[pl.ds(base + signal_row(b, part, r), DEVICES, stride=step), :] = natural[
                    pl.ds((2 * b + r) * PADDED + part, DEVICES, stride=OWN), :
                ]


def put_natural(natural, i, value):
    natural[i * PADDED + 376 : i * PADDED + 384, :] = jnp.zeros((8, LANES), F32)
    natural[i * PADDED : i * PADDED + CHANNELS, :] = value


def source_kernel(meta, x_ref, out_ref, natural, out):
    for b in range(2):
        for r in range(2):
            put_natural(natural, 2 * b + r, x_ref[b, :, block(r)] * valid_row(meta, b, r))
        length = meta[b]
        upper = lax.shift_right_logical(length, 7)
        out[pl.ds(12 + 2 * b, DEVICES, stride=16), :] = jnp.full((DEVICES, LANES), upper.astype(F32))
        out[pl.ds(13 + 2 * b, DEVICES, stride=16), :] = jnp.full(
            (DEVICES, LANES), (length - upper * 128).astype(F32)
        )
    natural_to_message(natural, out, 16, 0)
    out_ref[...] = out[...].reshape(DEVICES, 16, LANES).astype(BF16)


def generate_kernel(columns, hidden_w, own, place_row, time_row, first, second, twiddle, tab, spec, rows, pieces, x_ref, high, low):
    generate(columns, hidden_w, own, place_row, time_row, first, second, twiddle, tab, spec, rows, pieces, x_ref, high, low)


def forward_kernel(
    message_ref, kernel_spec, own, times, first, second, second_back, last, twiddle,
    out_ref, spec_ref, normed_ref, slope_ref, inv_ref, len_ref,
    message, x_ref, high, low, e_high, e_low, y_ref, out,
):
    message[...] = spread(message_ref[...])
    for y in range(4):
        for b in range(2):
            start = y * 16 + 12 + 2 * b
            len_ref[2 * y + b : 2 * y + b + 1, :] = (
                message[start : start + 1, :] * 128.0 + message[start + 1 : start + 2, :]
            )
    load_signals(message, 16, x_ref)
    convolve(x_ref, spec_ref, kernel_spec, high, low, e_high, e_low, (first, second, second_back, last, twiddle), y_ref)
    valid, tally = valid_of(times, len_ref), tally_of(len_ref)
    inv_ref[...] = jnp.zeros((8, LANES), F32)
    for part in range(OWN):
        normed, inv_std, active, slope = normalise(y_ref, own, valid, tally, part)
        normed_ref[:, block(part, 512)] = normed
        slope_ref[:, block(part, 512)] = slope
        inv_ref[part : part + 1, :] = jnp.broadcast_to(inv_std, (1, LANES))
        y_ref[:, block(part, 512)] = active
    store_signals(out, 16, 0, lambda part, y: y_ref[:, block(part * 4 + y)])
    out_ref[...] = out[...].reshape(DEVICES, 16, LANES).astype(BF16)


def gather_active(message, step, rhs):
    row = lax.broadcasted_iota(jnp.int32, (DEVICES, LANES), 0)
    for b in range(2):
        for r in range(2):
            for part in range(OWN):
                piece = message[pl.ds(signal_row(b, part, r), DEVICES, stride=step), :]
                if part == 2:
                    piece = jnp.where(row == SPOT - 2 * DEVICES, 1.0, piece)
                rhs[block(part), block(2 * b + r)] = piece.astype(BF16)


def masked_rows(meta, get, low):
    low[368:384, :] = jnp.zeros((16, 512), BF16)
    for b in range(2):
        for r in range(2):
            low[0:CHANNELS, block(2 * b + r)] = (get(b, r) * valid_row(meta, b, r)).astype(BF16)


def store_rows(value, out, step, base):
    for b in range(2):
        for r in range(2):
            for part in range(OWN):
                out[pl.ds(base + signal_row(b, part, r), DEVICES, stride=step), :] = value[
                    block(part), block(2 * b + r)
                ]


def mix_kernel(
    meta, message_ref, x_ref, cotangent, weight, weight_back, bias,
    out_ref, next_ref, active_ref, message, natural, out, low,
):
    message[...] = spread(message_ref[...])
    gather_active(message, 16, active_ref)
    mixed = dot(weight[...], active_ref[...]) + bias[...]
    for b in range(2):
        for r in range(2):
            valid = valid_row(meta, b, r)
            value = x_ref[b, :, block(r)] + mixed[0:CHANNELS, block(2 * b + r)] * valid
            next_ref[b, :, block(r)] = value
            put_natural(natural, 2 * b + r, value * valid)
    natural_to_message(natural, out, 24, 0)
    masked_rows(meta, lambda b, r: cotangent[b, :, block(r)], low)
    store_rows(dot(weight_back[...], low[...]), out, 24, 12)
    out_ref[...] = out[...].reshape(DEVICES, 24, LANES).astype(BF16)


def forward_backward_kernel(
    message_ref, kernel_spec, own, len_ref, times, first, second, second_back, last, twiddle,
    out_ref, grad_out, norm_out,
    message, x_ref, high, low, e_high, e_low, y_ref, out, spec_ref, grad_ref, normed_ref, slope_ref,
):
    consts = (first, second, second_back, last, twiddle)
    message[...] = spread(message_ref[...])
    load_signals(message, 24, x_ref)
    convolve(x_ref, spec_ref, kernel_spec, high, low, e_high, e_low, consts, y_ref)
    valid, tally = valid_of(times, len_ref), tally_of(len_ref)
    inv = []
    for part in range(OWN):
        normed, inv_std, active, slope = normalise(y_ref, own, valid, tally, part)
        normed_ref[:, block(part, 512)] = normed
        slope_ref[:, block(part, 512)] = slope
        inv.append(inv_std)
        y_ref[:, block(part, 512)] = active
    store_signals(out, 24, 0, lambda part, y: y_ref[:, block(part * 4 + y)])
    returned, sums = conv_backward(
        message, 24, 12, lambda part: normed_ref[:, block(part, 512)], lambda part: slope_ref[:, block(part, 512)],
        lambda part: inv[part], own, valid, tally, spec_ref, kernel_spec, x_ref, high, low, e_high, e_low, consts, grad_ref,
    )
    store_signals(out, 24, 12, lambda part, y: returned[:, block(part * 4 + y)])
    for part in range(OWN):
        grad_out[block(part, 64), :] = returned[0:64, block(SIGNALS + part)]
    norm_out[...] = with_norm_sums(jnp.zeros((8, LANES), F32), sums)
    out_ref[...] = out[...].reshape(DEVICES, 24, LANES).astype(BF16)


def generate_back_kernel(grad, norm, columns, hidden_w, own, place_row, time_row, tab, hidden_out, outer_out, rows, sums, mats):
    hidden, outer = generate_back(
        lambda part: grad[block(part, 64), :], columns, hidden_w, own, place_row, time_row, tab, rows, sums, mats
    )
    hidden_out[...] = hidden
    outer_out[...] = outer + norm[...]


def middle_kernel(
    meta, message_ref, x_ref, cotangent, weight, weight_back, bias, active_0, hidden_1,
    output_ref, flow_ref, out_ref, message, natural, out, low_0, low_1, active_1,
):
    message[...] = spread(message_ref[...])
    gather_active(message, 24, active_1)
    mixed = dot(weight[...], active_1[...]) + bias[...]
    for b in range(2):
        for r in range(2):
            output_ref[b, :, block(r)] = (
                x_ref[b, :, block(r)] + mixed[0:CHANNELS, block(2 * b + r)] * valid_row(meta, b, r)
            )
            for part in range(OWN):
                natural[pl.ds((2 * b + r) * PADDED + part, DEVICES, stride=OWN), :] = message[
                    pl.ds(12 + signal_row(b, part, r), DEVICES, stride=24), :
                ]
            flow_ref[b, :, block(r)] = (
                cotangent[b, :, block(r)]
                + natural[(2 * b + r) * PADDED : (2 * b + r) * PADDED + CHANNELS, :] * valid_row(meta, b, r)
            )
    masked_rows(meta, lambda b, r: flow_ref[b, :, block(r)], low_0)
    masked_rows(meta, lambda b, r: cotangent[b, :, block(r)], low_1)
    store_rows(dot(weight_back[...], low_0[...]), out, 32, 0)
    for layer, (active, low) in enumerate(((active_0, low_0), (active_1, low_1))):
        part_sum = dot_rows(active[...], low[...])
        for part in range(OWN):
            for third in range(3):
                out[pl.ds(12 + layer * 9 + part * 3 + third, DEVICES, stride=32), :] = part_sum[
                    block(part), block(third)
                ]
    high, low = high_low(hidden_1[...])
    out[pl.ds(30, DEVICES, stride=32), :] = jnp.concatenate([high, jnp.zeros((96, LANES), F32)], axis=0)
    out[pl.ds(31, DEVICES, stride=32), :] = jnp.concatenate([low, jnp.zeros((96, LANES), F32)], axis=0)
    out_ref[...] = out[...].reshape(DEVICES, 32, LANES).astype(BF16)


LAST_ROWS = 56


def backward_kernel(
    message_ref, spec_ref, kernel_spec, normed_ref, slope_ref, inv_ref, len_ref, own, times,
    first, second, second_back, last, twiddle, columns, hidden_w, place_row, time_row, tab, outer_1,
    out_ref,
    message, x_ref, high, low, e_high, e_low, out, grad_ref, returned_ref, rows, sums, mats,
):
    consts = (first, second, second_back, last, twiddle)
    message[...] = spread(message_ref[...])
    valid, tally = valid_of(times, len_ref), tally_of(len_ref)
    returned, norm_sums = conv_backward(
        message, 32, 0, lambda part: normed_ref[:, block(part, 512)], lambda part: slope_ref[:, block(part, 512)],
        lambda part: inv_ref[part : part + 1, 0:1], own, valid, tally, spec_ref, kernel_spec, x_ref, high, low,
        e_high, e_low, consts, grad_ref,
    )
    returned_ref[...] = returned
    store_signals(out, 16, 0, lambda part, y: returned_ref[:, block(part * 4 + y)])
    hidden, outer = generate_back(
        lambda part: returned_ref[0:64, block(SIGNALS + part)], columns, hidden_w, own, place_row, time_row, tab,
        rows, sums, mats,
    )
    outer = with_norm_sums(outer, norm_sums)
    gathered = jnp.sum(message[...].reshape(DEVICES, 32, LANES), axis=0)
    upper, lower = packed_hidden(hidden)
    hidden_1_high, hidden_1_low = high_low(gathered[30:31, :] + gathered[31:32, :])
    outer_0_high, outer_0_low = high_low(one_row(outer))
    outer_1_high, outer_1_low = high_low(one_row(outer_1[...]))
    shared = jnp.concatenate(
        [
            gathered[0:30, :], upper, lower, hidden_1_high, hidden_1_low,
            outer_0_high, outer_0_low, outer_1_high, outer_1_low,
        ],
        axis=0,
    )
    row = lax.broadcasted_iota(jnp.int32, (DEVICES, 16, LANES), 1)
    own_rows = jnp.where(row < 12, out[...].reshape(DEVICES, 16, LANES), shared[None, 0:16, :])
    rest = jnp.broadcast_to(shared[None, 16:LAST_ROWS, :], (DEVICES, LAST_ROWS - 16, LANES))
    out_ref[...] = jnp.concatenate([own_rows, rest], axis=1).astype(BF16)


def last_kernel(
    meta, message_ref, flow_ref, lookup,
    input_grad, gabor_grad, hidden_w_grad, hidden_b_grad, out_w_grad, out_b_grad, gain_grad, bias_grad,
    mix_w_grad, mix_b_grad, message, natural, owned, thirds,
):
    message[...] = spread(message_ref[...])

    def rows_of(k, count=DEVICES):
        return message[pl.ds(k, count, stride=LAST_ROWS), :]

    for b in range(2):
        for r in range(2):
            for part in range(OWN):
                natural[pl.ds(part, DEVICES, stride=OWN), :] = rows_of(signal_row(b, part, r))
            input_grad[b, :, block(r)] = flow_ref[b, :, block(r)] + natural[0:CHANNELS, :] * valid_row(meta, b, r)
    shared = jnp.sum(message[...].reshape(DEVICES, LAST_ROWS, LANES)[:, 24:56, :], axis=0)
    hidden_0 = unpacked_hidden(shared[6:22, :], shared[22:26, :])
    hidden_1 = rows_of(50, 32) + rows_of(51, 32)
    lane = lax.broadcasted_iota(jnp.int32, (DEVICES, LANES), 1)
    for layer, hidden in enumerate((hidden_0, hidden_1)):
        hidden_w_grad[layer, 0] = hidden[:, 0:32]
        hidden_w_grad[layer, 1] = pltpu.roll(hidden, 96, 1)[:, 0:32]
        turned = jnp.transpose(jnp.concatenate([hidden, jnp.zeros((96, LANES), F32)], axis=0))
        hidden_b_grad[layer] = turned[64:66, 0:32]
        for j in range(3):
            gabor_grad[layer, j] = turned[66 + 4 * j : 70 + 4 * j, 0:32]
        value = rows_of(52 + 2 * layer) + rows_of(53 + 2 * layer)
        for part in range(OWN):
            wide = pltpu.roll(value, (LANES - 32 * part) % LANES, 1)
            small = pltpu.roll(value, 64 - 3 * part, 1)
            owned[pl.ds(part, DEVICES, stride=OWN), :] = jnp.where(lane < 32, wide, small)
        out_w_grad[layer] = owned[0:CHANNELS, 0:32]
        turned = jnp.transpose(owned[...])
        out_b_grad[layer : layer + 1, :] = turned[32:33, 0:CHANNELS]
        gain_grad[layer : layer + 1, :] = turned[33:34, 0:CHANNELS]
        bias_grad[layer : layer + 1, :] = turned[34:35, 0:CHANNELS]
        bias_rows = []
        for part in range(OWN):
            for third in range(3):
                piece = rows_of(12 + layer * 9 + part * 3 + third)
                thirds[block(part), block(third)] = piece.astype(BF16)
                if part == 2:
                    bias_rows.append(piece[SPOT - 2 * DEVICES : SPOT - 2 * DEVICES + 1, :])
        mix_w_grad[layer] = dot_columns(thirds[...], lookup[...])[0:CHANNELS, 0:CHANNELS]
        mix_b_grad[layer : layer + 1, :] = jnp.concatenate(bias_rows, axis=1)[:, 0:CHANNELS]


def exchange(message):
    return lax.all_to_all(message, AXES, split_axis=0, concat_axis=0, tiled=True)


def shards(
    inputs, lengths, window, gabor_params, hidden_w, hidden_b, out_w, out_b, bn_gain, bn_bias, mix_w, mix_b, cotangent
):
    position = lax.axis_index("seq")
    number = position * 4 + lax.axis_index("clips")
    const = {name: jnp.asarray(value) for name, value in TABLES.items()}
    meta = jnp.concatenate([lengths, position[None].astype(jnp.int32)])
    wide = 2 * SIGNALS * LANES

    with jax.named_scope("source_0"):
        (message,) = run(
            source_kernel, [((DEVICES, 16, LANES), BF16)], [meta, inputs],
            [((4 * PADDED, LANES), F32), ((DEVICES * 16, LANES), F32)], "source_0", smem=(0,),
        )
        message = exchange(message)

    with jax.named_scope("parameters"):
        edges = window.astype(F32)
        packed = jnp.concatenate(
            [out_w, out_b[..., None], edges, bn_gain[..., None], bn_bias[..., None]], axis=2
        )
        packed = jnp.pad(packed, ((0, 0), (0, PADDED + 8 - CHANNELS), (0, LANES - packed.shape[2])))
        own = lax.dynamic_slice(packed, (0, number * OWN, 0), (2, 8, LANES))
        fix = jnp.zeros((2, 8, LANES), F32).at[:, :, 34].set(SAMPLES)
        row_ids = number * OWN + jnp.arange(8)
        own = jnp.where((row_ids < CHANNELS)[None, :, None], own, fix)
        columns = jnp.concatenate([gabor_params.reshape(2, 12, HIDDEN), hidden_b], axis=1)
        columns = jnp.pad(jnp.swapaxes(columns, 1, 2), ((0, 0), (0, 0), (0, 2)))
        look = const["lookup"][:, :CHANNELS]
        plain = jnp.eye(PADDED, CHANNELS, dtype=BF16)
        weight = jnp.einsum("ao,loc,pc->lap", plain, mix_w, look, preferred_element_type=F32).astype(BF16)
        weight_back = jnp.swapaxes(weight, 1, 2)
        bias = jnp.pad(mix_b, ((0, 0), (0, PADDED - CHANNELS)))[..., None]

    def generator(layer):
        return run(
            generate_kernel, [((8, HIDDEN, SAMPLES), F32), ((OWN * LANES, 2 * LANES), F32)],
            [
                columns[layer], hidden_w[layer], own[layer], const["place_row"], const["time_row"], const["first"],
                const["second"], const["twiddle"],
            ],
            [
                ((8, SAMPLES), F32), ((192, LANES), F32), ((256, OWN * LANES), BF16),
                ((OWN * LANES, 256), BF16), ((OWN * LANES, 256), BF16),
            ],
            f"generator_{layer}",
        )

    with jax.named_scope("generators"):
        tab_0, spec_k0 = generator(0)
        tab_1, spec_k1 = generator(1)

    def scratch(signals):
        rows = signals * LANES
        return [
            ((256, SIGNALS * LANES), BF16), ((rows, 256), BF16), ((rows, 256), BF16),
            ((256, rows), BF16), ((256, rows), BF16),
        ]

    shape_y = (LANES, SIGNALS * LANES)
    shape_s = (SIGNALS * LANES, 256)
    transforms = [const[name] for name in ("first", "second", "second_back", "last", "twiddle")]
    with jax.named_scope("conv_0"):
        message, spec_0, normed_0, slope_0, inv_0, lens = run(
            forward_kernel,
            [
                ((DEVICES, 16, LANES), BF16), (shape_s, F32), (shape_y, F32), (shape_y, F32), ((8, LANES), F32),
                ((8, LANES), F32),
            ],
            [message, spec_k0, own[0], const["times"], *transforms],
            [((DEVICES * 16, LANES), F32), *scratch(SIGNALS), (shape_y, F32), ((DEVICES * 16, LANES), F32)],
            "conv_0",
        )
        message = exchange(message)

    with jax.named_scope("mix_0"):
        message, middle, active_0 = run(
            mix_kernel,
            [((DEVICES, 24, LANES), BF16), (inputs.shape, F32), ((PADDED, 512), BF16)],
            [meta, message, inputs, cotangent, weight[0], weight_back[1], bias[0]],
            [
                ((DEVICES * 16, LANES), F32), ((4 * PADDED, LANES), F32), ((DEVICES * 24, LANES), F32),
                ((PADDED, 512), BF16),
            ],
            "mix_0", smem=(0,),
        )
        message = exchange(message)

    with jax.named_scope("conv_1"):
        message, kernel_grad_1, norm_1 = run(
            forward_backward_kernel,
            [((DEVICES, 24, LANES), BF16), ((OWN * 64, LANES), F32), ((8, LANES), F32)],
            [message, spec_k1, own[1], lens, const["times"], *transforms],
            [
                ((DEVICES * 24, LANES), F32), *scratch(SIGNALS + OWN), (shape_y, F32), ((DEVICES * 24, LANES), F32),
                (shape_s, F32), (shape_s, F32), (shape_y, F32), (shape_y, F32),
            ],
            "conv_1",
        )
        message = exchange(message)

    back_scratch = [((8, SAMPLES), F32), ((14 * 32, LANES), F32), ((72, LANES), F32)]
    with jax.named_scope("generator_back_1"):
        hidden_1, outer_1 = run(
            generate_back_kernel,
            [((HIDDEN, LANES), F32), ((8, LANES), F32)],
            [
                kernel_grad_1, norm_1, columns[1], hidden_w[1], own[1], const["place_row"], const["time_row"], tab_1,
            ],
            back_scratch, "generator_back_1",
        )

    with jax.named_scope("mix_1"):
        outputs, flow, message = run(
            middle_kernel,
            [(inputs.shape, F32), (inputs.shape, F32), ((DEVICES, 32, LANES), BF16)],
            [meta, message, middle, cotangent, weight[1], weight_back[0], bias[1], active_0, hidden_1],
            [
                ((DEVICES * 24, LANES), F32), ((4 * PADDED, LANES), F32), ((DEVICES * 32, LANES), F32),
                ((PADDED, 512), BF16), ((PADDED, 512), BF16), ((PADDED, 512), BF16),
            ],
            "mix_1", smem=(0,),
        )
        message = exchange(message)

    with jax.named_scope("conv_back_0"):
        (message,) = run(
            backward_kernel,
            [((DEVICES, LAST_ROWS, LANES), BF16)],
            [
                message, spec_0, spec_k0, normed_0, slope_0, inv_0, lens, own[0], const["times"], *transforms,
                columns[0], hidden_w[0], const["place_row"], const["time_row"], tab_0, outer_1,
            ],
            [
                ((DEVICES * 32, LANES), F32), *scratch(SIGNALS + OWN), ((DEVICES * 16, LANES), F32), (shape_s, F32),
                ((LANES, (SIGNALS + OWN) * LANES), F32), *back_scratch,
            ],
            "conv_back_0",
        )
        message = exchange(message)

    with jax.named_scope("gradients"):
        (
            input_grad, gabor_grad, hidden_w_grad, hidden_b_grad, out_w_grad, out_b_grad, gain_grad, bias_grad,
            mix_w_grad, mix_b_grad,
        ) = run(
            last_kernel,
            [
                (inputs.shape, F32), (gabor_params.shape, F32), (hidden_w.shape, F32), (hidden_b.shape, F32),
                (out_w.shape, F32), (out_b.shape, F32), (bn_gain.shape, F32), (bn_bias.shape, F32), (mix_w.shape, F32),
                (mix_b.shape, F32),
            ],
            [meta, message, flow, const["lookup"]],
            [
                ((DEVICES * LAST_ROWS, LANES), F32), ((PADDED, LANES), F32), ((PADDED, LANES), F32),
                ((PADDED, PADDED), BF16),
            ],
            "gradients", smem=(0,),
        )
    return (
        outputs, input_grad, gabor_grad, hidden_w_grad, hidden_b_grad, out_w_grad, out_b_grad, gain_grad, bias_grad,
        mix_w_grad, mix_b_grad,
    )


def solution(mesh):
    clip = P("clips", None, "seq")
    in_specs = (clip, P("clips")) + (P(),) * 10 + (clip,)
    out_specs = (clip, clip) + (P(),) * 9
    return jax.shard_map(shards, mesh=mesh, in_specs=in_specs, out_specs=out_specs, check_vma=False)
```

```python
import math

import jax
import jax.numpy as jnp
import ml_dtypes
import numpy as np
from jax import lax
from jax.experimental import pallas as pl
from jax.experimental.pallas import tpu as pltpu
from jax.sharding import PartitionSpec as P

F32 = jnp.float32
BF16 = jnp.bfloat16
AXES = ("seq", "clips")
DEVICES = 128
OWN = 3
CHANNELS = 380
PADDED = DEVICES * OWN
SAMPLES = 8192
PIECE = 256
HIDDEN = 32
LANES = 128
SIGNALS = 12
PERIOD = 2 * SAMPLES
EPSILON = 1e-05
MEGABYTE = 1024 * 1024
EXACT = lax.Precision.HIGHEST
SPOT = 2 * DEVICES + 126


def halves(table):
    high = table.astype(ml_dtypes.bfloat16)
    low = (table - high.astype(np.float64)).astype(ml_dtypes.bfloat16)
    return high, low


def tables():
    order = np.array([2 * j + r for r in range(2) for j in range(32)])
    k = np.arange(LANES)
    turn = 2 * np.pi * ((k[:, None] * order[None, :]) % LANES) / LANES
    c_high, c_low = halves(np.cos(turn))
    s_high, s_low = halves(np.sin(turn))
    first = np.concatenate(
        [
            np.concatenate([c_high, c_low, s_high, s_low], axis=1),
            np.concatenate([-s_high, -s_low, c_high, c_low], axis=1),
        ],
        axis=0,
    )
    turn = 2 * np.pi * ((k[:, None] * k[None, :]) % LANES) / LANES
    cosine, sine = np.cos(turn), np.sin(turn)
    second = halves(np.block([[cosine, -sine], [sine, cosine]]))
    second_back = halves(np.block([[cosine, sine], [-sine, cosine]]))
    turn = 2 * np.pi * ((order[:, None] * k[None, :]) % LANES) / LANES
    cosine, sine = np.cos(turn) / PERIOD, np.sin(turn) / PERIOD
    last = halves(np.block([[cosine, -sine], [sine, cosine]]))
    turn = 2 * np.pi * (k[:, None] * k[None, :]) / PERIOD
    twiddle = np.stack([np.cos(turn), np.sin(turn)]).astype(np.float32)
    times = (128 * order[:, None] + k[None, :]).astype(np.float32)
    places = (-1.0 + 2.0 * times / np.float32(SAMPLES - 1)).astype(np.float32)
    lookup = np.zeros((PADDED, PADDED), ml_dtypes.bfloat16)
    for part in range(OWN):
        for owner in range(DEVICES):
            lookup[part * DEVICES + owner, OWN * owner + part] = 1
    return dict(
        first=first,
        second=np.stack(second),
        second_back=np.stack(second_back),
        last=np.stack(last),
        twiddle=twiddle,
        times=np.concatenate([times, times], axis=0),
        time_row=times.reshape(1, SAMPLES),
        place_row=places.reshape(1, SAMPLES),
        starts=np.stack([np.pad(places[:, 0], (0, 64)), 2.0 * k / (SAMPLES - 1)]).astype(np.float32),
        lookup=lookup,
    )


TABLES = tables()


def run(body, outs, args, scratch, name, grant, smem=()):
    return pl.pallas_call(
        body,
        out_shape=[jax.ShapeDtypeStruct(shape, kind) for shape, kind in outs],
        in_specs=[
            pl.BlockSpec(memory_space=pltpu.SMEM if i in smem else pltpu.VMEM) for i in range(len(args))
        ],
        out_specs=[pl.BlockSpec(memory_space=pltpu.VMEM)] * len(outs),
        scratch_shapes=[pltpu.VMEM(shape, kind) for shape, kind in scratch],
        compiler_params=pltpu.CompilerParams(vmem_limit_bytes=grant * MEGABYTE),
        name=name,
    )(*args)


def dot(a, b):
    return jnp.dot(a, b, preferred_element_type=F32)


def dot_rows(a, b, precision=None):
    return lax.dot_general(a, b, (((1,), (1,)), ((), ())), precision=precision, preferred_element_type=F32)


def dot_columns(a, b, precision=None):
    return lax.dot_general(a, b, (((0,), (0,)), ((), ())), precision=precision, preferred_element_type=F32)


def triple(a_high, a_low, b_high, b_low):
    return dot(a_high, b_high) + dot(a_low, b_high) + dot(a_high, b_low)


def put_halves(high_ref, low_ref, rows, columns, value):
    high = value.astype(BF16)
    high_ref[rows, columns] = high
    low_ref[rows, columns] = (value - high.astype(F32)).astype(BF16)


def block(i, size=LANES):
    return slice(i * size, (i + 1) * size)


RE, IM = slice(0, LANES), slice(LANES, 2 * LANES)


def signal_row(b, part, r):
    return part * 4 + r * 2 + b


def spread(message):
    return message.astype(F32).reshape(-1, LANES)


def transform(x_ref, high_ref, low_ref, first, second, twiddle, count):
    part_a = dot(first[...], x_ref[:, : count * LANES])
    cosine, sine = twiddle[0], twiddle[1]
    for s in range(count):
        real, imag = part_a[:LANES, block(s)], part_a[LANES:, block(s)]
        put_halves(high_ref, low_ref, block(s), RE, real * cosine + imag * sine)
        put_halves(high_ref, low_ref, block(s), IM, imag * cosine - real * sine)
    rows = slice(0, count * LANES)
    return triple(high_ref[rows, :], low_ref[rows, :], second[0], second[1])


def transform_back(high_ref, low_ref, e_high, e_low, second_back, last, twiddle, count):
    rows = slice(0, count * LANES)
    part_d = triple(high_ref[rows, :], low_ref[rows, :], second_back[0], second_back[1])
    cosine, sine = twiddle[0], twiddle[1]
    for s in range(count):
        real, imag = part_d[block(s), RE], part_d[block(s), IM]
        put_halves(e_high, e_low, RE, block(s), real * cosine - imag * sine)
        put_halves(e_high, e_low, IM, block(s), real * sine + imag * cosine)
    return triple(last[0], last[1], e_high[:, rows], e_low[:, rows])


def erf_parts(value):
    cdf = 0.5 * (1.0 + lax.erf(value * math.sqrt(0.5)))
    return cdf, jnp.exp(-0.5 * value * value) * (1.0 / math.sqrt(2.0 * math.pi))


def total(value):
    return jnp.sum(jnp.sum(value, axis=0, keepdims=True), axis=1, keepdims=True)


def valid_of(times, len_ref):
    columns = []
    for y in range(4):
        upper = times[0:64, :] < len_ref[2 * y : 2 * y + 1, :]
        lower = times[64:128, :] < len_ref[2 * y + 1 : 2 * y + 2, :]
        columns.append(jnp.concatenate([upper, lower], axis=0).astype(F32))
    return jnp.concatenate(columns, axis=1)


def tally_of(len_ref):
    return jnp.sum(len_ref[:, 0:1], axis=0, keepdims=True)


def load_signals(message, step, x_ref):
    for part in range(OWN):
        for y in range(4):
            lanes = block(part * 4 + y)
            for b in range(2):
                for r in range(2):
                    start = y * step + signal_row(b, part, r)
                    piece = message[pl.ds(start, 32, stride=4 * step), :].astype(BF16)
                    x_ref[b * 128 + r * 32 : b * 128 + r * 32 + 32, lanes] = piece
                    x_ref[b * 128 + r * 32 + 64 : b * 128 + r * 32 + 96, lanes] = piece


def store_signals(out, step, base, get):
    for part in range(OWN):
        for y in range(4):
            value = get(part, y)
            for b in range(2):
                for r in range(2):
                    start = y * step + base + signal_row(b, part, r)
                    out[pl.ds(start, 32, stride=4 * step), :] = value[b * 64 + r * 32 : b * 64 + r * 32 + 32, :]


def convolve(x_ref, spec_ref, kernel_spec, high, low, e_high, e_low, consts, y_ref):
    first, second, second_back, last, twiddle = consts
    spec_ref[...] = transform(x_ref, high, low, first, second, twiddle, SIGNALS)
    for part in range(OWN):
        k_re, k_im = kernel_spec[block(part), RE], kernel_spec[block(part), IM]
        for y in range(4):
            rows = block(part * 4 + y)
            s_re, s_im = spec_ref[rows, RE], spec_ref[rows, IM]
            put_halves(high, low, rows, RE, s_re * k_re - s_im * k_im)
            put_halves(high, low, rows, IM, s_re * k_im + s_im * k_re)
    y_ref[...] = transform_back(high, low, e_high, e_low, second_back, last, twiddle, SIGNALS)


def normalise(y_ref, own, valid, tally, part):
    value = y_ref[:, block(part, 512)]
    mean = total(valid * value) / tally
    centred = value - mean
    var = total(valid * centred * centred) / tally
    inv_std = lax.rsqrt(var + EPSILON)
    normed = centred * inv_std
    pre_act = normed * own[part : part + 1, 35:36] + own[part : part + 1, 36:37]
    cdf, density = erf_parts(pre_act)
    return normed, inv_std, pre_act * cdf, cdf + pre_act * density


def conv_backward(
    message, step, base, normed_of, slope_of, inv_of, own, valid, tally, spec_ref, kernel_spec, x_ref, high, low,
    e_high, e_low, consts, grad_ref,
):
    first, second, second_back, last, twiddle = consts
    sums = []
    for part in range(OWN):
        columns = []
        for y in range(4):
            pieces = []
            for b in range(2):
                for r in range(2):
                    start = y * step + base + signal_row(b, part, r)
                    pieces.append(message[pl.ds(start, 32, stride=4 * step), :])
            columns.append(jnp.concatenate(pieces, axis=0))
        act_grad = jnp.concatenate(columns, axis=1)
        normed = normed_of(part)
        pre_grad = act_grad * slope_of(part)
        bias_total = total(pre_grad)
        gain_total = total(pre_grad * normed)
        gain = own[part : part + 1, 35:36]
        conv_grad = inv_of(part) * (
            gain * pre_grad - valid * (gain * bias_total + normed * (gain * gain_total)) / tally
        )
        conv_low = conv_grad.astype(BF16)
        for b in range(2):
            piece = conv_low[b * 64 : b * 64 + 64, :]
            x_ref[b * 128 : b * 128 + 64, block(part, 512)] = piece
            x_ref[b * 128 + 64 : b * 128 + 128, block(part, 512)] = piece
        sums.append((gain_total, bias_total))
    grad_ref[...] = transform(x_ref, high, low, first, second, twiddle, SIGNALS)
    for part in range(OWN):
        k_re, k_im = kernel_spec[block(part), RE], kernel_spec[block(part), IM]
        corr_re, corr_im = None, None
        for y in range(4):
            rows = block(part * 4 + y)
            g_re, g_im = grad_ref[rows, RE], grad_ref[rows, IM]
            s_re, s_im = spec_ref[rows, RE], spec_ref[rows, IM]
            put_halves(high, low, rows, RE, k_re * g_re + k_im * g_im)
            put_halves(high, low, rows, IM, k_re * g_im - k_im * g_re)
            now_re, now_im = s_re * g_re + s_im * g_im, s_re * g_im - s_im * g_re
            corr_re = now_re if corr_re is None else corr_re + now_re
            corr_im = now_im if corr_im is None else corr_im + now_im
        put_halves(high, low, block(SIGNALS + part), RE, corr_re)
        put_halves(high, low, block(SIGNALS + part), IM, corr_im)
    returned = transform_back(high, low, e_high, e_low, second_back, last, twiddle, SIGNALS + OWN)
    return returned, sums


def sin_cos(angle):
    turns = jnp.floor(angle * (2.0 / math.pi) + 0.5)
    rest = angle - turns * 1.5703125
    rest = rest - turns * 4.837512969970703125e-4
    rest = rest - turns * 7.549789948768648e-8
    square = rest * rest
    sine = rest + rest * square * (
        -1.6666654611e-1 + square * (8.3321608736e-3 + square * -1.9515295891e-4)
    )
    cosine = 1.0 - 0.5 * square + square * square * (
        4.166664568298827e-2 + square * (-1.388731625493765e-3 + square * 2.443315711809948e-5)
    )
    half = jnp.floor(turns * 0.5)
    odd = turns - 2.0 * half
    sign = 1.0 - 2.0 * (half - 2.0 * jnp.floor(half * 0.5))
    is_odd = odd > 0.5
    return sign * jnp.where(is_odd, cosine, sine), sign * jnp.where(is_odd, -sine, cosine)


CHUNK = 1024


def envelope_of(times, own):
    lower, upper = own[:, 33:34], own[:, 34:35]
    inside = (times >= lower) & (times < upper)
    offset = (times - lower) / (0.5 * (upper - lower))
    return jnp.where(inside, jnp.exp(-0.5 * offset * offset), 0.0)


def stacked_weight(weight):
    high, low = high_low(weight)
    return jnp.concatenate([high, high, low], axis=1).astype(BF16)


def stacked_dot(weight, value):
    high = value.astype(BF16)
    low = (value - high.astype(F32)).astype(BF16)
    return dot(weight, jnp.concatenate([high, low, high], axis=0))


def own_parameters(layer, number, out_w, out_b, window, gain, bias, gabor, hidden_b, wide, tall, own, columns):
    wide[...] = jnp.zeros(wide.shape, F32)
    wide[0:32, 0:CHANNELS] = out_w[layer]
    wide[32:33, 0:CHANNELS] = out_b[layer : layer + 1, :]
    wide[33:35, 0:CHANNELS] = window[layer].astype(F32)
    wide[35:36, 0:CHANNELS] = gain[layer : layer + 1, :]
    wide[36:37, 0:CHANNELS] = bias[layer : layer + 1, :]
    tall[0:PADDED, :] = jnp.transpose(wide[...])
    tall[PADDED : PADDED + 8, :] = jnp.zeros((8, LANES), F32)
    row = lax.broadcasted_iota(jnp.int32, (8, LANES), 0)
    lane = lax.broadcasted_iota(jnp.int32, (8, LANES), 1)
    mine = tall[pl.ds(number * OWN, 8), :]
    unused = (row >= OWN) | (number * OWN + row >= CHANNELS)
    own[...] = jnp.where(unused, jnp.where(lane == 34, float(SAMPLES), 0.0), mine)
    wide[:, 0:LANES] = jnp.zeros((LANES, LANES), F32)
    for j in range(3):
        wide[4 * j : 4 * j + 4, 0:HIDDEN] = gabor[layer, j]
    wide[12:14, 0:HIDDEN] = hidden_b[layer]
    columns[...] = jnp.transpose(wide[:, 0:LANES])[0:HIDDEN, :]


def generate(columns, hidden_w, own, place_row, time_row, starts, tab, rows):
    waves = []
    for j in range(3):
        frequency, phase = columns[:, 4 * j + 2 : 4 * j + 3], columns[:, 4 * j + 3 : 4 * j + 4]
        waves.append((sin_cos(frequency * starts[0:1, :] + phase), sin_cos(frequency * starts[1:2, :])))
    weights = [stacked_weight(hidden_w[0]), stacked_weight(hidden_w[1]), stacked_weight(own[:, 0:32])]

    def step(i, carry):
        span = pl.ds(pl.multiple_of(i * CHUNK, CHUNK), CHUNK)
        places = place_row[:, span]

        def level(j):
            (start_sin, start_cos), (rest_sin, rest_cos) = waves[j]
            shift = (LANES - i * (CHUNK // LANES)) % LANES
            start_sin, start_cos = pltpu.roll(start_sin, shift, 1), pltpu.roll(start_cos, shift, 1)
            sine, cosine = [], []
            for n in range(CHUNK // LANES):
                s_n, c_n = start_sin[:, n : n + 1], start_cos[:, n : n + 1]
                sine.append(s_n * rest_cos + c_n * rest_sin)
                cosine.append(c_n * rest_cos - s_n * rest_sin)
            width = columns[:, 4 * j : 4 * j + 1] * (places - columns[:, 4 * j + 1 : 4 * j + 2])
            bell = jnp.exp(-0.5 * width * width)
            return bell * jnp.concatenate(sine, axis=1), bell * jnp.concatenate(cosine, axis=1)

        f_0, c_0 = level(0)
        tab[0, :, span] = f_0
        tab[1, :, span] = c_0
        u_1 = stacked_dot(weights[0], f_0) + columns[:, 12:13]
        f_1, c_1 = level(1)
        z_1 = u_1 * f_1
        tab[2, :, span] = z_1
        tab[3, :, span] = u_1 * c_1
        tab[4, :, span] = f_1
        u_2 = stacked_dot(weights[1], z_1) + columns[:, 13:14]
        f_2, c_2 = level(2)
        z_2 = u_2 * f_2
        tab[5, :, span] = z_2
        tab[6, :, span] = u_2 * c_2
        tab[7, :, span] = f_2
        raw = stacked_dot(weights[2], z_2) + own[:, 32:33]
        rows[:, span] = raw * envelope_of(time_row[:, span], own)
        return carry

    lax.fori_loop(0, SAMPLES // CHUNK, step, 0)


def generate_back(kernel_grad, columns, hidden_w, own, place_row, time_row, tab, rows, sums, mats):
    rows[...] = jnp.zeros(rows.shape, F32)
    for part in range(OWN):
        grad = kernel_grad(part)
        for n in range(64):
            rows[part : part + 1, block(n)] = grad[n : n + 1, :]
    sums[...] = jnp.zeros(sums.shape, F32)
    mats[...] = jnp.zeros(mats.shape, F32)
    turned = jnp.transpose(jnp.concatenate([own[...], jnp.zeros((120, 128), F32)], axis=0))
    weight = [turned[0:32, part : part + 1] for part in range(OWN)]
    back = [stacked_weight(jnp.transpose(hidden_w[j])) for j in range(2)]

    def fold(value):
        acc = value[:, block(0)]
        for i in range(1, CHUNK // LANES):
            acc = acc + value[:, block(i)]
        return acc

    def add(k, value):
        sums[block(k, 32), :] += fold(value)

    def step(i, carry):
        span = pl.ds(pl.multiple_of(i * CHUNK, CHUNK), CHUNK)
        places = place_row[:, span]
        draw = rows[:, span] * envelope_of(time_row[:, span], own)
        dz_2 = weight[0] * draw[0:1, :] + weight[1] * draw[1:2, :] + weight[2] * draw[2:3, :]

        def level(j, e_value, g_value):
            centre = columns[:, 4 * j + 1 : 4 * j + 2]
            offset = places - centre
            moment = e_value * offset
            add(4 * j, moment * offset)
            add(4 * j + 1, moment)
            add(4 * j + 2, g_value * places)
            add(4 * j + 3, g_value)

        z_2 = tab[5, :, span]
        level(2, dz_2 * z_2, dz_2 * tab[6, :, span])
        du_2 = dz_2 * tab[7, :, span]
        add(13, du_2)
        dz_1 = stacked_dot(back[1], du_2)
        z_1 = tab[2, :, span]
        level(1, dz_1 * z_1, dz_1 * tab[3, :, span])
        du_1 = dz_1 * tab[4, :, span]
        add(12, du_1)
        dz_0 = stacked_dot(back[0], du_1)
        z_0 = tab[0, :, span]
        level(0, dz_0 * z_0, dz_0 * tab[1, :, span])
        sums[14 * 32 : 14 * 32 + 8, :] += fold(draw)
        left = jnp.concatenate([du_1, du_2, draw], axis=0)
        right = jnp.concatenate([z_0, z_1, z_2, jnp.zeros_like(z_0)], axis=0)
        left_high, right_high = left.astype(BF16), right.astype(BF16)
        left_low = (left - left_high.astype(F32)).astype(BF16)
        right_low = (right - right_high.astype(F32)).astype(BF16)
        mats[...] += (
            dot_rows(left_high, right_high) + dot_rows(left_low, right_high) + dot_rows(left_high, right_low)
        )
        return carry

    lax.fori_loop(0, SAMPLES // CHUNK, step, 0)
    lane = lax.broadcasted_iota(jnp.int32, (32, LANES), 1)
    hidden = jnp.where(lane < 32, mats[0:32, :], jnp.where(lane < 64, mats[32:64, :], 0.0))

    def column(k):
        return jnp.sum(sums[block(k, 32), :], axis=1, keepdims=True)

    hidden = jnp.where(lane == 64, column(12), hidden)
    hidden = jnp.where(lane == 65, column(13), hidden)
    for j in range(3):
        sharpness = columns[:, 4 * j : 4 * j + 1]
        hidden = jnp.where(lane == 66 + 4 * j, -sharpness * column(4 * j), hidden)
        hidden = jnp.where(lane == 67 + 4 * j, sharpness * sharpness * column(4 * j + 1), hidden)
        hidden = jnp.where(lane == 68 + 4 * j, column(4 * j + 2), hidden)
        hidden = jnp.where(lane == 69 + 4 * j, column(4 * j + 3), hidden)
    lane8 = lax.broadcasted_iota(jnp.int32, (8, LANES), 1)
    outer = pltpu.roll(mats[64:72, :], LANES - 64, 1)
    raw_total = jnp.sum(sums[14 * 32 : 14 * 32 + 8, :], axis=1, keepdims=True)
    outer = jnp.where(lane8 < 32, outer, 0.0)
    outer = jnp.where(lane8 == 32, raw_total, outer)
    return hidden, outer


def with_norm_sums(outer, sums):
    row = lax.broadcasted_iota(jnp.int32, (8, LANES), 0)
    lane = lax.broadcasted_iota(jnp.int32, (8, LANES), 1)
    for part in range(OWN):
        gain_total, bias_total = sums[part]
        outer = jnp.where((row == part) & (lane == 33), gain_total, outer)
        outer = jnp.where((row == part) & (lane == 34), bias_total, outer)
    return outer


def one_row(outer):
    lane = lax.broadcasted_iota(jnp.int32, (1, LANES), 1)
    result = jnp.zeros((1, LANES), F32)
    for part in range(OWN):
        row = outer[part : part + 1, :]
        moved = pltpu.roll(row, 32 * part, 1) if part else row
        result = jnp.where((lane >= 32 * part) & (lane < 32 * part + 32), moved, result)
        moved = pltpu.roll(row, 64 + 3 * part, 1)
        result = jnp.where((lane >= 96 + 3 * part) & (lane < 99 + 3 * part), moved, result)
    return result


def packed_hidden(hidden):
    lane16 = lax.broadcasted_iota(jnp.int32, (16, LANES), 1)
    upper = jnp.where(lane16 < 64, hidden[0:16, :], pltpu.roll(hidden[16:32, :], 64, 1))
    lane4 = lax.broadcasted_iota(jnp.int32, (4, LANES), 1)
    lower = jnp.zeros((4, LANES), F32)
    for g in range(8):
        moved = pltpu.roll(hidden, (64 + 16 * g) % LANES, 1)[4 * g : 4 * g + 4, :]
        lower = jnp.where((lane4 >= 16 * g) & (lane4 < 16 * g + 16), moved, lower)
    return upper, lower


def unpacked_hidden(upper, lower):
    lane16 = lax.broadcasted_iota(jnp.int32, (16, LANES), 1)
    lane32 = lax.broadcasted_iota(jnp.int32, (32, LANES), 1)
    top = jnp.concatenate([upper, pltpu.roll(upper, 64, 1)], axis=0)
    tiled = jnp.concatenate([lower] * 8, axis=0)
    row32 = lax.broadcasted_iota(jnp.int32, (32, LANES), 0)
    rest = jnp.zeros((32, LANES), F32)
    for g in range(8):
        moved = pltpu.roll(tiled, (64 - 16 * g) % LANES, 1)
        rest = jnp.where((row32 >= 4 * g) & (row32 < 4 * g + 4), moved, rest)
    return jnp.where(lane32 < 64, top, rest)


def high_low(value):
    high = value.astype(BF16).astype(F32)
    return high, value - high


def valid_row(meta, i):
    lane = lax.broadcasted_iota(jnp.int32, (1, LANES), 1)
    return (meta[2] * PIECE + (i // 2) * LANES + lane < meta[i % 2]).astype(F32)


def masked(meta, rows):
    mask = jnp.concatenate([valid_row(meta, i) for i in range(4)] * 2, axis=0)
    return (rows.reshape(-1, 8, LANES) * mask[None]).reshape(-1, LANES)


CLIP_ROWS = 4 * CHANNELS
PADDED_ROWS = 4 * PADDED


def put_padded(padded, rows):
    padded[0:CLIP_ROWS, :] = rows
    padded[CLIP_ROWS:PADDED_ROWS, :] = jnp.zeros((PADDED_ROWS - CLIP_ROWS, LANES), F32)


def rows_to_message(padded, out, step, base):
    for m in range(12):
        out[pl.ds(base + m, DEVICES, stride=step), :] = padded[pl.ds(m, DEVICES, stride=12), :]


def rows_of_channels(padded, i):
    return padded[pl.ds(i, PADDED, stride=4), :]


def source_kernel(meta, x_ref, out_ref, padded, out):
    put_padded(padded, masked(meta, x_ref[...]))
    for b in range(2):
        length = meta[b]
        upper = lax.shift_right_logical(length, 7)
        out[pl.ds(12 + 2 * b, DEVICES, stride=16), :] = jnp.full((DEVICES, LANES), upper.astype(F32))
        out[pl.ds(13 + 2 * b, DEVICES, stride=16), :] = jnp.full(
            (DEVICES, LANES), (length - upper * 128).astype(F32)
        )
    rows_to_message(padded, out, 16, 0)
    out_ref[...] = out[...].reshape(DEVICES, 16, LANES).astype(BF16)


def weights_kernel(mix_w, mix_b, lookup, weight, weight_back, bias, wide):
    for layer in range(2):
        wide[...] = jnp.zeros(wide.shape, BF16)
        wide[0:CHANNELS, 0:CHANNELS] = mix_w[layer]
        weight[layer] = dot_rows(wide[...], lookup[...]).astype(BF16)
        weight_back[layer] = dot_rows(lookup[...], wide[...]).astype(BF16)
    row = lax.broadcasted_iota(jnp.int32, (LANES, CHANNELS), 0)
    both = jnp.where(row == 0, mix_b[0:1, :], jnp.where(row == 1, mix_b[1:2, :], 0.0))
    bias[...] = jnp.transpose(jnp.concatenate([both, jnp.zeros((LANES, PADDED - CHANNELS), F32)], axis=1))


def generate_kernel(layer):
    def body(
        meta, out_w, out_b, window, gain, bias, gabor, hidden_b, hidden_w, place_row, time_row, starts,
        first, second, twiddle,
        tab, spec, own, columns,
        wide, tall, rows, pieces, x_ref, high, low,
    ):
        own_parameters(layer, meta[3], out_w, out_b, window, gain, bias, gabor, hidden_b, wide, tall, own, columns)
        generate(columns, hidden_w.at[layer], own, place_row, time_row, starts, tab, rows)
        for n in range(64):
            for part in range(OWN):
                pieces[part * 64 + n : part * 64 + n + 1, :] = rows[part : part + 1, block(n)]
        for part in range(OWN):
            piece = pieces[block(part, 64), :].astype(BF16)
            x_ref[0:64, block(part)] = piece
            x_ref[64:128, block(part)] = piece
            x_ref[128:256, block(part)] = jnp.zeros((128, LANES), BF16)
        spec[...] = transform(x_ref, high, low, first, second, twiddle, OWN)

    return body


def forward_kernel(
    message_ref, kernel_spec, own, times, first, second, second_back, last, twiddle,
    out_ref, spec_ref, normed_ref, slope_ref, inv_ref, len_ref,
    message, x_ref, high, low, e_high, e_low, y_ref, out,
):
    message[...] = spread(message_ref[...])
    for y in range(4):
        for b in range(2):
            start = y * 16 + 12 + 2 * b
            len_ref[2 * y + b : 2 * y + b + 1, :] = (
                message[start : start + 1, :] * 128.0 + message[start + 1 : start + 2, :]
            )
    load_signals(message, 16, x_ref)
    convolve(x_ref, spec_ref, kernel_spec, high, low, e_high, e_low, (first, second, second_back, last, twiddle), y_ref)
    valid, tally = valid_of(times, len_ref), tally_of(len_ref)
    inv_ref[...] = jnp.zeros((8, LANES), F32)
    for part in range(OWN):
        normed, inv_std, active, slope = normalise(y_ref, own, valid, tally, part)
        normed_ref[:, block(part, 512)] = normed
        slope_ref[:, block(part, 512)] = slope
        inv_ref[part : part + 1, :] = jnp.broadcast_to(inv_std, (1, LANES))
        y_ref[:, block(part, 512)] = active
    store_signals(out, 16, 0, lambda part, y: y_ref[:, block(part * 4 + y)])
    out_ref[...] = out[...].reshape(DEVICES, 16, LANES).astype(BF16)


def gather_active(message, step, rhs):
    row = lax.broadcasted_iota(jnp.int32, (DEVICES, LANES), 0)
    for i in range(4):
        for part in range(OWN):
            piece = message[pl.ds(part * 4 + i, DEVICES, stride=step), :]
            if part == 2:
                piece = jnp.where(row == SPOT - 2 * DEVICES, 1.0, piece)
            rhs[block(part), block(i)] = piece.astype(BF16)


def store_rows(value, out, step, base):
    for i in range(4):
        for part in range(OWN):
            out[pl.ds(base + part * 4 + i, DEVICES, stride=step), :] = value[block(part), block(i)]


def mix_kernel(
    meta, message_ref, x_ref, cotangent, weight, weight_back, bias,
    out_ref, next_ref, active_ref, message, padded, out, low,
):
    message[...] = spread(message_ref[...])
    gather_active(message, 16, active_ref)
    mixed = dot(weight[0], active_ref[...]) + bias[:, 0:1]
    put_padded(padded, x_ref[...])
    for i in range(4):
        valid = valid_row(meta, i)
        value = rows_of_channels(padded, i) + mixed[:, block(i)] * valid
        next_ref[pl.ds(i, PADDED, stride=4), :] = value
        padded[pl.ds(i, PADDED, stride=4), :] = value * valid
    rows_to_message(padded, out, 24, 0)
    put_padded(padded, masked(meta, cotangent[...]))
    for i in range(4):
        low[:, block(i)] = rows_of_channels(padded, i).astype(BF16)
    store_rows(dot(weight_back[1], low[...]), out, 24, 12)
    out_ref[...] = out[...].reshape(DEVICES, 24, LANES).astype(BF16)


def forward_backward_kernel(
    message_ref, kernel_spec, own, len_ref, times, first, second, second_back, last, twiddle,
    out_ref, grad_out, norm_out,
    message, x_ref, high, low, e_high, e_low, y_ref, out, spec_ref, grad_ref, normed_ref, slope_ref,
):
    consts = (first, second, second_back, last, twiddle)
    message[...] = spread(message_ref[...])
    load_signals(message, 24, x_ref)
    convolve(x_ref, spec_ref, kernel_spec, high, low, e_high, e_low, consts, y_ref)
    valid, tally = valid_of(times, len_ref), tally_of(len_ref)
    inv = []
    for part in range(OWN):
        normed, inv_std, active, slope = normalise(y_ref, own, valid, tally, part)
        normed_ref[:, block(part, 512)] = normed
        slope_ref[:, block(part, 512)] = slope
        inv.append(inv_std)
        y_ref[:, block(part, 512)] = active
    store_signals(out, 24, 0, lambda part, y: y_ref[:, block(part * 4 + y)])
    returned, sums = conv_backward(
        message, 24, 12, lambda part: normed_ref[:, block(part, 512)], lambda part: slope_ref[:, block(part, 512)],
        lambda part: inv[part], own, valid, tally, spec_ref, kernel_spec, x_ref, high, low, e_high, e_low, consts, grad_ref,
    )
    store_signals(out, 24, 12, lambda part, y: returned[:, block(part * 4 + y)])
    for part in range(OWN):
        grad_out[block(part, 64), :] = returned[0:64, block(SIGNALS + part)]
    norm_out[...] = with_norm_sums(jnp.zeros((8, LANES), F32), sums)
    out_ref[...] = out[...].reshape(DEVICES, 24, LANES).astype(BF16)


def generate_back_kernel(grad, norm, columns, hidden_w, own, place_row, time_row, tab, hidden_out, outer_out, rows, sums, mats):
    hidden, outer = generate_back(
        lambda part: grad[block(part, 64), :], columns, hidden_w.at[1], own, place_row, time_row, tab, rows, sums, mats
    )
    hidden_out[...] = hidden
    outer_out[...] = outer + norm[...]


def middle_kernel(
    meta, message_ref, x_ref, cotangent, weight, weight_back, bias, active_0, hidden_1,
    output_ref, flow_ref, out_ref, message, padded, out, low_0, low_1, active_1,
):
    message[...] = spread(message_ref[...])
    gather_active(message, 24, active_1)
    mixed = dot(weight[1], active_1[...]) + bias[:, 1:2]
    for i in range(4):
        padded[pl.ds(i, PADDED, stride=4), :] = rows_of_channels(x_ref, i) + mixed[:, block(i)] * valid_row(meta, i)
    output_ref[...] = padded[0:CLIP_ROWS, :]
    put_padded(flow_ref, cotangent[...])
    for i in range(4):
        low_1[:, block(i)] = (rows_of_channels(flow_ref, i) * valid_row(meta, i)).astype(BF16)
    for m in range(12):
        padded[pl.ds(m, DEVICES, stride=12), :] = message[pl.ds(12 + m, DEVICES, stride=24), :]
    flow_ref[...] += masked(meta, padded[...])
    for i in range(4):
        low_0[:, block(i)] = (rows_of_channels(flow_ref, i) * valid_row(meta, i)).astype(BF16)
    store_rows(dot(weight_back[0], low_0[...]), out, 32, 0)
    for layer, (active, low) in enumerate(((active_0, low_0), (active_1, low_1))):
        part_sum = dot_rows(active[...], low[...])
        for part in range(OWN):
            for third in range(3):
                out[pl.ds(12 + layer * 9 + part * 3 + third, DEVICES, stride=32), :] = part_sum[
                    block(part), block(third)
                ]
    high, low = high_low(hidden_1[...])
    out[pl.ds(30, DEVICES, stride=32), :] = jnp.concatenate([high, jnp.zeros((96, LANES), F32)], axis=0)
    out[pl.ds(31, DEVICES, stride=32), :] = jnp.concatenate([low, jnp.zeros((96, LANES), F32)], axis=0)
    out_ref[...] = out[...].reshape(DEVICES, 32, LANES).astype(BF16)


LAST_ROWS = 56


def backward_kernel(
    message_ref, spec_ref, kernel_spec, normed_ref, slope_ref, inv_ref, len_ref, own, times,
    first, second, second_back, last, twiddle, columns, hidden_w, place_row, time_row, tab, outer_1,
    out_ref,
    message, x_ref, high, low, e_high, e_low, out, grad_ref, returned_ref, rows, sums, mats,
):
    consts = (first, second, second_back, last, twiddle)
    message[...] = spread(message_ref[...])
    valid, tally = valid_of(times, len_ref), tally_of(len_ref)
    returned, norm_sums = conv_backward(
        message, 32, 0, lambda part: normed_ref[:, block(part, 512)], lambda part: slope_ref[:, block(part, 512)],
        lambda part: inv_ref[part : part + 1, 0:1], own, valid, tally, spec_ref, kernel_spec, x_ref, high, low,
        e_high, e_low, consts, grad_ref,
    )
    returned_ref[...] = returned
    store_signals(out, 16, 0, lambda part, y: returned_ref[:, block(part * 4 + y)])
    hidden, outer = generate_back(
        lambda part: returned_ref[0:64, block(SIGNALS + part)], columns, hidden_w.at[0], own, place_row, time_row, tab,
        rows, sums, mats,
    )
    outer = with_norm_sums(outer, norm_sums)
    gathered = jnp.sum(message[...].reshape(DEVICES, 32, LANES), axis=0)
    upper, lower = packed_hidden(hidden)
    hidden_1_high, hidden_1_low = high_low(gathered[30:31, :] + gathered[31:32, :])
    outer_0_high, outer_0_low = high_low(one_row(outer))
    outer_1_high, outer_1_low = high_low(one_row(outer_1[...]))
    shared = jnp.concatenate(
        [
            gathered[0:30, :], upper, lower, hidden_1_high, hidden_1_low,
            outer_0_high, outer_0_low, outer_1_high, outer_1_low,
        ],
        axis=0,
    )
    row = lax.broadcasted_iota(jnp.int32, (DEVICES, 16, LANES), 1)
    own_rows = jnp.where(row < 12, out[...].reshape(DEVICES, 16, LANES), shared[None, 0:16, :])
    rest = jnp.broadcast_to(shared[None, 16:LAST_ROWS, :], (DEVICES, LAST_ROWS - 16, LANES))
    out_ref[...] = jnp.concatenate([own_rows, rest], axis=1).astype(BF16)


def last_kernel(
    meta, message_ref, flow_ref, lookup,
    input_grad, gabor_grad, hidden_w_grad, hidden_b_grad, out_w_grad, out_b_grad, gain_grad, bias_grad,
    mix_w_grad, mix_b_grad, message, padded, owned, thirds,
):
    message[...] = spread(message_ref[...])

    def rows_of(k, count=DEVICES):
        return message[pl.ds(k, count, stride=LAST_ROWS), :]

    for m in range(12):
        padded[pl.ds(m, DEVICES, stride=12), :] = rows_of(m)
    input_grad[...] = flow_ref[0:CLIP_ROWS, :] + masked(meta, padded[0:CLIP_ROWS, :])
    shared = jnp.sum(message[...].reshape(DEVICES, LAST_ROWS, LANES)[:, 24:56, :], axis=0)
    hidden_0 = unpacked_hidden(shared[6:22, :], shared[22:26, :])
    hidden_1 = rows_of(50, 32) + rows_of(51, 32)
    lane = lax.broadcasted_iota(jnp.int32, (DEVICES, LANES), 1)
    for layer, hidden in enumerate((hidden_0, hidden_1)):
        hidden_w_grad[layer, 0] = hidden[:, 0:32]
        hidden_w_grad[layer, 1] = pltpu.roll(hidden, 96, 1)[:, 0:32]
        turned = jnp.transpose(jnp.concatenate([hidden, jnp.zeros((96, LANES), F32)], axis=0))
        hidden_b_grad[layer] = turned[64:66, 0:32]
        for j in range(3):
            gabor_grad[layer, j] = turned[66 + 4 * j : 70 + 4 * j, 0:32]
        value = rows_of(52 + 2 * layer) + rows_of(53 + 2 * layer)
        for part in range(OWN):
            wide = pltpu.roll(value, (LANES - 32 * part) % LANES, 1)
            small = pltpu.roll(value, 64 - 3 * part, 1)
            owned[pl.ds(part, DEVICES, stride=OWN), :] = jnp.where(lane < 32, wide, small)
        turned = jnp.transpose(owned[...])
        out_w_grad[layer] = turned[0:32, 0:CHANNELS]
        out_b_grad[layer : layer + 1, :] = turned[32:33, 0:CHANNELS]
        gain_grad[layer : layer + 1, :] = turned[33:34, 0:CHANNELS]
        bias_grad[layer : layer + 1, :] = turned[34:35, 0:CHANNELS]
        bias_rows = []
        for part in range(OWN):
            for third in range(3):
                piece = rows_of(12 + layer * 9 + part * 3 + third)
                thirds[block(part), block(third)] = piece.astype(BF16)
                if part == 2:
                    bias_rows.append(piece[SPOT - 2 * DEVICES : SPOT - 2 * DEVICES + 1, :])
        mix_w_grad[layer] = dot_columns(thirds[...], lookup[...])[0:CHANNELS, 0:CHANNELS]
        mix_b_grad[layer : layer + 1, :] = jnp.concatenate(bias_rows, axis=1)[:, 0:CHANNELS]


def exchange(message):
    return lax.all_to_all(message, AXES, split_axis=0, concat_axis=0, tiled=True)


def to_rows(clips):
    return clips.reshape(2, CHANNELS, 2, LANES).transpose(1, 2, 0, 3).reshape(CLIP_ROWS, LANES)


def from_rows(rows):
    return rows.reshape(CHANNELS, 2, 2, LANES).transpose(2, 0, 1, 3).reshape(2, CHANNELS, PIECE)


def shards(
    inputs, lengths, window, gabor_params, hidden_w, hidden_b, out_w, out_b, bn_gain, bn_bias, mix_w, mix_b, cotangent
):
    position = lax.axis_index("seq").astype(jnp.int32)
    number = position * 4 + lax.axis_index("clips").astype(jnp.int32)
    const = {name: jnp.asarray(value) for name, value in TABLES.items()}
    meta = jnp.concatenate([lengths, jnp.stack([position, number])])
    inputs, cotangent = to_rows(inputs), to_rows(cotangent)

    def rows(count):
        return ((count, LANES), F32)

    with jax.named_scope("source_0"):
        (message,) = run(
            source_kernel, [((DEVICES, 16, LANES), BF16)], [meta, inputs], [rows(PADDED_ROWS), rows(DEVICES * 16)],
            "source_0", 8, smem=(0,),
        )
        message = exchange(message)

    owns = [
        meta, jnp.swapaxes(out_w, 1, 2), out_b, jnp.swapaxes(window, 1, 2), bn_gain, bn_bias, gabor_params, hidden_b,
        hidden_w, const["place_row"], const["time_row"], const["starts"], const["first"], const["second"],
        const["twiddle"],
    ]

    def generator(layer):
        return run(
            generate_kernel(layer),
            [((8, HIDDEN, SAMPLES), F32), ((OWN * LANES, 2 * LANES), F32), rows(8), rows(HIDDEN)],
            owns,
            [
                ((LANES, PADDED), F32), rows(PADDED + 8), ((8, SAMPLES), F32), rows(192),
                ((256, OWN * LANES), BF16), ((OWN * LANES, 256), BF16), ((OWN * LANES, 256), BF16),
            ],
            f"generator_{layer}", 10, smem=(0,),
        )

    with jax.named_scope("generators"):
        tab_0, spec_k0, own_0, columns_0 = generator(0)
        tab_1, spec_k1, own_1, columns_1 = generator(1)

    square = (PADDED, PADDED)
    with jax.named_scope("weights"):
        weight, weight_back, bias = run(
            weights_kernel, [((2, *square), BF16), ((2, *square), BF16), rows(PADDED)], [mix_w, mix_b, const["lookup"]],
            [(square, BF16)], "weights", 8,
        )

    def scratch(signals):
        count = signals * LANES
        return [
            ((256, SIGNALS * LANES), BF16), ((count, 256), BF16), ((count, 256), BF16),
            ((256, count), BF16), ((256, count), BF16),
        ]

    shape_y = (LANES, SIGNALS * LANES)
    shape_s = (SIGNALS * LANES, 256)
    transforms = [const[name] for name in ("first", "second", "second_back", "last", "twiddle")]
    with jax.named_scope("conv_0"):
        message, spec_0, normed_0, slope_0, inv_0, lens = run(
            forward_kernel,
            [
                ((DEVICES, 16, LANES), BF16), (shape_s, F32), (shape_y, F32), (shape_y, F32), rows(8), rows(8),
            ],
            [message, spec_k0, own_0, const["times"], *transforms],
            [rows(DEVICES * 16), *scratch(SIGNALS), (shape_y, F32), rows(DEVICES * 16)],
            "conv_0", 20,
        )
        message = exchange(message)

    with jax.named_scope("mix_0"):
        message, middle, active_0 = run(
            mix_kernel,
            [((DEVICES, 24, LANES), BF16), rows(PADDED_ROWS), ((PADDED, 512), BF16)],
            [meta, message, inputs, cotangent, weight, weight_back, bias],
            [rows(DEVICES * 16), rows(PADDED_ROWS), rows(DEVICES * 24), ((PADDED, 512), BF16)],
            "mix_0", 12, smem=(0,),
        )
        message = exchange(message)

    with jax.named_scope("conv_1"):
        message, kernel_grad_1, norm_1 = run(
            forward_backward_kernel,
            [((DEVICES, 24, LANES), BF16), rows(OWN * 64), rows(8)],
            [message, spec_k1, own_1, lens, const["times"], *transforms],
            [
                rows(DEVICES * 24), *scratch(SIGNALS + OWN), (shape_y, F32), rows(DEVICES * 24),
                (shape_s, F32), (shape_s, F32), (shape_y, F32), (shape_y, F32),
            ],
            "conv_1", 26,
        )
        message = exchange(message)

    back_scratch = [((8, SAMPLES), F32), rows(14 * 32 + 8), rows(72)]
    with jax.named_scope("generator_back_1"):
        hidden_1, outer_1 = run(
            generate_back_kernel,
            [rows(HIDDEN), rows(8)],
            [kernel_grad_1, norm_1, columns_1, hidden_w, own_1, const["place_row"], const["time_row"], tab_1],
            back_scratch, "generator_back_1", 8,
        )

    with jax.named_scope("mix_1"):
        outputs, flow, message = run(
            middle_kernel,
            [rows(CLIP_ROWS), rows(PADDED_ROWS), ((DEVICES, 32, LANES), BF16)],
            [meta, message, middle, cotangent, weight, weight_back, bias, active_0, hidden_1],
            [
                rows(DEVICES * 24), rows(PADDED_ROWS), rows(DEVICES * 32),
                ((PADDED, 512), BF16), ((PADDED, 512), BF16), ((PADDED, 512), BF16),
            ],
            "mix_1", 12, smem=(0,),
        )
        message = exchange(message)

    with jax.named_scope("conv_back_0"):
        (message,) = run(
            backward_kernel,
            [((DEVICES, LAST_ROWS, LANES), BF16)],
            [
                message, spec_0, spec_k0, normed_0, slope_0, inv_0, lens, own_0, const["times"], *transforms,
                columns_0, hidden_w, const["place_row"], const["time_row"], tab_0, outer_1,
            ],
            [
                rows(DEVICES * 32), *scratch(SIGNALS + OWN), rows(DEVICES * 16), (shape_s, F32),
                ((LANES, (SIGNALS + OWN) * LANES), F32), *back_scratch,
            ],
            "conv_back_0", 26,
        )
        message = exchange(message)

    with jax.named_scope("gradients"):
        (
            input_grad, gabor_grad, hidden_w_grad, hidden_b_grad, out_w_grad, out_b_grad, gain_grad, bias_grad,
            mix_w_grad, mix_b_grad,
        ) = run(
            last_kernel,
            [
                rows(CLIP_ROWS), (gabor_params.shape, F32), (hidden_w.shape, F32), (hidden_b.shape, F32),
                ((2, HIDDEN, CHANNELS), F32), (out_b.shape, F32), (bn_gain.shape, F32), (bn_bias.shape, F32),
                (mix_w.shape, F32), (mix_b.shape, F32),
            ],
            [meta, message, flow, const["lookup"]],
            [rows(DEVICES * LAST_ROWS), rows(PADDED_ROWS), rows(PADDED), (square, BF16)],
            "gradients", 14, smem=(0,),
        )
    return (
        from_rows(outputs), from_rows(input_grad), gabor_grad, hidden_w_grad, hidden_b_grad,
        jnp.swapaxes(out_w_grad, 1, 2), out_b_grad, gain_grad, bias_grad, mix_w_grad, mix_b_grad,
    )


def solution(mesh):
    clip = P("clips", None, "seq")
    in_specs = (clip, P("clips")) + (P(),) * 10 + (clip,)
    out_specs = (clip, clip) + (P(),) * 9
    return jax.shard_map(shards, mesh=mesh, in_specs=in_specs, out_specs=out_specs, check_vma=False)
```

```python
import math

import jax
import jax.numpy as jnp
import ml_dtypes
import numpy as np
from jax import lax
from jax.experimental import pallas as pl
from jax.experimental.pallas import tpu as pltpu
from jax.sharding import PartitionSpec as P

F32 = jnp.float32
BF16 = jnp.bfloat16
AXES = ("seq", "clips")
DEVICES = 128
OWN = 3
CHANNELS = 380
PADDED = DEVICES * OWN
SAMPLES = 8192
PIECE = 256
HIDDEN = 32
LANES = 128
SIGNALS = 12
PERIOD = 2 * SAMPLES
EPSILON = 1e-05
MEGABYTE = 1024 * 1024
EXACT = lax.Precision.HIGHEST
SPOT = 2 * DEVICES + 126


def halves(table):
    high = table.astype(ml_dtypes.bfloat16)
    low = (table - high.astype(np.float64)).astype(ml_dtypes.bfloat16)
    return high, low


def tables():
    order = np.array([2 * j + r for r in range(2) for j in range(32)])
    k = np.arange(LANES)
    turn = 2 * np.pi * ((k[:, None] * order[None, :]) % LANES) / LANES
    c_high, c_low = halves(np.cos(turn))
    s_high, s_low = halves(np.sin(turn))
    first = np.concatenate(
        [
            np.concatenate([c_high, c_low, s_high, s_low], axis=1),
            np.concatenate([-s_high, -s_low, c_high, c_low], axis=1),
        ],
        axis=0,
    )
    turn = 2 * np.pi * ((k[:, None] * k[None, :]) % LANES) / LANES
    cosine, sine = np.cos(turn), np.sin(turn)
    second = halves(np.block([[cosine, -sine], [sine, cosine]]))
    second_back = halves(np.block([[cosine, sine], [-sine, cosine]]))
    turn = 2 * np.pi * ((order[:, None] * k[None, :]) % LANES) / LANES
    cosine, sine = np.cos(turn) / PERIOD, np.sin(turn) / PERIOD
    last = halves(np.block([[cosine, -sine], [sine, cosine]]))
    turn = 2 * np.pi * (k[:, None] * k[None, :]) / PERIOD
    twiddle = np.stack([np.cos(turn), np.sin(turn)]).astype(np.float32)
    times = (128 * order[:, None] + k[None, :]).astype(np.float32)
    places = (-1.0 + 2.0 * times / np.float32(SAMPLES - 1)).astype(np.float32)
    lookup = np.zeros((PADDED, PADDED), ml_dtypes.bfloat16)
    for part in range(OWN):
        for owner in range(DEVICES):
            lookup[part * DEVICES + owner, OWN * owner + part] = 1
    return dict(
        first=first,
        second=np.stack(second),
        second_back=np.stack(second_back),
        last=np.stack(last),
        twiddle=twiddle,
        times=np.concatenate([times, times], axis=0),
        time_row=times.reshape(1, SAMPLES),
        place_row=places.reshape(1, SAMPLES),
        starts=np.stack([np.pad(places[:, 0], (0, 64)), 2.0 * k / (SAMPLES - 1)]).astype(np.float32),
        lookup=lookup,
    )


TABLES = tables()


def run(body, outs, args, scratch, name, grant, smem=()):
    return pl.pallas_call(
        body,
        out_shape=[jax.ShapeDtypeStruct(shape, kind) for shape, kind in outs],
        in_specs=[
            pl.BlockSpec(memory_space=pltpu.SMEM if i in smem else pltpu.VMEM) for i in range(len(args))
        ],
        out_specs=[pl.BlockSpec(memory_space=pltpu.VMEM)] * len(outs),
        scratch_shapes=[pltpu.VMEM(shape, kind) for shape, kind in scratch],
        compiler_params=pltpu.CompilerParams(vmem_limit_bytes=grant * MEGABYTE),
        name=name,
    )(*args)


def dot(a, b):
    return jnp.dot(a, b, preferred_element_type=F32)


def dot_rows(a, b, precision=None):
    return lax.dot_general(a, b, (((1,), (1,)), ((), ())), precision=precision, preferred_element_type=F32)


def dot_columns(a, b, precision=None):
    return lax.dot_general(a, b, (((0,), (0,)), ((), ())), precision=precision, preferred_element_type=F32)


def triple(a_high, a_low, b_high, b_low):
    left = jnp.concatenate([a_high, a_low, a_high], axis=1)
    return dot(left, jnp.concatenate([b_high, b_high, b_low], axis=0))


def put_halves(high_ref, low_ref, rows, columns, value):
    high = value.astype(BF16)
    high_ref[rows, columns] = high
    low_ref[rows, columns] = (value - high.astype(F32)).astype(BF16)


def block(i, size=LANES):
    return slice(i * size, (i + 1) * size)


RE, IM = slice(0, LANES), slice(LANES, 2 * LANES)


def signal_row(b, part, r):
    return part * 4 + r * 2 + b


def spread(message):
    return message.astype(F32).reshape(-1, LANES)


def transform(x_ref, high_ref, low_ref, first, second, twiddle, count):
    part_a = dot(first[...], x_ref[:, : count * LANES])
    cosine, sine = twiddle[0], twiddle[1]
    for s in range(count):
        real, imag = part_a[:LANES, block(s)], part_a[LANES:, block(s)]
        put_halves(high_ref, low_ref, block(s), RE, real * cosine + imag * sine)
        put_halves(high_ref, low_ref, block(s), IM, imag * cosine - real * sine)
    rows = slice(0, count * LANES)
    return triple(high_ref[rows, :], low_ref[rows, :], second[0], second[1])


def transform_back(high_ref, low_ref, e_high, e_low, second_back, last, twiddle, count):
    rows = slice(0, count * LANES)
    part_d = triple(high_ref[rows, :], low_ref[rows, :], second_back[0], second_back[1])
    cosine, sine = twiddle[0], twiddle[1]
    for s in range(count):
        real, imag = part_d[block(s), RE], part_d[block(s), IM]
        put_halves(e_high, e_low, RE, block(s), real * cosine - imag * sine)
        put_halves(e_high, e_low, IM, block(s), real * sine + imag * cosine)
    return triple(last[0], last[1], e_high[:, rows], e_low[:, rows])


def erf_parts(value):
    cdf = 0.5 * (1.0 + lax.erf(value * math.sqrt(0.5)))
    return cdf, jnp.exp(-0.5 * value * value) * (1.0 / math.sqrt(2.0 * math.pi))


def total(value):
    return jnp.sum(jnp.sum(value, axis=0, keepdims=True), axis=1, keepdims=True)


def valid_of(times, len_ref):
    columns = []
    for y in range(4):
        upper = times[0:64, :] < len_ref[2 * y : 2 * y + 1, :]
        lower = times[64:128, :] < len_ref[2 * y + 1 : 2 * y + 2, :]
        columns.append(jnp.concatenate([upper, lower], axis=0).astype(F32))
    return jnp.concatenate(columns, axis=1)


def tally_of(len_ref):
    return jnp.sum(len_ref[:, 0:1], axis=0, keepdims=True)


def load_signals(message, step, x_ref):
    for part in range(OWN):
        for y in range(4):
            lanes = block(part * 4 + y)
            for b in range(2):
                for r in range(2):
                    start = y * step + signal_row(b, part, r)
                    piece = message[pl.ds(start, 32, stride=4 * step), :].astype(BF16)
                    x_ref[b * 128 + r * 32 : b * 128 + r * 32 + 32, lanes] = piece
                    x_ref[b * 128 + r * 32 + 64 : b * 128 + r * 32 + 96, lanes] = piece


def store_signals(out, step, base, get):
    for part in range(OWN):
        for y in range(4):
            value = get(part, y)
            for b in range(2):
                for r in range(2):
                    start = y * step + base + signal_row(b, part, r)
                    out[pl.ds(start, 32, stride=4 * step), :] = value[b * 64 + r * 32 : b * 64 + r * 32 + 32, :]


def convolve(x_ref, spec_ref, kernel_spec, high, low, e_high, e_low, consts, y_ref):
    first, second, second_back, last, twiddle = consts
    spec_ref[...] = transform(x_ref, high, low, first, second, twiddle, SIGNALS)
    for part in range(OWN):
        k_re, k_im = kernel_spec[block(part), RE], kernel_spec[block(part), IM]
        for y in range(4):
            rows = block(part * 4 + y)
            s_re, s_im = spec_ref[rows, RE], spec_ref[rows, IM]
            put_halves(high, low, rows, RE, s_re * k_re - s_im * k_im)
            put_halves(high, low, rows, IM, s_re * k_im + s_im * k_re)
    y_ref[...] = transform_back(high, low, e_high, e_low, second_back, last, twiddle, SIGNALS)


def normalise(y_ref, own, valid, tally, part):
    value = y_ref[:, block(part, 512)]
    mean = total(valid * value) / tally
    centred = value - mean
    var = total(valid * centred * centred) / tally
    inv_std = lax.rsqrt(var + EPSILON)
    normed = centred * inv_std
    pre_act = normed * own[part : part + 1, 35:36] + own[part : part + 1, 36:37]
    cdf, density = erf_parts(pre_act)
    return normed, inv_std, pre_act * cdf, cdf + pre_act * density


def conv_backward(
    message, step, base, normed_of, slope_of, inv_of, own, valid, tally, spec_ref, kernel_spec, x_ref, high, low,
    e_high, e_low, consts, grad_ref,
):
    first, second, second_back, last, twiddle = consts
    sums = []
    for part in range(OWN):
        columns = []
        for y in range(4):
            pieces = []
            for b in range(2):
                for r in range(2):
                    start = y * step + base + signal_row(b, part, r)
                    pieces.append(message[pl.ds(start, 32, stride=4 * step), :])
            columns.append(jnp.concatenate(pieces, axis=0))
        act_grad = jnp.concatenate(columns, axis=1)
        normed = normed_of(part)
        pre_grad = act_grad * slope_of(part)
        bias_total = total(pre_grad)
        gain_total = total(pre_grad * normed)
        gain = own[part : part + 1, 35:36]
        conv_grad = inv_of(part) * (
            gain * pre_grad - valid * (gain * bias_total + normed * (gain * gain_total)) / tally
        )
        conv_low = conv_grad.astype(BF16)
        for b in range(2):
            piece = conv_low[b * 64 : b * 64 + 64, :]
            x_ref[b * 128 : b * 128 + 64, block(part, 512)] = piece
            x_ref[b * 128 + 64 : b * 128 + 128, block(part, 512)] = piece
        sums.append((gain_total, bias_total))
    grad_ref[...] = transform(x_ref, high, low, first, second, twiddle, SIGNALS)
    for part in range(OWN):
        k_re, k_im = kernel_spec[block(part), RE], kernel_spec[block(part), IM]
        corr_re, corr_im = None, None
        for y in range(4):
            rows = block(part * 4 + y)
            g_re, g_im = grad_ref[rows, RE], grad_ref[rows, IM]
            s_re, s_im = spec_ref[rows, RE], spec_ref[rows, IM]
            put_halves(high, low, rows, RE, k_re * g_re + k_im * g_im)
            put_halves(high, low, rows, IM, k_re * g_im - k_im * g_re)
            now_re, now_im = s_re * g_re + s_im * g_im, s_re * g_im - s_im * g_re
            corr_re = now_re if corr_re is None else corr_re + now_re
            corr_im = now_im if corr_im is None else corr_im + now_im
        put_halves(high, low, block(SIGNALS + part), RE, corr_re)
        put_halves(high, low, block(SIGNALS + part), IM, corr_im)
    returned = transform_back(high, low, e_high, e_low, second_back, last, twiddle, SIGNALS + OWN)
    return returned, sums


def sin_cos(angle):
    turns = jnp.floor(angle * (2.0 / math.pi) + 0.5)
    rest = angle - turns * 1.5703125
    rest = rest - turns * 4.837512969970703125e-4
    rest = rest - turns * 7.549789948768648e-8
    square = rest * rest
    sine = rest + rest * square * (
        -1.6666654611e-1 + square * (8.3321608736e-3 + square * -1.9515295891e-4)
    )
    cosine = 1.0 - 0.5 * square + square * square * (
        4.166664568298827e-2 + square * (-1.388731625493765e-3 + square * 2.443315711809948e-5)
    )
    half = jnp.floor(turns * 0.5)
    odd = turns - 2.0 * half
    sign = 1.0 - 2.0 * (half - 2.0 * jnp.floor(half * 0.5))
    is_odd = odd > 0.5
    return sign * jnp.where(is_odd, cosine, sine), sign * jnp.where(is_odd, -sine, cosine)


CHUNK = 1024


def envelope_of(times, own):
    lower, upper = own[:, 33:34], own[:, 34:35]
    inside = (times >= lower) & (times < upper)
    offset = (times - lower) / (0.5 * (upper - lower))
    return jnp.where(inside, jnp.exp(-0.5 * offset * offset), 0.0)


def stacked_weight(weight):
    high, low = high_low(weight)
    return jnp.concatenate([high, high, low], axis=1).astype(BF16)


def stacked_dot(weight, value):
    high = value.astype(BF16)
    low = (value - high.astype(F32)).astype(BF16)
    return dot(weight, jnp.concatenate([high, low, high], axis=0))


def own_parameters(layer, number, out_w, out_b, window, gain, bias, gabor, hidden_b, wide, tall, own, columns):
    wide[...] = jnp.zeros(wide.shape, F32)
    wide[0:32, 0:CHANNELS] = out_w[layer]
    wide[32:33, 0:CHANNELS] = out_b[layer : layer + 1, :]
    wide[33:35, 0:CHANNELS] = window[layer].astype(F32)
    wide[35:36, 0:CHANNELS] = gain[layer : layer + 1, :]
    wide[36:37, 0:CHANNELS] = bias[layer : layer + 1, :]
    tall[0:PADDED, :] = jnp.transpose(wide[...])
    tall[PADDED : PADDED + 8, :] = jnp.zeros((8, LANES), F32)
    row = lax.broadcasted_iota(jnp.int32, (8, LANES), 0)
    lane = lax.broadcasted_iota(jnp.int32, (8, LANES), 1)
    mine = tall[pl.ds(number * OWN, 8), :]
    unused = (row >= OWN) | (number * OWN + row >= CHANNELS)
    own[...] = jnp.where(unused, jnp.where(lane == 34, float(SAMPLES), 0.0), mine)
    wide[:, 0:LANES] = jnp.zeros((LANES, LANES), F32)
    for j in range(3):
        wide[4 * j : 4 * j + 4, 0:HIDDEN] = gabor[layer, j]
    wide[12:14, 0:HIDDEN] = hidden_b[layer]
    columns[...] = jnp.transpose(wide[:, 0:LANES])[0:HIDDEN, :]


def chunk_span(i):
    return pl.ds(pl.multiple_of(i * CHUNK, CHUNK), CHUNK)


def generate(columns, hidden_w, own, place_row, time_row, starts, tab, rows):
    waves = []
    for j in range(3):
        frequency, phase = columns[:, 4 * j + 2 : 4 * j + 3], columns[:, 4 * j + 3 : 4 * j + 4]
        waves.append((sin_cos(frequency * starts[0:1, :] + phase), sin_cos(frequency * starts[1:2, :])))
    weights = [stacked_weight(hidden_w[0]), stacked_weight(hidden_w[1]), stacked_weight(own[:, 0:32])]

    def step(i, carry):
        span = chunk_span(i)
        places = place_row[:, span]

        def level(j):
            (start_sin, start_cos), (rest_sin, rest_cos) = waves[j]
            shift = (LANES - i * (CHUNK // LANES)) % LANES
            start_sin, start_cos = pltpu.roll(start_sin, shift, 1), pltpu.roll(start_cos, shift, 1)
            sine, cosine = [], []
            for n in range(CHUNK // LANES):
                s_n, c_n = start_sin[:, n : n + 1], start_cos[:, n : n + 1]
                sine.append(s_n * rest_cos + c_n * rest_sin)
                cosine.append(c_n * rest_cos - s_n * rest_sin)
            width = columns[:, 4 * j : 4 * j + 1] * (places - columns[:, 4 * j + 1 : 4 * j + 2])
            bell = jnp.exp(-0.5 * width * width)
            return bell * jnp.concatenate(sine, axis=1), bell * jnp.concatenate(cosine, axis=1)

        f_0, c_0 = level(0)
        tab[0, :, span] = f_0
        tab[1, :, span] = c_0
        u_1 = stacked_dot(weights[0], f_0) + columns[:, 12:13]
        f_1, c_1 = level(1)
        z_1 = u_1 * f_1
        tab[2, :, span] = z_1
        tab[3, :, span] = u_1 * c_1
        tab[4, :, span] = f_1
        u_2 = stacked_dot(weights[1], z_1) + columns[:, 13:14]
        f_2, c_2 = level(2)
        z_2 = u_2 * f_2
        tab[5, :, span] = z_2
        tab[6, :, span] = u_2 * c_2
        tab[7, :, span] = f_2
        raw = stacked_dot(weights[2], z_2) + own[:, 32:33]
        rows[:, span] = raw * envelope_of(time_row[:, span], own)
        return carry

    lax.fori_loop(0, SAMPLES // CHUNK, step, 0)


def generate_back(kernel_grad, columns, hidden_w, own, place_row, time_row, tab, rows, sums, mats):
    rows[...] = jnp.zeros(rows.shape, F32)
    for part in range(OWN):
        grad = kernel_grad(part)
        for n in range(64):
            rows[part : part + 1, block(n)] = grad[n : n + 1, :]
    sums[...] = jnp.zeros(sums.shape, F32)
    mats[...] = jnp.zeros(mats.shape, F32)
    turned = jnp.transpose(jnp.concatenate([own[...], jnp.zeros((120, 128), F32)], axis=0))
    weight = [turned[0:32, part : part + 1] for part in range(OWN)]
    back = [stacked_weight(jnp.transpose(hidden_w[j])) for j in range(2)]

    def fold(value):
        acc = value[:, block(0)]
        for i in range(1, CHUNK // LANES):
            acc = acc + value[:, block(i)]
        return acc

    def add(k, value):
        sums[block(k, 32), :] += fold(value)

    def step(i, carry):
        span = chunk_span(i)
        places = place_row[:, span]
        draw = rows[:, span] * envelope_of(time_row[:, span], own)
        dz_2 = weight[0] * draw[0:1, :] + weight[1] * draw[1:2, :] + weight[2] * draw[2:3, :]

        def level(j, e_value, g_value):
            centre = columns[:, 4 * j + 1 : 4 * j + 2]
            offset = places - centre
            moment = e_value * offset
            add(4 * j, moment * offset)
            add(4 * j + 1, moment)
            add(4 * j + 2, g_value * places)
            add(4 * j + 3, g_value)

        z_2 = tab[5, :, span]
        level(2, dz_2 * z_2, dz_2 * tab[6, :, span])
        du_2 = dz_2 * tab[7, :, span]
        add(13, du_2)
        dz_1 = stacked_dot(back[1], du_2)
        z_1 = tab[2, :, span]
        level(1, dz_1 * z_1, dz_1 * tab[3, :, span])
        du_1 = dz_1 * tab[4, :, span]
        add(12, du_1)
        dz_0 = stacked_dot(back[0], du_1)
        z_0 = tab[0, :, span]
        level(0, dz_0 * z_0, dz_0 * tab[1, :, span])
        sums[14 * 32 : 14 * 32 + 8, :] += fold(draw)
        left = jnp.concatenate([du_1, du_2, draw], axis=0)
        right = jnp.concatenate([z_0, z_1, z_2, jnp.zeros_like(z_0)], axis=0)
        left_high, right_high = left.astype(BF16), right.astype(BF16)
        left_low = (left - left_high.astype(F32)).astype(BF16)
        right_low = (right - right_high.astype(F32)).astype(BF16)
        mats[...] += (
            dot_rows(left_high, right_high) + dot_rows(left_low, right_high) + dot_rows(left_high, right_low)
        )
        return carry

    lax.fori_loop(0, SAMPLES // CHUNK, step, 0)
    lane = lax.broadcasted_iota(jnp.int32, (32, LANES), 1)
    hidden = jnp.where(lane < 32, mats[0:32, :], jnp.where(lane < 64, mats[32:64, :], 0.0))

    def column(k):
        return jnp.sum(sums[block(k, 32), :], axis=1, keepdims=True)

    hidden = jnp.where(lane == 64, column(12), hidden)
    hidden = jnp.where(lane == 65, column(13), hidden)
    for j in range(3):
        sharpness = columns[:, 4 * j : 4 * j + 1]
        hidden = jnp.where(lane == 66 + 4 * j, -sharpness * column(4 * j), hidden)
        hidden = jnp.where(lane == 67 + 4 * j, sharpness * sharpness * column(4 * j + 1), hidden)
        hidden = jnp.where(lane == 68 + 4 * j, column(4 * j + 2), hidden)
        hidden = jnp.where(lane == 69 + 4 * j, column(4 * j + 3), hidden)
    lane8 = lax.broadcasted_iota(jnp.int32, (8, LANES), 1)
    outer = pltpu.roll(mats[64:72, :], LANES - 64, 1)
    raw_total = jnp.sum(sums[14 * 32 : 14 * 32 + 8, :], axis=1, keepdims=True)
    outer = jnp.where(lane8 < 32, outer, 0.0)
    outer = jnp.where(lane8 == 32, raw_total, outer)
    return hidden, outer


def with_norm_sums(outer, sums):
    row = lax.broadcasted_iota(jnp.int32, (8, LANES), 0)
    lane = lax.broadcasted_iota(jnp.int32, (8, LANES), 1)
    for part in range(OWN):
        gain_total, bias_total = sums[part]
        outer = jnp.where((row == part) & (lane == 33), gain_total, outer)
        outer = jnp.where((row == part) & (lane == 34), bias_total, outer)
    return outer


def one_row(outer):
    lane = lax.broadcasted_iota(jnp.int32, (1, LANES), 1)
    result = jnp.zeros((1, LANES), F32)
    for part in range(OWN):
        row = outer[part : part + 1, :]
        moved = pltpu.roll(row, 32 * part, 1) if part else row
        result = jnp.where((lane >= 32 * part) & (lane < 32 * part + 32), moved, result)
        moved = pltpu.roll(row, 64 + 3 * part, 1)
        result = jnp.where((lane >= 96 + 3 * part) & (lane < 99 + 3 * part), moved, result)
    return result


def packed_hidden(hidden):
    lane16 = lax.broadcasted_iota(jnp.int32, (16, LANES), 1)
    upper = jnp.where(lane16 < 64, hidden[0:16, :], pltpu.roll(hidden[16:32, :], 64, 1))
    lane4 = lax.broadcasted_iota(jnp.int32, (4, LANES), 1)
    lower = jnp.zeros((4, LANES), F32)
    for g in range(8):
        moved = pltpu.roll(hidden, (64 + 16 * g) % LANES, 1)[4 * g : 4 * g + 4, :]
        lower = jnp.where((lane4 >= 16 * g) & (lane4 < 16 * g + 16), moved, lower)
    return upper, lower


def unpacked_hidden(upper, lower):
    lane16 = lax.broadcasted_iota(jnp.int32, (16, LANES), 1)
    lane32 = lax.broadcasted_iota(jnp.int32, (32, LANES), 1)
    top = jnp.concatenate([upper, pltpu.roll(upper, 64, 1)], axis=0)
    tiled = jnp.concatenate([lower] * 8, axis=0)
    row32 = lax.broadcasted_iota(jnp.int32, (32, LANES), 0)
    rest = jnp.zeros((32, LANES), F32)
    for g in range(8):
        moved = pltpu.roll(tiled, (64 - 16 * g) % LANES, 1)
        rest = jnp.where((row32 >= 4 * g) & (row32 < 4 * g + 4), moved, rest)
    return jnp.where(lane32 < 64, top, rest)


def high_low(value):
    high = value.astype(BF16).astype(F32)
    return high, value - high


def valid_row(meta, i):
    lane = lax.broadcasted_iota(jnp.int32, (1, LANES), 1)
    return (meta[2] * PIECE + (i // 2) * LANES + lane < meta[i % 2]).astype(F32)


def masked(meta, rows):
    mask = jnp.concatenate([valid_row(meta, i) for i in range(4)] * 2, axis=0)
    return (rows.reshape(-1, 8, LANES) * mask[None]).reshape(-1, LANES)


CLIP_ROWS = 4 * CHANNELS
PADDED_ROWS = 4 * PADDED


def put_padded(padded, rows):
    padded[0:CLIP_ROWS, :] = rows
    padded[CLIP_ROWS:PADDED_ROWS, :] = jnp.zeros((PADDED_ROWS - CLIP_ROWS, LANES), F32)


def rows_to_message(padded, out, step, base):
    for m in range(12):
        out[pl.ds(base + m, DEVICES, stride=step), :] = padded[pl.ds(m, DEVICES, stride=12), :]


def rows_of_channels(padded, i):
    return padded[pl.ds(i, PADDED, stride=4), :]


def source_kernel(meta, x_ref, own_0, own_1, bias, out_ref, padded, out):
    put_padded(padded, masked(meta, x_ref[...]))
    for b in range(2):
        length = meta[b]
        upper = lax.shift_right_logical(length, 7)
        out[pl.ds(12 + 2 * b, DEVICES, stride=16), :] = jnp.full((DEVICES, LANES), upper.astype(F32))
        out[pl.ds(13 + 2 * b, DEVICES, stride=16), :] = jnp.full(
            (DEVICES, LANES), (length - upper * 128).astype(F32)
        )
    rows_to_message(padded, out, 16, 0)
    out_ref[...] = out[...].reshape(DEVICES, 16, LANES).astype(BF16)


def weights_kernel(mix_w, mix_b, lookup, weight, weight_back, bias, wide):
    for layer in range(2):
        wide[...] = jnp.zeros(wide.shape, BF16)
        wide[0:CHANNELS, 0:CHANNELS] = mix_w[layer]
        weight[layer] = dot_rows(wide[...], lookup[...]).astype(BF16)
        weight_back[layer] = dot_rows(lookup[...], wide[...]).astype(BF16)
    row = lax.broadcasted_iota(jnp.int32, (LANES, CHANNELS), 0)
    both = jnp.where(row == 0, mix_b[0:1, :], jnp.where(row == 1, mix_b[1:2, :], 0.0))
    bias[...] = jnp.transpose(jnp.concatenate([both, jnp.zeros((LANES, PADDED - CHANNELS), F32)], axis=1))


def generate_kernel(layer):
    def body(
        meta, out_w, out_b, window, gain, bias, gabor, hidden_b, hidden_w, place_row, time_row, starts,
        first, second, twiddle,
        tab, spec, own, columns,
        wide, tall, rows, pieces, x_ref, high, low,
    ):
        own_parameters(layer, meta[3], out_w, out_b, window, gain, bias, gabor, hidden_b, wide, tall, own, columns)
        generate(columns, hidden_w.at[layer], own, place_row, time_row, starts, tab, rows)
        for n in range(64):
            for part in range(OWN):
                pieces[part * 64 + n : part * 64 + n + 1, :] = rows[part : part + 1, block(n)]
        for part in range(OWN):
            piece = pieces[block(part, 64), :].astype(BF16)
            x_ref[0:64, block(part)] = piece
            x_ref[64:128, block(part)] = piece
            x_ref[128:256, block(part)] = jnp.zeros((128, LANES), BF16)
        spec[...] = transform(x_ref, high, low, first, second, twiddle, OWN)

    return body


def forward_kernel(
    message_ref, kernel_spec, own, times, first, second, second_back, last, twiddle,
    out_ref, spec_ref, normed_ref, slope_ref, inv_ref, len_ref,
    message, x_ref, high, low, e_high, e_low, y_ref, out,
):
    message[...] = spread(message_ref[...])
    for y in range(4):
        for b in range(2):
            start = y * 16 + 12 + 2 * b
            len_ref[2 * y + b : 2 * y + b + 1, :] = (
                message[start : start + 1, :] * 128.0 + message[start + 1 : start + 2, :]
            )
    load_signals(message, 16, x_ref)
    convolve(x_ref, spec_ref, kernel_spec, high, low, e_high, e_low, (first, second, second_back, last, twiddle), y_ref)
    valid, tally = valid_of(times, len_ref), tally_of(len_ref)
    inv_ref[...] = jnp.zeros((8, LANES), F32)
    for part in range(OWN):
        normed, inv_std, active, slope = normalise(y_ref, own, valid, tally, part)
        normed_ref[:, block(part, 512)] = normed
        slope_ref[:, block(part, 512)] = slope
        inv_ref[part : part + 1, :] = jnp.broadcast_to(inv_std, (1, LANES))
        y_ref[:, block(part, 512)] = active
    store_signals(out, 16, 0, lambda part, y: y_ref[:, block(part * 4 + y)])
    out_ref[...] = out[...].reshape(DEVICES, 16, LANES).astype(BF16)


def gather_active(message, step, rhs):
    row = lax.broadcasted_iota(jnp.int32, (DEVICES, LANES), 0)
    for i in range(4):
        for part in range(OWN):
            piece = message[pl.ds(part * 4 + i, DEVICES, stride=step), :]
            if part == 2:
                piece = jnp.where(row == SPOT - 2 * DEVICES, 1.0, piece)
            rhs[block(part), block(i)] = piece.astype(BF16)


def store_rows(value, out, step, base):
    for i in range(4):
        for part in range(OWN):
            out[pl.ds(base + part * 4 + i, DEVICES, stride=step), :] = value[block(part), block(i)]


def mix_kernel(
    meta, message_ref, x_ref, cotangent, weight, weight_back, bias,
    out_ref, next_ref, active_ref, message, padded, out, low,
):
    message[...] = spread(message_ref[...])
    gather_active(message, 16, active_ref)
    mixed = dot(weight[0], active_ref[...]) + bias[:, 0:1]
    put_padded(padded, x_ref[...])
    for i in range(4):
        valid = valid_row(meta, i)
        value = rows_of_channels(padded, i) + mixed[:, block(i)] * valid
        next_ref[pl.ds(i, PADDED, stride=4), :] = value
        padded[pl.ds(i, PADDED, stride=4), :] = value * valid
    rows_to_message(padded, out, 24, 0)
    put_padded(padded, masked(meta, cotangent[...]))
    for i in range(4):
        low[:, block(i)] = rows_of_channels(padded, i).astype(BF16)
    store_rows(dot(weight_back[1], low[...]), out, 24, 12)
    out_ref[...] = out[...].reshape(DEVICES, 24, LANES).astype(BF16)


def forward_backward_kernel(
    message_ref, kernel_spec, own, len_ref, times, first, second, second_back, last, twiddle,
    columns, hidden_w, place_row, time_row, tab,
    out_ref, hidden_out, outer_out,
    message, x_ref, high, low, e_high, e_low, y_ref, out, spec_ref, grad_ref, normed_ref, slope_ref, returned_ref,
    rows, sums, mats,
):
    consts = (first, second, second_back, last, twiddle)
    message[...] = spread(message_ref[...])
    load_signals(message, 24, x_ref)
    convolve(x_ref, spec_ref, kernel_spec, high, low, e_high, e_low, consts, y_ref)
    valid, tally = valid_of(times, len_ref), tally_of(len_ref)
    inv = []
    for part in range(OWN):
        normed, inv_std, active, slope = normalise(y_ref, own, valid, tally, part)
        normed_ref[:, block(part, 512)] = normed
        slope_ref[:, block(part, 512)] = slope
        inv.append(inv_std)
        y_ref[:, block(part, 512)] = active
    store_signals(out, 24, 0, lambda part, y: y_ref[:, block(part * 4 + y)])
    returned, norm_sums = conv_backward(
        message, 24, 12, lambda part: normed_ref[:, block(part, 512)], lambda part: slope_ref[:, block(part, 512)],
        lambda part: inv[part], own, valid, tally, spec_ref, kernel_spec, x_ref, high, low, e_high, e_low, consts, grad_ref,
    )
    returned_ref[...] = returned
    store_signals(out, 24, 12, lambda part, y: returned_ref[:, block(part * 4 + y)])
    out_ref[...] = out[...].reshape(DEVICES, 24, LANES).astype(BF16)
    hidden, outer = generate_back(
        lambda part: returned_ref[0:64, block(SIGNALS + part)], columns, hidden_w.at[1], own, place_row, time_row, tab,
        rows, sums, mats,
    )
    hidden_out[...] = hidden
    outer_out[...] = with_norm_sums(outer, norm_sums)


def middle_kernel(
    meta, message_ref, x_ref, cotangent, weight, weight_back, bias, active_0, hidden_1,
    output_ref, flow_ref, out_ref, message, padded, out, low_0, low_1, active_1,
):
    message[...] = spread(message_ref[...])
    gather_active(message, 24, active_1)
    mixed = dot(weight[1], active_1[...]) + bias[:, 1:2]
    for i in range(4):
        padded[pl.ds(i, PADDED, stride=4), :] = rows_of_channels(x_ref, i) + mixed[:, block(i)] * valid_row(meta, i)
    output_ref[...] = padded[0:CLIP_ROWS, :]
    put_padded(flow_ref, cotangent[...])
    for i in range(4):
        low_1[:, block(i)] = (rows_of_channels(flow_ref, i) * valid_row(meta, i)).astype(BF16)
    for m in range(12):
        padded[pl.ds(m, DEVICES, stride=12), :] = message[pl.ds(12 + m, DEVICES, stride=24), :]
    flow_ref[...] += masked(meta, padded[...])
    for i in range(4):
        low_0[:, block(i)] = (rows_of_channels(flow_ref, i) * valid_row(meta, i)).astype(BF16)
    store_rows(dot(weight_back[0], low_0[...]), out, 32, 0)
    for layer, (active, low) in enumerate(((active_0, low_0), (active_1, low_1))):
        part_sum = dot_rows(active[...], low[...])
        for part in range(OWN):
            for third in range(3):
                out[pl.ds(12 + layer * 9 + part * 3 + third, DEVICES, stride=32), :] = part_sum[
                    block(part), block(third)
                ]
    high, low = high_low(hidden_1[...])
    out[pl.ds(30, DEVICES, stride=32), :] = jnp.concatenate([high, jnp.zeros((96, LANES), F32)], axis=0)
    out[pl.ds(31, DEVICES, stride=32), :] = jnp.concatenate([low, jnp.zeros((96, LANES), F32)], axis=0)
    out_ref[...] = out[...].reshape(DEVICES, 32, LANES).astype(BF16)


LAST_ROWS = 56


def backward_kernel(
    message_ref, spec_ref, kernel_spec, normed_ref, slope_ref, inv_ref, len_ref, own, times,
    first, second, second_back, last, twiddle, columns, hidden_w, place_row, time_row, tab, outer_1,
    out_ref,
    message, x_ref, high, low, e_high, e_low, out, grad_ref, returned_ref, rows, sums, mats,
):
    consts = (first, second, second_back, last, twiddle)
    message[...] = spread(message_ref[...])
    valid, tally = valid_of(times, len_ref), tally_of(len_ref)
    returned, norm_sums = conv_backward(
        message, 32, 0, lambda part: normed_ref[:, block(part, 512)], lambda part: slope_ref[:, block(part, 512)],
        lambda part: inv_ref[part : part + 1, 0:1], own, valid, tally, spec_ref, kernel_spec, x_ref, high, low,
        e_high, e_low, consts, grad_ref,
    )
    returned_ref[...] = returned
    store_signals(out, 16, 0, lambda part, y: returned_ref[:, block(part * 4 + y)])
    hidden, outer = generate_back(
        lambda part: returned_ref[0:64, block(SIGNALS + part)], columns, hidden_w.at[0], own, place_row, time_row, tab,
        rows, sums, mats,
    )
    outer = with_norm_sums(outer, norm_sums)
    gathered = jnp.sum(message[...].reshape(DEVICES, 32, LANES), axis=0)
    upper, lower = packed_hidden(hidden)
    hidden_1_high, hidden_1_low = high_low(gathered[30:31, :] + gathered[31:32, :])
    outer_0_high, outer_0_low = high_low(one_row(outer))
    outer_1_high, outer_1_low = high_low(one_row(outer_1[...]))
    shared = jnp.concatenate(
        [
            gathered[0:30, :], upper, lower, hidden_1_high, hidden_1_low,
            outer_0_high, outer_0_low, outer_1_high, outer_1_low,
        ],
        axis=0,
    )
    row = lax.broadcasted_iota(jnp.int32, (DEVICES, 16, LANES), 1)
    own_rows = jnp.where(row < 12, out[...].reshape(DEVICES, 16, LANES), shared[None, 0:16, :])
    rest = jnp.broadcast_to(shared[None, 16:LAST_ROWS, :], (DEVICES, LAST_ROWS - 16, LANES))
    out_ref[...] = jnp.concatenate([own_rows, rest], axis=1).astype(BF16)


def last_kernel(
    meta, message_ref, flow_ref, lookup,
    input_grad, gabor_grad, hidden_w_grad, hidden_b_grad, out_w_grad, out_b_grad, gain_grad, bias_grad,
    mix_w_grad, mix_b_grad, message, padded, owned, thirds,
):
    message[...] = spread(message_ref[...])

    def rows_of(k, count=DEVICES):
        return message[pl.ds(k, count, stride=LAST_ROWS), :]

    for m in range(12):
        padded[pl.ds(m, DEVICES, stride=12), :] = rows_of(m)
    input_grad[...] = flow_ref[0:CLIP_ROWS, :] + masked(meta, padded[0:CLIP_ROWS, :])
    shared = jnp.sum(message[...].reshape(DEVICES, LAST_ROWS, LANES)[:, 24:56, :], axis=0)
    hidden_0 = unpacked_hidden(shared[6:22, :], shared[22:26, :])
    hidden_1 = rows_of(50, 32) + rows_of(51, 32)
    lane = lax.broadcasted_iota(jnp.int32, (DEVICES, LANES), 1)
    for layer, hidden in enumerate((hidden_0, hidden_1)):
        hidden_w_grad[layer, 0] = hidden[:, 0:32]
        hidden_w_grad[layer, 1] = pltpu.roll(hidden, 96, 1)[:, 0:32]
        turned = jnp.transpose(jnp.concatenate([hidden, jnp.zeros((96, LANES), F32)], axis=0))
        hidden_b_grad[layer] = turned[64:66, 0:32]
        for j in range(3):
            gabor_grad[layer, j] = turned[66 + 4 * j : 70 + 4 * j, 0:32]
        value = rows_of(52 + 2 * layer) + rows_of(53 + 2 * layer)
        for part in range(OWN):
            wide = pltpu.roll(value, (LANES - 32 * part) % LANES, 1)
            small = pltpu.roll(value, 64 - 3 * part, 1)
            owned[pl.ds(part, DEVICES, stride=OWN), :] = jnp.where(lane < 32, wide, small)
        turned = jnp.transpose(owned[...])
        out_w_grad[layer] = turned[0:32, 0:CHANNELS]
        out_b_grad[layer : layer + 1, :] = turned[32:33, 0:CHANNELS]
        gain_grad[layer : layer + 1, :] = turned[33:34, 0:CHANNELS]
        bias_grad[layer : layer + 1, :] = turned[34:35, 0:CHANNELS]
        bias_rows = []
        for part in range(OWN):
            for third in range(3):
                piece = rows_of(12 + layer * 9 + part * 3 + third)
                thirds[block(part), block(third)] = piece.astype(BF16)
                if part == 2:
                    bias_rows.append(piece[SPOT - 2 * DEVICES : SPOT - 2 * DEVICES + 1, :])
        mix_w_grad[layer] = dot_columns(thirds[...], lookup[...])[0:CHANNELS, 0:CHANNELS]
        mix_b_grad[layer : layer + 1, :] = jnp.concatenate(bias_rows, axis=1)[:, 0:CHANNELS]


def exchange(message):
    return lax.all_to_all(message, AXES, split_axis=0, concat_axis=0, tiled=True)


def to_rows(clips):
    return clips.reshape(2, CHANNELS, 2, LANES).transpose(1, 2, 0, 3).reshape(CLIP_ROWS, LANES)


def from_rows(rows):
    return rows.reshape(CHANNELS, 2, 2, LANES).transpose(2, 0, 1, 3).reshape(2, CHANNELS, PIECE)


def shards(
    inputs, lengths, window, gabor_params, hidden_w, hidden_b, out_w, out_b, bn_gain, bn_bias, mix_w, mix_b, cotangent
):
    position = lax.axis_index("seq").astype(jnp.int32)
    number = position * 4 + lax.axis_index("clips").astype(jnp.int32)
    const = {name: jnp.asarray(value) for name, value in TABLES.items()}
    meta = jnp.concatenate([lengths, jnp.stack([position, number])])
    inputs, cotangent = to_rows(inputs), to_rows(cotangent)

    def rows(count):
        return ((count, LANES), F32)

    owns = [
        meta, jnp.swapaxes(out_w, 1, 2), out_b, jnp.swapaxes(window, 1, 2), bn_gain, bn_bias, gabor_params, hidden_b,
        hidden_w, const["place_row"], const["time_row"], const["starts"], const["first"], const["second"],
        const["twiddle"],
    ]

    shape_tab = ((8, HIDDEN, SAMPLES), F32)

    def generator(layer):
        return run(
            generate_kernel(layer),
            [shape_tab, ((OWN * LANES, 2 * LANES), F32), rows(8), rows(HIDDEN)],
            owns,
            [
                ((LANES, PADDED), F32), rows(PADDED + 8), ((8, SAMPLES), F32), rows(192),
                ((256, OWN * LANES), BF16), ((OWN * LANES, 256), BF16), ((OWN * LANES, 256), BF16),
            ],
            f"generator_{layer}", 10, smem=(0,),
        )

    with jax.named_scope("generators"):
        tab_0, spec_k0, own_0, columns_0 = generator(0)
        tab_1, spec_k1, own_1, columns_1 = generator(1)

    square = (PADDED, PADDED)
    with jax.named_scope("weights"):
        weight, weight_back, bias = run(
            weights_kernel, [((2, *square), BF16), ((2, *square), BF16), rows(PADDED)], [mix_w, mix_b, const["lookup"]],
            [(square, BF16)], "weights", 8,
        )

    with jax.named_scope("source_0"):
        (message,) = run(
            source_kernel, [((DEVICES, 16, LANES), BF16)], [meta, inputs, own_0, own_1, bias], [rows(PADDED_ROWS), rows(DEVICES * 16)],
            "source_0", 8, smem=(0,),
        )
        message = exchange(message)

    def scratch(signals):
        count = signals * LANES
        return [
            ((256, SIGNALS * LANES), BF16), ((count, 256), BF16), ((count, 256), BF16),
            ((256, count), BF16), ((256, count), BF16),
        ]

    shape_y = (LANES, SIGNALS * LANES)
    shape_s = (SIGNALS * LANES, 256)
    transforms = [const[name] for name in ("first", "second", "second_back", "last", "twiddle")]
    with jax.named_scope("conv_0"):
        message, spec_0, normed_0, slope_0, inv_0, lens = run(
            forward_kernel,
            [
                ((DEVICES, 16, LANES), BF16), (shape_s, F32), (shape_y, F32), (shape_y, F32), rows(8), rows(8),
            ],
            [message, spec_k0, own_0, const["times"], *transforms],
            [rows(DEVICES * 16), *scratch(SIGNALS), (shape_y, F32), rows(DEVICES * 16)],
            "conv_0", 20,
        )
        message = exchange(message)

    with jax.named_scope("mix_0"):
        message, middle, active_0 = run(
            mix_kernel,
            [((DEVICES, 24, LANES), BF16), rows(PADDED_ROWS), ((PADDED, 512), BF16)],
            [meta, message, inputs, cotangent, weight, weight_back, bias],
            [rows(DEVICES * 16), rows(PADDED_ROWS), rows(DEVICES * 24), ((PADDED, 512), BF16)],
            "mix_0", 12, smem=(0,),
        )
        message = exchange(message)

    back_scratch = [((8, SAMPLES), F32), rows(14 * 32 + 8), rows(72)]
    with jax.named_scope("conv_1"):
        message, hidden_1, outer_1 = run(
            forward_backward_kernel,
            [((DEVICES, 24, LANES), BF16), rows(HIDDEN), rows(8)],
            [
                message, spec_k1, own_1, lens, const["times"], *transforms, columns_1, hidden_w, const["place_row"],
                const["time_row"], tab_1,
            ],
            [
                rows(DEVICES * 24), *scratch(SIGNALS + OWN), (shape_y, F32), rows(DEVICES * 24),
                (shape_s, F32), (shape_s, F32), (shape_y, F32), (shape_y, F32),
                ((LANES, (SIGNALS + OWN) * LANES), F32), *back_scratch,
            ],
            "conv_1", 28,
        )
        message = exchange(message)

    with jax.named_scope("mix_1"):
        outputs, flow, message = run(
            middle_kernel,
            [rows(CLIP_ROWS), rows(PADDED_ROWS), ((DEVICES, 32, LANES), BF16)],
            [meta, message, middle, cotangent, weight, weight_back, bias, active_0, hidden_1],
            [
                rows(DEVICES * 24), rows(PADDED_ROWS), rows(DEVICES * 32),
                ((PADDED, 512), BF16), ((PADDED, 512), BF16), ((PADDED, 512), BF16),
            ],
            "mix_1", 12, smem=(0,),
        )
        message = exchange(message)

    with jax.named_scope("conv_back_0"):
        (message,) = run(
            backward_kernel,
            [((DEVICES, LAST_ROWS, LANES), BF16)],
            [
                message, spec_0, spec_k0, normed_0, slope_0, inv_0, lens, own_0, const["times"], *transforms,
                columns_0, hidden_w, const["place_row"], const["time_row"], tab_0, outer_1,
            ],
            [
                rows(DEVICES * 32), *scratch(SIGNALS + OWN), rows(DEVICES * 16), (shape_s, F32),
                ((LANES, (SIGNALS + OWN) * LANES), F32), *back_scratch,
            ],
            "conv_back_0", 28,
        )
        message = exchange(message)

    with jax.named_scope("gradients"):
        (
            input_grad, gabor_grad, hidden_w_grad, hidden_b_grad, out_w_grad, out_b_grad, gain_grad, bias_grad,
            mix_w_grad, mix_b_grad,
        ) = run(
            last_kernel,
            [
                rows(CLIP_ROWS), (gabor_params.shape, F32), (hidden_w.shape, F32), (hidden_b.shape, F32),
                ((2, HIDDEN, CHANNELS), F32), (out_b.shape, F32), (bn_gain.shape, F32), (bn_bias.shape, F32),
                (mix_w.shape, F32), (mix_b.shape, F32),
            ],
            [meta, message, flow, const["lookup"]],
            [rows(DEVICES * LAST_ROWS), rows(PADDED_ROWS), rows(PADDED), (square, BF16)],
            "gradients", 14, smem=(0,),
        )
    return (
        from_rows(outputs), from_rows(input_grad), gabor_grad, hidden_w_grad, hidden_b_grad,
        jnp.swapaxes(out_w_grad, 1, 2), out_b_grad, gain_grad, bias_grad, mix_w_grad, mix_b_grad,
    )


def solution(mesh):
    clip = P("clips", None, "seq")
    in_specs = (clip, P("clips")) + (P(),) * 10 + (clip,)
    out_specs = (clip, clip) + (P(),) * 9
    return jax.shard_map(shards, mesh=mesh, in_specs=in_specs, out_specs=out_specs, check_vma=False)
```

```python
import math

import jax
import jax.numpy as jnp
import ml_dtypes
import numpy as np
from jax import lax
from jax.experimental import pallas as pl
from jax.experimental.pallas import tpu as pltpu
from jax.sharding import PartitionSpec as P

F32 = jnp.float32
BF16 = jnp.bfloat16
AXES = ("seq", "clips")
DEVICES = 128
OWN = 3
CHANNELS = 380
PADDED = DEVICES * OWN
SAMPLES = 8192
PIECE = 256
HIDDEN = 32
LANES = 128
SIGNALS = 12
PERIOD = 2 * SAMPLES
EPSILON = 1e-05
MEGABYTE = 1024 * 1024
GRANT = 50
EXACT = lax.Precision.HIGHEST
SPOTS = (2 * DEVICES + 126, 2 * DEVICES + 127, 127)
SPOT = SPOTS[0]


def halves(table):
    high = table.astype(ml_dtypes.bfloat16)
    low = (table - high.astype(np.float64)).astype(ml_dtypes.bfloat16)
    return high, low


def tables():
    order = np.array([2 * j + r for r in range(2) for j in range(32)])
    k = np.arange(LANES)
    turn = 2 * np.pi * ((k[:, None] * order[None, :]) % LANES) / LANES
    c_high, c_low = halves(np.cos(turn))
    s_high, s_low = halves(np.sin(turn))
    first = np.concatenate(
        [
            np.concatenate([c_high, c_low, s_high, s_low], axis=1),
            np.concatenate([-s_high, -s_low, c_high, c_low], axis=1),
        ],
        axis=0,
    )
    turn = 2 * np.pi * ((k[:, None] * k[None, :]) % LANES) / LANES
    cosine, sine = np.cos(turn), np.sin(turn)
    second = halves(np.block([[cosine, -sine], [sine, cosine]]))
    second_back = halves(np.block([[cosine, sine], [-sine, cosine]]))
    turn = 2 * np.pi * ((order[:, None] * k[None, :]) % LANES) / LANES
    cosine, sine = np.cos(turn) / PERIOD, np.sin(turn) / PERIOD
    last = halves(np.block([[cosine, -sine], [sine, cosine]]))
    turn = 2 * np.pi * (k[:, None] * k[None, :]) / PERIOD
    twiddle = np.stack([np.cos(turn), np.sin(turn)]).astype(np.float32)
    times = (128 * order[:, None] + k[None, :]).astype(np.float32)
    places = (-1.0 + 2.0 * times / np.float32(SAMPLES - 1)).astype(np.float32)
    lookup = np.zeros((PADDED, PADDED), ml_dtypes.bfloat16)
    for part in range(OWN):
        for owner in range(DEVICES):
            lookup[part * DEVICES + owner, OWN * owner + part] = 1
    return dict(
        first=first,
        second=np.stack(second),
        second_back=np.stack(second_back),
        last=np.stack(last),
        twiddle=twiddle,
        times=np.concatenate([times, times], axis=0),
        time_row=times.reshape(1, SAMPLES),
        place_row=places.reshape(1, SAMPLES),
        starts=np.stack([np.pad(places[:, 0], (0, 64)), 2.0 * k / (SAMPLES - 1)]).astype(np.float32),
        lookup=lookup,
    )


TABLES = tables()


def run(body, outs, args, scratch, name, grant, smem=(), far=(), far_outs=(), copies=0):
    spaces = [pltpu.HBM if i in far else pltpu.SMEM if i in smem else pltpu.VMEM for i in range(len(args))]
    out_spaces = [pltpu.HBM if i in far_outs else pltpu.VMEM for i in range(len(outs))]
    return pl.pallas_call(
        body,
        out_shape=[jax.ShapeDtypeStruct(shape, kind) for shape, kind in outs],
        in_specs=[pl.BlockSpec(memory_space=space) for space in spaces],
        out_specs=[pl.BlockSpec(memory_space=space) for space in out_spaces],
        scratch_shapes=[pltpu.VMEM(shape, kind) for shape, kind in scratch]
        + ([pltpu.SemaphoreType.DMA((copies,))] if copies else []),
        compiler_params=pltpu.CompilerParams(vmem_limit_bytes=grant * MEGABYTE),
        name=name,
    )(*args)


def dot(a, b):
    return jnp.dot(a, b, preferred_element_type=F32)


def dot_rows(a, b, precision=None):
    return lax.dot_general(a, b, (((1,), (1,)), ((), ())), precision=precision, preferred_element_type=F32)


def dot_columns(a, b, precision=None):
    return lax.dot_general(a, b, (((0,), (0,)), ((), ())), precision=precision, preferred_element_type=F32)


def triple(a_high, a_low, b_high, b_low):
    left = jnp.concatenate([a_high, a_low, a_high], axis=1)
    return dot(left, jnp.concatenate([b_high, b_high, b_low], axis=0))


def put_halves(high_ref, low_ref, rows, columns, value):
    high = value.astype(BF16)
    high_ref[rows, columns] = high
    low_ref[rows, columns] = (value - high.astype(F32)).astype(BF16)


def block(i, size=LANES):
    return slice(i * size, (i + 1) * size)


RE, IM = slice(0, LANES), slice(LANES, 2 * LANES)


def signal_row(b, part, r):
    return part * 4 + r * 2 + b


def spread(message):
    return message.astype(F32).reshape(-1, LANES)


def transform(x_ref, high_ref, low_ref, first, second, twiddle, count):
    part_a = dot(first[...], x_ref[:, : count * LANES])
    cosine, sine = twiddle[0], twiddle[1]
    for s in range(count):
        real, imag = part_a[:LANES, block(s)], part_a[LANES:, block(s)]
        put_halves(high_ref, low_ref, block(s), RE, real * cosine + imag * sine)
        put_halves(high_ref, low_ref, block(s), IM, imag * cosine - real * sine)
    rows = slice(0, count * LANES)
    return triple(high_ref[rows, :], low_ref[rows, :], second[0], second[1])


def transform_back(high_ref, low_ref, e_high, e_low, second_back, last, twiddle, count):
    rows = slice(0, count * LANES)
    part_d = triple(high_ref[rows, :], low_ref[rows, :], second_back[0], second_back[1])
    cosine, sine = twiddle[0], twiddle[1]
    for s in range(count):
        real, imag = part_d[block(s), RE], part_d[block(s), IM]
        put_halves(e_high, e_low, RE, block(s), real * cosine - imag * sine)
        put_halves(e_high, e_low, IM, block(s), real * sine + imag * cosine)
    return triple(last[0], last[1], e_high[:, rows], e_low[:, rows])


def erf_parts(value):
    cdf = 0.5 * (1.0 + lax.erf(value * math.sqrt(0.5)))
    return cdf, jnp.exp(-0.5 * value * value) * (1.0 / math.sqrt(2.0 * math.pi))


def total(value):
    return jnp.sum(jnp.sum(value, axis=0, keepdims=True), axis=1, keepdims=True)


def valid_of(times, len_ref):
    columns = []
    for y in range(4):
        upper = times[0:64, :] < len_ref[2 * y : 2 * y + 1, :]
        lower = times[64:128, :] < len_ref[2 * y + 1 : 2 * y + 2, :]
        columns.append(jnp.concatenate([upper, lower], axis=0).astype(F32))
    return jnp.concatenate(columns, axis=1)


def tally_of(len_ref):
    return jnp.sum(len_ref[:, 0:1], axis=0, keepdims=True)


def load_signals(message, step, x_ref):
    for part in range(OWN):
        for y in range(4):
            lanes = block(part * 4 + y)
            for b in range(2):
                for r in range(2):
                    start = y * step + signal_row(b, part, r)
                    piece = message[pl.ds(start, 32, stride=4 * step), :].astype(BF16)
                    x_ref[b * 128 + r * 32 : b * 128 + r * 32 + 32, lanes] = piece
                    x_ref[b * 128 + r * 32 + 64 : b * 128 + r * 32 + 96, lanes] = piece


def store_signals(out, step, base, get):
    for part in range(OWN):
        for y in range(4):
            value = get(part, y)
            for b in range(2):
                for r in range(2):
                    start = y * step + base + signal_row(b, part, r)
                    out[pl.ds(start, 32, stride=4 * step), :] = value[b * 64 + r * 32 : b * 64 + r * 32 + 32, :]


SPEC_IM = OWN * LANES
OWN_ROWS = slice(2 * SPEC_IM, 2 * SPEC_IM + 8)
COLUMN_ROWS = slice(2 * SPEC_IM + 8, 2 * SPEC_IM + 8 + HIDDEN)
BUNDLE = 2 * SPEC_IM + 8 + HIDDEN


def kernel_parts(bundle, part):
    return bundle[block(part), :], bundle[SPEC_IM + part * LANES : SPEC_IM + (part + 1) * LANES, :]


def convolve(x_ref, spec_ref, kernel_spec, high, low, e_high, e_low, consts, y_ref):
    first, second, second_back, last, twiddle = consts
    spec_ref[...] = transform(x_ref, high, low, first, second, twiddle, SIGNALS)
    for part in range(OWN):
        k_re, k_im = kernel_parts(kernel_spec, part)
        for y in range(4):
            rows = block(part * 4 + y)
            s_re, s_im = spec_ref[rows, RE], spec_ref[rows, IM]
            put_halves(high, low, rows, RE, s_re * k_re - s_im * k_im)
            put_halves(high, low, rows, IM, s_re * k_im + s_im * k_re)
    y_ref[...] = transform_back(high, low, e_high, e_low, second_back, last, twiddle, SIGNALS)


def normalise(y_ref, own, valid, tally, part):
    value = y_ref[:, block(part, 512)]
    mean = total(valid * value) / tally
    centred = value - mean
    var = total(valid * centred * centred) / tally
    inv_std = lax.rsqrt(var + EPSILON)
    normed = centred * inv_std
    pre_act = normed * own[part : part + 1, 35:36] + own[part : part + 1, 36:37]
    cdf, density = erf_parts(pre_act)
    return normed, inv_std, pre_act * cdf, cdf + pre_act * density


def conv_backward(
    message, step, base, normed_of, slope_of, inv_of, own, valid, tally, spec_ref, kernel_spec, x_ref, high, low,
    e_high, e_low, consts, grad_ref,
):
    first, second, second_back, last, twiddle = consts
    sums = []
    for part in range(OWN):
        columns = []
        for y in range(4):
            pieces = []
            for b in range(2):
                for r in range(2):
                    start = y * step + base + signal_row(b, part, r)
                    pieces.append(message[pl.ds(start, 32, stride=4 * step), :])
            columns.append(jnp.concatenate(pieces, axis=0))
        act_grad = jnp.concatenate(columns, axis=1)
        normed = normed_of(part)
        pre_grad = act_grad * slope_of(part)
        bias_total = total(pre_grad)
        gain_total = total(pre_grad * normed)
        gain = own[part : part + 1, 35:36]
        conv_grad = inv_of(part) * (
            gain * pre_grad - valid * (gain * bias_total + normed * (gain * gain_total)) / tally
        )
        conv_low = conv_grad.astype(BF16)
        for b in range(2):
            piece = conv_low[b * 64 : b * 64 + 64, :]
            x_ref[b * 128 : b * 128 + 64, block(part, 512)] = piece
            x_ref[b * 128 + 64 : b * 128 + 128, block(part, 512)] = piece
        sums.append((gain_total, bias_total))
    grad_ref[...] = transform(x_ref, high, low, first, second, twiddle, SIGNALS)
    for part in range(OWN):
        k_re, k_im = kernel_parts(kernel_spec, part)
        corr_re, corr_im = None, None
        for y in range(4):
            rows = block(part * 4 + y)
            g_re, g_im = grad_ref[rows, RE], grad_ref[rows, IM]
            s_re, s_im = spec_ref[rows, RE], spec_ref[rows, IM]
            put_halves(high, low, rows, RE, k_re * g_re + k_im * g_im)
            put_halves(high, low, rows, IM, k_re * g_im - k_im * g_re)
            now_re, now_im = s_re * g_re + s_im * g_im, s_re * g_im - s_im * g_re
            corr_re = now_re if corr_re is None else corr_re + now_re
            corr_im = now_im if corr_im is None else corr_im + now_im
        put_halves(high, low, block(SIGNALS + part), RE, corr_re)
        put_halves(high, low, block(SIGNALS + part), IM, corr_im)
    returned = transform_back(high, low, e_high, e_low, second_back, last, twiddle, SIGNALS + OWN)
    return returned, sums


def sin_cos(angle):
    turns = jnp.floor(angle * (2.0 / math.pi) + 0.5)
    rest = angle - turns * 1.5703125
    rest = rest - turns * 4.837512969970703125e-4
    rest = rest - turns * 7.549789948768648e-8
    square = rest * rest
    sine = rest + rest * square * (
        -1.6666654611e-1 + square * (8.3321608736e-3 + square * -1.9515295891e-4)
    )
    cosine = 1.0 - 0.5 * square + square * square * (
        4.166664568298827e-2 + square * (-1.388731625493765e-3 + square * 2.443315711809948e-5)
    )
    half = jnp.floor(turns * 0.5)
    odd = turns - 2.0 * half
    sign = 1.0 - 2.0 * (half - 2.0 * jnp.floor(half * 0.5))
    is_odd = odd > 0.5
    return sign * jnp.where(is_odd, cosine, sine), sign * jnp.where(is_odd, -sine, cosine)


CHUNK = 1024


def envelope_of(times, own):
    lower, upper = own[:, 33:34], own[:, 34:35]
    inside = (times >= lower) & (times < upper)
    offset = (times - lower) / (0.5 * (upper - lower))
    return jnp.where(inside, jnp.exp(-0.5 * offset * offset), 0.0)


def stacked_weight(weight):
    high, low = high_low(weight)
    return jnp.concatenate([high, high, low], axis=1).astype(BF16)


def stacked_dot(weight, value):
    high = value.astype(BF16)
    low = (value - high.astype(F32)).astype(BF16)
    return dot(weight, jnp.concatenate([high, low, high], axis=0))


def own_parameters(layer, number, out_w, out_b, window, gain, bias, gabor, hidden_b, wide, tall, own, columns):
    wide[...] = jnp.zeros(wide.shape, F32)
    wide[0:32, 0:CHANNELS] = out_w[layer]
    wide[32:33, 0:CHANNELS] = out_b[layer : layer + 1, :]
    wide[33:35, 0:CHANNELS] = window[layer].astype(F32)
    wide[35:36, 0:CHANNELS] = gain[layer : layer + 1, :]
    wide[36:37, 0:CHANNELS] = bias[layer : layer + 1, :]
    tall[0:PADDED, :] = jnp.transpose(wide[...])
    tall[PADDED : PADDED + 8, :] = jnp.zeros((8, LANES), F32)
    row = lax.broadcasted_iota(jnp.int32, (8, LANES), 0)
    lane = lax.broadcasted_iota(jnp.int32, (8, LANES), 1)
    mine = tall[pl.ds(number * OWN, 8), :]
    unused = (row >= OWN) | (number * OWN + row >= CHANNELS)
    own[...] = jnp.where(unused, jnp.where(lane == 34, float(SAMPLES), 0.0), mine)
    wide[:, 0:LANES] = jnp.zeros((LANES, LANES), F32)
    for j in range(3):
        wide[4 * j : 4 * j + 4, 0:HIDDEN] = gabor[layer, j]
    wide[12:14, 0:HIDDEN] = hidden_b[layer]
    columns[...] = jnp.transpose(wide[:, 0:LANES])[0:HIDDEN, :]


TABLES_KEPT = 8


def table_copy(source, target, k, flags):
    return pltpu.make_async_copy(source.at[k], target.at[k], flags.at[k])


def start_tables(tab_far, tab, arrived):
    for k in range(TABLES_KEPT):
        table_copy(tab_far, tab, k, arrived).start()


def wait_tables(tab_far, tab, arrived):
    for k in range(TABLES_KEPT):
        table_copy(tab_far, tab, k, arrived).wait()


def generate(columns, hidden_w, own, place_row, time_row, starts, tab, rows, tab_far, sent):
    places = place_row[...]
    weights = [stacked_weight(hidden_w[0]), stacked_weight(hidden_w[1]), stacked_weight(own[:, 0:32])]

    def level(j):
        frequency, phase = columns[:, 4 * j + 2 : 4 * j + 3], columns[:, 4 * j + 3 : 4 * j + 4]
        start_sin, start_cos = sin_cos(frequency * starts[0:1, :] + phase)
        rest_sin, rest_cos = sin_cos(frequency * starts[1:2, :])
        sine, cosine = [], []
        for n in range(64):
            s_n, c_n = start_sin[:, n : n + 1], start_cos[:, n : n + 1]
            sine.append(s_n * rest_cos + c_n * rest_sin)
            cosine.append(c_n * rest_cos - s_n * rest_sin)
        width = columns[:, 4 * j : 4 * j + 1] * (places - columns[:, 4 * j + 1 : 4 * j + 2])
        bell = jnp.exp(-0.5 * width * width)
        return bell * jnp.concatenate(sine, axis=1), bell * jnp.concatenate(cosine, axis=1)

    def keep(k, value):
        tab[k] = value
        table_copy(tab, tab_far, k, sent).start()

    f_0, c_0 = level(0)
    keep(0, f_0)
    keep(1, c_0)
    u_1 = stacked_dot(weights[0], f_0) + columns[:, 12:13]
    f_1, c_1 = level(1)
    z_1 = u_1 * f_1
    keep(2, z_1)
    keep(3, u_1 * c_1)
    keep(4, f_1)
    u_2 = stacked_dot(weights[1], z_1) + columns[:, 13:14]
    f_2, c_2 = level(2)
    z_2 = u_2 * f_2
    keep(5, z_2)
    keep(6, u_2 * c_2)
    keep(7, f_2)
    raw = stacked_dot(weights[2], z_2) + own[:, 32:33]
    rows[...] = raw * envelope_of(time_row[...], own)


def generate_back(kernel_grad, columns, hidden_w, own, place_row, time_row, tab, rows, sums, mats):
    rows[...] = jnp.zeros(rows.shape, F32)
    for part in range(OWN):
        grad = kernel_grad(part)
        for n in range(64):
            rows[part : part + 1, block(n)] = grad[n : n + 1, :]
    sums[...] = jnp.zeros(sums.shape, F32)
    mats[...] = jnp.zeros(mats.shape, F32)
    turned = jnp.transpose(jnp.concatenate([own[...], jnp.zeros((120, 128), F32)], axis=0))
    weight = [turned[0:32, part : part + 1] for part in range(OWN)]
    back = [stacked_weight(jnp.transpose(hidden_w[j])) for j in range(2)]

    def fold(value):
        acc = value[:, block(0)]
        for i in range(1, CHUNK // LANES):
            acc = acc + value[:, block(i)]
        return acc

    def add(k, value):
        sums[block(k, 32), :] += fold(value)

    def step(i, carry):
        span = pl.ds(pl.multiple_of(i * CHUNK, CHUNK), CHUNK)
        places = place_row[:, span]
        draw = rows[:, span] * envelope_of(time_row[:, span], own)
        dz_2 = weight[0] * draw[0:1, :] + weight[1] * draw[1:2, :] + weight[2] * draw[2:3, :]

        def level(j, e_value, g_value):
            centre = columns[:, 4 * j + 1 : 4 * j + 2]
            offset = places - centre
            moment = e_value * offset
            add(4 * j, moment * offset)
            add(4 * j + 1, moment)
            add(4 * j + 2, g_value * places)
            add(4 * j + 3, g_value)

        z_2 = tab[5, :, span]
        level(2, dz_2 * z_2, dz_2 * tab[6, :, span])
        du_2 = dz_2 * tab[7, :, span]
        add(13, du_2)
        dz_1 = stacked_dot(back[1], du_2)
        z_1 = tab[2, :, span]
        level(1, dz_1 * z_1, dz_1 * tab[3, :, span])
        du_1 = dz_1 * tab[4, :, span]
        add(12, du_1)
        dz_0 = stacked_dot(back[0], du_1)
        z_0 = tab[0, :, span]
        level(0, dz_0 * z_0, dz_0 * tab[1, :, span])
        sums[14 * 32 : 14 * 32 + 8, :] += fold(draw)
        left = jnp.concatenate([du_1, du_2, draw], axis=0)
        right = jnp.concatenate([z_0, z_1, z_2, jnp.zeros_like(z_0)], axis=0)
        left_high, right_high = left.astype(BF16), right.astype(BF16)
        left_low = (left - left_high.astype(F32)).astype(BF16)
        right_low = (right - right_high.astype(F32)).astype(BF16)
        mats[...] += (
            dot_rows(left_high, right_high) + dot_rows(left_low, right_high) + dot_rows(left_high, right_low)
        )
        return carry

    lax.fori_loop(0, SAMPLES // CHUNK, step, 0, unroll=SAMPLES // CHUNK)
    lane = lax.broadcasted_iota(jnp.int32, (32, LANES), 1)
    hidden = jnp.where(lane < 32, mats[0:32, :], jnp.where(lane < 64, mats[32:64, :], 0.0))

    def column(k):
        return jnp.sum(sums[block(k, 32), :], axis=1, keepdims=True)

    hidden = jnp.where(lane == 64, column(12), hidden)
    hidden = jnp.where(lane == 65, column(13), hidden)
    for j in range(3):
        sharpness = columns[:, 4 * j : 4 * j + 1]
        hidden = jnp.where(lane == 66 + 4 * j, -sharpness * column(4 * j), hidden)
        hidden = jnp.where(lane == 67 + 4 * j, sharpness * sharpness * column(4 * j + 1), hidden)
        hidden = jnp.where(lane == 68 + 4 * j, column(4 * j + 2), hidden)
        hidden = jnp.where(lane == 69 + 4 * j, column(4 * j + 3), hidden)
    lane8 = lax.broadcasted_iota(jnp.int32, (8, LANES), 1)
    outer = pltpu.roll(mats[64:72, :], LANES - 64, 1)
    raw_total = jnp.sum(sums[14 * 32 : 14 * 32 + 8, :], axis=1, keepdims=True)
    outer = jnp.where(lane8 < 32, outer, 0.0)
    outer = jnp.where(lane8 == 32, raw_total, outer)
    return hidden, outer


def with_norm_sums(outer, sums):
    row = lax.broadcasted_iota(jnp.int32, (8, LANES), 0)
    lane = lax.broadcasted_iota(jnp.int32, (8, LANES), 1)
    for part in range(OWN):
        gain_total, bias_total = sums[part]
        outer = jnp.where((row == part) & (lane == 33), gain_total, outer)
        outer = jnp.where((row == part) & (lane == 34), bias_total, outer)
    return outer


def one_row(outer):
    lane = lax.broadcasted_iota(jnp.int32, (1, LANES), 1)
    result = jnp.zeros((1, LANES), F32)
    for part in range(OWN):
        row = outer[part : part + 1, :]
        moved = pltpu.roll(row, 32 * part, 1) if part else row
        result = jnp.where((lane >= 32 * part) & (lane < 32 * part + 32), moved, result)
        moved = pltpu.roll(row, 64 + 3 * part, 1)
        result = jnp.where((lane >= 96 + 3 * part) & (lane < 99 + 3 * part), moved, result)
    return result


def packed_hidden(hidden):
    lane16 = lax.broadcasted_iota(jnp.int32, (16, LANES), 1)
    upper = jnp.where(lane16 < 64, hidden[0:16, :], pltpu.roll(hidden[16:32, :], 64, 1))
    lane4 = lax.broadcasted_iota(jnp.int32, (4, LANES), 1)
    lower = jnp.zeros((4, LANES), F32)
    for g in range(8):
        moved = pltpu.roll(hidden, (64 + 16 * g) % LANES, 1)[4 * g : 4 * g + 4, :]
        lower = jnp.where((lane4 >= 16 * g) & (lane4 < 16 * g + 16), moved, lower)
    return upper, lower


def unpacked_hidden(upper, lower):
    lane16 = lax.broadcasted_iota(jnp.int32, (16, LANES), 1)
    lane32 = lax.broadcasted_iota(jnp.int32, (32, LANES), 1)
    top = jnp.concatenate([upper, pltpu.roll(upper, 64, 1)], axis=0)
    tiled = jnp.concatenate([lower] * 8, axis=0)
    row32 = lax.broadcasted_iota(jnp.int32, (32, LANES), 0)
    rest = jnp.zeros((32, LANES), F32)
    for g in range(8):
        moved = pltpu.roll(tiled, (64 - 16 * g) % LANES, 1)
        rest = jnp.where((row32 >= 4 * g) & (row32 < 4 * g + 4), moved, rest)
    return jnp.where(lane32 < 64, top, rest)


def high_low(value):
    high = value.astype(BF16).astype(F32)
    return high, value - high


def valid_row(meta, i):
    lane = lax.broadcasted_iota(jnp.int32, (1, LANES), 1)
    return (meta[2] * PIECE + (i // 2) * LANES + lane < meta[i % 2]).astype(F32)


def masked(meta, rows):
    mask = jnp.concatenate([valid_row(meta, i) for i in range(4)] * 2, axis=0)
    return (rows.reshape(-1, 8, LANES) * mask[None]).reshape(-1, LANES)


CLIP_ROWS = 4 * CHANNELS
PADDED_ROWS = 4 * PADDED


def put_padded(padded, rows):
    padded[0:CLIP_ROWS, :] = rows
    padded[CLIP_ROWS:PADDED_ROWS, :] = jnp.zeros((PADDED_ROWS - CLIP_ROWS, LANES), F32)


def rows_to_message(padded, out, step, base):
    for m in range(12):
        out[pl.ds(base + m, DEVICES, stride=step), :] = padded[pl.ds(m, DEVICES, stride=12), :]


def rows_of_channels(padded, i):
    return padded[pl.ds(i, PADDED, stride=4), :]


def source_kernel(meta, x_ref, out_ref, padded, out):
    put_padded(padded, masked(meta, x_ref[...]))
    for b in range(2):
        length = meta[b]
        upper = lax.shift_right_logical(length, 7)
        out[pl.ds(12 + 2 * b, DEVICES, stride=16), :] = jnp.full((DEVICES, LANES), upper.astype(F32))
        out[pl.ds(13 + 2 * b, DEVICES, stride=16), :] = jnp.full(
            (DEVICES, LANES), (length - upper * 128).astype(F32)
        )
    rows_to_message(padded, out, 16, 0)
    out_ref[...] = out[...].reshape(DEVICES, 16, LANES).astype(BF16)


def weights_kernel(mix_w, mix_b, lookup, weights, wide):
    row = lax.broadcasted_iota(jnp.int32, (LANES, CHANNELS), 0)
    both = jnp.where(row == 0, mix_b[0:1, :], jnp.where(row == 1, mix_b[1:2, :], 0.0))
    bias = jnp.transpose(jnp.concatenate([both, jnp.zeros((LANES, PADDED - CHANNELS), F32)], axis=1))
    lane = lax.broadcasted_iota(jnp.int32, (PADDED, PADDED), 1)
    for layer in range(2):
        wide[...] = jnp.zeros(wide.shape, BF16)
        wide[0:CHANNELS, 0:CHANNELS] = mix_w[layer]
        value = dot_rows(wide[...], lookup[...])
        rest = bias[:, layer : layer + 1]
        for spot in SPOTS:
            high, rest = high_low(rest)
            value = jnp.where(lane == spot, high, value)
        weights[layer] = value.astype(BF16)
        weights[2 + layer] = dot_rows(lookup[...], wide[...]).astype(BF16)


def generate_kernel(layer):
    def body(
        meta, out_w, out_b, window, gain, bias, gabor, hidden_b, hidden_w, place_row, time_row, starts,
        first, second, twiddle, earlier,
        tab_far, bundle,
        wide, tall, rows, pieces, x_ref, high, low, tab, sent,
    ):
        own, columns = bundle.at[OWN_ROWS, :], bundle.at[COLUMN_ROWS, :]
        own_parameters(layer, meta[3], out_w, out_b, window, gain, bias, gabor, hidden_b, wide, tall, own, columns)
        generate(columns, hidden_w.at[layer], own, place_row, time_row, starts, tab, rows, tab_far, sent)
        for n in range(64):
            for part in range(OWN):
                pieces[part * 64 + n : part * 64 + n + 1, :] = rows[part : part + 1, block(n)]
        for part in range(OWN):
            piece = pieces[block(part, 64), :].astype(BF16)
            x_ref[0:64, block(part)] = piece
            x_ref[64:128, block(part)] = piece
            x_ref[128:256, block(part)] = jnp.zeros((128, LANES), BF16)
        spec = transform(x_ref, high, low, first, second, twiddle, OWN)
        bundle[0:SPEC_IM, :] = spec[:, RE]
        bundle[SPEC_IM : 2 * SPEC_IM, :] = spec[:, IM]
        wait_tables(tab, tab_far, sent)

    return body


def forward_kernel(
    message_ref, kernel_spec, times, first, second, second_back, last, twiddle,
    out_ref, spec_ref, normed_ref, slope_ref, inv_ref, len_ref,
    message, x_ref, high, low, e_high, e_low, y_ref, out,
):
    own = kernel_spec.at[OWN_ROWS, :]
    message[...] = spread(message_ref[...])
    for y in range(4):
        for b in range(2):
            start = y * 16 + 12 + 2 * b
            len_ref[2 * y + b : 2 * y + b + 1, :] = (
                message[start : start + 1, :] * 128.0 + message[start + 1 : start + 2, :]
            )
    load_signals(message, 16, x_ref)
    convolve(x_ref, spec_ref, kernel_spec, high, low, e_high, e_low, (first, second, second_back, last, twiddle), y_ref)
    valid, tally = valid_of(times, len_ref), tally_of(len_ref)
    inv_ref[...] = jnp.zeros((8, LANES), F32)
    for part in range(OWN):
        normed, inv_std, active, slope = normalise(y_ref, own, valid, tally, part)
        normed_ref[:, block(part, 512)] = normed
        slope_ref[:, block(part, 512)] = slope
        inv_ref[part : part + 1, :] = jnp.broadcast_to(inv_std, (1, LANES))
        y_ref[:, block(part, 512)] = active
    store_signals(out, 16, 0, lambda part, y: y_ref[:, block(part * 4 + y)])
    out_ref[...] = out[...].reshape(DEVICES, 16, LANES).astype(BF16)


def gather_active(message, step, rhs):
    row = lax.broadcasted_iota(jnp.int32, (DEVICES, LANES), 0)
    for i in range(4):
        for part in range(OWN):
            piece = message[pl.ds(part * 4 + i, DEVICES, stride=step), :]
            if part != 1:
                piece = jnp.where(row >= (126 if part == 2 else 127), 1.0, piece)
            rhs[block(part), block(i)] = piece.astype(BF16)


def store_rows(value, out, step, base):
    for i in range(4):
        for part in range(OWN):
            out[pl.ds(base + part * 4 + i, DEVICES, stride=step), :] = value[block(part), block(i)]


def mix_kernel(
    meta, message_ref, x_ref, cotangent, weights,
    out_ref, next_ref, active_ref, message, padded, out, low,
):
    message[...] = spread(message_ref[...])
    gather_active(message, 16, active_ref)
    mixed = dot(weights[0], active_ref[...])
    put_padded(padded, x_ref[...])
    for i in range(4):
        valid = valid_row(meta, i)
        value = rows_of_channels(padded, i) + mixed[:, block(i)] * valid
        next_ref[pl.ds(i, PADDED, stride=4), :] = value
        padded[pl.ds(i, PADDED, stride=4), :] = value * valid
    rows_to_message(padded, out, 24, 0)
    put_padded(padded, masked(meta, cotangent[...]))
    for i in range(4):
        low[:, block(i)] = rows_of_channels(padded, i).astype(BF16)
    store_rows(dot(weights[3], low[...]), out, 24, 12)
    out_ref[...] = out[...].reshape(DEVICES, 24, LANES).astype(BF16)


def forward_backward_kernel(
    message_ref, kernel_spec, len_ref, times, first, second, second_back, last, twiddle,
    hidden_w, place_row, time_row, tab_far,
    out_ref, hidden_out, outer_out,
    message, x_ref, high, low, e_high, e_low, y_ref, out, spec_ref, grad_ref, normed_ref, slope_ref, returned_ref,
    rows, sums, mats, tab, arrived,
):
    start_tables(tab_far, tab, arrived)
    own, columns = kernel_spec.at[OWN_ROWS, :], kernel_spec.at[COLUMN_ROWS, :]
    consts = (first, second, second_back, last, twiddle)
    message[...] = spread(message_ref[...])
    load_signals(message, 24, x_ref)
    convolve(x_ref, spec_ref, kernel_spec, high, low, e_high, e_low, consts, y_ref)
    valid, tally = valid_of(times, len_ref), tally_of(len_ref)
    inv = []
    for part in range(OWN):
        normed, inv_std, active, slope = normalise(y_ref, own, valid, tally, part)
        normed_ref[:, block(part, 512)] = normed
        slope_ref[:, block(part, 512)] = slope
        inv.append(inv_std)
        y_ref[:, block(part, 512)] = active
    store_signals(out, 24, 0, lambda part, y: y_ref[:, block(part * 4 + y)])
    returned, norm_sums = conv_backward(
        message, 24, 12, lambda part: normed_ref[:, block(part, 512)], lambda part: slope_ref[:, block(part, 512)],
        lambda part: inv[part], own, valid, tally, spec_ref, kernel_spec, x_ref, high, low, e_high, e_low, consts, grad_ref,
    )
    returned_ref[...] = returned
    store_signals(out, 24, 12, lambda part, y: returned_ref[:, block(part * 4 + y)])
    out_ref[...] = out[...].reshape(DEVICES, 24, LANES).astype(BF16)
    wait_tables(tab_far, tab, arrived)
    hidden, outer = generate_back(
        lambda part: returned_ref[0:64, block(SIGNALS + part)], columns, hidden_w.at[1], own, place_row, time_row, tab,
        rows, sums, mats,
    )
    hidden_out[...] = hidden
    outer_out[...] = with_norm_sums(outer, norm_sums)


def middle_kernel(
    meta, message_ref, x_ref, cotangent, weights, active_0, hidden_1,
    output_ref, flow_ref, out_ref, message, padded, out, low_0, low_1, active_1,
):
    message[...] = spread(message_ref[...])
    gather_active(message, 24, active_1)
    mixed = dot(weights[1], active_1[...])
    for i in range(4):
        padded[pl.ds(i, PADDED, stride=4), :] = rows_of_channels(x_ref, i) + mixed[:, block(i)] * valid_row(meta, i)
    output_ref[...] = padded[0:CLIP_ROWS, :]
    put_padded(flow_ref, cotangent[...])
    for i in range(4):
        low_1[:, block(i)] = (rows_of_channels(flow_ref, i) * valid_row(meta, i)).astype(BF16)
    for m in range(12):
        padded[pl.ds(m, DEVICES, stride=12), :] = message[pl.ds(12 + m, DEVICES, stride=24), :]
    flow_ref[...] += masked(meta, padded[...])
    for i in range(4):
        low_0[:, block(i)] = (rows_of_channels(flow_ref, i) * valid_row(meta, i)).astype(BF16)
    store_rows(dot(weights[2], low_0[...]), out, 32, 0)
    for layer, (active, low) in enumerate(((active_0, low_0), (active_1, low_1))):
        part_sum = dot_rows(active[...], low[...])
        for part in range(OWN):
            for third in range(3):
                out[pl.ds(12 + layer * 9 + part * 3 + third, DEVICES, stride=32), :] = part_sum[
                    block(part), block(third)
                ]
    high, low = high_low(hidden_1[...])
    out[pl.ds(30, DEVICES, stride=32), :] = jnp.concatenate([high, jnp.zeros((96, LANES), F32)], axis=0)
    out[pl.ds(31, DEVICES, stride=32), :] = jnp.concatenate([low, jnp.zeros((96, LANES), F32)], axis=0)
    out_ref[...] = out[...].reshape(DEVICES, 32, LANES).astype(BF16)


LAST_ROWS = 56


def backward_kernel(
    message_ref, spec_ref, kernel_spec, normed_ref, slope_ref, inv_ref, len_ref, times,
    first, second, second_back, last, twiddle, hidden_w, place_row, time_row, tab_far, outer_1,
    out_ref,
    message, x_ref, high, low, e_high, e_low, out, grad_ref, returned_ref, rows, sums, mats, tab, arrived,
):
    start_tables(tab_far, tab, arrived)
    own, columns = kernel_spec.at[OWN_ROWS, :], kernel_spec.at[COLUMN_ROWS, :]
    consts = (first, second, second_back, last, twiddle)
    message[...] = spread(message_ref[...])
    valid, tally = valid_of(times, len_ref), tally_of(len_ref)
    returned, norm_sums = conv_backward(
        message, 32, 0, lambda part: normed_ref[:, block(part, 512)], lambda part: slope_ref[:, block(part, 512)],
        lambda part: inv_ref[part : part + 1, 0:1], own, valid, tally, spec_ref, kernel_spec, x_ref, high, low,
        e_high, e_low, consts, grad_ref,
    )
    returned_ref[...] = returned
    store_signals(out, 16, 0, lambda part, y: returned_ref[:, block(part * 4 + y)])
    wait_tables(tab_far, tab, arrived)
    hidden, outer = generate_back(
        lambda part: returned_ref[0:64, block(SIGNALS + part)], columns, hidden_w.at[0], own, place_row, time_row, tab,
        rows, sums, mats,
    )
    outer = with_norm_sums(outer, norm_sums)
    gathered = jnp.sum(message[...].reshape(DEVICES, 32, LANES), axis=0)
    upper, lower = packed_hidden(hidden)
    hidden_1_high, hidden_1_low = high_low(gathered[30:31, :] + gathered[31:32, :])
    outer_0_high, outer_0_low = high_low(one_row(outer))
    outer_1_high, outer_1_low = high_low(one_row(outer_1[...]))
    shared = jnp.concatenate(
        [
            gathered[0:30, :], upper, lower, hidden_1_high, hidden_1_low,
            outer_0_high, outer_0_low, outer_1_high, outer_1_low,
        ],
        axis=0,
    )
    row = lax.broadcasted_iota(jnp.int32, (DEVICES, 16, LANES), 1)
    own_rows = jnp.where(row < 12, out[...].reshape(DEVICES, 16, LANES), shared[None, 0:16, :])
    rest = jnp.broadcast_to(shared[None, 16:LAST_ROWS, :], (DEVICES, LAST_ROWS - 16, LANES))
    out_ref[...] = jnp.concatenate([own_rows, rest], axis=1).astype(BF16)


def last_kernel(
    meta, message_ref, flow_ref, lookup,
    input_grad, gabor_grad, hidden_w_grad, hidden_b_grad, out_w_grad, out_b_grad, gain_grad, bias_grad,
    mix_w_grad, mix_b_grad, message, padded, owned, thirds,
):
    message[...] = spread(message_ref[...])

    def rows_of(k, count=DEVICES):
        return message[pl.ds(k, count, stride=LAST_ROWS), :]

    for m in range(12):
        padded[pl.ds(m, DEVICES, stride=12), :] = rows_of(m)
    input_grad[...] = flow_ref[0:CLIP_ROWS, :] + masked(meta, padded[0:CLIP_ROWS, :])
    shared = jnp.sum(message[...].reshape(DEVICES, LAST_ROWS, LANES)[:, 24:56, :], axis=0)
    hidden_0 = unpacked_hidden(shared[6:22, :], shared[22:26, :])
    hidden_1 = rows_of(50, 32) + rows_of(51, 32)
    lane = lax.broadcasted_iota(jnp.int32, (DEVICES, LANES), 1)
    for layer, hidden in enumerate((hidden_0, hidden_1)):
        hidden_w_grad[layer, 0] = hidden[:, 0:32]
        hidden_w_grad[layer, 1] = pltpu.roll(hidden, 96, 1)[:, 0:32]
        turned = jnp.transpose(jnp.concatenate([hidden, jnp.zeros((96, LANES), F32)], axis=0))
        hidden_b_grad[layer] = turned[64:66, 0:32]
        for j in range(3):
            gabor_grad[layer, j] = turned[66 + 4 * j : 70 + 4 * j, 0:32]
        value = rows_of(52 + 2 * layer) + rows_of(53 + 2 * layer)
        for part in range(OWN):
            wide = pltpu.roll(value, (LANES - 32 * part) % LANES, 1)
            small = pltpu.roll(value, 64 - 3 * part, 1)
            owned[pl.ds(part, DEVICES, stride=OWN), :] = jnp.where(lane < 32, wide, small)
        turned = jnp.transpose(owned[...])
        out_w_grad[layer] = turned[0:32, 0:CHANNELS]
        out_b_grad[layer : layer + 1, :] = turned[32:33, 0:CHANNELS]
        gain_grad[layer : layer + 1, :] = turned[33:34, 0:CHANNELS]
        bias_grad[layer : layer + 1, :] = turned[34:35, 0:CHANNELS]
        bias_rows = []
        for part in range(OWN):
            for third in range(3):
                piece = rows_of(12 + layer * 9 + part * 3 + third)
                thirds[block(part), block(third)] = piece.astype(BF16)
                if part == 2:
                    bias_rows.append(piece[SPOT - 2 * DEVICES : SPOT - 2 * DEVICES + 1, :])
        mix_w_grad[layer] = dot_columns(thirds[...], lookup[...])[0:CHANNELS, 0:CHANNELS]
        mix_b_grad[layer : layer + 1, :] = jnp.concatenate(bias_rows, axis=1)[:, 0:CHANNELS]


def exchange(message):
    return lax.all_to_all(message, AXES, split_axis=0, concat_axis=0, tiled=True)


def to_rows(clips):
    return clips.reshape(2, CHANNELS, 2, LANES).transpose(1, 2, 0, 3).reshape(CLIP_ROWS, LANES)


def from_rows(rows):
    return rows.reshape(CHANNELS, 2, 2, LANES).transpose(2, 0, 1, 3).reshape(2, CHANNELS, PIECE)


def shards(
    inputs, lengths, window, gabor_params, hidden_w, hidden_b, out_w, out_b, bn_gain, bn_bias, mix_w, mix_b, cotangent
):
    position = lax.axis_index("seq").astype(jnp.int32)
    number = position * 4 + lax.axis_index("clips").astype(jnp.int32)
    const = {name: jnp.asarray(value) for name, value in TABLES.items()}
    meta = jnp.concatenate([lengths, jnp.stack([position, number])])
    inputs, cotangent = to_rows(inputs), to_rows(cotangent)

    def rows(count):
        return ((count, LANES), F32)

    with jax.named_scope("source_0"):
        (message,) = run(
            source_kernel, [((DEVICES, 16, LANES), BF16)], [meta, inputs], [rows(PADDED_ROWS), rows(DEVICES * 16)],
            "source_0", 8, smem=(0,),
        )
        message = exchange(message)

    owns = [
        meta, jnp.swapaxes(out_w, 1, 2), out_b, jnp.swapaxes(window, 1, 2), bn_gain, bn_bias, gabor_params, hidden_b,
        hidden_w, const["place_row"], const["time_row"], const["starts"], const["first"], const["second"],
        const["twiddle"],
    ]

    shape_tab = ((8, HIDDEN, SAMPLES), F32)

    def generator(layer, earlier):
        return run(
            generate_kernel(layer),
            [shape_tab, rows(BUNDLE)],
            [*owns, earlier],
            [
                ((LANES, PADDED), F32), rows(PADDED + 8), ((8, SAMPLES), F32), rows(192),
                ((256, OWN * LANES), BF16), ((OWN * LANES, 256), BF16), ((OWN * LANES, 256), BF16),
                shape_tab,
            ],
            f"generator_{layer}", GRANT, smem=(0,), far=(len(owns),), far_outs=(0,), copies=TABLES_KEPT,
        )

    square = (PADDED, PADDED)
    with jax.named_scope("weights"):
        (weights,) = run(
            weights_kernel, [((4, *square), BF16)], [mix_w, mix_b, const["lookup"]], [(square, BF16)], "weights", 8,
        )

    with jax.named_scope("generators"):
        tab_1, bundle_1 = generator(1, weights)
        tab_0, bundle_0 = generator(0, bundle_1)

    def scratch(signals):
        count = signals * LANES
        return [
            ((256, SIGNALS * LANES), BF16), ((count, 256), BF16), ((count, 256), BF16),
            ((256, count), BF16), ((256, count), BF16),
        ]

    shape_y = (LANES, SIGNALS * LANES)
    shape_s = (SIGNALS * LANES, 256)
    transforms = [const[name] for name in ("first", "second", "second_back", "last", "twiddle")]
    with jax.named_scope("conv_0"):
        message, spec_0, normed_0, slope_0, inv_0, lens = run(
            forward_kernel,
            [
                ((DEVICES, 16, LANES), BF16), (shape_s, F32), (shape_y, F32), (shape_y, F32), rows(8), rows(8),
            ],
            [message, bundle_0, const["times"], *transforms],
            [rows(DEVICES * 16), *scratch(SIGNALS), (shape_y, F32), rows(DEVICES * 16)],
            "conv_0", 20,
        )
        message = exchange(message)

    with jax.named_scope("mix_0"):
        message, middle, active_0 = run(
            mix_kernel,
            [((DEVICES, 24, LANES), BF16), rows(PADDED_ROWS), ((PADDED, 512), BF16)],
            [meta, message, inputs, cotangent, weights],
            [rows(DEVICES * 16), rows(PADDED_ROWS), rows(DEVICES * 24), ((PADDED, 512), BF16)],
            "mix_0", 12, smem=(0,),
        )
        message = exchange(message)

    back_scratch = [((8, SAMPLES), F32), rows(14 * 32 + 8), rows(72), shape_tab]
    with jax.named_scope("conv_1"):
        message, hidden_1, outer_1 = run(
            forward_backward_kernel,
            [((DEVICES, 24, LANES), BF16), rows(HIDDEN), rows(8)],
            [
                message, bundle_1, lens, const["times"], *transforms, hidden_w, const["place_row"], const["time_row"],
                tab_1,
            ],
            [
                rows(DEVICES * 24), *scratch(SIGNALS + OWN), (shape_y, F32), rows(DEVICES * 24),
                (shape_s, F32), (shape_s, F32), (shape_y, F32), (shape_y, F32),
                ((LANES, (SIGNALS + OWN) * LANES), F32), *back_scratch,
            ],
            "conv_1", GRANT, far=(12,), copies=TABLES_KEPT,
        )
        message = exchange(message)

    with jax.named_scope("mix_1"):
        outputs, flow, message = run(
            middle_kernel,
            [rows(CLIP_ROWS), rows(PADDED_ROWS), ((DEVICES, 32, LANES), BF16)],
            [meta, message, middle, cotangent, weights, active_0, hidden_1],
            [
                rows(DEVICES * 24), rows(PADDED_ROWS), rows(DEVICES * 32),
                ((PADDED, 512), BF16), ((PADDED, 512), BF16), ((PADDED, 512), BF16),
            ],
            "mix_1", 12, smem=(0,),
        )
        message = exchange(message)

    with jax.named_scope("conv_back_0"):
        (message,) = run(
            backward_kernel,
            [((DEVICES, LAST_ROWS, LANES), BF16)],
            [
                message, spec_0, bundle_0, normed_0, slope_0, inv_0, lens, const["times"], *transforms,
                hidden_w, const["place_row"], const["time_row"], tab_0, outer_1,
            ],
            [
                rows(DEVICES * 32), *scratch(SIGNALS + OWN), rows(DEVICES * 16), (shape_s, F32),
                ((LANES, (SIGNALS + OWN) * LANES), F32), *back_scratch,
            ],
            "conv_back_0", GRANT, far=(16,), copies=TABLES_KEPT,
        )
        message = exchange(message)

    with jax.named_scope("gradients"):
        (
            input_grad, gabor_grad, hidden_w_grad, hidden_b_grad, out_w_grad, out_b_grad, gain_grad, bias_grad,
            mix_w_grad, mix_b_grad,
        ) = run(
            last_kernel,
            [
                rows(CLIP_ROWS), (gabor_params.shape, F32), (hidden_w.shape, F32), (hidden_b.shape, F32),
                ((2, HIDDEN, CHANNELS), F32), (out_b.shape, F32), (bn_gain.shape, F32), (bn_bias.shape, F32),
                (mix_w.shape, F32), (mix_b.shape, F32),
            ],
            [meta, message, flow, const["lookup"]],
            [rows(DEVICES * LAST_ROWS), rows(PADDED_ROWS), rows(PADDED), (square, BF16)],
            "gradients", 14, smem=(0,),
        )
    return (
        from_rows(outputs), from_rows(input_grad), gabor_grad, hidden_w_grad, hidden_b_grad,
        jnp.swapaxes(out_w_grad, 1, 2), out_b_grad, gain_grad, bias_grad, mix_w_grad, mix_b_grad,
    )


def solution(mesh):
    clip = P("clips", None, "seq")
    in_specs = (clip, P("clips")) + (P(),) * 10 + (clip,)
    out_specs = (clip, clip) + (P(),) * 9
    return jax.shard_map(shards, mesh=mesh, in_specs=in_specs, out_specs=out_specs, check_vma=False)
```

```python
import math

import jax
import jax.numpy as jnp
import ml_dtypes
import numpy as np
from jax import lax
from jax.experimental import pallas as pl
from jax.experimental.pallas import tpu as pltpu
from jax.sharding import PartitionSpec as P

F32 = jnp.float32
BF16 = jnp.bfloat16
AXES = ("seq", "clips")
DEVICES = 128
OWN = 3
CHANNELS = 380
PADDED = DEVICES * OWN
SAMPLES = 8192
PIECE = 256
HIDDEN = 32
LANES = 128
SIGNALS = 12
PERIOD = 2 * SAMPLES
EPSILON = 1e-05
MEGABYTE = 1024 * 1024
EXACT = lax.Precision.HIGHEST
SPOTS = (2 * DEVICES + 126, 2 * DEVICES + 127, 127)
SPOT = SPOTS[0]


def halves(table):
    high = table.astype(ml_dtypes.bfloat16)
    low = (table - high.astype(np.float64)).astype(ml_dtypes.bfloat16)
    return high, low


def tables():
    order = np.array([2 * j + r for r in range(2) for j in range(32)])
    k = np.arange(LANES)
    turn = 2 * np.pi * ((k[:, None] * order[None, :]) % LANES) / LANES
    c_high, c_low = halves(np.cos(turn))
    s_high, s_low = halves(np.sin(turn))
    first = np.concatenate(
        [
            np.concatenate([c_high, c_low, s_high, s_low], axis=1),
            np.concatenate([-s_high, -s_low, c_high, c_low], axis=1),
        ],
        axis=0,
    )
    turn = 2 * np.pi * ((k[:, None] * k[None, :]) % LANES) / LANES
    cosine, sine = np.cos(turn), np.sin(turn)
    second = halves(np.block([[cosine, -sine], [sine, cosine]]))
    second_back = halves(np.block([[cosine, sine], [-sine, cosine]]))
    turn = 2 * np.pi * ((order[:, None] * k[None, :]) % LANES) / LANES
    cosine, sine = np.cos(turn) / PERIOD, np.sin(turn) / PERIOD
    last = halves(np.block([[cosine, -sine], [sine, cosine]]))
    turn = 2 * np.pi * (k[:, None] * k[None, :]) / PERIOD
    twiddle = np.stack([np.cos(turn), np.sin(turn)]).astype(np.float32)
    times = (128 * order[:, None] + k[None, :]).astype(np.float32)
    places = (-1.0 + 2.0 * times / np.float32(SAMPLES - 1)).astype(np.float32)
    lookup = np.zeros((PADDED, PADDED), ml_dtypes.bfloat16)
    for part in range(OWN):
        for owner in range(DEVICES):
            lookup[part * DEVICES + owner, OWN * owner + part] = 1
    return dict(
        first=first,
        second=np.stack(second),
        second_back=np.stack(second_back),
        last=np.stack(last),
        twiddle=twiddle,
        times=np.concatenate([times, times], axis=0),
        time_row=times.reshape(1, SAMPLES),
        place_row=places.reshape(1, SAMPLES),
        starts=np.stack([np.pad(places[:, 0], (0, 64)), 2.0 * k / (SAMPLES - 1)]).astype(np.float32),
        lookup=lookup,
    )


TABLES = tables()


def run(body, outs, args, scratch, name, grant, smem=(), far=()):
    spaces = [pltpu.HBM if i in far else pltpu.SMEM if i in smem else pltpu.VMEM for i in range(len(args))]
    return pl.pallas_call(
        body,
        out_shape=[jax.ShapeDtypeStruct(shape, kind) for shape, kind in outs],
        in_specs=[pl.BlockSpec(memory_space=space) for space in spaces],
        out_specs=[pl.BlockSpec(memory_space=pltpu.VMEM)] * len(outs),
        scratch_shapes=[pltpu.VMEM(shape, kind) for shape, kind in scratch],
        compiler_params=pltpu.CompilerParams(vmem_limit_bytes=grant * MEGABYTE),
        name=name,
    )(*args)


def dot(a, b):
    return jnp.dot(a, b, preferred_element_type=F32)


def dot_rows(a, b, precision=None):
    return lax.dot_general(a, b, (((1,), (1,)), ((), ())), precision=precision, preferred_element_type=F32)


def dot_columns(a, b, precision=None):
    return lax.dot_general(a, b, (((0,), (0,)), ((), ())), precision=precision, preferred_element_type=F32)


def triple(a_high, a_low, b_high, b_low):
    left = jnp.concatenate([a_high, a_low, a_high], axis=1)
    return dot(left, jnp.concatenate([b_high, b_high, b_low], axis=0))


def put_halves(high_ref, low_ref, rows, columns, value):
    high = value.astype(BF16)
    high_ref[rows, columns] = high
    low_ref[rows, columns] = (value - high.astype(F32)).astype(BF16)


def block(i, size=LANES):
    return slice(i * size, (i + 1) * size)


RE, IM = slice(0, LANES), slice(LANES, 2 * LANES)


def signal_row(b, part, r):
    return part * 4 + r * 2 + b


def spread(message):
    return message.astype(F32).reshape(-1, LANES)


def transform(x_ref, high_ref, low_ref, first, second, twiddle, count):
    part_a = dot(first[...], x_ref[:, : count * LANES])
    cosine, sine = twiddle[0], twiddle[1]
    for s in range(count):
        real, imag = part_a[:LANES, block(s)], part_a[LANES:, block(s)]
        put_halves(high_ref, low_ref, block(s), RE, real * cosine + imag * sine)
        put_halves(high_ref, low_ref, block(s), IM, imag * cosine - real * sine)
    rows = slice(0, count * LANES)
    return triple(high_ref[rows, :], low_ref[rows, :], second[0], second[1])


def transform_back(high_ref, low_ref, e_high, e_low, second_back, last, twiddle, count):
    rows = slice(0, count * LANES)
    part_d = triple(high_ref[rows, :], low_ref[rows, :], second_back[0], second_back[1])
    cosine, sine = twiddle[0], twiddle[1]
    for s in range(count):
        real, imag = part_d[block(s), RE], part_d[block(s), IM]
        put_halves(e_high, e_low, RE, block(s), real * cosine - imag * sine)
        put_halves(e_high, e_low, IM, block(s), real * sine + imag * cosine)
    return triple(last[0], last[1], e_high[:, rows], e_low[:, rows])


def erf_parts(value):
    cdf = 0.5 * (1.0 + lax.erf(value * math.sqrt(0.5)))
    return cdf, jnp.exp(-0.5 * value * value) * (1.0 / math.sqrt(2.0 * math.pi))


def total(value):
    return jnp.sum(jnp.sum(value, axis=0, keepdims=True), axis=1, keepdims=True)


def valid_of(times, len_ref):
    columns = []
    for y in range(4):
        upper = times[0:64, :] < len_ref[2 * y : 2 * y + 1, :]
        lower = times[64:128, :] < len_ref[2 * y + 1 : 2 * y + 2, :]
        columns.append(jnp.concatenate([upper, lower], axis=0).astype(F32))
    return jnp.concatenate(columns, axis=1)


def tally_of(len_ref):
    return jnp.sum(len_ref[:, 0:1], axis=0, keepdims=True)


def load_signals(message, step, x_ref):
    for part in range(OWN):
        for y in range(4):
            lanes = block(part * 4 + y)
            for b in range(2):
                for r in range(2):
                    start = y * step + signal_row(b, part, r)
                    piece = message[pl.ds(start, 32, stride=4 * step), :].astype(BF16)
                    x_ref[b * 128 + r * 32 : b * 128 + r * 32 + 32, lanes] = piece
                    x_ref[b * 128 + r * 32 + 64 : b * 128 + r * 32 + 96, lanes] = piece


def store_signals(out, step, base, get):
    for part in range(OWN):
        for y in range(4):
            value = get(part, y)
            for b in range(2):
                for r in range(2):
                    start = y * step + base + signal_row(b, part, r)
                    out[pl.ds(start, 32, stride=4 * step), :] = value[b * 64 + r * 32 : b * 64 + r * 32 + 32, :]


SPEC_IM = OWN * LANES
OWN_ROWS = slice(2 * SPEC_IM, 2 * SPEC_IM + 8)
COLUMN_ROWS = slice(2 * SPEC_IM + 8, 2 * SPEC_IM + 8 + HIDDEN)
BUNDLE = 2 * SPEC_IM + 8 + HIDDEN


def kernel_parts(bundle, part):
    return bundle[block(part), :], bundle[SPEC_IM + part * LANES : SPEC_IM + (part + 1) * LANES, :]


def convolve(x_ref, spec_ref, kernel_spec, high, low, e_high, e_low, consts, y_ref):
    first, second, second_back, last, twiddle = consts
    spec_ref[...] = transform(x_ref, high, low, first, second, twiddle, SIGNALS)
    for part in range(OWN):
        k_re, k_im = kernel_parts(kernel_spec, part)
        for y in range(4):
            rows = block(part * 4 + y)
            s_re, s_im = spec_ref[rows, RE], spec_ref[rows, IM]
            put_halves(high, low, rows, RE, s_re * k_re - s_im * k_im)
            put_halves(high, low, rows, IM, s_re * k_im + s_im * k_re)
    y_ref[...] = transform_back(high, low, e_high, e_low, second_back, last, twiddle, SIGNALS)


def normalise(y_ref, own, valid, tally, part):
    value = y_ref[:, block(part, 512)]
    mean = total(valid * value) / tally
    centred = value - mean
    var = total(valid * centred * centred) / tally
    inv_std = lax.rsqrt(var + EPSILON)
    normed = centred * inv_std
    pre_act = normed * own[part : part + 1, 35:36] + own[part : part + 1, 36:37]
    cdf, density = erf_parts(pre_act)
    return normed, inv_std, pre_act * cdf, cdf + pre_act * density


def conv_backward(
    message, step, base, normed_of, slope_of, inv_of, own, valid, tally, spec_ref, kernel_spec, x_ref, high, low,
    e_high, e_low, consts, grad_ref,
):
    first, second, second_back, last, twiddle = consts
    sums = []
    for part in range(OWN):
        columns = []
        for y in range(4):
            pieces = []
            for b in range(2):
                for r in range(2):
                    start = y * step + base + signal_row(b, part, r)
                    pieces.append(message[pl.ds(start, 32, stride=4 * step), :])
            columns.append(jnp.concatenate(pieces, axis=0))
        act_grad = jnp.concatenate(columns, axis=1)
        normed = normed_of(part)
        pre_grad = act_grad * slope_of(part)
        bias_total = total(pre_grad)
        gain_total = total(pre_grad * normed)
        gain = own[part : part + 1, 35:36]
        conv_grad = inv_of(part) * (
            gain * pre_grad - valid * (gain * bias_total + normed * (gain * gain_total)) / tally
        )
        conv_low = conv_grad.astype(BF16)
        for b in range(2):
            piece = conv_low[b * 64 : b * 64 + 64, :]
            x_ref[b * 128 : b * 128 + 64, block(part, 512)] = piece
            x_ref[b * 128 + 64 : b * 128 + 128, block(part, 512)] = piece
        sums.append((gain_total, bias_total))
    grad_ref[...] = transform(x_ref, high, low, first, second, twiddle, SIGNALS)
    for part in range(OWN):
        k_re, k_im = kernel_parts(kernel_spec, part)
        corr_re, corr_im = None, None
        for y in range(4):
            rows = block(part * 4 + y)
            g_re, g_im = grad_ref[rows, RE], grad_ref[rows, IM]
            s_re, s_im = spec_ref[rows, RE], spec_ref[rows, IM]
            put_halves(high, low, rows, RE, k_re * g_re + k_im * g_im)
            put_halves(high, low, rows, IM, k_re * g_im - k_im * g_re)
            now_re, now_im = s_re * g_re + s_im * g_im, s_re * g_im - s_im * g_re
            corr_re = now_re if corr_re is None else corr_re + now_re
            corr_im = now_im if corr_im is None else corr_im + now_im
        put_halves(high, low, block(SIGNALS + part), RE, corr_re)
        put_halves(high, low, block(SIGNALS + part), IM, corr_im)
    returned = transform_back(high, low, e_high, e_low, second_back, last, twiddle, SIGNALS + OWN)
    return returned, sums


def sin_cos(angle):
    turns = jnp.floor(angle * (2.0 / math.pi) + 0.5)
    rest = angle - turns * 1.5703125
    rest = rest - turns * 4.837512969970703125e-4
    rest = rest - turns * 7.549789948768648e-8
    square = rest * rest
    sine = rest + rest * square * (
        -1.6666654611e-1 + square * (8.3321608736e-3 + square * -1.9515295891e-4)
    )
    cosine = 1.0 - 0.5 * square + square * square * (
        4.166664568298827e-2 + square * (-1.388731625493765e-3 + square * 2.443315711809948e-5)
    )
    half = jnp.floor(turns * 0.5)
    odd = turns - 2.0 * half
    sign = 1.0 - 2.0 * (half - 2.0 * jnp.floor(half * 0.5))
    is_odd = odd > 0.5
    return sign * jnp.where(is_odd, cosine, sine), sign * jnp.where(is_odd, -sine, cosine)


CHUNK = 1024


def envelope_of(times, own):
    lower, upper = own[:, 33:34], own[:, 34:35]
    inside = (times >= lower) & (times < upper)
    offset = (times - lower) / (0.5 * (upper - lower))
    return jnp.where(inside, jnp.exp(-0.5 * offset * offset), 0.0)


def stacked_weight(weight):
    high, low = high_low(weight)
    return jnp.concatenate([high, high, low], axis=1).astype(BF16)


def stacked_dot(weight, value):
    high = value.astype(BF16)
    low = (value - high.astype(F32)).astype(BF16)
    return dot(weight, jnp.concatenate([high, low, high], axis=0))


def own_parameters(layer, number, out_w, out_b, window, gain, bias, gabor, hidden_b, wide, tall, own, columns):
    wide[...] = jnp.zeros(wide.shape, F32)
    wide[0:32, 0:CHANNELS] = out_w[layer]
    wide[32:33, 0:CHANNELS] = out_b[layer : layer + 1, :]
    wide[33:35, 0:CHANNELS] = window[layer].astype(F32)
    wide[35:36, 0:CHANNELS] = gain[layer : layer + 1, :]
    wide[36:37, 0:CHANNELS] = bias[layer : layer + 1, :]
    tall[0:PADDED, :] = jnp.transpose(wide[...])
    tall[PADDED : PADDED + 8, :] = jnp.zeros((8, LANES), F32)
    row = lax.broadcasted_iota(jnp.int32, (8, LANES), 0)
    lane = lax.broadcasted_iota(jnp.int32, (8, LANES), 1)
    mine = tall[pl.ds(number * OWN, 8), :]
    unused = (row >= OWN) | (number * OWN + row >= CHANNELS)
    own[...] = jnp.where(unused, jnp.where(lane == 34, float(SAMPLES), 0.0), mine)
    wide[:, 0:LANES] = jnp.zeros((LANES, LANES), F32)
    for j in range(3):
        wide[4 * j : 4 * j + 4, 0:HIDDEN] = gabor[layer, j]
    wide[12:14, 0:HIDDEN] = hidden_b[layer]
    columns[...] = jnp.transpose(wide[:, 0:LANES])[0:HIDDEN, :]


def generate(columns, hidden_w, own, place_row, time_row, starts, tab, rows):
    places = place_row[...]
    weights = [stacked_weight(hidden_w[0]), stacked_weight(hidden_w[1]), stacked_weight(own[:, 0:32])]

    def level(j):
        frequency, phase = columns[:, 4 * j + 2 : 4 * j + 3], columns[:, 4 * j + 3 : 4 * j + 4]
        start_sin, start_cos = sin_cos(frequency * starts[0:1, :] + phase)
        rest_sin, rest_cos = sin_cos(frequency * starts[1:2, :])
        sine, cosine = [], []
        for n in range(64):
            s_n, c_n = start_sin[:, n : n + 1], start_cos[:, n : n + 1]
            sine.append(s_n * rest_cos + c_n * rest_sin)
            cosine.append(c_n * rest_cos - s_n * rest_sin)
        width = columns[:, 4 * j : 4 * j + 1] * (places - columns[:, 4 * j + 1 : 4 * j + 2])
        bell = jnp.exp(-0.5 * width * width)
        return bell * jnp.concatenate(sine, axis=1), bell * jnp.concatenate(cosine, axis=1)

    def keep(k, value):
        tab[k] = value

    f_0, c_0 = level(0)
    keep(0, f_0)
    keep(1, c_0)
    u_1 = stacked_dot(weights[0], f_0) + columns[:, 12:13]
    f_1, c_1 = level(1)
    z_1 = u_1 * f_1
    keep(2, z_1)
    keep(3, u_1 * c_1)
    keep(4, f_1)
    u_2 = stacked_dot(weights[1], z_1) + columns[:, 13:14]
    f_2, c_2 = level(2)
    z_2 = u_2 * f_2
    keep(5, z_2)
    keep(6, u_2 * c_2)
    keep(7, f_2)
    raw = stacked_dot(weights[2], z_2) + own[:, 32:33]
    rows[...] = raw * envelope_of(time_row[...], own)


def generate_back(kernel_grad, columns, hidden_w, own, place_row, time_row, tab, rows, sums, mats):
    rows[...] = jnp.zeros(rows.shape, F32)
    for part in range(OWN):
        grad = kernel_grad(part)
        for n in range(64):
            rows[part : part + 1, block(n)] = grad[n : n + 1, :]
    sums[...] = jnp.zeros(sums.shape, F32)
    mats[...] = jnp.zeros(mats.shape, F32)
    turned = jnp.transpose(jnp.concatenate([own[...], jnp.zeros((120, 128), F32)], axis=0))
    weight = [turned[0:32, part : part + 1] for part in range(OWN)]
    back = [stacked_weight(jnp.transpose(hidden_w[j])) for j in range(2)]

    def fold(value):
        acc = value[:, block(0)]
        for i in range(1, CHUNK // LANES):
            acc = acc + value[:, block(i)]
        return acc

    def add(k, value):
        sums[block(k, 32), :] += fold(value)

    def step(i, carry):
        span = pl.ds(pl.multiple_of(i * CHUNK, CHUNK), CHUNK)
        places = place_row[:, span]
        draw = rows[:, span] * envelope_of(time_row[:, span], own)
        dz_2 = weight[0] * draw[0:1, :] + weight[1] * draw[1:2, :] + weight[2] * draw[2:3, :]

        def level(j, e_value, g_value):
            centre = columns[:, 4 * j + 1 : 4 * j + 2]
            offset = places - centre
            moment = e_value * offset
            add(4 * j, moment * offset)
            add(4 * j + 1, moment)
            add(4 * j + 2, g_value * places)
            add(4 * j + 3, g_value)

        z_2 = tab[5, :, span]
        level(2, dz_2 * z_2, dz_2 * tab[6, :, span])
        du_2 = dz_2 * tab[7, :, span]
        add(13, du_2)
        dz_1 = stacked_dot(back[1], du_2)
        z_1 = tab[2, :, span]
        level(1, dz_1 * z_1, dz_1 * tab[3, :, span])
        du_1 = dz_1 * tab[4, :, span]
        add(12, du_1)
        dz_0 = stacked_dot(back[0], du_1)
        z_0 = tab[0, :, span]
        level(0, dz_0 * z_0, dz_0 * tab[1, :, span])
        sums[14 * 32 : 14 * 32 + 8, :] += fold(draw)
        left = jnp.concatenate([du_1, du_2, draw], axis=0)
        right = jnp.concatenate([z_0, z_1, z_2, jnp.zeros_like(z_0)], axis=0)
        left_high, right_high = left.astype(BF16), right.astype(BF16)
        left_low = (left - left_high.astype(F32)).astype(BF16)
        right_low = (right - right_high.astype(F32)).astype(BF16)
        mats[...] += (
            dot_rows(left_high, right_high) + dot_rows(left_low, right_high) + dot_rows(left_high, right_low)
        )
        return carry

    lax.fori_loop(0, SAMPLES // CHUNK, step, 0, unroll=SAMPLES // CHUNK)
    lane = lax.broadcasted_iota(jnp.int32, (32, LANES), 1)
    hidden = jnp.where(lane < 32, mats[0:32, :], jnp.where(lane < 64, mats[32:64, :], 0.0))

    def column(k):
        return jnp.sum(sums[block(k, 32), :], axis=1, keepdims=True)

    hidden = jnp.where(lane == 64, column(12), hidden)
    hidden = jnp.where(lane == 65, column(13), hidden)
    for j in range(3):
        sharpness = columns[:, 4 * j : 4 * j + 1]
        hidden = jnp.where(lane == 66 + 4 * j, -sharpness * column(4 * j), hidden)
        hidden = jnp.where(lane == 67 + 4 * j, sharpness * sharpness * column(4 * j + 1), hidden)
        hidden = jnp.where(lane == 68 + 4 * j, column(4 * j + 2), hidden)
        hidden = jnp.where(lane == 69 + 4 * j, column(4 * j + 3), hidden)
    lane8 = lax.broadcasted_iota(jnp.int32, (8, LANES), 1)
    outer = pltpu.roll(mats[64:72, :], LANES - 64, 1)
    raw_total = jnp.sum(sums[14 * 32 : 14 * 32 + 8, :], axis=1, keepdims=True)
    outer = jnp.where(lane8 < 32, outer, 0.0)
    outer = jnp.where(lane8 == 32, raw_total, outer)
    return hidden, outer


def with_norm_sums(outer, sums):
    row = lax.broadcasted_iota(jnp.int32, (8, LANES), 0)
    lane = lax.broadcasted_iota(jnp.int32, (8, LANES), 1)
    for part in range(OWN):
        gain_total, bias_total = sums[part]
        outer = jnp.where((row == part) & (lane == 33), gain_total, outer)
        outer = jnp.where((row == part) & (lane == 34), bias_total, outer)
    return outer


def one_row(outer):
    lane = lax.broadcasted_iota(jnp.int32, (1, LANES), 1)
    result = jnp.zeros((1, LANES), F32)
    for part in range(OWN):
        row = outer[part : part + 1, :]
        moved = pltpu.roll(row, 32 * part, 1) if part else row
        result = jnp.where((lane >= 32 * part) & (lane < 32 * part + 32), moved, result)
        moved = pltpu.roll(row, 64 + 3 * part, 1)
        result = jnp.where((lane >= 96 + 3 * part) & (lane < 99 + 3 * part), moved, result)
    return result


def packed_hidden(hidden):
    lane16 = lax.broadcasted_iota(jnp.int32, (16, LANES), 1)
    upper = jnp.where(lane16 < 64, hidden[0:16, :], pltpu.roll(hidden[16:32, :], 64, 1))
    lane4 = lax.broadcasted_iota(jnp.int32, (4, LANES), 1)
    lower = jnp.zeros((4, LANES), F32)
    for g in range(8):
        moved = pltpu.roll(hidden, (64 + 16 * g) % LANES, 1)[4 * g : 4 * g + 4, :]
        lower = jnp.where((lane4 >= 16 * g) & (lane4 < 16 * g + 16), moved, lower)
    return upper, lower


def unpacked_hidden(upper, lower):
    lane16 = lax.broadcasted_iota(jnp.int32, (16, LANES), 1)
    lane32 = lax.broadcasted_iota(jnp.int32, (32, LANES), 1)
    top = jnp.concatenate([upper, pltpu.roll(upper, 64, 1)], axis=0)
    tiled = jnp.concatenate([lower] * 8, axis=0)
    row32 = lax.broadcasted_iota(jnp.int32, (32, LANES), 0)
    rest = jnp.zeros((32, LANES), F32)
    for g in range(8):
        moved = pltpu.roll(tiled, (64 - 16 * g) % LANES, 1)
        rest = jnp.where((row32 >= 4 * g) & (row32 < 4 * g + 4), moved, rest)
    return jnp.where(lane32 < 64, top, rest)


def high_low(value):
    high = value.astype(BF16).astype(F32)
    return high, value - high


def valid_row(meta, i):
    lane = lax.broadcasted_iota(jnp.int32, (1, LANES), 1)
    return (meta[2] * PIECE + (i // 2) * LANES + lane < meta[i % 2]).astype(F32)


def masked(meta, rows):
    mask = jnp.concatenate([valid_row(meta, i) for i in range(4)] * 2, axis=0)
    return (rows.reshape(-1, 8, LANES) * mask[None]).reshape(-1, LANES)


CLIP_ROWS = 4 * CHANNELS
PADDED_ROWS = 4 * PADDED


def put_padded(padded, rows):
    padded[0:CLIP_ROWS, :] = rows
    padded[CLIP_ROWS:PADDED_ROWS, :] = jnp.zeros((PADDED_ROWS - CLIP_ROWS, LANES), F32)


def rows_to_message(padded, out, step, base):
    for m in range(12):
        out[pl.ds(base + m, DEVICES, stride=step), :] = padded[pl.ds(m, DEVICES, stride=12), :]


def rows_of_channels(padded, i):
    return padded[pl.ds(i, PADDED, stride=4), :]


def source_kernel(meta, x_ref, mix_w, out_ref, padded, out):
    put_padded(padded, masked(meta, x_ref[...]))
    for b in range(2):
        length = meta[b]
        upper = lax.shift_right_logical(length, 7)
        out[pl.ds(12 + 2 * b, DEVICES, stride=16), :] = jnp.full((DEVICES, LANES), upper.astype(F32))
        out[pl.ds(13 + 2 * b, DEVICES, stride=16), :] = jnp.full(
            (DEVICES, LANES), (length - upper * 128).astype(F32)
        )
    rows_to_message(padded, out, 16, 0)
    out_ref[...] = out[...].reshape(DEVICES, 16, LANES).astype(BF16)


def make_weights(mix_w, mix_b, lookup, forward, back, wide, weight, weight_back):
    wide[...] = jnp.zeros(wide.shape, BF16)
    wide[0:CHANNELS, 0:CHANNELS] = mix_w[back]
    weight_back[...] = dot_rows(lookup[...], wide[...]).astype(BF16)
    wide[0:CHANNELS, 0:CHANNELS] = mix_w[forward]
    value = dot_rows(wide[...], lookup[...])
    row = lax.broadcasted_iota(jnp.int32, (LANES, CHANNELS), 0)
    line = jnp.where(row == 0, mix_b[forward : forward + 1, :], 0.0)
    rest = jnp.transpose(jnp.concatenate([line, jnp.zeros((LANES, PADDED - CHANNELS), F32)], axis=1))[:, 0:1]
    lane = lax.broadcasted_iota(jnp.int32, (PADDED, PADDED), 1)
    for spot in SPOTS:
        high, rest = high_low(rest)
        value = jnp.where(lane == spot, high, value)
    weight[...] = value.astype(BF16)


def make_kernel(layer, meta, params, consts, bundle, tab, scratch):
    out_w, out_b, window, gain, bias, gabor, hidden_b, hidden_w, place_row, time_row, starts = params
    first, second, _, _, twiddle = consts
    wide, tall, rows, pieces, x_ref, high, low = scratch
    own, columns = bundle.at[OWN_ROWS, :], bundle.at[COLUMN_ROWS, :]
    own_parameters(layer, meta[3], out_w, out_b, window, gain, bias, gabor, hidden_b, wide, tall, own, columns)
    generate(columns, hidden_w.at[layer], own, place_row, time_row, starts, tab, rows)
    for n in range(64):
        for part in range(OWN):
            pieces[part * 64 + n : part * 64 + n + 1, :] = rows[part : part + 1, block(n)]
    for part in range(OWN):
        piece = pieces[block(part, 64), :].astype(BF16)
        x_ref[0:64, block(part)] = piece
        x_ref[64:128, block(part)] = piece
        x_ref[128:256, block(part)] = jnp.zeros((128, LANES), BF16)
    spec = transform(x_ref, high, low, first, second, twiddle, OWN)
    bundle[0:SPEC_IM, :] = spec[:, RE]
    bundle[SPEC_IM : 2 * SPEC_IM, :] = spec[:, IM]


def forward_kernel(
    meta, message_ref, out_w, out_b, window, gain, bias, gabor, hidden_b, hidden_w, place_row, time_row, starts,
    times, first, second, second_back, last, twiddle,
    out_ref, spec_ref, normed_ref, slope_ref, inv_ref, len_ref, kernel_spec, tab,
    message, x_ref, high, low, e_high, e_low, y_ref, out, *make_scratch,
):
    own = kernel_spec.at[OWN_ROWS, :]
    params = (out_w, out_b, window, gain, bias, gabor, hidden_b, hidden_w, place_row, time_row, starts)
    make_kernel(0, meta, params, (first, second, second_back, last, twiddle), kernel_spec, tab, make_scratch)
    message[...] = spread(message_ref[...])
    for y in range(4):
        for b in range(2):
            start = y * 16 + 12 + 2 * b
            len_ref[2 * y + b : 2 * y + b + 1, :] = (
                message[start : start + 1, :] * 128.0 + message[start + 1 : start + 2, :]
            )
    load_signals(message, 16, x_ref)
    convolve(x_ref, spec_ref, kernel_spec, high, low, e_high, e_low, (first, second, second_back, last, twiddle), y_ref)
    valid, tally = valid_of(times, len_ref), tally_of(len_ref)
    inv_ref[...] = jnp.zeros((8, LANES), F32)
    for part in range(OWN):
        normed, inv_std, active, slope = normalise(y_ref, own, valid, tally, part)
        normed_ref[:, block(part, 512)] = normed
        slope_ref[:, block(part, 512)] = slope
        inv_ref[part : part + 1, :] = jnp.broadcast_to(inv_std, (1, LANES))
        y_ref[:, block(part, 512)] = active
    store_signals(out, 16, 0, lambda part, y: y_ref[:, block(part * 4 + y)])
    out_ref[...] = out[...].reshape(DEVICES, 16, LANES).astype(BF16)


def gather_active(message, step, rhs):
    row = lax.broadcasted_iota(jnp.int32, (DEVICES, LANES), 0)
    for i in range(4):
        for part in range(OWN):
            piece = message[pl.ds(part * 4 + i, DEVICES, stride=step), :]
            if part != 1:
                piece = jnp.where(row >= (126 if part == 2 else 127), 1.0, piece)
            rhs[block(part), block(i)] = piece.astype(BF16)


def store_rows(value, out, step, base):
    for i in range(4):
        for part in range(OWN):
            out[pl.ds(base + part * 4 + i, DEVICES, stride=step), :] = value[block(part), block(i)]


def mix_kernel(
    meta, message_ref, x_ref, cotangent, mix_w, mix_b, lookup,
    out_ref, next_ref, active_ref, message, padded, out, low, wide, weight, weight_back,
):
    make_weights(mix_w, mix_b, lookup, 0, 1, wide, weight, weight_back)
    message[...] = spread(message_ref[...])
    gather_active(message, 16, active_ref)
    mixed = dot(weight[...], active_ref[...])
    put_padded(padded, x_ref[...])
    for i in range(4):
        valid = valid_row(meta, i)
        value = rows_of_channels(padded, i) + mixed[:, block(i)] * valid
        next_ref[pl.ds(i, PADDED, stride=4), :] = value
        padded[pl.ds(i, PADDED, stride=4), :] = value * valid
    rows_to_message(padded, out, 24, 0)
    put_padded(padded, masked(meta, cotangent[...]))
    for i in range(4):
        low[:, block(i)] = rows_of_channels(padded, i).astype(BF16)
    store_rows(dot(weight_back[...], low[...]), out, 24, 12)
    out_ref[...] = out[...].reshape(DEVICES, 24, LANES).astype(BF16)


def forward_backward_kernel(
    meta, message_ref, out_w, out_b, window, gain, bias, gabor, hidden_b, hidden_w, place_row, time_row, starts,
    len_ref, times, first, second, second_back, last, twiddle,
    out_ref, hidden_out, outer_out,
    message, x_ref, high, low, e_high, e_low, y_ref, out, spec_ref, grad_ref, normed_ref, slope_ref, returned_ref,
    rows, sums, mats, kernel_spec, tab, *make_scratch,
):
    own, columns = kernel_spec.at[OWN_ROWS, :], kernel_spec.at[COLUMN_ROWS, :]
    consts = (first, second, second_back, last, twiddle)
    params = (out_w, out_b, window, gain, bias, gabor, hidden_b, hidden_w, place_row, time_row, starts)
    make_kernel(1, meta, params, consts, kernel_spec, tab, make_scratch)
    message[...] = spread(message_ref[...])
    load_signals(message, 24, x_ref)
    convolve(x_ref, spec_ref, kernel_spec, high, low, e_high, e_low, consts, y_ref)
    valid, tally = valid_of(times, len_ref), tally_of(len_ref)
    inv = []
    for part in range(OWN):
        normed, inv_std, active, slope = normalise(y_ref, own, valid, tally, part)
        normed_ref[:, block(part, 512)] = normed
        slope_ref[:, block(part, 512)] = slope
        inv.append(inv_std)
        y_ref[:, block(part, 512)] = active
    store_signals(out, 24, 0, lambda part, y: y_ref[:, block(part * 4 + y)])
    returned, norm_sums = conv_backward(
        message, 24, 12, lambda part: normed_ref[:, block(part, 512)], lambda part: slope_ref[:, block(part, 512)],
        lambda part: inv[part], own, valid, tally, spec_ref, kernel_spec, x_ref, high, low, e_high, e_low, consts, grad_ref,
    )
    returned_ref[...] = returned
    store_signals(out, 24, 12, lambda part, y: returned_ref[:, block(part * 4 + y)])
    out_ref[...] = out[...].reshape(DEVICES, 24, LANES).astype(BF16)
    hidden, outer = generate_back(
        lambda part: returned_ref[0:64, block(SIGNALS + part)], columns, hidden_w.at[1], own, place_row, time_row, tab,
        rows, sums, mats,
    )
    hidden_out[...] = hidden
    outer_out[...] = with_norm_sums(outer, norm_sums)


def middle_kernel(
    meta, message_ref, x_ref, cotangent, mix_w, mix_b, lookup, active_0, hidden_1,
    output_ref, flow_ref, out_ref, message, padded, out, low_0, low_1, active_1, wide, weight, weight_back,
):
    make_weights(mix_w, mix_b, lookup, 1, 0, wide, weight, weight_back)
    message[...] = spread(message_ref[...])
    gather_active(message, 24, active_1)
    mixed = dot(weight[...], active_1[...])
    for i in range(4):
        padded[pl.ds(i, PADDED, stride=4), :] = rows_of_channels(x_ref, i) + mixed[:, block(i)] * valid_row(meta, i)
    output_ref[...] = padded[0:CLIP_ROWS, :]
    put_padded(flow_ref, cotangent[...])
    for i in range(4):
        low_1[:, block(i)] = (rows_of_channels(flow_ref, i) * valid_row(meta, i)).astype(BF16)
    for m in range(12):
        padded[pl.ds(m, DEVICES, stride=12), :] = message[pl.ds(12 + m, DEVICES, stride=24), :]
    flow_ref[...] += masked(meta, padded[...])
    for i in range(4):
        low_0[:, block(i)] = (rows_of_channels(flow_ref, i) * valid_row(meta, i)).astype(BF16)
    store_rows(dot(weight_back[...], low_0[...]), out, 32, 0)
    for layer, (active, low) in enumerate(((active_0, low_0), (active_1, low_1))):
        part_sum = dot_rows(active[...], low[...])
        for part in range(OWN):
            for third in range(3):
                out[pl.ds(12 + layer * 9 + part * 3 + third, DEVICES, stride=32), :] = part_sum[
                    block(part), block(third)
                ]
    high, low = high_low(hidden_1[...])
    out[pl.ds(30, DEVICES, stride=32), :] = jnp.concatenate([high, jnp.zeros((96, LANES), F32)], axis=0)
    out[pl.ds(31, DEVICES, stride=32), :] = jnp.concatenate([low, jnp.zeros((96, LANES), F32)], axis=0)
    out_ref[...] = out[...].reshape(DEVICES, 32, LANES).astype(BF16)


LAST_ROWS = 56


def backward_kernel(
    message_ref, spec_ref, kernel_spec, normed_ref, slope_ref, inv_ref, len_ref, times,
    first, second, second_back, last, twiddle, hidden_w, place_row, time_row, tab, outer_1,
    out_ref,
    message, x_ref, high, low, e_high, e_low, out, grad_ref, returned_ref, rows, sums, mats,
):
    own, columns = kernel_spec.at[OWN_ROWS, :], kernel_spec.at[COLUMN_ROWS, :]
    consts = (first, second, second_back, last, twiddle)
    message[...] = spread(message_ref[...])
    valid, tally = valid_of(times, len_ref), tally_of(len_ref)
    returned, norm_sums = conv_backward(
        message, 32, 0, lambda part: normed_ref[:, block(part, 512)], lambda part: slope_ref[:, block(part, 512)],
        lambda part: inv_ref[part : part + 1, 0:1], own, valid, tally, spec_ref, kernel_spec, x_ref, high, low,
        e_high, e_low, consts, grad_ref,
    )
    returned_ref[...] = returned
    store_signals(out, 16, 0, lambda part, y: returned_ref[:, block(part * 4 + y)])
    hidden, outer = generate_back(
        lambda part: returned_ref[0:64, block(SIGNALS + part)], columns, hidden_w.at[0], own, place_row, time_row, tab,
        rows, sums, mats,
    )
    outer = with_norm_sums(outer, norm_sums)
    gathered = jnp.sum(message[...].reshape(DEVICES, 32, LANES), axis=0)
    upper, lower = packed_hidden(hidden)
    hidden_1_high, hidden_1_low = high_low(gathered[30:31, :] + gathered[31:32, :])
    outer_0_high, outer_0_low = high_low(one_row(outer))
    outer_1_high, outer_1_low = high_low(one_row(outer_1[...]))
    shared = jnp.concatenate(
        [
            gathered[0:30, :], upper, lower, hidden_1_high, hidden_1_low,
            outer_0_high, outer_0_low, outer_1_high, outer_1_low,
        ],
        axis=0,
    )
    row = lax.broadcasted_iota(jnp.int32, (DEVICES, 16, LANES), 1)
    own_rows = jnp.where(row < 12, out[...].reshape(DEVICES, 16, LANES), shared[None, 0:16, :])
    rest = jnp.broadcast_to(shared[None, 16:LAST_ROWS, :], (DEVICES, LAST_ROWS - 16, LANES))
    out_ref[...] = jnp.concatenate([own_rows, rest], axis=1).astype(BF16)


def last_kernel(
    meta, message_ref, flow_ref, lookup,
    input_grad, gabor_grad, hidden_w_grad, hidden_b_grad, out_w_grad, out_b_grad, gain_grad, bias_grad,
    mix_w_grad, mix_b_grad, message, padded, owned, thirds,
):
    message[...] = spread(message_ref[...])

    def rows_of(k, count=DEVICES):
        return message[pl.ds(k, count, stride=LAST_ROWS), :]

    for m in range(12):
        padded[pl.ds(m, DEVICES, stride=12), :] = rows_of(m)
    input_grad[...] = flow_ref[0:CLIP_ROWS, :] + masked(meta, padded[0:CLIP_ROWS, :])
    shared = jnp.sum(message[...].reshape(DEVICES, LAST_ROWS, LANES)[:, 24:56, :], axis=0)
    hidden_0 = unpacked_hidden(shared[6:22, :], shared[22:26, :])
    hidden_1 = rows_of(50, 32) + rows_of(51, 32)
    lane = lax.broadcasted_iota(jnp.int32, (DEVICES, LANES), 1)
    for layer, hidden in enumerate((hidden_0, hidden_1)):
        hidden_w_grad[layer, 0] = hidden[:, 0:32]
        hidden_w_grad[layer, 1] = pltpu.roll(hidden, 96, 1)[:, 0:32]
        turned = jnp.transpose(jnp.concatenate([hidden, jnp.zeros((96, LANES), F32)], axis=0))
        hidden_b_grad[layer] = turned[64:66, 0:32]
        for j in range(3):
            gabor_grad[layer, j] = turned[66 + 4 * j : 70 + 4 * j, 0:32]
        value = rows_of(52 + 2 * layer) + rows_of(53 + 2 * layer)
        for part in range(OWN):
            wide = pltpu.roll(value, (LANES - 32 * part) % LANES, 1)
            small = pltpu.roll(value, 64 - 3 * part, 1)
            owned[pl.ds(part, DEVICES, stride=OWN), :] = jnp.where(lane < 32, wide, small)
        turned = jnp.transpose(owned[...])
        out_w_grad[layer] = turned[0:32, 0:CHANNELS]
        out_b_grad[layer : layer + 1, :] = turned[32:33, 0:CHANNELS]
        gain_grad[layer : layer + 1, :] = turned[33:34, 0:CHANNELS]
        bias_grad[layer : layer + 1, :] = turned[34:35, 0:CHANNELS]
        bias_rows = []
        for part in range(OWN):
            for third in range(3):
                piece = rows_of(12 + layer * 9 + part * 3 + third)
                thirds[block(part), block(third)] = piece.astype(BF16)
                if part == 2:
                    bias_rows.append(piece[SPOT - 2 * DEVICES : SPOT - 2 * DEVICES + 1, :])
        mix_w_grad[layer] = dot_columns(thirds[...], lookup[...])[0:CHANNELS, 0:CHANNELS]
        mix_b_grad[layer : layer + 1, :] = jnp.concatenate(bias_rows, axis=1)[:, 0:CHANNELS]


def exchange(message):
    return lax.all_to_all(message, AXES, split_axis=0, concat_axis=0, tiled=True)


def to_rows(clips):
    return clips.reshape(2, CHANNELS, 2, LANES).transpose(1, 2, 0, 3).reshape(CLIP_ROWS, LANES)


def from_rows(rows):
    return rows.reshape(CHANNELS, 2, 2, LANES).transpose(2, 0, 1, 3).reshape(2, CHANNELS, PIECE)


def shards(
    inputs, lengths, window, gabor_params, hidden_w, hidden_b, out_w, out_b, bn_gain, bn_bias, mix_w, mix_b, cotangent
):
    position = lax.axis_index("seq").astype(jnp.int32)
    number = position * 4 + lax.axis_index("clips").astype(jnp.int32)
    const = {name: jnp.asarray(value) for name, value in TABLES.items()}
    meta = jnp.concatenate([lengths, jnp.stack([position, number])])
    inputs, cotangent = to_rows(inputs), to_rows(cotangent)

    def rows(count):
        return ((count, LANES), F32)

    with jax.named_scope("source_0"):
        (message,) = run(
            source_kernel, [((DEVICES, 16, LANES), BF16)], [meta, inputs, mix_w],
            [rows(PADDED_ROWS), rows(DEVICES * 16)], "source_0", 8, smem=(0,), far=(2,),
        )
        message = exchange(message)

    square = (PADDED, PADDED)
    generator = [
        jnp.swapaxes(out_w, 1, 2), out_b, jnp.swapaxes(window, 1, 2), bn_gain, bn_bias, gabor_params, hidden_b,
        hidden_w, const["place_row"], const["time_row"], const["starts"],
    ]
    shape_tab = ((8, HIDDEN, SAMPLES), F32)
    make_scratch = [
        ((LANES, PADDED), F32), rows(PADDED + 8), ((8, SAMPLES), F32), rows(192),
        ((256, OWN * LANES), BF16), ((OWN * LANES, 256), BF16), ((OWN * LANES, 256), BF16),
    ]
    mixer = [mix_w, mix_b, const["lookup"]]
    mixer_scratch = [(square, BF16)] * 3

    def scratch(signals):
        count = signals * LANES
        return [
            ((256, SIGNALS * LANES), BF16), ((count, 256), BF16), ((count, 256), BF16),
            ((256, count), BF16), ((256, count), BF16),
        ]

    shape_y = (LANES, SIGNALS * LANES)
    shape_s = (SIGNALS * LANES, 256)
    transforms = [const[name] for name in ("first", "second", "second_back", "last", "twiddle")]
    with jax.named_scope("conv_0"):
        message, spec_0, normed_0, slope_0, inv_0, lens, bundle_0, tab_0 = run(
            forward_kernel,
            [
                ((DEVICES, 16, LANES), BF16), (shape_s, F32), (shape_y, F32), (shape_y, F32), rows(8), rows(8),
                rows(BUNDLE), shape_tab,
            ],
            [meta, message, *generator, const["times"], *transforms],
            [rows(DEVICES * 16), *scratch(SIGNALS), (shape_y, F32), rows(DEVICES * 16), *make_scratch],
            "conv_0", 28, smem=(0,),
        )
        message = exchange(message)

    with jax.named_scope("mix_0"):
        message, middle, active_0 = run(
            mix_kernel,
            [((DEVICES, 24, LANES), BF16), rows(PADDED_ROWS), ((PADDED, 512), BF16)],
            [meta, message, inputs, cotangent, *mixer],
            [rows(DEVICES * 16), rows(PADDED_ROWS), rows(DEVICES * 24), ((PADDED, 512), BF16), *mixer_scratch],
            "mix_0", 12, smem=(0,),
        )
        message = exchange(message)

    back_scratch = [((8, SAMPLES), F32), rows(14 * 32 + 8), rows(72)]
    with jax.named_scope("conv_1"):
        message, hidden_1, outer_1 = run(
            forward_backward_kernel,
            [((DEVICES, 24, LANES), BF16), rows(HIDDEN), rows(8)],
            [
                meta, message, *generator, lens, const["times"], *transforms,
            ],
            [
                rows(DEVICES * 24), *scratch(SIGNALS + OWN), (shape_y, F32), rows(DEVICES * 24),
                (shape_s, F32), (shape_s, F32), (shape_y, F32), (shape_y, F32),
                ((LANES, (SIGNALS + OWN) * LANES), F32), *back_scratch, rows(BUNDLE), shape_tab, *make_scratch,
            ],
            "conv_1", 40, smem=(0,),
        )
        message = exchange(message)

    with jax.named_scope("mix_1"):
        outputs, flow, message = run(
            middle_kernel,
            [rows(CLIP_ROWS), rows(PADDED_ROWS), ((DEVICES, 32, LANES), BF16)],
            [meta, message, middle, cotangent, *mixer, active_0, hidden_1],
            [
                rows(DEVICES * 24), rows(PADDED_ROWS), rows(DEVICES * 32),
                ((PADDED, 512), BF16), ((PADDED, 512), BF16), ((PADDED, 512), BF16), *mixer_scratch,
            ],
            "mix_1", 12, smem=(0,),
        )
        message = exchange(message)

    with jax.named_scope("conv_back_0"):
        (message,) = run(
            backward_kernel,
            [((DEVICES, LAST_ROWS, LANES), BF16)],
            [
                message, spec_0, bundle_0, normed_0, slope_0, inv_0, lens, const["times"], *transforms,
                hidden_w, const["place_row"], const["time_row"], tab_0, outer_1,
            ],
            [
                rows(DEVICES * 32), *scratch(SIGNALS + OWN), rows(DEVICES * 16), (shape_s, F32),
                ((LANES, (SIGNALS + OWN) * LANES), F32), *back_scratch,
            ],
            "conv_back_0", 28,
        )
        message = exchange(message)

    with jax.named_scope("gradients"):
        (
            input_grad, gabor_grad, hidden_w_grad, hidden_b_grad, out_w_grad, out_b_grad, gain_grad, bias_grad,
            mix_w_grad, mix_b_grad,
        ) = run(
            last_kernel,
            [
                rows(CLIP_ROWS), (gabor_params.shape, F32), (hidden_w.shape, F32), (hidden_b.shape, F32),
                ((2, HIDDEN, CHANNELS), F32), (out_b.shape, F32), (bn_gain.shape, F32), (bn_bias.shape, F32),
                (mix_w.shape, F32), (mix_b.shape, F32),
            ],
            [meta, message, flow, const["lookup"]],
            [rows(DEVICES * LAST_ROWS), rows(PADDED_ROWS), rows(PADDED), (square, BF16)],
            "gradients", 14, smem=(0,),
        )
    return (
        from_rows(outputs), from_rows(input_grad), gabor_grad, hidden_w_grad, hidden_b_grad,
        jnp.swapaxes(out_w_grad, 1, 2), out_b_grad, gain_grad, bias_grad, mix_w_grad, mix_b_grad,
    )


def solution(mesh):
    clip = P("clips", None, "seq")
    in_specs = (clip, P("clips")) + (P(),) * 10 + (clip,)
    out_specs = (clip, clip) + (P(),) * 9
    return jax.shard_map(shards, mesh=mesh, in_specs=in_specs, out_specs=out_specs, check_vma=False)
```

```python
import math

import jax
import jax.numpy as jnp
import ml_dtypes
import numpy as np
from jax import lax
from jax.experimental import pallas as pl
from jax.experimental.pallas import tpu as pltpu
from jax.sharding import PartitionSpec as P

F32 = jnp.float32
BF16 = jnp.bfloat16
AXES = ("seq", "clips")
DEVICES = 128
OWN = 3
CHANNELS = 380
PADDED = DEVICES * OWN
SAMPLES = 8192
PIECE = 256
HIDDEN = 32
LANES = 128
SIGNALS = 12
TABLE_NAMES = ("first", "second", "last", "twiddle")
PERIOD = 2 * SAMPLES
EPSILON = 1e-05
MEGABYTE = 1024 * 1024
EXACT = lax.Precision.HIGHEST
SPOTS = (2 * DEVICES + 126, 2 * DEVICES + 127, 127)
SPOT = SPOTS[0]


def halves(table):
    high = table.astype(ml_dtypes.bfloat16)
    low = (table - high.astype(np.float64)).astype(ml_dtypes.bfloat16)
    return high, low


def tables():
    order = np.array([2 * j + r for r in range(2) for j in range(32)])
    k = np.arange(LANES)
    turn = 2 * np.pi * ((k[:, None] * order[None, :]) % LANES) / LANES
    c_high, c_low = halves(np.cos(turn))
    s_high, s_low = halves(np.sin(turn))
    first = np.concatenate(
        [
            np.concatenate([c_high, c_low, s_high, s_low], axis=1),
            np.concatenate([-s_high, -s_low, c_high, c_low], axis=1),
        ],
        axis=0,
    )
    turn = 2 * np.pi * ((k[:, None] * k[None, :]) % LANES) / LANES
    cosine, sine = np.cos(turn), np.sin(turn)
    second = halves(np.block([[cosine, -sine], [sine, cosine]]))
    turn = 2 * np.pi * ((order[:, None] * k[None, :]) % LANES) / LANES
    cosine, sine = np.cos(turn) / PERIOD, np.sin(turn) / PERIOD
    last = halves(np.block([[cosine, -sine], [sine, cosine]]))
    turn = 2 * np.pi * (k[:, None] * k[None, :]) / PERIOD
    twiddle = np.stack([np.cos(turn), np.sin(turn)]).astype(np.float32)
    return dict(
        first=first,
        second=np.stack(second),
        last=np.stack(last),
        twiddle=twiddle,
    )


TABLES = tables()


def run(body, outs, args, scratch, name, grant, smem=(), far=()):
    spaces = [pltpu.HBM if i in far else pltpu.SMEM if i in smem else pltpu.VMEM for i in range(len(args))]
    return pl.pallas_call(
        body,
        out_shape=[jax.ShapeDtypeStruct(shape, kind) for shape, kind in outs],
        in_specs=[pl.BlockSpec(memory_space=space) for space in spaces],
        out_specs=[pl.BlockSpec(memory_space=pltpu.VMEM)] * len(outs),
        scratch_shapes=[pltpu.VMEM(shape, kind) for shape, kind in scratch],
        compiler_params=pltpu.CompilerParams(vmem_limit_bytes=grant * MEGABYTE),
        name=name,
    )(*args)


def dot(a, b):
    return jnp.dot(a, b, preferred_element_type=F32)


def dot_rows(a, b, precision=None):
    return lax.dot_general(a, b, (((1,), (1,)), ((), ())), precision=precision, preferred_element_type=F32)


def dot_columns(a, b, precision=None):
    return lax.dot_general(a, b, (((0,), (0,)), ((), ())), precision=precision, preferred_element_type=F32)


def triple(a_high, a_low, b_high, b_low):
    left = jnp.concatenate([a_high, a_low, a_high], axis=1)
    return dot(left, jnp.concatenate([b_high, b_high, b_low], axis=0))


def triple_rows(a_high, a_low, b_high, b_low):
    left = jnp.concatenate([a_high, a_low, a_high], axis=1)
    return dot_rows(left, jnp.concatenate([b_high, b_high, b_low], axis=1))


def put_halves(high_ref, low_ref, rows, columns, value):
    high = value.astype(BF16)
    high_ref[rows, columns] = high
    low_ref[rows, columns] = (value - high.astype(F32)).astype(BF16)


def block(i, size=LANES):
    return slice(i * size, (i + 1) * size)


RE, IM = slice(0, LANES), slice(LANES, 2 * LANES)


def signal_row(b, part, r):
    return part * 4 + r * 2 + b


def spread(message):
    return message.astype(F32).reshape(-1, LANES)


def transform(x_ref, high_ref, low_ref, first, second, twiddle, count):
    part_a = dot(first[...], x_ref[:, : count * LANES])
    cosine, sine = twiddle[0], twiddle[1]
    for s in range(count):
        real, imag = part_a[:LANES, block(s)], part_a[LANES:, block(s)]
        put_halves(high_ref, low_ref, block(s), RE, real * cosine + imag * sine)
        put_halves(high_ref, low_ref, block(s), IM, imag * cosine - real * sine)
    rows = slice(0, count * LANES)
    return triple(high_ref[rows, :], low_ref[rows, :], second[0], second[1])


def transform_back(high_ref, low_ref, e_high, e_low, second, last, twiddle, count):
    rows = slice(0, count * LANES)
    part_d = triple_rows(high_ref[rows, :], low_ref[rows, :], second[0], second[1])
    cosine, sine = twiddle[0], twiddle[1]
    for s in range(count):
        real, imag = part_d[block(s), RE], part_d[block(s), IM]
        put_halves(e_high, e_low, RE, block(s), real * cosine - imag * sine)
        put_halves(e_high, e_low, IM, block(s), real * sine + imag * cosine)
    return triple(last[0], last[1], e_high[:, rows], e_low[:, rows])


def erf_parts(value):
    cdf = 0.5 * (1.0 + lax.erf(value * math.sqrt(0.5)))
    return cdf, jnp.exp(-0.5 * value * value) * (1.0 / math.sqrt(2.0 * math.pi))


def total(value):
    return jnp.sum(jnp.sum(value, axis=0, keepdims=True), axis=1, keepdims=True)


def times_of(row, lane):
    return (256 * (row & 31) + 128 * lax.shift_right_logical(row, 5 * jnp.ones_like(row)) + lane).astype(F32)


def valid_of(len_ref):
    row = lax.broadcasted_iota(jnp.int32, (LANES, LANES), 0) & 63
    times = times_of(row, lax.broadcasted_iota(jnp.int32, (LANES, LANES), 1))
    columns = []
    for y in range(4):
        upper = times[0:64, :] < len_ref[2 * y : 2 * y + 1, :]
        lower = times[64:128, :] < len_ref[2 * y + 1 : 2 * y + 2, :]
        columns.append(jnp.concatenate([upper, lower], axis=0).astype(F32))
    return jnp.concatenate(columns, axis=1)


def tally_of(len_ref):
    return jnp.sum(len_ref[:, 0:1], axis=0, keepdims=True)


def load_signals(message, step, x_ref):
    for part in range(OWN):
        for y in range(4):
            lanes = block(part * 4 + y)
            for b in range(2):
                for r in range(2):
                    start = y * step + signal_row(b, part, r)
                    piece = message[pl.ds(start, 32, stride=4 * step), :].astype(BF16)
                    x_ref[b * 128 + r * 32 : b * 128 + r * 32 + 32, lanes] = piece
                    x_ref[b * 128 + r * 32 + 64 : b * 128 + r * 32 + 96, lanes] = piece


def store_signals(out, step, base, get):
    for part in range(OWN):
        for y in range(4):
            value = get(part, y)
            for b in range(2):
                for r in range(2):
                    start = y * step + base + signal_row(b, part, r)
                    out[pl.ds(start, 32, stride=4 * step), :] = value[b * 64 + r * 32 : b * 64 + r * 32 + 32, :]


SPEC_IM = OWN * LANES
OWN_ROWS = slice(2 * SPEC_IM, 2 * SPEC_IM + 8)
COLUMN_ROWS = slice(2 * SPEC_IM + 8, 2 * SPEC_IM + 8 + HIDDEN)
BUNDLE = 2 * SPEC_IM + 8 + HIDDEN


def kernel_parts(bundle, part):
    return bundle[block(part), :], bundle[SPEC_IM + part * LANES : SPEC_IM + (part + 1) * LANES, :]


def convolve(x_ref, spec_ref, kernel_spec, high, low, e_high, e_low, consts, y_ref):
    first, second, last, twiddle = consts
    spec_ref[...] = transform(x_ref, high, low, first, second, twiddle, SIGNALS)
    for part in range(OWN):
        k_re, k_im = kernel_parts(kernel_spec, part)
        for y in range(4):
            rows = block(part * 4 + y)
            s_re, s_im = spec_ref[rows, RE], spec_ref[rows, IM]
            put_halves(high, low, rows, RE, s_re * k_re - s_im * k_im)
            put_halves(high, low, rows, IM, s_re * k_im + s_im * k_re)
    y_ref[...] = transform_back(high, low, e_high, e_low, second, last, twiddle, SIGNALS)


def normalise(y_ref, own, valid, tally, part):
    value = y_ref[:, block(part, 512)]
    mean = total(valid * value) / tally
    centred = value - mean
    var = total(valid * centred * centred) / tally
    inv_std = lax.rsqrt(var + EPSILON)
    normed = centred * inv_std
    pre_act = normed * own[part : part + 1, 35:36] + own[part : part + 1, 36:37]
    cdf, density = erf_parts(pre_act)
    return normed, inv_std, pre_act * cdf, cdf + pre_act * density


def conv_backward(
    message, step, base, normed_of, slope_of, inv_of, own, valid, tally, spec_ref, kernel_spec, x_ref, high, low,
    e_high, e_low, consts, grad_ref,
):
    first, second, last, twiddle = consts
    sums = []
    for part in range(OWN):
        columns = []
        for y in range(4):
            pieces = []
            for b in range(2):
                for r in range(2):
                    start = y * step + base + signal_row(b, part, r)
                    pieces.append(message[pl.ds(start, 32, stride=4 * step), :])
            columns.append(jnp.concatenate(pieces, axis=0))
        act_grad = jnp.concatenate(columns, axis=1)
        normed = normed_of(part)
        pre_grad = act_grad * slope_of(part)
        bias_total = total(pre_grad)
        gain_total = total(pre_grad * normed)
        gain = own[part : part + 1, 35:36]
        conv_grad = inv_of(part) * (
            gain * pre_grad - valid * (gain * bias_total + normed * (gain * gain_total)) / tally
        )
        conv_low = conv_grad.astype(BF16)
        for b in range(2):
            piece = conv_low[b * 64 : b * 64 + 64, :]
            x_ref[b * 128 : b * 128 + 64, block(part, 512)] = piece
            x_ref[b * 128 + 64 : b * 128 + 128, block(part, 512)] = piece
        sums.append((gain_total, bias_total))
    grad_ref[...] = transform(x_ref, high, low, first, second, twiddle, SIGNALS)
    for part in range(OWN):
        k_re, k_im = kernel_parts(kernel_spec, part)
        corr_re, corr_im = None, None
        for y in range(4):
            rows = block(part * 4 + y)
            g_re, g_im = grad_ref[rows, RE], grad_ref[rows, IM]
            s_re, s_im = spec_ref[rows, RE], spec_ref[rows, IM]
            put_halves(high, low, rows, RE, k_re * g_re + k_im * g_im)
            put_halves(high, low, rows, IM, k_re * g_im - k_im * g_re)
            now_re, now_im = s_re * g_re + s_im * g_im, s_re * g_im - s_im * g_re
            corr_re = now_re if corr_re is None else corr_re + now_re
            corr_im = now_im if corr_im is None else corr_im + now_im
        put_halves(high, low, block(SIGNALS + part), RE, corr_re)
        put_halves(high, low, block(SIGNALS + part), IM, corr_im)
    returned = transform_back(high, low, e_high, e_low, second, last, twiddle, SIGNALS + OWN)
    return returned, sums


def sin_cos(angle):
    turns = jnp.floor(angle * (2.0 / math.pi) + 0.5)
    rest = angle - turns * 1.5703125
    rest = rest - turns * 4.837512969970703125e-4
    rest = rest - turns * 7.549789948768648e-8
    square = rest * rest
    sine = rest + rest * square * (
        -1.6666654611e-1 + square * (8.3321608736e-3 + square * -1.9515295891e-4)
    )
    cosine = 1.0 - 0.5 * square + square * square * (
        4.166664568298827e-2 + square * (-1.388731625493765e-3 + square * 2.443315711809948e-5)
    )
    half = jnp.floor(turns * 0.5)
    odd = turns - 2.0 * half
    sign = 1.0 - 2.0 * (half - 2.0 * jnp.floor(half * 0.5))
    is_odd = odd > 0.5
    return sign * jnp.where(is_odd, cosine, sine), sign * jnp.where(is_odd, -sine, cosine)


CHUNK = 1024
F_TABLE = (0, 4, 7)
C_TABLE = (1, 3, 6)


def envelope_of(times, own):
    lower, upper = own[:, 33:34], own[:, 34:35]
    inside = (times >= lower) & (times < upper)
    offset = (times - lower) / (0.5 * (upper - lower))
    return jnp.where(inside, jnp.exp(-0.5 * offset * offset), 0.0)


def stacked_weight(weight):
    high, low = high_low(weight)
    return jnp.concatenate([high, high, low], axis=1).astype(BF16)


def stacked_dot(weight, value):
    high = value.astype(BF16)
    low = (value - high.astype(F32)).astype(BF16)
    return dot(weight, jnp.concatenate([high, low, high], axis=0))


def own_parameters(layer, number, out_w, out_b, window, gain, bias, gabor, hidden_b, wide, tall, own, columns):
    wide[...] = jnp.zeros(wide.shape, F32)
    wide[0:32, 0:CHANNELS] = out_w[layer]
    wide[32:33, 0:CHANNELS] = out_b[layer : layer + 1, :]
    wide[33:35, 0:CHANNELS] = window[layer].astype(F32)
    wide[35:36, 0:CHANNELS] = gain[layer : layer + 1, :]
    wide[36:37, 0:CHANNELS] = bias[layer : layer + 1, :]
    tall[0:PADDED, :] = jnp.transpose(wide[...])
    tall[PADDED : PADDED + 8, :] = jnp.zeros((8, LANES), F32)
    row = lax.broadcasted_iota(jnp.int32, (8, LANES), 0)
    lane = lax.broadcasted_iota(jnp.int32, (8, LANES), 1)
    mine = tall[pl.ds(number * OWN, 8), :]
    unused = (row >= OWN) | (number * OWN + row >= CHANNELS)
    own[...] = jnp.where(unused, jnp.where(lane == 34, float(SAMPLES), 0.0), mine)
    wide[:, 0:LANES] = jnp.zeros((LANES, LANES), F32)
    for j in range(3):
        wide[4 * j : 4 * j + 4, 0:HIDDEN] = gabor[layer, j]
    wide[12:14, 0:HIDDEN] = hidden_b[layer]
    columns[...] = jnp.transpose(wide[:, 0:LANES])[0:HIDDEN, :]


def sample_rows(first_lane, count):
    lane = first_lane + lax.broadcasted_iota(jnp.int32, (1, count), 1)
    times = times_of(lax.shift_right_logical(lane, 7 * jnp.ones_like(lane)), lane & 127)
    return times, times * (2.0 / (SAMPLES - 1)) - 1.0


def generate(columns, hidden_w, own, tab, rows):
    turns = []
    for j in range(3):
        turn = sin_cos(columns[:, 4 * j + 2 : 4 * j + 3] * (512.0 / (SAMPLES - 1)))
        turns.append([jnp.broadcast_to(value, (HIDDEN, LANES)) for value in turn])

    def step(i, carry):
        _, places = sample_rows(i * CHUNK, CHUNK)
        for j in range(3):
            sharpness, centre = columns[:, 4 * j : 4 * j + 1], columns[:, 4 * j + 1 : 4 * j + 2]
            frequency, phase = columns[:, 4 * j + 2 : 4 * j + 3], columns[:, 4 * j + 3 : 4 * j + 4]
            sine, cosine = sin_cos(frequency * places[:, 0:LANES] + phase)
            turn_sin, turn_cos = turns[j]
            for n in range(CHUNK // LANES):
                width = sharpness * (places[:, block(n)] - centre)
                bell = jnp.exp(-0.5 * width * width)
                here = pl.ds(pl.multiple_of(i * CHUNK + n * LANES, LANES), LANES)
                tab[F_TABLE[j], :, here] = bell * sine
                tab[C_TABLE[j], :, here] = bell * cosine
                sine, cosine = sine * turn_cos + cosine * turn_sin, cosine * turn_cos - sine * turn_sin
        return carry

    lax.fori_loop(0, SAMPLES // CHUNK, step, 0)
    weights = [stacked_weight(hidden_w[0]), stacked_weight(hidden_w[1]), stacked_weight(own[:, 0:32])]
    u_1 = stacked_dot(weights[0], tab[0]) + columns[:, 12:13]
    z_1 = u_1 * tab[4]
    tab[2] = z_1
    tab[3] = u_1 * tab[3]
    u_2 = stacked_dot(weights[1], z_1) + columns[:, 13:14]
    z_2 = u_2 * tab[7]
    tab[5] = z_2
    tab[6] = u_2 * tab[6]
    raw = stacked_dot(weights[2], z_2) + own[:, 32:33]
    times, _ = sample_rows(0, SAMPLES)
    rows[...] = raw * envelope_of(times, own)


def generate_back(kernel_grad, columns, hidden_w, own, tab, rows, sums, mats):
    rows[...] = jnp.zeros(rows.shape, F32)
    for part in range(OWN):
        grad = kernel_grad(part)
        for n in range(64):
            rows[part : part + 1, block(n)] = grad[n : n + 1, :]
    sums[...] = jnp.zeros(sums.shape, F32)
    mats[...] = jnp.zeros(mats.shape, F32)
    turned = jnp.transpose(jnp.concatenate([own[...], jnp.zeros((120, 128), F32)], axis=0))
    weight = [turned[0:32, part : part + 1] for part in range(OWN)]
    back = [stacked_weight(jnp.transpose(hidden_w[j])) for j in range(2)]

    def fold(value):
        acc = value[:, block(0)]
        for i in range(1, CHUNK // LANES):
            acc = acc + value[:, block(i)]
        return acc

    def add(k, value):
        sums[block(k, 32), :] += fold(value)

    def step(i, carry):
        span = pl.ds(pl.multiple_of(i * CHUNK, CHUNK), CHUNK)
        times, places = sample_rows(i * CHUNK, CHUNK)
        draw = rows[:, span] * envelope_of(times, own)
        dz_2 = weight[0] * draw[0:1, :] + weight[1] * draw[1:2, :] + weight[2] * draw[2:3, :]

        def level(j, e_value, g_value):
            centre = columns[:, 4 * j + 1 : 4 * j + 2]
            offset = places - centre
            moment = e_value * offset
            add(4 * j, moment * offset)
            add(4 * j + 1, moment)
            add(4 * j + 2, g_value * places)
            add(4 * j + 3, g_value)

        z_2 = tab[5, :, span]
        level(2, dz_2 * z_2, dz_2 * tab[6, :, span])
        du_2 = dz_2 * tab[7, :, span]
        add(13, du_2)
        dz_1 = stacked_dot(back[1], du_2)
        z_1 = tab[2, :, span]
        level(1, dz_1 * z_1, dz_1 * tab[3, :, span])
        du_1 = dz_1 * tab[4, :, span]
        add(12, du_1)
        dz_0 = stacked_dot(back[0], du_1)
        z_0 = tab[0, :, span]
        level(0, dz_0 * z_0, dz_0 * tab[1, :, span])
        sums[14 * 32 : 14 * 32 + 8, :] += fold(draw)
        left = jnp.concatenate([du_1, du_2, draw], axis=0)
        right = jnp.concatenate([z_0, z_1, z_2, jnp.zeros_like(z_0)], axis=0)
        left_high, right_high = left.astype(BF16), right.astype(BF16)
        left_low = (left - left_high.astype(F32)).astype(BF16)
        right_low = (right - right_high.astype(F32)).astype(BF16)
        mats[...] += (
            dot_rows(left_high, right_high) + dot_rows(left_low, right_high) + dot_rows(left_high, right_low)
        )
        return carry

    lax.fori_loop(0, SAMPLES // CHUNK, step, 0, unroll=SAMPLES // CHUNK)
    lane = lax.broadcasted_iota(jnp.int32, (32, LANES), 1)
    hidden = jnp.where(lane < 32, mats[0:32, :], jnp.where(lane < 64, mats[32:64, :], 0.0))

    def column(k):
        return jnp.sum(sums[block(k, 32), :], axis=1, keepdims=True)

    hidden = jnp.where(lane == 64, column(12), hidden)
    hidden = jnp.where(lane == 65, column(13), hidden)
    for j in range(3):
        sharpness = columns[:, 4 * j : 4 * j + 1]
        hidden = jnp.where(lane == 66 + 4 * j, -sharpness * column(4 * j), hidden)
        hidden = jnp.where(lane == 67 + 4 * j, sharpness * sharpness * column(4 * j + 1), hidden)
        hidden = jnp.where(lane == 68 + 4 * j, column(4 * j + 2), hidden)
        hidden = jnp.where(lane == 69 + 4 * j, column(4 * j + 3), hidden)
    lane8 = lax.broadcasted_iota(jnp.int32, (8, LANES), 1)
    outer = pltpu.roll(mats[64:72, :], LANES - 64, 1)
    raw_total = jnp.sum(sums[14 * 32 : 14 * 32 + 8, :], axis=1, keepdims=True)
    outer = jnp.where(lane8 < 32, outer, 0.0)
    outer = jnp.where(lane8 == 32, raw_total, outer)
    return hidden, outer


def with_norm_sums(outer, sums):
    row = lax.broadcasted_iota(jnp.int32, (8, LANES), 0)
    lane = lax.broadcasted_iota(jnp.int32, (8, LANES), 1)
    for part in range(OWN):
        gain_total, bias_total = sums[part]
        outer = jnp.where((row == part) & (lane == 33), gain_total, outer)
        outer = jnp.where((row == part) & (lane == 34), bias_total, outer)
    return outer


def one_row(outer):
    lane = lax.broadcasted_iota(jnp.int32, (1, LANES), 1)
    result = jnp.zeros((1, LANES), F32)
    for part in range(OWN):
        row = outer[part : part + 1, :]
        moved = pltpu.roll(row, 32 * part, 1) if part else row
        result = jnp.where((lane >= 32 * part) & (lane < 32 * part + 32), moved, result)
        moved = pltpu.roll(row, 64 + 3 * part, 1)
        result = jnp.where((lane >= 96 + 3 * part) & (lane < 99 + 3 * part), moved, result)
    return result


def packed_hidden(hidden):
    lane16 = lax.broadcasted_iota(jnp.int32, (16, LANES), 1)
    upper = jnp.where(lane16 < 64, hidden[0:16, :], pltpu.roll(hidden[16:32, :], 64, 1))
    lane4 = lax.broadcasted_iota(jnp.int32, (4, LANES), 1)
    lower = jnp.zeros((4, LANES), F32)
    for g in range(8):
        moved = pltpu.roll(hidden, (64 + 16 * g) % LANES, 1)[4 * g : 4 * g + 4, :]
        lower = jnp.where((lane4 >= 16 * g) & (lane4 < 16 * g + 16), moved, lower)
    return upper, lower


def unpacked_hidden(upper, lower):
    lane16 = lax.broadcasted_iota(jnp.int32, (16, LANES), 1)
    lane32 = lax.broadcasted_iota(jnp.int32, (32, LANES), 1)
    top = jnp.concatenate([upper, pltpu.roll(upper, 64, 1)], axis=0)
    tiled = jnp.concatenate([lower] * 8, axis=0)
    row32 = lax.broadcasted_iota(jnp.int32, (32, LANES), 0)
    rest = jnp.zeros((32, LANES), F32)
    for g in range(8):
        moved = pltpu.roll(tiled, (64 - 16 * g) % LANES, 1)
        rest = jnp.where((row32 >= 4 * g) & (row32 < 4 * g + 4), moved, rest)
    return jnp.where(lane32 < 64, top, rest)


def high_low(value):
    high = value.astype(BF16).astype(F32)
    return high, value - high


def valid_row(meta, i):
    lane = lax.broadcasted_iota(jnp.int32, (1, LANES), 1)
    return (meta[2] * PIECE + (i // 2) * LANES + lane < meta[i % 2]).astype(F32)


def masked(meta, rows):
    mask = jnp.concatenate([valid_row(meta, i) for i in range(4)] * 2, axis=0)
    return (rows.reshape(-1, 8, LANES) * mask[None]).reshape(-1, LANES)


CLIP_ROWS = 4 * CHANNELS
PADDED_ROWS = 4 * PADDED


def put_padded(padded, rows):
    padded[0:CLIP_ROWS, :] = rows
    padded[CLIP_ROWS:PADDED_ROWS, :] = jnp.zeros((PADDED_ROWS - CLIP_ROWS, LANES), F32)


def rows_to_message(padded, out, step, base):
    for m in range(12):
        out[pl.ds(base + m, DEVICES, stride=step), :] = padded[pl.ds(m, DEVICES, stride=12), :]


def rows_of_channels(padded, i):
    return padded[pl.ds(i, PADDED, stride=4), :]


def source_kernel(meta, x_ref, mix_w, out_ref, padded, out):
    put_padded(padded, masked(meta, x_ref[...]))
    for b in range(2):
        length = meta[b]
        upper = lax.shift_right_logical(length, 7)
        out[pl.ds(12 + 2 * b, DEVICES, stride=16), :] = jnp.full((DEVICES, LANES), upper.astype(F32))
        out[pl.ds(13 + 2 * b, DEVICES, stride=16), :] = jnp.full(
            (DEVICES, LANES), (length - upper * 128).astype(F32)
        )
    rows_to_message(padded, out, 16, 0)
    out_ref[...] = out[...].reshape(DEVICES, 16, LANES).astype(BF16)


def make_lookup(lookup):
    row = lax.broadcasted_iota(jnp.int32, (DEVICES, PADDED), 0)
    column = lax.broadcasted_iota(jnp.int32, (DEVICES, PADDED), 1)
    for part in range(OWN):
        lookup[block(part), :] = (column == OWN * row + part).astype(F32).astype(BF16)


def make_weights(mix_w, mix_b, forward, back, wide, weight, weight_back, lookup):
    make_lookup(lookup)
    wide[...] = jnp.zeros(wide.shape, BF16)
    wide[0:CHANNELS, 0:CHANNELS] = mix_w[back]
    weight_back[...] = dot_rows(lookup[...], wide[...]).astype(BF16)
    wide[0:CHANNELS, 0:CHANNELS] = mix_w[forward]
    value = dot_rows(wide[...], lookup[...])
    row = lax.broadcasted_iota(jnp.int32, (LANES, CHANNELS), 0)
    line = jnp.where(row == 0, mix_b[forward : forward + 1, :], 0.0)
    rest = jnp.transpose(jnp.concatenate([line, jnp.zeros((LANES, PADDED - CHANNELS), F32)], axis=1))[:, 0:1]
    lane = lax.broadcasted_iota(jnp.int32, (PADDED, PADDED), 1)
    for spot in SPOTS:
        high, rest = high_low(rest)
        value = jnp.where(lane == spot, high, value)
    weight[...] = value.astype(BF16)


def make_kernel(layer, meta, params, consts, bundle, tab, scratch):
    out_w, out_b, window, gain, bias, gabor, hidden_b, hidden_w = params
    first, second, _, twiddle = consts
    wide, tall, rows, pieces, x_ref, high, low = scratch
    own, columns = bundle.at[OWN_ROWS, :], bundle.at[COLUMN_ROWS, :]
    own_parameters(layer, meta[3], out_w, out_b, window, gain, bias, gabor, hidden_b, wide, tall, own, columns)
    generate(columns, hidden_w.at[layer], own, tab, rows)
    for n in range(64):
        for part in range(OWN):
            pieces[part * 64 + n : part * 64 + n + 1, :] = rows[part : part + 1, block(n)]
    for part in range(OWN):
        piece = pieces[block(part, 64), :].astype(BF16)
        x_ref[0:64, block(part)] = piece
        x_ref[64:128, block(part)] = piece
        x_ref[128:256, block(part)] = jnp.zeros((128, LANES), BF16)
    spec = transform(x_ref, high, low, first, second, twiddle, OWN)
    bundle[0:SPEC_IM, :] = spec[:, RE]
    bundle[SPEC_IM : 2 * SPEC_IM, :] = spec[:, IM]


def forward_kernel(
    meta, message_ref, out_w, out_b, window, gain, bias, gabor, hidden_b, hidden_w,
    first, second, last, twiddle,
    out_ref, spec_ref, normed_ref, slope_ref, inv_ref, len_ref, kernel_spec, tab,
    message, x_ref, high, low, e_high, e_low, y_ref, out, *make_scratch,
):
    own = kernel_spec.at[OWN_ROWS, :]
    params = (out_w, out_b, window, gain, bias, gabor, hidden_b, hidden_w)
    make_kernel(0, meta, params, (first, second, last, twiddle), kernel_spec, tab, make_scratch)
    message[...] = spread(message_ref[...])
    for y in range(4):
        for b in range(2):
            start = y * 16 + 12 + 2 * b
            len_ref[2 * y + b : 2 * y + b + 1, :] = (
                message[start : start + 1, :] * 128.0 + message[start + 1 : start + 2, :]
            )
    load_signals(message, 16, x_ref)
    convolve(x_ref, spec_ref, kernel_spec, high, low, e_high, e_low, (first, second, last, twiddle), y_ref)
    valid, tally = valid_of(len_ref), tally_of(len_ref)
    inv_ref[...] = jnp.zeros((8, LANES), F32)
    for part in range(OWN):
        normed, inv_std, active, slope = normalise(y_ref, own, valid, tally, part)
        normed_ref[:, block(part, 512)] = normed
        slope_ref[:, block(part, 512)] = slope
        inv_ref[part : part + 1, :] = jnp.broadcast_to(inv_std, (1, LANES))
        y_ref[:, block(part, 512)] = active
    store_signals(out, 16, 0, lambda part, y: y_ref[:, block(part * 4 + y)])
    out_ref[...] = out[...].reshape(DEVICES, 16, LANES).astype(BF16)


def gather_active(message, step, rhs):
    row = lax.broadcasted_iota(jnp.int32, (DEVICES, LANES), 0)
    for i in range(4):
        for part in range(OWN):
            piece = message[pl.ds(part * 4 + i, DEVICES, stride=step), :]
            if part != 1:
                piece = jnp.where(row >= (126 if part == 2 else 127), 1.0, piece)
            rhs[block(part), block(i)] = piece.astype(BF16)


def store_rows(value, out, step, base):
    for i in range(4):
        for part in range(OWN):
            out[pl.ds(base + part * 4 + i, DEVICES, stride=step), :] = value[block(part), block(i)]


def mix_kernel(
    meta, message_ref, x_ref, cotangent, mix_w, mix_b,
    out_ref, next_ref, active_ref, message, padded, out, low, wide, weight, weight_back, lookup,
):
    make_weights(mix_w, mix_b, 0, 1, wide, weight, weight_back, lookup)
    message[...] = spread(message_ref[...])
    gather_active(message, 16, active_ref)
    mixed = dot(weight[...], active_ref[...])
    put_padded(padded, x_ref[...])
    for i in range(4):
        valid = valid_row(meta, i)
        value = rows_of_channels(padded, i) + mixed[:, block(i)] * valid
        next_ref[pl.ds(i, PADDED, stride=4), :] = value
        padded[pl.ds(i, PADDED, stride=4), :] = value * valid
    rows_to_message(padded, out, 24, 0)
    put_padded(padded, masked(meta, cotangent[...]))
    for i in range(4):
        low[:, block(i)] = rows_of_channels(padded, i).astype(BF16)
    store_rows(dot(weight_back[...], low[...]), out, 24, 12)
    out_ref[...] = out[...].reshape(DEVICES, 24, LANES).astype(BF16)


def forward_backward_kernel(
    meta, message_ref, out_w, out_b, window, gain, bias, gabor, hidden_b, hidden_w,
    len_ref, first, second, last, twiddle,
    out_ref, hidden_out, outer_out,
    message, x_ref, high, low, e_high, e_low, y_ref, out, spec_ref, grad_ref, normed_ref, slope_ref, returned_ref,
    rows, sums, mats, kernel_spec, tab, *make_scratch,
):
    own, columns = kernel_spec.at[OWN_ROWS, :], kernel_spec.at[COLUMN_ROWS, :]
    consts = (first, second, last, twiddle)
    params = (out_w, out_b, window, gain, bias, gabor, hidden_b, hidden_w)
    make_kernel(1, meta, params, consts, kernel_spec, tab, make_scratch)
    message[...] = spread(message_ref[...])
    load_signals(message, 24, x_ref)
    convolve(x_ref, spec_ref, kernel_spec, high, low, e_high, e_low, consts, y_ref)
    valid, tally = valid_of(len_ref), tally_of(len_ref)
    inv = []
    for part in range(OWN):
        normed, inv_std, active, slope = normalise(y_ref, own, valid, tally, part)
        normed_ref[:, block(part, 512)] = normed
        slope_ref[:, block(part, 512)] = slope
        inv.append(inv_std)
        y_ref[:, block(part, 512)] = active
    store_signals(out, 24, 0, lambda part, y: y_ref[:, block(part * 4 + y)])
    returned, norm_sums = conv_backward(
        message, 24, 12, lambda part: normed_ref[:, block(part, 512)], lambda part: slope_ref[:, block(part, 512)],
        lambda part: inv[part], own, valid, tally, spec_ref, kernel_spec, x_ref, high, low, e_high, e_low, consts, grad_ref,
    )
    returned_ref[...] = returned
    store_signals(out, 24, 12, lambda part, y: returned_ref[:, block(part * 4 + y)])
    out_ref[...] = out[...].reshape(DEVICES, 24, LANES).astype(BF16)
    hidden, outer = generate_back(
        lambda part: returned_ref[0:64, block(SIGNALS + part)], columns, hidden_w.at[1], own, tab,
        rows, sums, mats,
    )
    hidden_out[...] = hidden
    outer_out[...] = with_norm_sums(outer, norm_sums)


def middle_kernel(
    meta, message_ref, x_ref, cotangent, mix_w, mix_b, active_0, hidden_1,
    output_ref, flow_ref, out_ref, message, padded, out, low_0, low_1, active_1, wide, weight, weight_back, lookup,
):
    make_weights(mix_w, mix_b, 1, 0, wide, weight, weight_back, lookup)
    message[...] = spread(message_ref[...])
    gather_active(message, 24, active_1)
    mixed = dot(weight[...], active_1[...])
    for i in range(4):
        padded[pl.ds(i, PADDED, stride=4), :] = rows_of_channels(x_ref, i) + mixed[:, block(i)] * valid_row(meta, i)
    output_ref[...] = padded[0:CLIP_ROWS, :]
    put_padded(flow_ref, cotangent[...])
    for i in range(4):
        low_1[:, block(i)] = (rows_of_channels(flow_ref, i) * valid_row(meta, i)).astype(BF16)
    for m in range(12):
        padded[pl.ds(m, DEVICES, stride=12), :] = message[pl.ds(12 + m, DEVICES, stride=24), :]
    flow_ref[...] += masked(meta, padded[...])
    for i in range(4):
        low_0[:, block(i)] = (rows_of_channels(flow_ref, i) * valid_row(meta, i)).astype(BF16)
    store_rows(dot(weight_back[...], low_0[...]), out, 32, 0)
    for layer, (active, low) in enumerate(((active_0, low_0), (active_1, low_1))):
        part_sum = dot_rows(active[...], low[...])
        for part in range(OWN):
            for third in range(3):
                out[pl.ds(12 + layer * 9 + part * 3 + third, DEVICES, stride=32), :] = part_sum[
                    block(part), block(third)
                ]
    high, low = high_low(hidden_1[...])
    out[pl.ds(30, DEVICES, stride=32), :] = jnp.concatenate([high, jnp.zeros((96, LANES), F32)], axis=0)
    out[pl.ds(31, DEVICES, stride=32), :] = jnp.concatenate([low, jnp.zeros((96, LANES), F32)], axis=0)
    out_ref[...] = out[...].reshape(DEVICES, 32, LANES).astype(BF16)


LAST_ROWS = 56


def backward_kernel(
    message_ref, spec_ref, kernel_spec, normed_ref, slope_ref, inv_ref, len_ref,
    first, second, last, twiddle, hidden_w, tab, outer_1,
    out_ref,
    message, x_ref, high, low, e_high, e_low, out, grad_ref, returned_ref, rows, sums, mats,
):
    own, columns = kernel_spec.at[OWN_ROWS, :], kernel_spec.at[COLUMN_ROWS, :]
    consts = (first, second, last, twiddle)
    message[...] = spread(message_ref[...])
    valid, tally = valid_of(len_ref), tally_of(len_ref)
    returned, norm_sums = conv_backward(
        message, 32, 0, lambda part: normed_ref[:, block(part, 512)], lambda part: slope_ref[:, block(part, 512)],
        lambda part: inv_ref[part : part + 1, 0:1], own, valid, tally, spec_ref, kernel_spec, x_ref, high, low,
        e_high, e_low, consts, grad_ref,
    )
    returned_ref[...] = returned
    store_signals(out, 16, 0, lambda part, y: returned_ref[:, block(part * 4 + y)])
    hidden, outer = generate_back(
        lambda part: returned_ref[0:64, block(SIGNALS + part)], columns, hidden_w.at[0], own, tab,
        rows, sums, mats,
    )
    outer = with_norm_sums(outer, norm_sums)
    gathered = jnp.sum(message[...].reshape(DEVICES, 32, LANES), axis=0)
    upper, lower = packed_hidden(hidden)
    hidden_1_high, hidden_1_low = high_low(gathered[30:31, :] + gathered[31:32, :])
    outer_0_high, outer_0_low = high_low(one_row(outer))
    outer_1_high, outer_1_low = high_low(one_row(outer_1[...]))
    shared = jnp.concatenate(
        [
            gathered[0:30, :], upper, lower, hidden_1_high, hidden_1_low,
            outer_0_high, outer_0_low, outer_1_high, outer_1_low,
        ],
        axis=0,
    )
    row = lax.broadcasted_iota(jnp.int32, (DEVICES, 16, LANES), 1)
    own_rows = jnp.where(row < 12, out[...].reshape(DEVICES, 16, LANES), shared[None, 0:16, :])
    rest = jnp.broadcast_to(shared[None, 16:LAST_ROWS, :], (DEVICES, LAST_ROWS - 16, LANES))
    out_ref[...] = jnp.concatenate([own_rows, rest], axis=1).astype(BF16)


def last_kernel(
    meta, message_ref, flow_ref,
    input_grad, gabor_grad, hidden_w_grad, hidden_b_grad, out_w_grad, out_b_grad, gain_grad, bias_grad,
    mix_w_grad, mix_b_grad, message, padded, owned, thirds, lookup,
):
    make_lookup(lookup)
    message[...] = spread(message_ref[...])

    def rows_of(k, count=DEVICES):
        return message[pl.ds(k, count, stride=LAST_ROWS), :]

    for m in range(12):
        padded[pl.ds(m, DEVICES, stride=12), :] = rows_of(m)
    input_grad[...] = flow_ref[0:CLIP_ROWS, :] + masked(meta, padded[0:CLIP_ROWS, :])
    shared = jnp.sum(message[...].reshape(DEVICES, LAST_ROWS, LANES)[:, 24:56, :], axis=0)
    hidden_0 = unpacked_hidden(shared[6:22, :], shared[22:26, :])
    hidden_1 = rows_of(50, 32) + rows_of(51, 32)
    lane = lax.broadcasted_iota(jnp.int32, (DEVICES, LANES), 1)
    for layer, hidden in enumerate((hidden_0, hidden_1)):
        hidden_w_grad[layer, 0] = hidden[:, 0:32]
        hidden_w_grad[layer, 1] = pltpu.roll(hidden, 96, 1)[:, 0:32]
        turned = jnp.transpose(jnp.concatenate([hidden, jnp.zeros((96, LANES), F32)], axis=0))
        hidden_b_grad[layer] = turned[64:66, 0:32]
        for j in range(3):
            gabor_grad[layer, j] = turned[66 + 4 * j : 70 + 4 * j, 0:32]
        value = rows_of(52 + 2 * layer) + rows_of(53 + 2 * layer)
        for part in range(OWN):
            wide = pltpu.roll(value, (LANES - 32 * part) % LANES, 1)
            small = pltpu.roll(value, 64 - 3 * part, 1)
            owned[pl.ds(part, DEVICES, stride=OWN), :] = jnp.where(lane < 32, wide, small)
        turned = jnp.transpose(owned[...])
        out_w_grad[layer] = turned[0:32, 0:CHANNELS]
        out_b_grad[layer : layer + 1, :] = turned[32:33, 0:CHANNELS]
        gain_grad[layer : layer + 1, :] = turned[33:34, 0:CHANNELS]
        bias_grad[layer : layer + 1, :] = turned[34:35, 0:CHANNELS]
        bias_rows = []
        for part in range(OWN):
            for third in range(3):
                piece = rows_of(12 + layer * 9 + part * 3 + third)
                thirds[block(part), block(third)] = piece.astype(BF16)
                if part == 2:
                    bias_rows.append(piece[SPOT - 2 * DEVICES : SPOT - 2 * DEVICES + 1, :])
        mix_w_grad[layer] = dot_columns(thirds[...], lookup[...])[0:CHANNELS, 0:CHANNELS]
        mix_b_grad[layer : layer + 1, :] = jnp.concatenate(bias_rows, axis=1)[:, 0:CHANNELS]


def exchange(message):
    return lax.all_to_all(message, AXES, split_axis=0, concat_axis=0, tiled=True)


def to_rows(clips):
    return clips.reshape(2, CHANNELS, 2, LANES).transpose(1, 2, 0, 3).reshape(CLIP_ROWS, LANES)


def from_rows(rows):
    return rows.reshape(CHANNELS, 2, 2, LANES).transpose(2, 0, 1, 3).reshape(2, CHANNELS, PIECE)


def shards(
    inputs, lengths, window, gabor_params, hidden_w, hidden_b, out_w, out_b, bn_gain, bn_bias, mix_w, mix_b, cotangent
):
    position = lax.axis_index("seq").astype(jnp.int32)
    number = position * 4 + lax.axis_index("clips").astype(jnp.int32)
    const = {name: jnp.asarray(value) for name, value in TABLES.items()}
    meta = jnp.concatenate([lengths, jnp.stack([position, number])])
    inputs, cotangent = to_rows(inputs), to_rows(cotangent)

    def rows(count):
        return ((count, LANES), F32)

    with jax.named_scope("source_0"):
        (message,) = run(
            source_kernel, [((DEVICES, 16, LANES), BF16)], [meta, inputs, mix_w],
            [rows(PADDED_ROWS), rows(DEVICES * 16)], "source_0", 8, smem=(0,), far=(2,),
        )
        message = exchange(message)

    square = (PADDED, PADDED)
    generator = [
        jnp.swapaxes(out_w, 1, 2), out_b, jnp.swapaxes(window, 1, 2), bn_gain, bn_bias, gabor_params, hidden_b,
        hidden_w,
    ]
    shape_tab = ((8, HIDDEN, SAMPLES), F32)
    make_scratch = [
        ((LANES, PADDED), F32), rows(PADDED + 8), ((8, SAMPLES), F32), rows(192),
        ((256, OWN * LANES), BF16), ((OWN * LANES, 256), BF16), ((OWN * LANES, 256), BF16),
    ]
    mixer = [mix_w, mix_b]
    mixer_scratch = [(square, BF16)] * 4

    def scratch(signals):
        count = signals * LANES
        return [
            ((256, SIGNALS * LANES), BF16), ((count, 256), BF16), ((count, 256), BF16),
            ((256, count), BF16), ((256, count), BF16),
        ]

    shape_y = (LANES, SIGNALS * LANES)
    shape_s = (SIGNALS * LANES, 256)
    transforms = [const[name] for name in TABLE_NAMES]
    with jax.named_scope("conv_0"):
        message, spec_0, normed_0, slope_0, inv_0, lens, bundle_0, tab_0 = run(
            forward_kernel,
            [
                ((DEVICES, 16, LANES), BF16), (shape_s, F32), (shape_y, F32), (shape_y, F32), rows(8), rows(8),
                rows(BUNDLE), shape_tab,
            ],
            [meta, message, *generator, *transforms],
            [rows(DEVICES * 16), *scratch(SIGNALS), (shape_y, F32), rows(DEVICES * 16), *make_scratch],
            "conv_0", 28, smem=(0,),
        )
        message = exchange(message)

    with jax.named_scope("mix_0"):
        message, middle, active_0 = run(
            mix_kernel,
            [((DEVICES, 24, LANES), BF16), rows(PADDED_ROWS), ((PADDED, 512), BF16)],
            [meta, message, inputs, cotangent, *mixer],
            [rows(DEVICES * 16), rows(PADDED_ROWS), rows(DEVICES * 24), ((PADDED, 512), BF16), *mixer_scratch],
            "mix_0", 12, smem=(0,),
        )
        message = exchange(message)

    back_scratch = [((8, SAMPLES), F32), rows(14 * 32 + 8), rows(72)]
    with jax.named_scope("conv_1"):
        message, hidden_1, outer_1 = run(
            forward_backward_kernel,
            [((DEVICES, 24, LANES), BF16), rows(HIDDEN), rows(8)],
            [
                meta, message, *generator, lens, *transforms,
            ],
            [
                rows(DEVICES * 24), *scratch(SIGNALS + OWN), (shape_y, F32), rows(DEVICES * 24),
                (shape_s, F32), (shape_s, F32), (shape_y, F32), (shape_y, F32),
                ((LANES, (SIGNALS + OWN) * LANES), F32), *back_scratch, rows(BUNDLE), shape_tab, *make_scratch,
            ],
            "conv_1", 40, smem=(0,),
        )
        message = exchange(message)

    with jax.named_scope("mix_1"):
        outputs, flow, message = run(
            middle_kernel,
            [rows(CLIP_ROWS), rows(PADDED_ROWS), ((DEVICES, 32, LANES), BF16)],
            [meta, message, middle, cotangent, *mixer, active_0, hidden_1],
            [
                rows(DEVICES * 24), rows(PADDED_ROWS), rows(DEVICES * 32),
                ((PADDED, 512), BF16), ((PADDED, 512), BF16), ((PADDED, 512), BF16), *mixer_scratch,
            ],
            "mix_1", 12, smem=(0,),
        )
        message = exchange(message)

    with jax.named_scope("conv_back_0"):
        (message,) = run(
            backward_kernel,
            [((DEVICES, LAST_ROWS, LANES), BF16)],
            [
                message, spec_0, bundle_0, normed_0, slope_0, inv_0, lens, *transforms,
                hidden_w, tab_0, outer_1,
            ],
            [
                rows(DEVICES * 32), *scratch(SIGNALS + OWN), rows(DEVICES * 16), (shape_s, F32),
                ((LANES, (SIGNALS + OWN) * LANES), F32), *back_scratch,
            ],
            "conv_back_0", 28,
        )
        message = exchange(message)

    with jax.named_scope("gradients"):
        (
            input_grad, gabor_grad, hidden_w_grad, hidden_b_grad, out_w_grad, out_b_grad, gain_grad, bias_grad,
            mix_w_grad, mix_b_grad,
        ) = run(
            last_kernel,
            [
                rows(CLIP_ROWS), (gabor_params.shape, F32), (hidden_w.shape, F32), (hidden_b.shape, F32),
                ((2, HIDDEN, CHANNELS), F32), (out_b.shape, F32), (bn_gain.shape, F32), (bn_bias.shape, F32),
                (mix_w.shape, F32), (mix_b.shape, F32),
            ],
            [meta, message, flow],
            [rows(DEVICES * LAST_ROWS), rows(PADDED_ROWS), rows(PADDED), (square, BF16), (square, BF16)],
            "gradients", 14, smem=(0,),
        )
    return (
        from_rows(outputs), from_rows(input_grad), gabor_grad, hidden_w_grad, hidden_b_grad,
        jnp.swapaxes(out_w_grad, 1, 2), out_b_grad, gain_grad, bias_grad, mix_w_grad, mix_b_grad,
    )


def solution(mesh):
    clip = P("clips", None, "seq")
    in_specs = (clip, P("clips")) + (P(),) * 10 + (clip,)
    out_specs = (clip, clip) + (P(),) * 9
    return jax.shard_map(shards, mesh=mesh, in_specs=in_specs, out_specs=out_specs, check_vma=False)
```

```python
import math

import jax
import jax.numpy as jnp
import ml_dtypes
import numpy as np
from jax import lax
from jax.experimental import pallas as pl
from jax.experimental.pallas import tpu as pltpu
from jax.sharding import PartitionSpec as P

F32 = jnp.float32
BF16 = jnp.bfloat16
AXES = ("seq", "clips")
DEVICES = 128
OWN = 3
CHANNELS = 380
PADDED = DEVICES * OWN
SAMPLES = 8192
PIECE = 256
HIDDEN = 32
LANES = 128
SIGNALS = 12
TABLE_NAMES = ("first", "second", "last", "twiddle")
PERIOD = 2 * SAMPLES
EPSILON = 1e-05
MEGABYTE = 1024 * 1024
EXACT = lax.Precision.HIGHEST
SPOTS = (2 * DEVICES + 126, 2 * DEVICES + 127, 127)
SPOT = SPOTS[0]


def halves(table):
    high = table.astype(ml_dtypes.bfloat16)
    low = (table - high.astype(np.float64)).astype(ml_dtypes.bfloat16)
    return high, low


def tables():
    order = np.array([2 * j + r for r in range(2) for j in range(32)])
    k = np.arange(LANES)
    turn = 2 * np.pi * ((k[:, None] * order[None, :]) % LANES) / LANES
    c_high, c_low = halves(np.cos(turn))
    s_high, s_low = halves(np.sin(turn))
    first = np.concatenate(
        [
            np.concatenate([c_high, c_low, s_high, s_low], axis=1),
            np.concatenate([-s_high, -s_low, c_high, c_low], axis=1),
        ],
        axis=0,
    )
    turn = 2 * np.pi * ((k[:, None] * k[None, :]) % LANES) / LANES
    cosine, sine = np.cos(turn), np.sin(turn)
    second = halves(np.block([[cosine, -sine], [sine, cosine]]))
    turn = 2 * np.pi * ((order[:, None] * k[None, :]) % LANES) / LANES
    cosine, sine = np.cos(turn) / PERIOD, np.sin(turn) / PERIOD
    last = halves(np.block([[cosine, -sine], [sine, cosine]]))
    turn = 2 * np.pi * (k[:, None] * k[None, :]) / PERIOD
    twiddle = np.stack([np.cos(turn), np.sin(turn)]).astype(np.float32)
    return dict(
        first=first,
        second=np.stack(second),
        last=np.stack(last),
        twiddle=twiddle,
    )


TABLES = tables()


def run(body, outs, args, scratch, name, grant, smem=(), far=()):
    spaces = [pltpu.HBM if i in far else pltpu.SMEM if i in smem else pltpu.VMEM for i in range(len(args))]
    return pl.pallas_call(
        body,
        out_shape=[jax.ShapeDtypeStruct(shape, kind) for shape, kind in outs],
        in_specs=[pl.BlockSpec(memory_space=space) for space in spaces],
        out_specs=[pl.BlockSpec(memory_space=pltpu.VMEM)] * len(outs),
        scratch_shapes=[pltpu.VMEM(shape, kind) for shape, kind in scratch],
        compiler_params=pltpu.CompilerParams(vmem_limit_bytes=grant * MEGABYTE),
        name=name,
    )(*args)


def dot(a, b):
    return jnp.dot(a, b, preferred_element_type=F32)


def dot_rows(a, b, precision=None):
    return lax.dot_general(a, b, (((1,), (1,)), ((), ())), precision=precision, preferred_element_type=F32)


def dot_columns(a, b, precision=None):
    return lax.dot_general(a, b, (((0,), (0,)), ((), ())), precision=precision, preferred_element_type=F32)


def triple(a_high, a_low, b_high, b_low):
    left = jnp.concatenate([a_high, a_low, a_high], axis=1)
    return dot(left, jnp.concatenate([b_high, b_high, b_low], axis=0))


def triple_rows(a_high, a_low, b_high, b_low):
    left = jnp.concatenate([a_high, a_low, a_high], axis=1)
    return dot_rows(left, jnp.concatenate([b_high, b_high, b_low], axis=1))


def put_halves(high_ref, low_ref, rows, columns, value):
    high = value.astype(BF16)
    high_ref[rows, columns] = high
    low_ref[rows, columns] = (value - high.astype(F32)).astype(BF16)


def block(i, size=LANES):
    return slice(i * size, (i + 1) * size)


RE, IM = slice(0, LANES), slice(LANES, 2 * LANES)


def signal_row(b, part, r):
    return part * 4 + r * 2 + b


def spread(message):
    return message.astype(F32).reshape(-1, LANES)


def transform(x_ref, high_ref, low_ref, first, second, twiddle, count):
    part_a = dot(first[...], x_ref[:, : count * LANES])
    cosine, sine = twiddle[0], twiddle[1]
    for s in range(count):
        real, imag = part_a[:LANES, block(s)], part_a[LANES:, block(s)]
        put_halves(high_ref, low_ref, block(s), RE, real * cosine + imag * sine)
        put_halves(high_ref, low_ref, block(s), IM, imag * cosine - real * sine)
    rows = slice(0, count * LANES)
    return triple(high_ref[rows, :], low_ref[rows, :], second[0], second[1])


def transform_back(high_ref, low_ref, e_high, e_low, second, last, twiddle, count):
    rows = slice(0, count * LANES)
    part_d = triple_rows(high_ref[rows, :], low_ref[rows, :], second[0], second[1])
    cosine, sine = twiddle[0], twiddle[1]
    for s in range(count):
        real, imag = part_d[block(s), RE], part_d[block(s), IM]
        put_halves(e_high, e_low, RE, block(s), real * cosine - imag * sine)
        put_halves(e_high, e_low, IM, block(s), real * sine + imag * cosine)
    return triple(last[0], last[1], e_high[:, rows], e_low[:, rows])


def erf_parts(value):
    cdf = 0.5 * (1.0 + lax.erf(value * math.sqrt(0.5)))
    return cdf, jnp.exp(-0.5 * value * value) * (1.0 / math.sqrt(2.0 * math.pi))


def total(value):
    return jnp.sum(jnp.sum(value, axis=0, keepdims=True), axis=1, keepdims=True)


def times_of(row, lane):
    return (256 * (row & 31) + 128 * lax.shift_right_logical(row, 5 * jnp.ones_like(row)) + lane).astype(F32)


def valid_of(len_ref):
    row = lax.broadcasted_iota(jnp.int32, (LANES, LANES), 0) & 63
    times = times_of(row, lax.broadcasted_iota(jnp.int32, (LANES, LANES), 1))
    columns = []
    for y in range(4):
        upper = times[0:64, :] < len_ref[2 * y : 2 * y + 1, :]
        lower = times[64:128, :] < len_ref[2 * y + 1 : 2 * y + 2, :]
        columns.append(jnp.concatenate([upper, lower], axis=0).astype(F32))
    return jnp.concatenate(columns, axis=1)


def tally_of(len_ref):
    return jnp.sum(len_ref[:, 0:1], axis=0, keepdims=True)


def load_signals(message, step, x_ref):
    for part in range(OWN):
        for y in range(4):
            lanes = block(part * 4 + y)
            for b in range(2):
                for r in range(2):
                    start = y * step + signal_row(b, part, r)
                    piece = message[pl.ds(start, 32, stride=4 * step), :].astype(BF16)
                    x_ref[b * 128 + r * 32 : b * 128 + r * 32 + 32, lanes] = piece
                    x_ref[b * 128 + r * 32 + 64 : b * 128 + r * 32 + 96, lanes] = piece


def store_signals(out, step, base, get):
    for part in range(OWN):
        for y in range(4):
            value = get(part, y)
            for b in range(2):
                for r in range(2):
                    start = y * step + base + signal_row(b, part, r)
                    out[pl.ds(start, 32, stride=4 * step), :] = value[b * 64 + r * 32 : b * 64 + r * 32 + 32, :]


SPEC_IM = OWN * LANES
OWN_ROWS = slice(2 * SPEC_IM, 2 * SPEC_IM + 8)
COLUMN_ROWS = slice(2 * SPEC_IM + 8, 2 * SPEC_IM + 8 + HIDDEN)
BUNDLE = 2 * SPEC_IM + 8 + HIDDEN


def kernel_parts(bundle, part):
    return bundle[block(part), :], bundle[SPEC_IM + part * LANES : SPEC_IM + (part + 1) * LANES, :]


def convolve(x_ref, spec_ref, kernel_spec, high, low, e_high, e_low, consts, y_ref):
    first, second, last, twiddle = consts
    spec_ref[...] = transform(x_ref, high, low, first, second, twiddle, SIGNALS)
    for part in range(OWN):
        k_re, k_im = kernel_parts(kernel_spec, part)
        for y in range(4):
            rows = block(part * 4 + y)
            s_re, s_im = spec_ref[rows, RE], spec_ref[rows, IM]
            put_halves(high, low, rows, RE, s_re * k_re - s_im * k_im)
            put_halves(high, low, rows, IM, s_re * k_im + s_im * k_re)
    y_ref[...] = transform_back(high, low, e_high, e_low, second, last, twiddle, SIGNALS)


def normalise(y_ref, own, valid, tally, part):
    value = y_ref[:, block(part, 512)]
    mean = total(valid * value) / tally
    centred = value - mean
    var = total(valid * centred * centred) / tally
    inv_std = lax.rsqrt(var + EPSILON)
    normed = centred * inv_std
    pre_act = normed * own[part : part + 1, 35:36] + own[part : part + 1, 36:37]
    cdf, density = erf_parts(pre_act)
    return normed, inv_std, pre_act * cdf, cdf + pre_act * density


def conv_backward(
    message, step, base, normed_of, slope_of, inv_of, own, valid, tally, spec_ref, kernel_spec, x_ref, high, low,
    e_high, e_low, consts, grad_ref,
):
    first, second, last, twiddle = consts
    sums = []
    for part in range(OWN):
        columns = []
        for y in range(4):
            pieces = []
            for b in range(2):
                for r in range(2):
                    start = y * step + base + signal_row(b, part, r)
                    pieces.append(message[pl.ds(start, 32, stride=4 * step), :])
            columns.append(jnp.concatenate(pieces, axis=0))
        act_grad = jnp.concatenate(columns, axis=1)
        normed = normed_of(part)
        pre_grad = act_grad * slope_of(part)
        bias_total = total(pre_grad)
        gain_total = total(pre_grad * normed)
        gain = own[part : part + 1, 35:36]
        conv_grad = inv_of(part) * (
            gain * pre_grad - valid * (gain * bias_total + normed * (gain * gain_total)) / tally
        )
        conv_low = conv_grad.astype(BF16)
        for b in range(2):
            piece = conv_low[b * 64 : b * 64 + 64, :]
            x_ref[b * 128 : b * 128 + 64, block(part, 512)] = piece
            x_ref[b * 128 + 64 : b * 128 + 128, block(part, 512)] = piece
        sums.append((gain_total, bias_total))
    grad_ref[...] = transform(x_ref, high, low, first, second, twiddle, SIGNALS)
    for part in range(OWN):
        k_re, k_im = kernel_parts(kernel_spec, part)
        corr_re, corr_im = None, None
        for y in range(4):
            rows = block(part * 4 + y)
            g_re, g_im = grad_ref[rows, RE], grad_ref[rows, IM]
            s_re, s_im = spec_ref[rows, RE], spec_ref[rows, IM]
            put_halves(high, low, rows, RE, k_re * g_re + k_im * g_im)
            put_halves(high, low, rows, IM, k_re * g_im - k_im * g_re)
            now_re, now_im = s_re * g_re + s_im * g_im, s_re * g_im - s_im * g_re
            corr_re = now_re if corr_re is None else corr_re + now_re
            corr_im = now_im if corr_im is None else corr_im + now_im
        put_halves(high, low, block(SIGNALS + part), RE, corr_re)
        put_halves(high, low, block(SIGNALS + part), IM, corr_im)
    returned = transform_back(high, low, e_high, e_low, second, last, twiddle, SIGNALS + OWN)
    return returned, sums


def sin_cos(angle):
    turns = jnp.floor(angle * (2.0 / math.pi) + 0.5)
    rest = angle - turns * 1.5703125
    rest = rest - turns * 4.837512969970703125e-4
    rest = rest - turns * 7.549789948768648e-8
    square = rest * rest
    sine = rest + rest * square * (
        -1.6666654611e-1 + square * (8.3321608736e-3 + square * -1.9515295891e-4)
    )
    cosine = 1.0 - 0.5 * square + square * square * (
        4.166664568298827e-2 + square * (-1.388731625493765e-3 + square * 2.443315711809948e-5)
    )
    half = jnp.floor(turns * 0.5)
    odd = turns - 2.0 * half
    sign = 1.0 - 2.0 * (half - 2.0 * jnp.floor(half * 0.5))
    is_odd = odd > 0.5
    return sign * jnp.where(is_odd, cosine, sine), sign * jnp.where(is_odd, -sine, cosine)


CHUNK = 1024
F_TABLE = (0, 4, 7)
C_TABLE = (1, 3, 6)


def envelope_of(times, own):
    lower, upper = own[:, 33:34], own[:, 34:35]
    inside = (times >= lower) & (times < upper)
    offset = (times - lower) / (0.5 * (upper - lower))
    return jnp.where(inside, jnp.exp(-0.5 * offset * offset), 0.0)


def stacked_weight(weight):
    high, low = high_low(weight)
    return jnp.concatenate([high, high, low], axis=1).astype(BF16)


def stacked_dot(weight, value):
    high = value.astype(BF16)
    low = (value - high.astype(F32)).astype(BF16)
    return dot(weight, jnp.concatenate([high, low, high], axis=0))


def own_parameters(layer, number, out_w, out_b, window, gain, bias, gabor, hidden_b, wide, tall, own, columns):
    wide[...] = jnp.zeros(wide.shape, F32)
    wide[0:32, 0:CHANNELS] = out_w[layer]
    wide[32:33, 0:CHANNELS] = out_b[layer : layer + 1, :]
    wide[33:35, 0:CHANNELS] = window[layer].astype(F32)
    wide[35:36, 0:CHANNELS] = gain[layer : layer + 1, :]
    wide[36:37, 0:CHANNELS] = bias[layer : layer + 1, :]
    tall[0:PADDED, :] = jnp.transpose(wide[...])
    tall[PADDED : PADDED + 8, :] = jnp.zeros((8, LANES), F32)
    row = lax.broadcasted_iota(jnp.int32, (8, LANES), 0)
    lane = lax.broadcasted_iota(jnp.int32, (8, LANES), 1)
    mine = tall[pl.ds(number * OWN, 8), :]
    unused = (row >= OWN) | (number * OWN + row >= CHANNELS)
    own[...] = jnp.where(unused, jnp.where(lane == 34, float(SAMPLES), 0.0), mine)
    wide[:, 0:LANES] = jnp.zeros((LANES, LANES), F32)
    for j in range(3):
        wide[4 * j : 4 * j + 4, 0:HIDDEN] = gabor[layer, j]
    wide[12:14, 0:HIDDEN] = hidden_b[layer]
    columns[...] = jnp.transpose(wide[:, 0:LANES])[0:HIDDEN, :]


def sample_rows(first_lane, count):
    lane = first_lane + lax.broadcasted_iota(jnp.int32, (1, count), 1)
    times = times_of(lax.shift_right_logical(lane, 7 * jnp.ones_like(lane)), lane & 127)
    return times, times * (2.0 / (SAMPLES - 1)) - 1.0


def generate(columns, hidden_w, own, tab, rows):
    turns = []
    for j in range(3):
        turn = sin_cos(columns[:, 4 * j + 2 : 4 * j + 3] * (512.0 / (SAMPLES - 1)))
        turns.append([jnp.broadcast_to(value, (HIDDEN, LANES)) for value in turn])

    def step(i, carry):
        _, places = sample_rows(i * CHUNK, CHUNK)
        for j in range(3):
            sharpness, centre = columns[:, 4 * j : 4 * j + 1], columns[:, 4 * j + 1 : 4 * j + 2]
            frequency, phase = columns[:, 4 * j + 2 : 4 * j + 3], columns[:, 4 * j + 3 : 4 * j + 4]
            sine, cosine = sin_cos(frequency * places[:, 0:LANES] + phase)
            turn_sin, turn_cos = turns[j]
            for n in range(CHUNK // LANES):
                width = sharpness * (places[:, block(n)] - centre)
                bell = jnp.exp(-0.5 * width * width)
                here = pl.ds(pl.multiple_of(i * CHUNK + n * LANES, LANES), LANES)
                tab[F_TABLE[j], :, here] = bell * sine
                tab[C_TABLE[j], :, here] = bell * cosine
                sine, cosine = sine * turn_cos + cosine * turn_sin, cosine * turn_cos - sine * turn_sin
        return carry

    lax.fori_loop(0, SAMPLES // CHUNK, step, 0)
    weights = [stacked_weight(hidden_w[0]), stacked_weight(hidden_w[1]), stacked_weight(own[:, 0:32])]
    u_1 = stacked_dot(weights[0], tab[0]) + columns[:, 12:13]
    z_1 = u_1 * tab[4]
    tab[2] = z_1
    tab[3] = u_1 * tab[3]
    u_2 = stacked_dot(weights[1], z_1) + columns[:, 13:14]
    z_2 = u_2 * tab[7]
    tab[5] = z_2
    tab[6] = u_2 * tab[6]
    raw = stacked_dot(weights[2], z_2) + own[:, 32:33]
    times, _ = sample_rows(0, SAMPLES)
    rows[...] = raw * envelope_of(times, own)


def generate_back(kernel_grad, columns, hidden_w, own, tab, rows, sums, mats):
    rows[...] = jnp.zeros(rows.shape, F32)
    for part in range(OWN):
        grad = kernel_grad(part)
        for n in range(64):
            rows[part : part + 1, block(n)] = grad[n : n + 1, :]
    sums[...] = jnp.zeros(sums.shape, F32)
    mats[...] = jnp.zeros(mats.shape, F32)
    turned = jnp.transpose(jnp.concatenate([own[...], jnp.zeros((120, 128), F32)], axis=0))
    weight = [turned[0:32, part : part + 1] for part in range(OWN)]
    back = [stacked_weight(jnp.transpose(hidden_w[j])) for j in range(2)]

    def fold(value):
        acc = value[:, block(0)]
        for i in range(1, CHUNK // LANES):
            acc = acc + value[:, block(i)]
        return acc

    def add(k, value):
        sums[block(k, 32), :] += fold(value)

    def step(i, carry):
        span = pl.ds(pl.multiple_of(i * CHUNK, CHUNK), CHUNK)
        times, places = sample_rows(i * CHUNK, CHUNK)
        draw = rows[:, span] * envelope_of(times, own)
        dz_2 = weight[0] * draw[0:1, :] + weight[1] * draw[1:2, :] + weight[2] * draw[2:3, :]

        def level(j, e_value, g_value):
            centre = columns[:, 4 * j + 1 : 4 * j + 2]
            offset = places - centre
            moment = e_value * offset
            add(4 * j, moment * offset)
            add(4 * j + 1, moment)
            add(4 * j + 2, g_value * places)
            add(4 * j + 3, g_value)

        z_2 = tab[5, :, span]
        level(2, dz_2 * z_2, dz_2 * tab[6, :, span])
        du_2 = dz_2 * tab[7, :, span]
        add(13, du_2)
        dz_1 = stacked_dot(back[1], du_2)
        z_1 = tab[2, :, span]
        level(1, dz_1 * z_1, dz_1 * tab[3, :, span])
        du_1 = dz_1 * tab[4, :, span]
        add(12, du_1)
        dz_0 = stacked_dot(back[0], du_1)
        z_0 = tab[0, :, span]
        level(0, dz_0 * z_0, dz_0 * tab[1, :, span])
        sums[14 * 32 : 14 * 32 + 8, :] += fold(draw)
        left = jnp.concatenate([du_1, du_2, draw], axis=0)
        right = jnp.concatenate([z_0, z_1, z_2, jnp.zeros_like(z_0)], axis=0)
        left_high, right_high = left.astype(BF16), right.astype(BF16)
        left_low = (left - left_high.astype(F32)).astype(BF16)
        right_low = (right - right_high.astype(F32)).astype(BF16)
        mats[...] += (
            dot_rows(left_high, right_high) + dot_rows(left_low, right_high) + dot_rows(left_high, right_low)
        )
        return carry

    lax.fori_loop(0, SAMPLES // CHUNK, step, 0, unroll=SAMPLES // CHUNK)
    lane = lax.broadcasted_iota(jnp.int32, (32, LANES), 1)
    hidden = jnp.where(lane < 32, mats[0:32, :], jnp.where(lane < 64, mats[32:64, :], 0.0))

    def column(k):
        return jnp.sum(sums[block(k, 32), :], axis=1, keepdims=True)

    hidden = jnp.where(lane == 64, column(12), hidden)
    hidden = jnp.where(lane == 65, column(13), hidden)
    for j in range(3):
        sharpness = columns[:, 4 * j : 4 * j + 1]
        hidden = jnp.where(lane == 66 + 4 * j, -sharpness * column(4 * j), hidden)
        hidden = jnp.where(lane == 67 + 4 * j, sharpness * sharpness * column(4 * j + 1), hidden)
        hidden = jnp.where(lane == 68 + 4 * j, column(4 * j + 2), hidden)
        hidden = jnp.where(lane == 69 + 4 * j, column(4 * j + 3), hidden)
    lane8 = lax.broadcasted_iota(jnp.int32, (8, LANES), 1)
    outer = pltpu.roll(mats[64:72, :], LANES - 64, 1)
    raw_total = jnp.sum(sums[14 * 32 : 14 * 32 + 8, :], axis=1, keepdims=True)
    outer = jnp.where(lane8 < 32, outer, 0.0)
    outer = jnp.where(lane8 == 32, raw_total, outer)
    return hidden, outer


def with_norm_sums(outer, sums):
    row = lax.broadcasted_iota(jnp.int32, (8, LANES), 0)
    lane = lax.broadcasted_iota(jnp.int32, (8, LANES), 1)
    for part in range(OWN):
        gain_total, bias_total = sums[part]
        outer = jnp.where((row == part) & (lane == 33), gain_total, outer)
        outer = jnp.where((row == part) & (lane == 34), bias_total, outer)
    return outer


def one_row(outer):
    lane = lax.broadcasted_iota(jnp.int32, (1, LANES), 1)
    result = jnp.zeros((1, LANES), F32)
    for part in range(OWN):
        row = outer[part : part + 1, :]
        moved = pltpu.roll(row, 32 * part, 1) if part else row
        result = jnp.where((lane >= 32 * part) & (lane < 32 * part + 32), moved, result)
        moved = pltpu.roll(row, 64 + 3 * part, 1)
        result = jnp.where((lane >= 96 + 3 * part) & (lane < 99 + 3 * part), moved, result)
    return result


def packed_hidden(hidden):
    lane16 = lax.broadcasted_iota(jnp.int32, (16, LANES), 1)
    upper = jnp.where(lane16 < 64, hidden[0:16, :], pltpu.roll(hidden[16:32, :], 64, 1))
    lane4 = lax.broadcasted_iota(jnp.int32, (4, LANES), 1)
    lower = jnp.zeros((4, LANES), F32)
    for g in range(8):
        moved = pltpu.roll(hidden, (64 + 16 * g) % LANES, 1)[4 * g : 4 * g + 4, :]
        lower = jnp.where((lane4 >= 16 * g) & (lane4 < 16 * g + 16), moved, lower)
    return upper, lower


def unpacked_hidden(upper, lower):
    lane16 = lax.broadcasted_iota(jnp.int32, (16, LANES), 1)
    lane32 = lax.broadcasted_iota(jnp.int32, (32, LANES), 1)
    top = jnp.concatenate([upper, pltpu.roll(upper, 64, 1)], axis=0)
    tiled = jnp.concatenate([lower] * 8, axis=0)
    row32 = lax.broadcasted_iota(jnp.int32, (32, LANES), 0)
    rest = jnp.zeros((32, LANES), F32)
    for g in range(8):
        moved = pltpu.roll(tiled, (64 - 16 * g) % LANES, 1)
        rest = jnp.where((row32 >= 4 * g) & (row32 < 4 * g + 4), moved, rest)
    return jnp.where(lane32 < 64, top, rest)


def high_low(value):
    high = value.astype(BF16).astype(F32)
    return high, value - high


def valid_row(meta, i):
    lane = lax.broadcasted_iota(jnp.int32, (1, LANES), 1)
    return (meta[2] * PIECE + (i // 2) * LANES + lane < meta[i % 2]).astype(F32)


def masked(meta, rows):
    mask = jnp.concatenate([valid_row(meta, i) for i in range(4)] * 2, axis=0)
    return (rows.reshape(-1, 8, LANES) * mask[None]).reshape(-1, LANES)


CLIP_ROWS = 4 * CHANNELS
PADDED_ROWS = 4 * PADDED


def put_padded(padded, rows):
    padded[0:CLIP_ROWS, :] = rows
    padded[CLIP_ROWS:PADDED_ROWS, :] = jnp.zeros((PADDED_ROWS - CLIP_ROWS, LANES), F32)


def rows_to_message(padded, out, step, base):
    for m in range(12):
        out[pl.ds(base + m, DEVICES, stride=step), :] = padded[pl.ds(m, DEVICES, stride=12), :]


def rows_of_channels(padded, i):
    return padded[pl.ds(i, PADDED, stride=4), :]


def source_kernel(meta, x_ref, out_ref, padded, out):
    put_padded(padded, masked(meta, x_ref[...]))
    for b in range(2):
        length = meta[b]
        upper = lax.shift_right_logical(length, 7)
        out[pl.ds(12 + 2 * b, DEVICES, stride=16), :] = jnp.full((DEVICES, LANES), upper.astype(F32))
        out[pl.ds(13 + 2 * b, DEVICES, stride=16), :] = jnp.full(
            (DEVICES, LANES), (length - upper * 128).astype(F32)
        )
    rows_to_message(padded, out, 16, 0)
    out_ref[...] = out[...].reshape(DEVICES, 16, LANES).astype(BF16)


def make_lookup(lookup):
    row = lax.broadcasted_iota(jnp.int32, (DEVICES, PADDED), 0)
    column = lax.broadcasted_iota(jnp.int32, (DEVICES, PADDED), 1)
    for part in range(OWN):
        lookup[block(part), :] = (column == OWN * row + part).astype(F32).astype(BF16)


def make_weights(mix_w, mix_b, wide, lookup, weights, weights_back):
    make_lookup(lookup)
    wide[...] = jnp.zeros(wide.shape, BF16)
    row = lax.broadcasted_iota(jnp.int32, (LANES, CHANNELS), 0)
    lines = jnp.where(row == 0, mix_b[0:1, :], jnp.where(row == 1, mix_b[1:2, :], 0.0))
    turned = jnp.transpose(jnp.concatenate([lines, jnp.zeros((LANES, PADDED - CHANNELS), F32)], axis=1))
    lane = lax.broadcasted_iota(jnp.int32, (PADDED, PADDED), 1)
    for layer in range(2):
        wide[0:CHANNELS, 0:CHANNELS] = mix_w[:, layer, :]
        weights_back[layer] = dot_rows(lookup[...], wide[...]).astype(BF16)
        value = dot_rows(wide[...], lookup[...])
        rest = turned[:, layer : layer + 1]
        for spot in SPOTS:
            high, rest = high_low(rest)
            value = jnp.where(lane == spot, high, value)
        weights[layer] = value.astype(BF16)


def make_kernel(layer, meta, params, consts, bundle, tab, scratch):
    out_w, out_b, window, gain, bias, gabor, hidden_b, hidden_w = params
    first, second, _, twiddle = consts
    wide, tall, rows, pieces, x_ref, high, low = scratch
    own, columns = bundle.at[OWN_ROWS, :], bundle.at[COLUMN_ROWS, :]
    own_parameters(layer, meta[3], out_w, out_b, window, gain, bias, gabor, hidden_b, wide, tall, own, columns)
    generate(columns, hidden_w.at[layer], own, tab, rows)
    for n in range(64):
        for part in range(OWN):
            pieces[part * 64 + n : part * 64 + n + 1, :] = rows[part : part + 1, block(n)]
    for part in range(OWN):
        piece = pieces[block(part, 64), :].astype(BF16)
        x_ref[0:64, block(part)] = piece
        x_ref[64:128, block(part)] = piece
        x_ref[128:256, block(part)] = jnp.zeros((128, LANES), BF16)
    spec = transform(x_ref, high, low, first, second, twiddle, OWN)
    bundle[0:SPEC_IM, :] = spec[:, RE]
    bundle[SPEC_IM : 2 * SPEC_IM, :] = spec[:, IM]


def forward_kernel(
    meta, message_ref, out_w, out_b, window, gain, bias, gabor, hidden_b, hidden_w,
    first, second, last, twiddle,
    out_ref, spec_ref, normed_ref, slope_ref, inv_ref, len_ref, kernel_spec, tab,
    message, x_ref, high, low, e_high, e_low, y_ref, out, *make_scratch,
):
    own = kernel_spec.at[OWN_ROWS, :]
    params = (out_w, out_b, window, gain, bias, gabor, hidden_b, hidden_w)
    make_kernel(0, meta, params, (first, second, last, twiddle), kernel_spec, tab, make_scratch)
    message[...] = spread(message_ref[...])
    for y in range(4):
        for b in range(2):
            start = y * 16 + 12 + 2 * b
            len_ref[2 * y + b : 2 * y + b + 1, :] = (
                message[start : start + 1, :] * 128.0 + message[start + 1 : start + 2, :]
            )
    load_signals(message, 16, x_ref)
    convolve(x_ref, spec_ref, kernel_spec, high, low, e_high, e_low, (first, second, last, twiddle), y_ref)
    valid, tally = valid_of(len_ref), tally_of(len_ref)
    inv_ref[...] = jnp.zeros((8, LANES), F32)
    for part in range(OWN):
        normed, inv_std, active, slope = normalise(y_ref, own, valid, tally, part)
        normed_ref[:, block(part, 512)] = normed
        slope_ref[:, block(part, 512)] = slope
        inv_ref[part : part + 1, :] = jnp.broadcast_to(inv_std, (1, LANES))
        y_ref[:, block(part, 512)] = active
    store_signals(out, 16, 0, lambda part, y: y_ref[:, block(part * 4 + y)])
    out_ref[...] = out[...].reshape(DEVICES, 16, LANES).astype(BF16)


def gather_active(message, step, rhs):
    row = lax.broadcasted_iota(jnp.int32, (DEVICES, LANES), 0)
    for i in range(4):
        for part in range(OWN):
            piece = message[pl.ds(part * 4 + i, DEVICES, stride=step), :]
            if part != 1:
                piece = jnp.where(row >= (126 if part == 2 else 127), 1.0, piece)
            rhs[block(part), block(i)] = piece.astype(BF16)


def store_rows(value, out, step, base):
    for i in range(4):
        for part in range(OWN):
            out[pl.ds(base + part * 4 + i, DEVICES, stride=step), :] = value[block(part), block(i)]


def mix_kernel(
    meta, message_ref, x_ref, cotangent, mix_w, mix_b,
    out_ref, next_ref, active_ref, weights, weights_back, message, padded, out, low, wide, lookup,
):
    make_weights(mix_w, mix_b, wide, lookup, weights, weights_back)
    message[...] = spread(message_ref[...])
    gather_active(message, 16, active_ref)
    mixed = dot(weights[0], active_ref[...])
    put_padded(padded, x_ref[...])
    for i in range(4):
        valid = valid_row(meta, i)
        value = rows_of_channels(padded, i) + mixed[:, block(i)] * valid
        next_ref[pl.ds(i, PADDED, stride=4), :] = value
        padded[pl.ds(i, PADDED, stride=4), :] = value * valid
    rows_to_message(padded, out, 24, 0)
    put_padded(padded, masked(meta, cotangent[...]))
    for i in range(4):
        low[:, block(i)] = rows_of_channels(padded, i).astype(BF16)
    store_rows(dot(weights_back[1], low[...]), out, 24, 12)
    out_ref[...] = out[...].reshape(DEVICES, 24, LANES).astype(BF16)


def forward_backward_kernel(
    meta, message_ref, out_w, out_b, window, gain, bias, gabor, hidden_b, hidden_w,
    len_ref, first, second, last, twiddle,
    out_ref, hidden_out, outer_out,
    message, x_ref, high, low, e_high, e_low, y_ref, out, spec_ref, grad_ref, normed_ref, slope_ref, returned_ref,
    rows, sums, mats, kernel_spec, tab, *make_scratch,
):
    own, columns = kernel_spec.at[OWN_ROWS, :], kernel_spec.at[COLUMN_ROWS, :]
    consts = (first, second, last, twiddle)
    params = (out_w, out_b, window, gain, bias, gabor, hidden_b, hidden_w)
    make_kernel(1, meta, params, consts, kernel_spec, tab, make_scratch)
    message[...] = spread(message_ref[...])
    load_signals(message, 24, x_ref)
    convolve(x_ref, spec_ref, kernel_spec, high, low, e_high, e_low, consts, y_ref)
    valid, tally = valid_of(len_ref), tally_of(len_ref)
    inv = []
    for part in range(OWN):
        normed, inv_std, active, slope = normalise(y_ref, own, valid, tally, part)
        normed_ref[:, block(part, 512)] = normed
        slope_ref[:, block(part, 512)] = slope
        inv.append(inv_std)
        y_ref[:, block(part, 512)] = active
    store_signals(out, 24, 0, lambda part, y: y_ref[:, block(part * 4 + y)])
    returned, norm_sums = conv_backward(
        message, 24, 12, lambda part: normed_ref[:, block(part, 512)], lambda part: slope_ref[:, block(part, 512)],
        lambda part: inv[part], own, valid, tally, spec_ref, kernel_spec, x_ref, high, low, e_high, e_low, consts, grad_ref,
    )
    returned_ref[...] = returned
    store_signals(out, 24, 12, lambda part, y: returned_ref[:, block(part * 4 + y)])
    out_ref[...] = out[...].reshape(DEVICES, 24, LANES).astype(BF16)
    hidden, outer = generate_back(
        lambda part: returned_ref[0:64, block(SIGNALS + part)], columns, hidden_w.at[1], own, tab,
        rows, sums, mats,
    )
    hidden_out[...] = hidden
    outer_out[...] = with_norm_sums(outer, norm_sums)


def middle_kernel(
    meta, message_ref, x_ref, cotangent, weights, weights_back, active_0, hidden_1,
    output_ref, flow_ref, out_ref, message, padded, out, low_0, low_1, active_1,
):
    message[...] = spread(message_ref[...])
    gather_active(message, 24, active_1)
    mixed = dot(weights[1], active_1[...])
    for i in range(4):
        padded[pl.ds(i, PADDED, stride=4), :] = rows_of_channels(x_ref, i) + mixed[:, block(i)] * valid_row(meta, i)
    output_ref[...] = padded[0:CLIP_ROWS, :]
    put_padded(flow_ref, cotangent[...])
    for i in range(4):
        low_1[:, block(i)] = (rows_of_channels(flow_ref, i) * valid_row(meta, i)).astype(BF16)
    for m in range(12):
        padded[pl.ds(m, DEVICES, stride=12), :] = message[pl.ds(12 + m, DEVICES, stride=24), :]
    flow_ref[...] += masked(meta, padded[...])
    for i in range(4):
        low_0[:, block(i)] = (rows_of_channels(flow_ref, i) * valid_row(meta, i)).astype(BF16)
    store_rows(dot(weights_back[0], low_0[...]), out, 32, 0)
    for layer, (active, low) in enumerate(((active_0, low_0), (active_1, low_1))):
        part_sum = dot_rows(active[...], low[...])
        for part in range(OWN):
            for third in range(3):
                out[pl.ds(12 + layer * 9 + part * 3 + third, DEVICES, stride=32), :] = part_sum[
                    block(part), block(third)
                ]
    high, low = high_low(hidden_1[...])
    out[pl.ds(30, DEVICES, stride=32), :] = jnp.concatenate([high, jnp.zeros((96, LANES), F32)], axis=0)
    out[pl.ds(31, DEVICES, stride=32), :] = jnp.concatenate([low, jnp.zeros((96, LANES), F32)], axis=0)
    out_ref[...] = out[...].reshape(DEVICES, 32, LANES).astype(BF16)


LAST_ROWS = 56


def backward_kernel(
    message_ref, spec_ref, kernel_spec, normed_ref, slope_ref, inv_ref, len_ref,
    first, second, last, twiddle, hidden_w, tab, outer_1,
    out_ref,
    message, x_ref, high, low, e_high, e_low, out, grad_ref, returned_ref, rows, sums, mats,
):
    own, columns = kernel_spec.at[OWN_ROWS, :], kernel_spec.at[COLUMN_ROWS, :]
    consts = (first, second, last, twiddle)
    message[...] = spread(message_ref[...])
    valid, tally = valid_of(len_ref), tally_of(len_ref)
    returned, norm_sums = conv_backward(
        message, 32, 0, lambda part: normed_ref[:, block(part, 512)], lambda part: slope_ref[:, block(part, 512)],
        lambda part: inv_ref[part : part + 1, 0:1], own, valid, tally, spec_ref, kernel_spec, x_ref, high, low,
        e_high, e_low, consts, grad_ref,
    )
    returned_ref[...] = returned
    store_signals(out, 16, 0, lambda part, y: returned_ref[:, block(part * 4 + y)])
    hidden, outer = generate_back(
        lambda part: returned_ref[0:64, block(SIGNALS + part)], columns, hidden_w.at[0], own, tab,
        rows, sums, mats,
    )
    outer = with_norm_sums(outer, norm_sums)
    gathered = jnp.sum(message[...].reshape(DEVICES, 32, LANES), axis=0)
    upper, lower = packed_hidden(hidden)
    hidden_1_high, hidden_1_low = high_low(gathered[30:31, :] + gathered[31:32, :])
    outer_0_high, outer_0_low = high_low(one_row(outer))
    outer_1_high, outer_1_low = high_low(one_row(outer_1[...]))
    shared = jnp.concatenate(
        [
            gathered[0:30, :], upper, lower, hidden_1_high, hidden_1_low,
            outer_0_high, outer_0_low, outer_1_high, outer_1_low,
        ],
        axis=0,
    )
    row = lax.broadcasted_iota(jnp.int32, (DEVICES, 16, LANES), 1)
    own_rows = jnp.where(row < 12, out[...].reshape(DEVICES, 16, LANES), shared[None, 0:16, :])
    rest = jnp.broadcast_to(shared[None, 16:LAST_ROWS, :], (DEVICES, LAST_ROWS - 16, LANES))
    out_ref[...] = jnp.concatenate([own_rows, rest], axis=1).astype(BF16)


def last_kernel(
    meta, message_ref, flow_ref,
    input_grad, gabor_grad, hidden_w_grad, hidden_b_grad, out_w_grad, out_b_grad, gain_grad, bias_grad,
    mix_w_grad, mix_b_grad, message, padded, owned, thirds, lookup,
):
    make_lookup(lookup)
    message[...] = spread(message_ref[...])

    def rows_of(k, count=DEVICES):
        return message[pl.ds(k, count, stride=LAST_ROWS), :]

    for m in range(12):
        padded[pl.ds(m, DEVICES, stride=12), :] = rows_of(m)
    input_grad[...] = flow_ref[0:CLIP_ROWS, :] + masked(meta, padded[0:CLIP_ROWS, :])
    shared = jnp.sum(message[...].reshape(DEVICES, LAST_ROWS, LANES)[:, 24:56, :], axis=0)
    hidden_0 = unpacked_hidden(shared[6:22, :], shared[22:26, :])
    hidden_1 = rows_of(50, 32) + rows_of(51, 32)
    lane = lax.broadcasted_iota(jnp.int32, (DEVICES, LANES), 1)
    for layer, hidden in enumerate((hidden_0, hidden_1)):
        hidden_w_grad[layer, 0] = hidden[:, 0:32]
        hidden_w_grad[layer, 1] = pltpu.roll(hidden, 96, 1)[:, 0:32]
        turned = jnp.transpose(jnp.concatenate([hidden, jnp.zeros((96, LANES), F32)], axis=0))
        hidden_b_grad[layer] = turned[64:66, 0:32]
        for j in range(3):
            gabor_grad[layer, j] = turned[66 + 4 * j : 70 + 4 * j, 0:32]
        value = rows_of(52 + 2 * layer) + rows_of(53 + 2 * layer)
        for part in range(OWN):
            wide = pltpu.roll(value, (LANES - 32 * part) % LANES, 1)
            small = pltpu.roll(value, 64 - 3 * part, 1)
            owned[pl.ds(part, DEVICES, stride=OWN), :] = jnp.where(lane < 32, wide, small)
        turned = jnp.transpose(owned[...])
        out_w_grad[layer] = turned[0:32, 0:CHANNELS]
        out_b_grad[layer : layer + 1, :] = turned[32:33, 0:CHANNELS]
        gain_grad[layer : layer + 1, :] = turned[33:34, 0:CHANNELS]
        bias_grad[layer : layer + 1, :] = turned[34:35, 0:CHANNELS]
        bias_rows = []
        for part in range(OWN):
            for third in range(3):
                piece = rows_of(12 + layer * 9 + part * 3 + third)
                thirds[block(part), block(third)] = piece.astype(BF16)
                if part == 2:
                    bias_rows.append(piece[SPOT - 2 * DEVICES : SPOT - 2 * DEVICES + 1, :])
        mix_w_grad[:, layer, :] = dot_columns(thirds[...], lookup[...])[0:CHANNELS, 0:CHANNELS]
        mix_b_grad[layer : layer + 1, :] = jnp.concatenate(bias_rows, axis=1)[:, 0:CHANNELS]


def exchange(message):
    return lax.all_to_all(message, AXES, split_axis=0, concat_axis=0, tiled=True)


def to_rows(clips):
    return clips.reshape(2, CHANNELS, 2, LANES).transpose(1, 2, 0, 3).reshape(CLIP_ROWS, LANES)


def from_rows(rows):
    return rows.reshape(CHANNELS, 2, 2, LANES).transpose(2, 0, 1, 3).reshape(2, CHANNELS, PIECE)


def shards(
    inputs, lengths, window, gabor_params, hidden_w, hidden_b, out_w, out_b, bn_gain, bn_bias, mix_w, mix_b, cotangent
):
    position = lax.axis_index("seq").astype(jnp.int32)
    number = position * 4 + lax.axis_index("clips").astype(jnp.int32)
    const = {name: jnp.asarray(value) for name, value in TABLES.items()}
    meta = jnp.concatenate([lengths, jnp.stack([position, number])])
    inputs, cotangent = to_rows(inputs), to_rows(cotangent)

    def rows(count):
        return ((count, LANES), F32)

    with jax.named_scope("source_0"):
        (message,) = run(
            source_kernel, [((DEVICES, 16, LANES), BF16)], [meta, inputs],
            [rows(PADDED_ROWS), rows(DEVICES * 16)], "source_0", 8, smem=(0,),
        )
        message = exchange(message)

    square = (PADDED, PADDED)
    generator = [
        jnp.swapaxes(out_w, 1, 2), out_b, jnp.swapaxes(window, 1, 2), bn_gain, bn_bias, gabor_params, hidden_b,
        hidden_w,
    ]
    shape_tab = ((8, HIDDEN, SAMPLES), F32)
    make_scratch = [
        ((LANES, PADDED), F32), rows(PADDED + 8), ((8, SAMPLES), F32), rows(192),
        ((256, OWN * LANES), BF16), ((OWN * LANES, 256), BF16), ((OWN * LANES, 256), BF16),
    ]
    mixers = ((2, *square), BF16)

    def scratch(signals):
        count = signals * LANES
        return [
            ((256, SIGNALS * LANES), BF16), ((count, 256), BF16), ((count, 256), BF16),
            ((256, count), BF16), ((256, count), BF16),
        ]

    shape_y = (LANES, SIGNALS * LANES)
    shape_s = (SIGNALS * LANES, 256)
    transforms = [const[name] for name in TABLE_NAMES]
    with jax.named_scope("conv_0"):
        message, spec_0, normed_0, slope_0, inv_0, lens, bundle_0, tab_0 = run(
            forward_kernel,
            [
                ((DEVICES, 16, LANES), BF16), (shape_s, F32), (shape_y, F32), (shape_y, F32), rows(8), rows(8),
                rows(BUNDLE), shape_tab,
            ],
            [meta, message, *generator, *transforms],
            [rows(DEVICES * 16), *scratch(SIGNALS), (shape_y, F32), rows(DEVICES * 16), *make_scratch],
            "conv_0", 16, smem=(0,),
        )
        message = exchange(message)

    with jax.named_scope("mix_0"):
        message, middle, active_0, weights, weights_back = run(
            mix_kernel,
            [((DEVICES, 24, LANES), BF16), rows(PADDED_ROWS), ((PADDED, 512), BF16), mixers, mixers],
            [meta, message, inputs, cotangent, jnp.swapaxes(mix_w, 0, 1), mix_b],
            [rows(DEVICES * 16), rows(PADDED_ROWS), rows(DEVICES * 24), ((PADDED, 512), BF16), (square, BF16), (square, BF16)],
            "mix_0", 12, smem=(0,),
        )
        message = exchange(message)

    back_scratch = [((8, SAMPLES), F32), rows(14 * 32 + 8), rows(72)]
    with jax.named_scope("conv_1"):
        message, hidden_1, outer_1 = run(
            forward_backward_kernel,
            [((DEVICES, 24, LANES), BF16), rows(HIDDEN), rows(8)],
            [
                meta, message, *generator, lens, *transforms,
            ],
            [
                rows(DEVICES * 24), *scratch(SIGNALS + OWN), (shape_y, F32), rows(DEVICES * 24),
                (shape_s, F32), (shape_s, F32), (shape_y, F32), (shape_y, F32),
                ((LANES, (SIGNALS + OWN) * LANES), F32), *back_scratch, rows(BUNDLE), shape_tab, *make_scratch,
            ],
            "conv_1", 26, smem=(0,),
        )
        message = exchange(message)

    with jax.named_scope("mix_1"):
        outputs, flow, message = run(
            middle_kernel,
            [rows(CLIP_ROWS), rows(PADDED_ROWS), ((DEVICES, 32, LANES), BF16)],
            [meta, message, middle, cotangent, weights, weights_back, active_0, hidden_1],
            [
                rows(DEVICES * 24), rows(PADDED_ROWS), rows(DEVICES * 32),
                ((PADDED, 512), BF16), ((PADDED, 512), BF16), ((PADDED, 512), BF16),
            ],
            "mix_1", 12, smem=(0,),
        )
        message = exchange(message)

    with jax.named_scope("conv_back_0"):
        (message,) = run(
            backward_kernel,
            [((DEVICES, LAST_ROWS, LANES), BF16)],
            [
                message, spec_0, bundle_0, normed_0, slope_0, inv_0, lens, *transforms,
                hidden_w, tab_0, outer_1,
            ],
            [
                rows(DEVICES * 32), *scratch(SIGNALS + OWN), rows(DEVICES * 16), (shape_s, F32),
                ((LANES, (SIGNALS + OWN) * LANES), F32), *back_scratch,
            ],
            "conv_back_0", 16,
        )
        message = exchange(message)

    with jax.named_scope("gradients"):
        (
            input_grad, gabor_grad, hidden_w_grad, hidden_b_grad, out_w_grad, out_b_grad, gain_grad, bias_grad,
            mix_w_grad, mix_b_grad,
        ) = run(
            last_kernel,
            [
                rows(CLIP_ROWS), (gabor_params.shape, F32), (hidden_w.shape, F32), (hidden_b.shape, F32),
                ((2, HIDDEN, CHANNELS), F32), (out_b.shape, F32), (bn_gain.shape, F32), (bn_bias.shape, F32),
                ((CHANNELS, 2, CHANNELS), F32), (mix_b.shape, F32),
            ],
            [meta, message, flow],
            [rows(DEVICES * LAST_ROWS), rows(PADDED_ROWS), rows(PADDED), (square, BF16), (square, BF16)],
            "gradients", 14, smem=(0,),
        )
    return (
        from_rows(outputs), from_rows(input_grad), gabor_grad, hidden_w_grad, hidden_b_grad,
        jnp.swapaxes(out_w_grad, 1, 2), out_b_grad, gain_grad, bias_grad, jnp.swapaxes(mix_w_grad, 0, 1), mix_b_grad,
    )


def solution(mesh):
    clip = P("clips", None, "seq")
    in_specs = (clip, P("clips")) + (P(),) * 10 + (clip,)
    out_specs = (clip, clip) + (P(),) * 9
    return jax.shard_map(shards, mesh=mesh, in_specs=in_specs, out_specs=out_specs, check_vma=False)
```

```python
import math

import jax
import jax.numpy as jnp
import ml_dtypes
import numpy as np
from jax import lax
from jax.experimental import pallas as pl
from jax.experimental.pallas import tpu as pltpu
from jax.sharding import PartitionSpec as P

F32 = jnp.float32
BF16 = jnp.bfloat16
AXES = ("seq", "clips")
DEVICES = 128
OWN = 3
CHANNELS = 380
PADDED = DEVICES * OWN
SAMPLES = 8192
PIECE = 256
HIDDEN = 32
LANES = 128
SIGNALS = 12
TABLE_NAMES = ("first", "second", "last", "twiddle")
PERIOD = 2 * SAMPLES
EPSILON = 1e-05
MEGABYTE = 1024 * 1024
EXACT = lax.Precision.HIGHEST
SPOTS = (2 * DEVICES + 126, 2 * DEVICES + 127, 127)
SPOT = SPOTS[0]


def halves(table):
    high = table.astype(ml_dtypes.bfloat16)
    low = (table - high.astype(np.float64)).astype(ml_dtypes.bfloat16)
    return high, low


def tables():
    order = np.array([2 * j + r for r in range(2) for j in range(32)])
    k = np.arange(LANES)
    turn = 2 * np.pi * ((k[:, None] * order[None, :]) % LANES) / LANES
    c_high, c_low = halves(np.cos(turn))
    s_high, s_low = halves(np.sin(turn))
    first = np.concatenate(
        [
            np.concatenate([c_high, c_low, s_high, s_low], axis=1),
            np.concatenate([-s_high, -s_low, c_high, c_low], axis=1),
        ],
        axis=0,
    )
    turn = 2 * np.pi * ((k[:, None] * k[None, :]) % LANES) / LANES
    cosine, sine = np.cos(turn), np.sin(turn)
    second = halves(np.block([[cosine, -sine], [sine, cosine]]))
    turn = 2 * np.pi * ((order[:, None] * k[None, :]) % LANES) / LANES
    cosine, sine = np.cos(turn) / PERIOD, np.sin(turn) / PERIOD
    last = halves(np.block([[cosine, -sine], [sine, cosine]]))
    turn = 2 * np.pi * (k[:, None] * k[None, :]) / PERIOD
    twiddle = np.stack([np.cos(turn), np.sin(turn)]).astype(np.float32)
    return dict(
        first=first,
        second=np.stack(second),
        last=np.stack(last),
        twiddle=twiddle,
    )


TABLES = tables()


def run(body, outs, args, scratch, name, grant, smem=(), far=()):
    spaces = [pltpu.HBM if i in far else pltpu.SMEM if i in smem else pltpu.VMEM for i in range(len(args))]
    return pl.pallas_call(
        body,
        out_shape=[jax.ShapeDtypeStruct(shape, kind) for shape, kind in outs],
        in_specs=[pl.BlockSpec(memory_space=space) for space in spaces],
        out_specs=[pl.BlockSpec(memory_space=pltpu.VMEM)] * len(outs),
        scratch_shapes=[pltpu.VMEM(shape, kind) for shape, kind in scratch],
        compiler_params=pltpu.CompilerParams(vmem_limit_bytes=grant * MEGABYTE),
        name=name,
    )(*args)


def dot(a, b):
    return jnp.dot(a, b, preferred_element_type=F32)


def dot_rows(a, b, precision=None):
    return lax.dot_general(a, b, (((1,), (1,)), ((), ())), precision=precision, preferred_element_type=F32)


def dot_columns(a, b, precision=None):
    return lax.dot_general(a, b, (((0,), (0,)), ((), ())), precision=precision, preferred_element_type=F32)


def triple(a_high, a_low, b_high, b_low):
    left = jnp.concatenate([a_high, a_low, a_high], axis=1)
    return dot(left, jnp.concatenate([b_high, b_high, b_low], axis=0))


def triple_rows(a_high, a_low, b_high, b_low):
    left = jnp.concatenate([a_high, a_low, a_high], axis=1)
    return dot_rows(left, jnp.concatenate([b_high, b_high, b_low], axis=1))


def put_halves(high_ref, low_ref, rows, columns, value):
    high = value.astype(BF16)
    high_ref[rows, columns] = high
    low_ref[rows, columns] = (value - high.astype(F32)).astype(BF16)


def block(i, size=LANES):
    return slice(i * size, (i + 1) * size)


RE, IM = slice(0, LANES), slice(LANES, 2 * LANES)


def signal_row(b, part, r):
    return part * 4 + r * 2 + b


def spread(message):
    return message.astype(F32).reshape(-1, LANES)


def transform(x_ref, high_ref, low_ref, first, second, twiddle, count):
    part_a = dot(first[...], x_ref[:, : count * LANES])
    cosine, sine = twiddle[0], twiddle[1]
    for s in range(count):
        real, imag = part_a[:LANES, block(s)], part_a[LANES:, block(s)]
        put_halves(high_ref, low_ref, block(s), RE, real * cosine + imag * sine)
        put_halves(high_ref, low_ref, block(s), IM, imag * cosine - real * sine)
    rows = slice(0, count * LANES)
    return triple(high_ref[rows, :], low_ref[rows, :], second[0], second[1])


def transform_back(high_ref, low_ref, e_high, e_low, second, last, twiddle, count):
    rows = slice(0, count * LANES)
    part_d = triple_rows(high_ref[rows, :], low_ref[rows, :], second[0], second[1])
    cosine, sine = twiddle[0], twiddle[1]
    for s in range(count):
        real, imag = part_d[block(s), RE], part_d[block(s), IM]
        put_halves(e_high, e_low, RE, block(s), real * cosine - imag * sine)
        put_halves(e_high, e_low, IM, block(s), real * sine + imag * cosine)
    return triple(last[0], last[1], e_high[:, rows], e_low[:, rows])


def erf_parts(value):
    cdf = 0.5 * (1.0 + lax.erf(value * math.sqrt(0.5)))
    return cdf, jnp.exp(-0.5 * value * value) * (1.0 / math.sqrt(2.0 * math.pi))


def total(value):
    return jnp.sum(jnp.sum(value, axis=0, keepdims=True), axis=1, keepdims=True)


def times_of(row, lane):
    return (256 * (row & 31) + 128 * lax.shift_right_logical(row, 5 * jnp.ones_like(row)) + lane).astype(F32)


def valid_of(len_ref):
    row = lax.broadcasted_iota(jnp.int32, (LANES, LANES), 0) & 63
    times = times_of(row, lax.broadcasted_iota(jnp.int32, (LANES, LANES), 1))
    columns = []
    for y in range(4):
        upper = times[0:64, :] < len_ref[2 * y : 2 * y + 1, :]
        lower = times[64:128, :] < len_ref[2 * y + 1 : 2 * y + 2, :]
        columns.append(jnp.concatenate([upper, lower], axis=0).astype(F32))
    return jnp.concatenate(columns, axis=1)


def tally_of(len_ref):
    return jnp.sum(len_ref[:, 0:1], axis=0, keepdims=True)


def load_signals(message, step, x_ref):
    for part in range(OWN):
        for y in range(4):
            lanes = block(part * 4 + y)
            for b in range(2):
                for r in range(2):
                    start = y * step + signal_row(b, part, r)
                    piece = message[pl.ds(start, 32, stride=4 * step), :].astype(BF16)
                    x_ref[b * 128 + r * 32 : b * 128 + r * 32 + 32, lanes] = piece
                    x_ref[b * 128 + r * 32 + 64 : b * 128 + r * 32 + 96, lanes] = piece


def store_signals(out, step, base, get):
    for part in range(OWN):
        for y in range(4):
            value = get(part, y)
            for b in range(2):
                for r in range(2):
                    start = y * step + base + signal_row(b, part, r)
                    out[pl.ds(start, 32, stride=4 * step), :] = value[b * 64 + r * 32 : b * 64 + r * 32 + 32, :]


SPEC_IM = OWN * LANES
OWN_ROWS = slice(2 * SPEC_IM, 2 * SPEC_IM + 8)
COLUMN_ROWS = slice(2 * SPEC_IM + 8, 2 * SPEC_IM + 8 + HIDDEN)
BUNDLE = 2 * SPEC_IM + 8 + HIDDEN


def kernel_parts(bundle, part):
    return bundle[block(part), :], bundle[SPEC_IM + part * LANES : SPEC_IM + (part + 1) * LANES, :]


def convolve(x_ref, spec_ref, kernel_spec, high, low, e_high, e_low, consts, y_ref):
    first, second, last, twiddle = consts
    spec_ref[...] = transform(x_ref, high, low, first, second, twiddle, SIGNALS)
    for part in range(OWN):
        k_re, k_im = kernel_parts(kernel_spec, part)
        for y in range(4):
            rows = block(part * 4 + y)
            s_re, s_im = spec_ref[rows, RE], spec_ref[rows, IM]
            put_halves(high, low, rows, RE, s_re * k_re - s_im * k_im)
            put_halves(high, low, rows, IM, s_re * k_im + s_im * k_re)
    y_ref[...] = transform_back(high, low, e_high, e_low, second, last, twiddle, SIGNALS)


def normalise(y_ref, own, valid, tally, part):
    value = y_ref[:, block(part, 512)]
    mean = total(valid * value) / tally
    centred = value - mean
    var = total(valid * centred * centred) / tally
    inv_std = lax.rsqrt(var + EPSILON)
    normed = centred * inv_std
    pre_act = normed * own[part : part + 1, 35:36] + own[part : part + 1, 36:37]
    cdf, density = erf_parts(pre_act)
    return normed, inv_std, pre_act * cdf, cdf + pre_act * density


def normalise_all(y_ref, own, len_ref, normed_ref, slope_ref, inv_ref):
    valid, tally = valid_of(len_ref), tally_of(len_ref)
    inv_ref[...] = jnp.zeros((8, LANES), F32)
    for part in range(OWN):
        normed, inv_std, active, slope = normalise(y_ref, own, valid, tally, part)
        normed_ref[:, block(part, 512)] = normed
        slope_ref[:, block(part, 512)] = slope
        inv_ref[part : part + 1, :] = jnp.broadcast_to(inv_std, (1, LANES))
        y_ref[:, block(part, 512)] = active


def conv_backward(
    message, step, base, normed_of, slope_of, inv_of, own, valid, tally, spec_ref, kernel_spec, x_ref, high, low,
    e_high, e_low, consts, grad_ref,
):
    first, second, last, twiddle = consts
    sums = []
    for part in range(OWN):
        columns = []
        for y in range(4):
            pieces = []
            for b in range(2):
                for r in range(2):
                    start = y * step + base + signal_row(b, part, r)
                    pieces.append(message[pl.ds(start, 32, stride=4 * step), :])
            columns.append(jnp.concatenate(pieces, axis=0))
        act_grad = jnp.concatenate(columns, axis=1)
        normed = normed_of(part)
        pre_grad = act_grad * slope_of(part)
        bias_total = total(pre_grad)
        gain_total = total(pre_grad * normed)
        gain = own[part : part + 1, 35:36]
        conv_grad = inv_of(part) * (
            gain * pre_grad - valid * (gain * bias_total + normed * (gain * gain_total)) / tally
        )
        conv_low = conv_grad.astype(BF16)
        for b in range(2):
            piece = conv_low[b * 64 : b * 64 + 64, :]
            x_ref[b * 128 : b * 128 + 64, block(part, 512)] = piece
            x_ref[b * 128 + 64 : b * 128 + 128, block(part, 512)] = piece
        sums.append((gain_total, bias_total))
    grad_ref[...] = transform(x_ref, high, low, first, second, twiddle, SIGNALS)
    for part in range(OWN):
        k_re, k_im = kernel_parts(kernel_spec, part)
        corr_re, corr_im = None, None
        for y in range(4):
            rows = block(part * 4 + y)
            g_re, g_im = grad_ref[rows, RE], grad_ref[rows, IM]
            s_re, s_im = spec_ref[rows, RE], spec_ref[rows, IM]
            put_halves(high, low, rows, RE, k_re * g_re + k_im * g_im)
            put_halves(high, low, rows, IM, k_re * g_im - k_im * g_re)
            now_re, now_im = s_re * g_re + s_im * g_im, s_re * g_im - s_im * g_re
            corr_re = now_re if corr_re is None else corr_re + now_re
            corr_im = now_im if corr_im is None else corr_im + now_im
        put_halves(high, low, block(SIGNALS + part), RE, corr_re)
        put_halves(high, low, block(SIGNALS + part), IM, corr_im)
    returned = transform_back(high, low, e_high, e_low, second, last, twiddle, SIGNALS + OWN)
    return returned, sums


def sin_cos(angle):
    turns = jnp.floor(angle * (2.0 / math.pi) + 0.5)
    rest = angle - turns * 1.5703125
    rest = rest - turns * 4.837512969970703125e-4
    rest = rest - turns * 7.549789948768648e-8
    square = rest * rest
    sine = rest + rest * square * (
        -1.6666654611e-1 + square * (8.3321608736e-3 + square * -1.9515295891e-4)
    )
    cosine = 1.0 - 0.5 * square + square * square * (
        4.166664568298827e-2 + square * (-1.388731625493765e-3 + square * 2.443315711809948e-5)
    )
    half = jnp.floor(turns * 0.5)
    odd = turns - 2.0 * half
    sign = 1.0 - 2.0 * (half - 2.0 * jnp.floor(half * 0.5))
    is_odd = odd > 0.5
    return sign * jnp.where(is_odd, cosine, sine), sign * jnp.where(is_odd, -sine, cosine)


CHUNK = 1024
F_TABLE = (0, 4, 7)
C_TABLE = (1, 3, 6)


def envelope_of(times, own):
    lower, upper = own[:, 33:34], own[:, 34:35]
    inside = (times >= lower) & (times < upper)
    offset = (times - lower) / (0.5 * (upper - lower))
    return jnp.where(inside, jnp.exp(-0.5 * offset * offset), 0.0)


def stacked_weight(weight):
    high, low = high_low(weight)
    return jnp.concatenate([high, high, low], axis=1).astype(BF16)


def stacked_dot(weight, value):
    high = value.astype(BF16)
    low = (value - high.astype(F32)).astype(BF16)
    return dot(weight, jnp.concatenate([high, low, high], axis=0))


def own_parameters(layer, number, out_w, out_b, window, gain, bias, gabor, hidden_b, wide, tall, own, columns):
    wide[...] = jnp.zeros(wide.shape, F32)
    wide[0:32, 0:CHANNELS] = out_w[layer]
    wide[32:33, 0:CHANNELS] = out_b[layer : layer + 1, :]
    wide[33:35, 0:CHANNELS] = window[layer].astype(F32)
    wide[35:36, 0:CHANNELS] = gain[layer : layer + 1, :]
    wide[36:37, 0:CHANNELS] = bias[layer : layer + 1, :]
    tall[0:PADDED, :] = jnp.transpose(wide[...])
    tall[PADDED : PADDED + 8, :] = jnp.zeros((8, LANES), F32)
    row = lax.broadcasted_iota(jnp.int32, (8, LANES), 0)
    lane = lax.broadcasted_iota(jnp.int32, (8, LANES), 1)
    mine = tall[pl.ds(number * OWN, 8), :]
    unused = (row >= OWN) | (number * OWN + row >= CHANNELS)
    own[...] = jnp.where(unused, jnp.where(lane == 34, float(SAMPLES), 0.0), mine)
    wide[:, 0:LANES] = jnp.zeros((LANES, LANES), F32)
    for j in range(3):
        wide[4 * j : 4 * j + 4, 0:HIDDEN] = gabor[layer, j]
    wide[12:14, 0:HIDDEN] = hidden_b[layer]
    columns[...] = jnp.transpose(wide[:, 0:LANES])[0:HIDDEN, :]


def sample_rows(first_lane, count):
    lane = first_lane + lax.broadcasted_iota(jnp.int32, (1, count), 1)
    times = times_of(lax.shift_right_logical(lane, 7 * jnp.ones_like(lane)), lane & 127)
    return times, times * (2.0 / (SAMPLES - 1)) - 1.0


def generate(columns, hidden_w, own, tab, rows):
    turns = []
    for j in range(3):
        turn = sin_cos(columns[:, 4 * j + 2 : 4 * j + 3] * (512.0 / (SAMPLES - 1)))
        turns.append([jnp.broadcast_to(value, (HIDDEN, LANES)) for value in turn])

    def step(i, carry):
        _, places = sample_rows(i * CHUNK, CHUNK)
        for j in range(3):
            sharpness, centre = columns[:, 4 * j : 4 * j + 1], columns[:, 4 * j + 1 : 4 * j + 2]
            frequency, phase = columns[:, 4 * j + 2 : 4 * j + 3], columns[:, 4 * j + 3 : 4 * j + 4]
            sine, cosine = sin_cos(frequency * places[:, 0:LANES] + phase)
            turn_sin, turn_cos = turns[j]
            for n in range(CHUNK // LANES):
                width = sharpness * (places[:, block(n)] - centre)
                bell = jnp.exp(-0.5 * width * width)
                here = pl.ds(pl.multiple_of(i * CHUNK + n * LANES, LANES), LANES)
                tab[F_TABLE[j], :, here] = bell * sine
                tab[C_TABLE[j], :, here] = bell * cosine
                sine, cosine = sine * turn_cos + cosine * turn_sin, cosine * turn_cos - sine * turn_sin
        return carry

    lax.fori_loop(0, SAMPLES // CHUNK, step, 0)
    weights = [stacked_weight(hidden_w[0]), stacked_weight(hidden_w[1]), stacked_weight(own[:, 0:32])]
    u_1 = stacked_dot(weights[0], tab[0]) + columns[:, 12:13]
    z_1 = u_1 * tab[4]
    tab[2] = z_1
    tab[3] = u_1 * tab[3]
    u_2 = stacked_dot(weights[1], z_1) + columns[:, 13:14]
    z_2 = u_2 * tab[7]
    tab[5] = z_2
    tab[6] = u_2 * tab[6]
    raw = stacked_dot(weights[2], z_2) + own[:, 32:33]
    times, _ = sample_rows(0, SAMPLES)
    rows[...] = raw * envelope_of(times, own)


def generate_back(kernel_grad, columns, hidden_w, own, tab, rows, sums, mats):
    rows[...] = jnp.zeros(rows.shape, F32)
    for part in range(OWN):
        grad = kernel_grad(part)
        for n in range(64):
            rows[part : part + 1, block(n)] = grad[n : n + 1, :]
    sums[...] = jnp.zeros(sums.shape, F32)
    mats[...] = jnp.zeros(mats.shape, F32)
    turned = jnp.transpose(jnp.concatenate([own[...], jnp.zeros((120, 128), F32)], axis=0))
    weight = [turned[0:32, part : part + 1] for part in range(OWN)]
    back = [stacked_weight(jnp.transpose(hidden_w[j])) for j in range(2)]

    def fold(value):
        acc = value[:, block(0)]
        for i in range(1, CHUNK // LANES):
            acc = acc + value[:, block(i)]
        return acc

    def add(k, value):
        sums[block(k, 32), :] += fold(value)

    def step(i, carry):
        span = pl.ds(pl.multiple_of(i * CHUNK, CHUNK), CHUNK)
        times, places = sample_rows(i * CHUNK, CHUNK)
        draw = rows[:, span] * envelope_of(times, own)
        dz_2 = weight[0] * draw[0:1, :] + weight[1] * draw[1:2, :] + weight[2] * draw[2:3, :]

        def level(j, e_value, g_value):
            centre = columns[:, 4 * j + 1 : 4 * j + 2]
            offset = places - centre
            moment = e_value * offset
            add(4 * j, moment * offset)
            add(4 * j + 1, moment)
            add(4 * j + 2, g_value * places)
            add(4 * j + 3, g_value)

        z_2 = tab[5, :, span]
        level(2, dz_2 * z_2, dz_2 * tab[6, :, span])
        du_2 = dz_2 * tab[7, :, span]
        add(13, du_2)
        dz_1 = stacked_dot(back[1], du_2)
        z_1 = tab[2, :, span]
        level(1, dz_1 * z_1, dz_1 * tab[3, :, span])
        du_1 = dz_1 * tab[4, :, span]
        add(12, du_1)
        dz_0 = stacked_dot(back[0], du_1)
        z_0 = tab[0, :, span]
        level(0, dz_0 * z_0, dz_0 * tab[1, :, span])
        sums[14 * 32 : 14 * 32 + 8, :] += fold(draw)
        left = jnp.concatenate([du_1, du_2, draw], axis=0)
        right = jnp.concatenate([z_0, z_1, z_2, jnp.zeros_like(z_0)], axis=0)
        left_high, right_high = left.astype(BF16), right.astype(BF16)
        left_low = (left - left_high.astype(F32)).astype(BF16)
        right_low = (right - right_high.astype(F32)).astype(BF16)
        mats[...] += (
            dot_rows(left_high, right_high) + dot_rows(left_low, right_high) + dot_rows(left_high, right_low)
        )
        return carry

    lax.fori_loop(0, SAMPLES // CHUNK, step, 0, unroll=SAMPLES // CHUNK)
    lane = lax.broadcasted_iota(jnp.int32, (32, LANES), 1)
    hidden = jnp.where(lane < 32, mats[0:32, :], jnp.where(lane < 64, mats[32:64, :], 0.0))

    def column(k):
        return jnp.sum(sums[block(k, 32), :], axis=1, keepdims=True)

    hidden = jnp.where(lane == 64, column(12), hidden)
    hidden = jnp.where(lane == 65, column(13), hidden)
    for j in range(3):
        sharpness = columns[:, 4 * j : 4 * j + 1]
        hidden = jnp.where(lane == 66 + 4 * j, -sharpness * column(4 * j), hidden)
        hidden = jnp.where(lane == 67 + 4 * j, sharpness * sharpness * column(4 * j + 1), hidden)
        hidden = jnp.where(lane == 68 + 4 * j, column(4 * j + 2), hidden)
        hidden = jnp.where(lane == 69 + 4 * j, column(4 * j + 3), hidden)
    lane8 = lax.broadcasted_iota(jnp.int32, (8, LANES), 1)
    outer = pltpu.roll(mats[64:72, :], LANES - 64, 1)
    raw_total = jnp.sum(sums[14 * 32 : 14 * 32 + 8, :], axis=1, keepdims=True)
    outer = jnp.where(lane8 < 32, outer, 0.0)
    outer = jnp.where(lane8 == 32, raw_total, outer)
    return hidden, outer


def with_norm_sums(outer, sums):
    row = lax.broadcasted_iota(jnp.int32, (8, LANES), 0)
    lane = lax.broadcasted_iota(jnp.int32, (8, LANES), 1)
    for part in range(OWN):
        gain_total, bias_total = sums[part]
        outer = jnp.where((row == part) & (lane == 33), gain_total, outer)
        outer = jnp.where((row == part) & (lane == 34), bias_total, outer)
    return outer


def one_row(outer):
    lane = lax.broadcasted_iota(jnp.int32, (1, LANES), 1)
    result = jnp.zeros((1, LANES), F32)
    for part in range(OWN):
        row = outer[part : part + 1, :]
        moved = pltpu.roll(row, 32 * part, 1) if part else row
        result = jnp.where((lane >= 32 * part) & (lane < 32 * part + 32), moved, result)
        moved = pltpu.roll(row, 64 + 3 * part, 1)
        result = jnp.where((lane >= 96 + 3 * part) & (lane < 99 + 3 * part), moved, result)
    return result


def packed_hidden(hidden):
    lane16 = lax.broadcasted_iota(jnp.int32, (16, LANES), 1)
    upper = jnp.where(lane16 < 64, hidden[0:16, :], pltpu.roll(hidden[16:32, :], 64, 1))
    lane4 = lax.broadcasted_iota(jnp.int32, (4, LANES), 1)
    lower = jnp.zeros((4, LANES), F32)
    for g in range(8):
        moved = pltpu.roll(hidden, (64 + 16 * g) % LANES, 1)[4 * g : 4 * g + 4, :]
        lower = jnp.where((lane4 >= 16 * g) & (lane4 < 16 * g + 16), moved, lower)
    return upper, lower


def unpacked_hidden(upper, lower):
    lane16 = lax.broadcasted_iota(jnp.int32, (16, LANES), 1)
    lane32 = lax.broadcasted_iota(jnp.int32, (32, LANES), 1)
    top = jnp.concatenate([upper, pltpu.roll(upper, 64, 1)], axis=0)
    tiled = jnp.concatenate([lower] * 8, axis=0)
    row32 = lax.broadcasted_iota(jnp.int32, (32, LANES), 0)
    rest = jnp.zeros((32, LANES), F32)
    for g in range(8):
        moved = pltpu.roll(tiled, (64 - 16 * g) % LANES, 1)
        rest = jnp.where((row32 >= 4 * g) & (row32 < 4 * g + 4), moved, rest)
    return jnp.where(lane32 < 64, top, rest)


def high_low(value):
    high = value.astype(BF16).astype(F32)
    return high, value - high


def valid_row(meta, i):
    lane = lax.broadcasted_iota(jnp.int32, (1, LANES), 1)
    return (meta[2] * PIECE + (i // 2) * LANES + lane < meta[i % 2]).astype(F32)


def masked(meta, rows):
    mask = jnp.concatenate([valid_row(meta, i) for i in range(4)] * 2, axis=0)
    return (rows.reshape(-1, 8, LANES) * mask[None]).reshape(-1, LANES)


CLIP_ROWS = 4 * CHANNELS
PADDED_ROWS = 4 * PADDED


def put_padded(padded, rows):
    padded[0:CLIP_ROWS, :] = rows
    padded[CLIP_ROWS:PADDED_ROWS, :] = jnp.zeros((PADDED_ROWS - CLIP_ROWS, LANES), F32)


def rows_to_message(padded, out, step, base):
    for m in range(12):
        out[pl.ds(base + m, DEVICES, stride=step), :] = padded[pl.ds(m, DEVICES, stride=12), :]


def rows_of_channels(padded, i):
    return padded[pl.ds(i, PADDED, stride=4), :]


def source_kernel(meta, x_ref, out_ref, padded, out):
    put_padded(padded, masked(meta, x_ref[...]))
    for b in range(2):
        length = meta[b]
        upper = lax.shift_right_logical(length, 7)
        out[pl.ds(12 + 2 * b, DEVICES, stride=16), :] = jnp.full((DEVICES, LANES), upper.astype(F32))
        out[pl.ds(13 + 2 * b, DEVICES, stride=16), :] = jnp.full(
            (DEVICES, LANES), (length - upper * 128).astype(F32)
        )
    rows_to_message(padded, out, 16, 0)
    out_ref[...] = out[...].reshape(DEVICES, 16, LANES).astype(BF16)


def make_lookup(lookup):
    row = lax.broadcasted_iota(jnp.int32, (DEVICES, PADDED), 0)
    column = lax.broadcasted_iota(jnp.int32, (DEVICES, PADDED), 1)
    for part in range(OWN):
        lookup[block(part), :] = (column == OWN * row + part).astype(F32).astype(BF16)


def make_weights(mix_w, mix_b, wide, lookup, weights, weights_back):
    make_lookup(lookup)
    wide[...] = jnp.zeros(wide.shape, BF16)
    row = lax.broadcasted_iota(jnp.int32, (LANES, CHANNELS), 0)
    lines = jnp.where(row == 0, mix_b[0:1, :], jnp.where(row == 1, mix_b[1:2, :], 0.0))
    turned = jnp.transpose(jnp.concatenate([lines, jnp.zeros((LANES, PADDED - CHANNELS), F32)], axis=1))
    lane = lax.broadcasted_iota(jnp.int32, (PADDED, PADDED), 1)
    for layer in range(2):
        wide[0:CHANNELS, 0:CHANNELS] = mix_w[:, layer, :]
        weights_back[layer] = dot_rows(lookup[...], wide[...]).astype(BF16)
        value = dot_rows(wide[...], lookup[...])
        rest = turned[:, layer : layer + 1]
        for spot in SPOTS:
            high, rest = high_low(rest)
            value = jnp.where(lane == spot, high, value)
        weights[layer] = value.astype(BF16)


def make_kernel(layer, meta, params, consts, bundle, tab, scratch):
    out_w, out_b, window, gain, bias, gabor, hidden_b, hidden_w = params
    first, second, _, twiddle = consts
    wide, tall, rows, pieces, x_ref, high, low = scratch
    own, columns = bundle.at[OWN_ROWS, :], bundle.at[COLUMN_ROWS, :]
    own_parameters(layer, meta[3], out_w, out_b, window, gain, bias, gabor, hidden_b, wide, tall, own, columns)
    generate(columns, hidden_w.at[layer], own, tab, rows)
    for n in range(64):
        for part in range(OWN):
            pieces[part * 64 + n : part * 64 + n + 1, :] = rows[part : part + 1, block(n)]
    for part in range(OWN):
        piece = pieces[block(part, 64), :].astype(BF16)
        x_ref[0:64, block(part)] = piece
        x_ref[64:128, block(part)] = piece
        x_ref[128:256, block(part)] = jnp.zeros((128, LANES), BF16)
    spec = transform(x_ref, high, low, first, second, twiddle, OWN)
    bundle[0:SPEC_IM, :] = spec[:, RE]
    bundle[SPEC_IM : 2 * SPEC_IM, :] = spec[:, IM]


def forward_kernel(
    meta, message_ref, out_w, out_b, window, gain, bias, gabor, hidden_b, hidden_w,
    first, second, last, twiddle,
    out_ref, spec_ref, normed_ref, slope_ref, inv_ref, len_ref, kernel_spec, tab,
    message, x_ref, high, low, e_high, e_low, y_ref, out, *make_scratch,
):
    own = kernel_spec.at[OWN_ROWS, :]
    params = (out_w, out_b, window, gain, bias, gabor, hidden_b, hidden_w)
    make_kernel(0, meta, params, (first, second, last, twiddle), kernel_spec, tab, make_scratch)
    message[...] = spread(message_ref[...])
    for y in range(4):
        for b in range(2):
            start = y * 16 + 12 + 2 * b
            len_ref[2 * y + b : 2 * y + b + 1, :] = (
                message[start : start + 1, :] * 128.0 + message[start + 1 : start + 2, :]
            )
    load_signals(message, 16, x_ref)
    convolve(x_ref, spec_ref, kernel_spec, high, low, e_high, e_low, (first, second, last, twiddle), y_ref)
    normalise_all(y_ref, own, len_ref, normed_ref, slope_ref, inv_ref)
    store_signals(out, 16, 0, lambda part, y: y_ref[:, block(part * 4 + y)])
    out_ref[...] = out[...].reshape(DEVICES, 16, LANES).astype(BF16)


def gather_active(message, step, rhs):
    row = lax.broadcasted_iota(jnp.int32, (DEVICES, LANES), 0)
    for i in range(4):
        for part in range(OWN):
            piece = message[pl.ds(part * 4 + i, DEVICES, stride=step), :]
            if part != 1:
                piece = jnp.where(row >= (126 if part == 2 else 127), 1.0, piece)
            rhs[block(part), block(i)] = piece.astype(BF16)


def store_rows(value, out, step, base):
    for i in range(4):
        for part in range(OWN):
            out[pl.ds(base + part * 4 + i, DEVICES, stride=step), :] = value[block(part), block(i)]


def mix_kernel(
    meta, message_ref, x_ref, cotangent, mix_w, mix_b,
    out_ref, next_ref, active_ref, weights, weights_back, message, padded, out, low, wide, lookup,
):
    make_weights(mix_w, mix_b, wide, lookup, weights, weights_back)
    message[...] = spread(message_ref[...])
    gather_active(message, 16, active_ref)
    mixed = dot(weights[0], active_ref[...])
    put_padded(padded, x_ref[...])
    for i in range(4):
        valid = valid_row(meta, i)
        value = rows_of_channels(padded, i) + mixed[:, block(i)] * valid
        next_ref[pl.ds(i, PADDED, stride=4), :] = value
        padded[pl.ds(i, PADDED, stride=4), :] = value * valid
    rows_to_message(padded, out, 24, 0)
    put_padded(padded, masked(meta, cotangent[...]))
    for i in range(4):
        low[:, block(i)] = rows_of_channels(padded, i).astype(BF16)
    store_rows(dot(weights_back[1], low[...]), out, 24, 12)
    out_ref[...] = out[...].reshape(DEVICES, 24, LANES).astype(BF16)


def forward_1_kernel(
    meta, message_ref, out_w, out_b, window, gain, bias, gabor, hidden_b, hidden_w,
    len_ref, first, second, last, twiddle,
    y_ref, spec_ref, normed_ref, slope_ref, inv_ref, kernel_spec, tab,
    message, x_ref, high, low, e_high, e_low, *make_scratch,
):
    own = kernel_spec.at[OWN_ROWS, :]
    consts = (first, second, last, twiddle)
    params = (out_w, out_b, window, gain, bias, gabor, hidden_b, hidden_w)
    make_kernel(1, meta, params, consts, kernel_spec, tab, make_scratch)
    message[...] = spread(message_ref[...])
    load_signals(message, 24, x_ref)
    convolve(x_ref, spec_ref, kernel_spec, high, low, e_high, e_low, consts, y_ref)
    normalise_all(y_ref, own, len_ref, normed_ref, slope_ref, inv_ref)


def backward_1_kernel(
    message_ref, active_ref, spec_ref, kernel_spec, normed_ref, slope_ref, inv_ref, len_ref,
    first, second, last, twiddle, hidden_w, tab,
    out_ref, hidden_out, outer_out,
    message, x_ref, high, low, e_high, e_low, out, grad_ref, returned_ref, rows, sums, mats,
):
    own, columns = kernel_spec.at[OWN_ROWS, :], kernel_spec.at[COLUMN_ROWS, :]
    message[...] = spread(message_ref[...])
    valid, tally = valid_of(len_ref), tally_of(len_ref)
    returned, norm_sums = conv_backward(
        message, 24, 12, lambda part: normed_ref[:, block(part, 512)], lambda part: slope_ref[:, block(part, 512)],
        lambda part: inv_ref[part : part + 1, 0:1], own, valid, tally, spec_ref, kernel_spec, x_ref, high, low,
        e_high, e_low, (first, second, last, twiddle), grad_ref,
    )
    returned_ref[...] = returned
    store_signals(out, 24, 0, lambda part, y: active_ref[:, block(part * 4 + y)])
    store_signals(out, 24, 12, lambda part, y: returned_ref[:, block(part * 4 + y)])
    out_ref[...] = out[...].reshape(DEVICES, 24, LANES).astype(BF16)
    hidden, outer = generate_back(
        lambda part: returned_ref[0:64, block(SIGNALS + part)], columns, hidden_w.at[1], own, tab, rows, sums, mats
    )
    hidden_out[...] = hidden
    outer_out[...] = with_norm_sums(outer, norm_sums)


def middle_kernel(
    meta, message_ref, x_ref, cotangent, weights, weights_back, active_0, hidden_1,
    output_ref, flow_ref, out_ref, message, padded, out, low_0, low_1, active_1,
):
    message[...] = spread(message_ref[...])
    gather_active(message, 24, active_1)
    mixed = dot(weights[1], active_1[...])
    for i in range(4):
        padded[pl.ds(i, PADDED, stride=4), :] = rows_of_channels(x_ref, i) + mixed[:, block(i)] * valid_row(meta, i)
    output_ref[...] = padded[0:CLIP_ROWS, :]
    put_padded(flow_ref, cotangent[...])
    for i in range(4):
        low_1[:, block(i)] = (rows_of_channels(flow_ref, i) * valid_row(meta, i)).astype(BF16)
    for m in range(12):
        padded[pl.ds(m, DEVICES, stride=12), :] = message[pl.ds(12 + m, DEVICES, stride=24), :]
    flow_ref[...] += masked(meta, padded[...])
    for i in range(4):
        low_0[:, block(i)] = (rows_of_channels(flow_ref, i) * valid_row(meta, i)).astype(BF16)
    store_rows(dot(weights_back[0], low_0[...]), out, 32, 0)
    for layer, (active, low) in enumerate(((active_0, low_0), (active_1, low_1))):
        part_sum = dot_rows(active[...], low[...])
        for part in range(OWN):
            for third in range(3):
                out[pl.ds(12 + layer * 9 + part * 3 + third, DEVICES, stride=32), :] = part_sum[
                    block(part), block(third)
                ]
    high, low = high_low(hidden_1[...])
    out[pl.ds(30, DEVICES, stride=32), :] = jnp.concatenate([high, jnp.zeros((96, LANES), F32)], axis=0)
    out[pl.ds(31, DEVICES, stride=32), :] = jnp.concatenate([low, jnp.zeros((96, LANES), F32)], axis=0)
    out_ref[...] = out[...].reshape(DEVICES, 32, LANES).astype(BF16)


LAST_ROWS = 56


def backward_kernel(
    message_ref, spec_ref, kernel_spec, normed_ref, slope_ref, inv_ref, len_ref,
    first, second, last, twiddle, hidden_w, tab, outer_1,
    out_ref,
    message, x_ref, high, low, e_high, e_low, out, grad_ref, returned_ref, rows, sums, mats,
):
    own, columns = kernel_spec.at[OWN_ROWS, :], kernel_spec.at[COLUMN_ROWS, :]
    consts = (first, second, last, twiddle)
    message[...] = spread(message_ref[...])
    valid, tally = valid_of(len_ref), tally_of(len_ref)
    returned, norm_sums = conv_backward(
        message, 32, 0, lambda part: normed_ref[:, block(part, 512)], lambda part: slope_ref[:, block(part, 512)],
        lambda part: inv_ref[part : part + 1, 0:1], own, valid, tally, spec_ref, kernel_spec, x_ref, high, low,
        e_high, e_low, consts, grad_ref,
    )
    returned_ref[...] = returned
    store_signals(out, 16, 0, lambda part, y: returned_ref[:, block(part * 4 + y)])
    hidden, outer = generate_back(
        lambda part: returned_ref[0:64, block(SIGNALS + part)], columns, hidden_w.at[0], own, tab,
        rows, sums, mats,
    )
    outer = with_norm_sums(outer, norm_sums)
    gathered = jnp.sum(message[...].reshape(DEVICES, 32, LANES), axis=0)
    upper, lower = packed_hidden(hidden)
    hidden_1_high, hidden_1_low = high_low(gathered[30:31, :] + gathered[31:32, :])
    outer_0_high, outer_0_low = high_low(one_row(outer))
    outer_1_high, outer_1_low = high_low(one_row(outer_1[...]))
    shared = jnp.concatenate(
        [
            gathered[0:30, :], upper, lower, hidden_1_high, hidden_1_low,
            outer_0_high, outer_0_low, outer_1_high, outer_1_low,
        ],
        axis=0,
    )
    row = lax.broadcasted_iota(jnp.int32, (DEVICES, 16, LANES), 1)
    own_rows = jnp.where(row < 12, out[...].reshape(DEVICES, 16, LANES), shared[None, 0:16, :])
    rest = jnp.broadcast_to(shared[None, 16:LAST_ROWS, :], (DEVICES, LAST_ROWS - 16, LANES))
    out_ref[...] = jnp.concatenate([own_rows, rest], axis=1).astype(BF16)


def last_kernel(
    meta, message_ref, flow_ref,
    input_grad, gabor_grad, hidden_w_grad, hidden_b_grad, out_w_grad, out_b_grad, gain_grad, bias_grad,
    mix_w_grad, mix_b_grad, message, padded, owned, thirds, lookup,
):
    make_lookup(lookup)
    message[...] = spread(message_ref[...])

    def rows_of(k, count=DEVICES):
        return message[pl.ds(k, count, stride=LAST_ROWS), :]

    for m in range(12):
        padded[pl.ds(m, DEVICES, stride=12), :] = rows_of(m)
    input_grad[...] = flow_ref[0:CLIP_ROWS, :] + masked(meta, padded[0:CLIP_ROWS, :])
    shared = jnp.sum(message[...].reshape(DEVICES, LAST_ROWS, LANES)[:, 24:56, :], axis=0)
    hidden_0 = unpacked_hidden(shared[6:22, :], shared[22:26, :])
    hidden_1 = rows_of(50, 32) + rows_of(51, 32)
    lane = lax.broadcasted_iota(jnp.int32, (DEVICES, LANES), 1)
    for layer, hidden in enumerate((hidden_0, hidden_1)):
        hidden_w_grad[layer, 0] = hidden[:, 0:32]
        hidden_w_grad[layer, 1] = pltpu.roll(hidden, 96, 1)[:, 0:32]
        turned = jnp.transpose(jnp.concatenate([hidden, jnp.zeros((96, LANES), F32)], axis=0))
        hidden_b_grad[layer] = turned[64:66, 0:32]
        for j in range(3):
            gabor_grad[layer, j] = turned[66 + 4 * j : 70 + 4 * j, 0:32]
        value = rows_of(52 + 2 * layer) + rows_of(53 + 2 * layer)
        for part in range(OWN):
            wide = pltpu.roll(value, (LANES - 32 * part) % LANES, 1)
            small = pltpu.roll(value, 64 - 3 * part, 1)
            owned[pl.ds(part, DEVICES, stride=OWN), :] = jnp.where(lane < 32, wide, small)
        turned = jnp.transpose(owned[...])
        out_w_grad[layer] = turned[0:32, 0:CHANNELS]
        out_b_grad[layer : layer + 1, :] = turned[32:33, 0:CHANNELS]
        gain_grad[layer : layer + 1, :] = turned[33:34, 0:CHANNELS]
        bias_grad[layer : layer + 1, :] = turned[34:35, 0:CHANNELS]
        bias_rows = []
        for part in range(OWN):
            for third in range(3):
                piece = rows_of(12 + layer * 9 + part * 3 + third)
                thirds[block(part), block(third)] = piece.astype(BF16)
                if part == 2:
                    bias_rows.append(piece[SPOT - 2 * DEVICES : SPOT - 2 * DEVICES + 1, :])
        mix_w_grad[:, layer, :] = dot_columns(thirds[...], lookup[...])[0:CHANNELS, 0:CHANNELS]
        mix_b_grad[layer : layer + 1, :] = jnp.concatenate(bias_rows, axis=1)[:, 0:CHANNELS]


def exchange(message):
    return lax.all_to_all(message, AXES, split_axis=0, concat_axis=0, tiled=True)


def to_rows(clips):
    return clips.reshape(2, CHANNELS, 2, LANES).transpose(1, 2, 0, 3).reshape(CLIP_ROWS, LANES)


def from_rows(rows):
    return rows.reshape(CHANNELS, 2, 2, LANES).transpose(2, 0, 1, 3).reshape(2, CHANNELS, PIECE)


def shards(
    inputs, lengths, window, gabor_params, hidden_w, hidden_b, out_w, out_b, bn_gain, bn_bias, mix_w, mix_b, cotangent
):
    position = lax.axis_index("seq").astype(jnp.int32)
    number = position * 4 + lax.axis_index("clips").astype(jnp.int32)
    const = {name: jnp.asarray(value) for name, value in TABLES.items()}
    meta = jnp.concatenate([lengths, jnp.stack([position, number])])
    inputs, cotangent = to_rows(inputs), to_rows(cotangent)

    def rows(count):
        return ((count, LANES), F32)

    with jax.named_scope("source_0"):
        (message,) = run(
            source_kernel, [((DEVICES, 16, LANES), BF16)], [meta, inputs],
            [rows(PADDED_ROWS), rows(DEVICES * 16)], "source_0", 8, smem=(0,),
        )
        message = exchange(message)

    square = (PADDED, PADDED)
    generator = [
        jnp.swapaxes(out_w, 1, 2), out_b, jnp.swapaxes(window, 1, 2), bn_gain, bn_bias, gabor_params, hidden_b,
        hidden_w,
    ]
    shape_tab = ((8, HIDDEN, SAMPLES), F32)
    make_scratch = [
        ((LANES, PADDED), F32), rows(PADDED + 8), ((8, SAMPLES), F32), rows(192),
        ((256, OWN * LANES), BF16), ((OWN * LANES, 256), BF16), ((OWN * LANES, 256), BF16),
    ]
    mixers = ((2, *square), BF16)

    def scratch(signals):
        count = signals * LANES
        return [
            ((256, SIGNALS * LANES), BF16), ((count, 256), BF16), ((count, 256), BF16),
            ((256, count), BF16), ((256, count), BF16),
        ]

    shape_y = (LANES, SIGNALS * LANES)
    shape_s = (SIGNALS * LANES, 256)
    transforms = [const[name] for name in TABLE_NAMES]
    with jax.named_scope("conv_0"):
        message, spec_0, normed_0, slope_0, inv_0, lens, bundle_0, tab_0 = run(
            forward_kernel,
            [
                ((DEVICES, 16, LANES), BF16), (shape_s, F32), (shape_y, F32), (shape_y, F32), rows(8), rows(8),
                rows(BUNDLE), shape_tab,
            ],
            [meta, message, *generator, *transforms],
            [rows(DEVICES * 16), *scratch(SIGNALS), (shape_y, F32), rows(DEVICES * 16), *make_scratch],
            "conv_0", 16, smem=(0,),
        )
        message = exchange(message)

    with jax.named_scope("mix_0"):
        message, middle, active_0, weights, weights_back = run(
            mix_kernel,
            [((DEVICES, 24, LANES), BF16), rows(PADDED_ROWS), ((PADDED, 512), BF16), mixers, mixers],
            [meta, message, inputs, cotangent, jnp.swapaxes(mix_w, 0, 1), mix_b],
            [rows(DEVICES * 16), rows(PADDED_ROWS), rows(DEVICES * 24), ((PADDED, 512), BF16), (square, BF16), (square, BF16)],
            "mix_0", 12, smem=(0,),
        )
        message = exchange(message)

    back_scratch = [((8, SAMPLES), F32), rows(14 * 32 + 8), rows(72)]
    with jax.named_scope("conv_1"):
        active_1, spec_1, normed_1, slope_1, inv_1, bundle_1, tab_1 = run(
            forward_1_kernel,
            [
                (shape_y, F32), (shape_s, F32), (shape_y, F32), (shape_y, F32), rows(8), rows(BUNDLE), shape_tab,
            ],
            [meta, message, *generator, lens, *transforms],
            [rows(DEVICES * 24), *scratch(SIGNALS), *make_scratch],
            "conv_1", 16, smem=(0,),
        )
        message, hidden_1, outer_1 = run(
            backward_1_kernel,
            [((DEVICES, 24, LANES), BF16), rows(HIDDEN), rows(8)],
            [message, active_1, spec_1, bundle_1, normed_1, slope_1, inv_1, lens, *transforms, hidden_w, tab_1],
            [
                rows(DEVICES * 24), *scratch(SIGNALS + OWN), rows(DEVICES * 24), (shape_s, F32),
                ((LANES, (SIGNALS + OWN) * LANES), F32), *back_scratch,
            ],
            "conv_back_1", 18,
        )
        message = exchange(message)

    with jax.named_scope("mix_1"):
        outputs, flow, message = run(
            middle_kernel,
            [rows(CLIP_ROWS), rows(PADDED_ROWS), ((DEVICES, 32, LANES), BF16)],
            [meta, message, middle, cotangent, weights, weights_back, active_0, hidden_1],
            [
                rows(DEVICES * 24), rows(PADDED_ROWS), rows(DEVICES * 32),
                ((PADDED, 512), BF16), ((PADDED, 512), BF16), ((PADDED, 512), BF16),
            ],
            "mix_1", 12, smem=(0,),
        )
        message = exchange(message)

    with jax.named_scope("conv_back_0"):
        (message,) = run(
            backward_kernel,
            [((DEVICES, LAST_ROWS, LANES), BF16)],
            [
                message, spec_0, bundle_0, normed_0, slope_0, inv_0, lens, *transforms,
                hidden_w, tab_0, outer_1,
            ],
            [
                rows(DEVICES * 32), *scratch(SIGNALS + OWN), rows(DEVICES * 16), (shape_s, F32),
                ((LANES, (SIGNALS + OWN) * LANES), F32), *back_scratch,
            ],
            "conv_back_0", 16,
        )
        message = exchange(message)

    with jax.named_scope("gradients"):
        (
            input_grad, gabor_grad, hidden_w_grad, hidden_b_grad, out_w_grad, out_b_grad, gain_grad, bias_grad,
            mix_w_grad, mix_b_grad,
        ) = run(
            last_kernel,
            [
                rows(CLIP_ROWS), (gabor_params.shape, F32), (hidden_w.shape, F32), (hidden_b.shape, F32),
                ((2, HIDDEN, CHANNELS), F32), (out_b.shape, F32), (bn_gain.shape, F32), (bn_bias.shape, F32),
                ((CHANNELS, 2, CHANNELS), F32), (mix_b.shape, F32),
            ],
            [meta, message, flow],
            [rows(DEVICES * LAST_ROWS), rows(PADDED_ROWS), rows(PADDED), (square, BF16), (square, BF16)],
            "gradients", 14, smem=(0,),
        )
    return (
        from_rows(outputs), from_rows(input_grad), gabor_grad, hidden_w_grad, hidden_b_grad,
        jnp.swapaxes(out_w_grad, 1, 2), out_b_grad, gain_grad, bias_grad, jnp.swapaxes(mix_w_grad, 0, 1), mix_b_grad,
    )


def solution(mesh):
    clip = P("clips", None, "seq")
    in_specs = (clip, P("clips")) + (P(),) * 10 + (clip,)
    out_specs = (clip, clip) + (P(),) * 9
    return jax.shard_map(shards, mesh=mesh, in_specs=in_specs, out_specs=out_specs, check_vma=False)
```

```python
import math

import jax
import jax.numpy as jnp
import ml_dtypes
import numpy as np
from jax import lax
from jax.experimental import pallas as pl
from jax.experimental.pallas import tpu as pltpu
from jax.sharding import PartitionSpec as P

F32 = jnp.float32
BF16 = jnp.bfloat16
AXES = ("seq", "clips")
DEVICES = 128
OWN = 3
CHANNELS = 380
PADDED = DEVICES * OWN
SAMPLES = 8192
PIECE = 256
HIDDEN = 32
LANES = 128
SIGNALS = 12
TABLE_NAMES = ("first", "second", "last", "twiddle")
PERIOD = 2 * SAMPLES
EPSILON = 1e-05
MEGABYTE = 1024 * 1024
EXACT = lax.Precision.HIGHEST
SPOTS = (2 * DEVICES + 126, 2 * DEVICES + 127, 127)
SPOT = SPOTS[0]


def halves(table):
    high = table.astype(ml_dtypes.bfloat16)
    low = (table - high.astype(np.float64)).astype(ml_dtypes.bfloat16)
    return high, low


def tables():
    order = np.array([2 * j + r for r in range(2) for j in range(32)])
    k = np.arange(LANES)
    turn = 2 * np.pi * ((k[:, None] * order[None, :]) % LANES) / LANES
    c_high, c_low = halves(np.cos(turn))
    s_high, s_low = halves(np.sin(turn))
    first = np.concatenate(
        [
            np.concatenate([c_high, c_low, s_high, s_low], axis=1),
            np.concatenate([-s_high, -s_low, c_high, c_low], axis=1),
        ],
        axis=0,
    )
    turn = 2 * np.pi * ((k[:, None] * k[None, :]) % LANES) / LANES
    cosine, sine = np.cos(turn), np.sin(turn)
    second = halves(np.block([[cosine, -sine], [sine, cosine]]))
    turn = 2 * np.pi * ((order[:, None] * k[None, :]) % LANES) / LANES
    cosine, sine = np.cos(turn) / PERIOD, np.sin(turn) / PERIOD
    last = halves(np.block([[cosine, -sine], [sine, cosine]]))
    turn = 2 * np.pi * (k[:, None] * k[None, :]) / PERIOD
    twiddle = np.stack([np.cos(turn), np.sin(turn)]).astype(np.float32)
    return dict(
        first=first,
        second=np.stack(second),
        last=np.stack(last),
        twiddle=twiddle,
    )


TABLES = tables()


def run(body, outs, args, scratch, name, grant, smem=(), far=()):
    spaces = [pltpu.HBM if i in far else pltpu.SMEM if i in smem else pltpu.VMEM for i in range(len(args))]
    return pl.pallas_call(
        body,
        out_shape=[jax.ShapeDtypeStruct(shape, kind) for shape, kind in outs],
        in_specs=[pl.BlockSpec(memory_space=space) for space in spaces],
        out_specs=[pl.BlockSpec(memory_space=pltpu.VMEM)] * len(outs),
        scratch_shapes=[pltpu.VMEM(shape, kind) for shape, kind in scratch],
        compiler_params=pltpu.CompilerParams(vmem_limit_bytes=grant * MEGABYTE),
        name=name,
    )(*args)


def dot(a, b):
    return jnp.dot(a, b, preferred_element_type=F32)


def dot_rows(a, b, precision=None):
    return lax.dot_general(a, b, (((1,), (1,)), ((), ())), precision=precision, preferred_element_type=F32)


def dot_columns(a, b, precision=None):
    return lax.dot_general(a, b, (((0,), (0,)), ((), ())), precision=precision, preferred_element_type=F32)


def triple(a_high, a_low, b_high, b_low):
    left = jnp.concatenate([a_high, a_low, a_high], axis=1)
    return dot(left, jnp.concatenate([b_high, b_high, b_low], axis=0))


def triple_rows(a_high, a_low, b_high, b_low):
    left = jnp.concatenate([a_high, a_low, a_high], axis=1)
    return dot_rows(left, jnp.concatenate([b_high, b_high, b_low], axis=1))


def put_halves(high_ref, low_ref, rows, columns, value):
    high = value.astype(BF16)
    high_ref[rows, columns] = high
    low_ref[rows, columns] = (value - high.astype(F32)).astype(BF16)


def block(i, size=LANES):
    return slice(i * size, (i + 1) * size)


RE, IM = slice(0, LANES), slice(LANES, 2 * LANES)


def signal_row(b, part, r):
    return part * 4 + r * 2 + b


def spread(message):
    return message.astype(F32).reshape(-1, LANES)


def transform(x_ref, high_ref, low_ref, first, second, twiddle, count):
    part_a = dot(first[...], x_ref[:, : count * LANES])
    cosine, sine = twiddle[0], twiddle[1]
    for s in range(count):
        real, imag = part_a[:LANES, block(s)], part_a[LANES:, block(s)]
        put_halves(high_ref, low_ref, block(s), RE, real * cosine + imag * sine)
        put_halves(high_ref, low_ref, block(s), IM, imag * cosine - real * sine)
    rows = slice(0, count * LANES)
    return triple(high_ref[rows, :], low_ref[rows, :], second[0], second[1])


def transform_back(high_ref, low_ref, e_high, e_low, second, last, twiddle, count):
    rows = slice(0, count * LANES)
    part_d = triple_rows(high_ref[rows, :], low_ref[rows, :], second[0], second[1])
    cosine, sine = twiddle[0], twiddle[1]
    for s in range(count):
        real, imag = part_d[block(s), RE], part_d[block(s), IM]
        put_halves(e_high, e_low, RE, block(s), real * cosine - imag * sine)
        put_halves(e_high, e_low, IM, block(s), real * sine + imag * cosine)
    return triple(last[0], last[1], e_high[:, rows], e_low[:, rows])


def erf_parts(value):
    cdf = 0.5 * (1.0 + lax.erf(value * math.sqrt(0.5)))
    return cdf, jnp.exp(-0.5 * value * value) * (1.0 / math.sqrt(2.0 * math.pi))


def total(value):
    return jnp.sum(jnp.sum(value, axis=0, keepdims=True), axis=1, keepdims=True)


def times_of(row, lane):
    return (256 * (row & 31) + 128 * lax.shift_right_logical(row, 5 * jnp.ones_like(row)) + lane).astype(F32)


def valid_of(len_ref):
    row = lax.broadcasted_iota(jnp.int32, (LANES, LANES), 0) & 63
    times = times_of(row, lax.broadcasted_iota(jnp.int32, (LANES, LANES), 1))
    columns = []
    for y in range(4):
        upper = times[0:64, :] < len_ref[2 * y : 2 * y + 1, :]
        lower = times[64:128, :] < len_ref[2 * y + 1 : 2 * y + 2, :]
        columns.append(jnp.concatenate([upper, lower], axis=0).astype(F32))
    return jnp.concatenate(columns, axis=1)


def tally_of(len_ref):
    return jnp.sum(len_ref[:, 0:1], axis=0, keepdims=True)


def load_signals(message, step, x_ref):
    for part in range(OWN):
        for y in range(4):
            lanes = block(part * 4 + y)
            for b in range(2):
                for r in range(2):
                    start = y * step + signal_row(b, part, r)
                    piece = message[pl.ds(start, 32, stride=4 * step), :].astype(BF16)
                    x_ref[b * 128 + r * 32 : b * 128 + r * 32 + 32, lanes] = piece
                    x_ref[b * 128 + r * 32 + 64 : b * 128 + r * 32 + 96, lanes] = piece


def store_signals(out, step, base, get):
    for part in range(OWN):
        for y in range(4):
            value = get(part, y)
            for b in range(2):
                for r in range(2):
                    start = y * step + base + signal_row(b, part, r)
                    out[pl.ds(start, 32, stride=4 * step), :] = value[b * 64 + r * 32 : b * 64 + r * 32 + 32, :]


SPEC_IM = OWN * LANES
OWN_ROWS = slice(2 * SPEC_IM, 2 * SPEC_IM + 8)
COLUMN_ROWS = slice(2 * SPEC_IM + 8, 2 * SPEC_IM + 8 + HIDDEN)
BUNDLE = 2 * SPEC_IM + 8 + HIDDEN


def kernel_parts(bundle, part):
    return bundle[block(part), :], bundle[SPEC_IM + part * LANES : SPEC_IM + (part + 1) * LANES, :]


def convolve(x_ref, spec_ref, kernel_spec, high, low, e_high, e_low, consts, y_ref):
    first, second, last, twiddle = consts
    spec_ref[...] = transform(x_ref, high, low, first, second, twiddle, SIGNALS)
    for part in range(OWN):
        k_re, k_im = kernel_parts(kernel_spec, part)
        for y in range(4):
            rows = block(part * 4 + y)
            s_re, s_im = spec_ref[rows, RE], spec_ref[rows, IM]
            put_halves(high, low, rows, RE, s_re * k_re - s_im * k_im)
            put_halves(high, low, rows, IM, s_re * k_im + s_im * k_re)
    y_ref[...] = transform_back(high, low, e_high, e_low, second, last, twiddle, SIGNALS)


def normalise(y_ref, own, valid, tally, part):
    value = y_ref[:, block(part, 512)]
    mean = total(valid * value) / tally
    centred = value - mean
    var = total(valid * centred * centred) / tally
    inv_std = lax.rsqrt(var + EPSILON)
    normed = centred * inv_std
    pre_act = normed * own[part : part + 1, 35:36] + own[part : part + 1, 36:37]
    cdf, density = erf_parts(pre_act)
    return normed, inv_std, pre_act * cdf, cdf + pre_act * density


def normalise_all(y_ref, own, len_ref, normed_ref, slope_ref, inv_ref):
    valid, tally = valid_of(len_ref), tally_of(len_ref)
    inv_ref[...] = jnp.zeros((8, LANES), F32)
    for part in range(OWN):
        normed, inv_std, active, slope = normalise(y_ref, own, valid, tally, part)
        normed_ref[:, block(part, 512)] = normed
        slope_ref[:, block(part, 512)] = slope
        inv_ref[part : part + 1, :] = jnp.broadcast_to(inv_std, (1, LANES))
        y_ref[:, block(part, 512)] = active


def conv_backward(
    message, step, base, normed_of, slope_of, inv_of, own, valid, tally, spec_ref, kernel_spec, x_ref, high, low,
    e_high, e_low, consts, grad_ref,
):
    first, second, last, twiddle = consts
    sums = []
    for part in range(OWN):
        columns = []
        for y in range(4):
            pieces = []
            for b in range(2):
                for r in range(2):
                    start = y * step + base + signal_row(b, part, r)
                    pieces.append(message[pl.ds(start, 32, stride=4 * step), :])
            columns.append(jnp.concatenate(pieces, axis=0))
        act_grad = jnp.concatenate(columns, axis=1)
        normed = normed_of(part)
        pre_grad = act_grad * slope_of(part)
        bias_total = total(pre_grad)
        gain_total = total(pre_grad * normed)
        gain = own[part : part + 1, 35:36]
        conv_grad = inv_of(part) * (
            gain * pre_grad - valid * (gain * bias_total + normed * (gain * gain_total)) / tally
        )
        conv_low = conv_grad.astype(BF16)
        for b in range(2):
            piece = conv_low[b * 64 : b * 64 + 64, :]
            x_ref[b * 128 : b * 128 + 64, block(part, 512)] = piece
            x_ref[b * 128 + 64 : b * 128 + 128, block(part, 512)] = piece
        sums.append((gain_total, bias_total))
    grad_ref[...] = transform(x_ref, high, low, first, second, twiddle, SIGNALS)
    for part in range(OWN):
        k_re, k_im = kernel_parts(kernel_spec, part)
        corr_re, corr_im = None, None
        for y in range(4):
            rows = block(part * 4 + y)
            g_re, g_im = grad_ref[rows, RE], grad_ref[rows, IM]
            s_re, s_im = spec_ref[rows, RE], spec_ref[rows, IM]
            put_halves(high, low, rows, RE, k_re * g_re + k_im * g_im)
            put_halves(high, low, rows, IM, k_re * g_im - k_im * g_re)
            now_re, now_im = s_re * g_re + s_im * g_im, s_re * g_im - s_im * g_re
            corr_re = now_re if corr_re is None else corr_re + now_re
            corr_im = now_im if corr_im is None else corr_im + now_im
        put_halves(high, low, block(SIGNALS + part), RE, corr_re)
        put_halves(high, low, block(SIGNALS + part), IM, corr_im)
    returned = transform_back(high, low, e_high, e_low, second, last, twiddle, SIGNALS + OWN)
    return returned, sums


def sin_cos(angle):
    turns = jnp.floor(angle * (2.0 / math.pi) + 0.5)
    rest = angle - turns * 1.5703125
    rest = rest - turns * 4.837512969970703125e-4
    rest = rest - turns * 7.549789948768648e-8
    square = rest * rest
    sine = rest + rest * square * (
        -1.6666654611e-1 + square * (8.3321608736e-3 + square * -1.9515295891e-4)
    )
    cosine = 1.0 - 0.5 * square + square * square * (
        4.166664568298827e-2 + square * (-1.388731625493765e-3 + square * 2.443315711809948e-5)
    )
    half = jnp.floor(turns * 0.5)
    odd = turns - 2.0 * half
    sign = 1.0 - 2.0 * (half - 2.0 * jnp.floor(half * 0.5))
    is_odd = odd > 0.5
    return sign * jnp.where(is_odd, cosine, sine), sign * jnp.where(is_odd, -sine, cosine)


CHUNK = 1024
F_TABLE = (0, 4, 7)
C_TABLE = (1, 3, 6)


def envelope_of(times, own):
    lower, upper = own[:, 33:34], own[:, 34:35]
    inside = (times >= lower) & (times < upper)
    offset = (times - lower) / (0.5 * (upper - lower))
    return jnp.where(inside, jnp.exp(-0.5 * offset * offset), 0.0)


def stacked_weight(weight):
    high, low = high_low(weight)
    return jnp.concatenate([high, high, low], axis=1).astype(BF16)


def stacked_dot(weight, value):
    high = value.astype(BF16)
    low = (value - high.astype(F32)).astype(BF16)
    return dot(weight, jnp.concatenate([high, low, high], axis=0))


def own_parameters(layer, number, out_w, out_b, window, gain, bias, gabor, hidden_b, wide, tall, own, columns):
    wide[...] = jnp.zeros(wide.shape, F32)
    wide[0:32, 0:CHANNELS] = out_w[layer]
    wide[32:33, 0:CHANNELS] = out_b[layer : layer + 1, :]
    wide[33:35, 0:CHANNELS] = window[layer].astype(F32)
    wide[35:36, 0:CHANNELS] = gain[layer : layer + 1, :]
    wide[36:37, 0:CHANNELS] = bias[layer : layer + 1, :]
    tall[0:PADDED, :] = jnp.transpose(wide[...])
    tall[PADDED : PADDED + 8, :] = jnp.zeros((8, LANES), F32)
    row = lax.broadcasted_iota(jnp.int32, (8, LANES), 0)
    lane = lax.broadcasted_iota(jnp.int32, (8, LANES), 1)
    mine = tall[pl.ds(number * OWN, 8), :]
    unused = (row >= OWN) | (number * OWN + row >= CHANNELS)
    own[...] = jnp.where(unused, jnp.where(lane == 34, float(SAMPLES), 0.0), mine)
    wide[:, 0:LANES] = jnp.zeros((LANES, LANES), F32)
    for j in range(3):
        wide[4 * j : 4 * j + 4, 0:HIDDEN] = gabor[layer, j]
    wide[12:14, 0:HIDDEN] = hidden_b[layer]
    columns[...] = jnp.transpose(wide[:, 0:LANES])[0:HIDDEN, :]


def sample_rows(first_lane, count):
    lane = first_lane + lax.broadcasted_iota(jnp.int32, (1, count), 1)
    times = times_of(lax.shift_right_logical(lane, 7 * jnp.ones_like(lane)), lane & 127)
    return times, times * (2.0 / (SAMPLES - 1)) - 1.0


def generate(columns, hidden_w, own, tab, rows):
    turns = []
    for j in range(3):
        turn = sin_cos(columns[:, 4 * j + 2 : 4 * j + 3] * (512.0 / (SAMPLES - 1)))
        turns.append([jnp.broadcast_to(value, (HIDDEN, LANES)) for value in turn])

    def step(i, carry):
        _, places = sample_rows(i * CHUNK, CHUNK)
        for j in range(3):
            sharpness, centre = columns[:, 4 * j : 4 * j + 1], columns[:, 4 * j + 1 : 4 * j + 2]
            frequency, phase = columns[:, 4 * j + 2 : 4 * j + 3], columns[:, 4 * j + 3 : 4 * j + 4]
            sine, cosine = sin_cos(frequency * places[:, 0:LANES] + phase)
            turn_sin, turn_cos = turns[j]
            for n in range(CHUNK // LANES):
                width = sharpness * (places[:, block(n)] - centre)
                bell = jnp.exp(-0.5 * width * width)
                here = pl.ds(pl.multiple_of(i * CHUNK + n * LANES, LANES), LANES)
                tab[F_TABLE[j], :, here] = bell * sine
                tab[C_TABLE[j], :, here] = bell * cosine
                sine, cosine = sine * turn_cos + cosine * turn_sin, cosine * turn_cos - sine * turn_sin
        return carry

    lax.fori_loop(0, SAMPLES // CHUNK, step, 0)
    weights = [stacked_weight(hidden_w[0]), stacked_weight(hidden_w[1]), stacked_weight(own[:, 0:32])]
    u_1 = stacked_dot(weights[0], tab[0]) + columns[:, 12:13]
    z_1 = u_1 * tab[4]
    tab[2] = z_1
    tab[3] = u_1 * tab[3]
    u_2 = stacked_dot(weights[1], z_1) + columns[:, 13:14]
    z_2 = u_2 * tab[7]
    tab[5] = z_2
    tab[6] = u_2 * tab[6]
    raw = stacked_dot(weights[2], z_2) + own[:, 32:33]
    times, _ = sample_rows(0, SAMPLES)
    rows[...] = raw * envelope_of(times, own)


def generate_back(kernel_grad, columns, hidden_w, own, tab, rows, sums, mats):
    rows[...] = jnp.zeros(rows.shape, F32)
    for part in range(OWN):
        grad = kernel_grad(part)
        for n in range(64):
            rows[part : part + 1, block(n)] = grad[n : n + 1, :]
    sums[...] = jnp.zeros(sums.shape, F32)
    mats[...] = jnp.zeros(mats.shape, F32)
    turned = jnp.transpose(jnp.concatenate([own[...], jnp.zeros((120, 128), F32)], axis=0))
    weight = [turned[0:32, part : part + 1] for part in range(OWN)]
    back = [stacked_weight(jnp.transpose(hidden_w[j])) for j in range(2)]

    def fold(value):
        acc = value[:, block(0)]
        for i in range(1, CHUNK // LANES):
            acc = acc + value[:, block(i)]
        return acc

    def add(k, value):
        sums[block(k, 32), :] += fold(value)

    def step(i, carry):
        span = pl.ds(pl.multiple_of(i * CHUNK, CHUNK), CHUNK)
        times, places = sample_rows(i * CHUNK, CHUNK)
        draw = rows[:, span] * envelope_of(times, own)
        dz_2 = weight[0] * draw[0:1, :] + weight[1] * draw[1:2, :] + weight[2] * draw[2:3, :]

        def level(j, e_value, g_value):
            centre = columns[:, 4 * j + 1 : 4 * j + 2]
            offset = places - centre
            moment = e_value * offset
            add(4 * j, moment * offset)
            add(4 * j + 1, moment)
            add(4 * j + 2, g_value * places)
            add(4 * j + 3, g_value)

        z_2 = tab[5, :, span]
        level(2, dz_2 * z_2, dz_2 * tab[6, :, span])
        du_2 = dz_2 * tab[7, :, span]
        add(13, du_2)
        dz_1 = stacked_dot(back[1], du_2)
        z_1 = tab[2, :, span]
        level(1, dz_1 * z_1, dz_1 * tab[3, :, span])
        du_1 = dz_1 * tab[4, :, span]
        add(12, du_1)
        dz_0 = stacked_dot(back[0], du_1)
        z_0 = tab[0, :, span]
        level(0, dz_0 * z_0, dz_0 * tab[1, :, span])
        sums[14 * 32 : 14 * 32 + 8, :] += fold(draw)
        left = jnp.concatenate([du_1, du_2, draw], axis=0)
        right = jnp.concatenate([z_0, z_1, z_2, jnp.zeros_like(z_0)], axis=0)
        left_high, right_high = left.astype(BF16), right.astype(BF16)
        left_low = (left - left_high.astype(F32)).astype(BF16)
        right_low = (right - right_high.astype(F32)).astype(BF16)
        mats[...] += (
            dot_rows(left_high, right_high) + dot_rows(left_low, right_high) + dot_rows(left_high, right_low)
        )
        return carry

    lax.fori_loop(0, SAMPLES // CHUNK, step, 0, unroll=SAMPLES // CHUNK)
    lane = lax.broadcasted_iota(jnp.int32, (32, LANES), 1)
    hidden = jnp.where(lane < 32, mats[0:32, :], jnp.where(lane < 64, mats[32:64, :], 0.0))

    def column(k):
        return jnp.sum(sums[block(k, 32), :], axis=1, keepdims=True)

    hidden = jnp.where(lane == 64, column(12), hidden)
    hidden = jnp.where(lane == 65, column(13), hidden)
    for j in range(3):
        sharpness = columns[:, 4 * j : 4 * j + 1]
        hidden = jnp.where(lane == 66 + 4 * j, -sharpness * column(4 * j), hidden)
        hidden = jnp.where(lane == 67 + 4 * j, sharpness * sharpness * column(4 * j + 1), hidden)
        hidden = jnp.where(lane == 68 + 4 * j, column(4 * j + 2), hidden)
        hidden = jnp.where(lane == 69 + 4 * j, column(4 * j + 3), hidden)
    lane8 = lax.broadcasted_iota(jnp.int32, (8, LANES), 1)
    outer = pltpu.roll(mats[64:72, :], LANES - 64, 1)
    raw_total = jnp.sum(sums[14 * 32 : 14 * 32 + 8, :], axis=1, keepdims=True)
    outer = jnp.where(lane8 < 32, outer, 0.0)
    outer = jnp.where(lane8 == 32, raw_total, outer)
    return hidden, outer


def with_norm_sums(outer, sums):
    row = lax.broadcasted_iota(jnp.int32, (8, LANES), 0)
    lane = lax.broadcasted_iota(jnp.int32, (8, LANES), 1)
    for part in range(OWN):
        gain_total, bias_total = sums[part]
        outer = jnp.where((row == part) & (lane == 33), gain_total, outer)
        outer = jnp.where((row == part) & (lane == 34), bias_total, outer)
    return outer


def one_row(outer):
    lane = lax.broadcasted_iota(jnp.int32, (1, LANES), 1)
    result = jnp.zeros((1, LANES), F32)
    for part in range(OWN):
        row = outer[part : part + 1, :]
        moved = pltpu.roll(row, 32 * part, 1) if part else row
        result = jnp.where((lane >= 32 * part) & (lane < 32 * part + 32), moved, result)
        moved = pltpu.roll(row, 64 + 3 * part, 1)
        result = jnp.where((lane >= 96 + 3 * part) & (lane < 99 + 3 * part), moved, result)
    return result


def packed_hidden(hidden):
    lane16 = lax.broadcasted_iota(jnp.int32, (16, LANES), 1)
    upper = jnp.where(lane16 < 64, hidden[0:16, :], pltpu.roll(hidden[16:32, :], 64, 1))
    lane4 = lax.broadcasted_iota(jnp.int32, (4, LANES), 1)
    lower = jnp.zeros((4, LANES), F32)
    for g in range(8):
        moved = pltpu.roll(hidden, (64 + 16 * g) % LANES, 1)[4 * g : 4 * g + 4, :]
        lower = jnp.where((lane4 >= 16 * g) & (lane4 < 16 * g + 16), moved, lower)
    return upper, lower


def unpacked_hidden(upper, lower):
    lane16 = lax.broadcasted_iota(jnp.int32, (16, LANES), 1)
    lane32 = lax.broadcasted_iota(jnp.int32, (32, LANES), 1)
    top = jnp.concatenate([upper, pltpu.roll(upper, 64, 1)], axis=0)
    tiled = jnp.concatenate([lower] * 8, axis=0)
    row32 = lax.broadcasted_iota(jnp.int32, (32, LANES), 0)
    rest = jnp.zeros((32, LANES), F32)
    for g in range(8):
        moved = pltpu.roll(tiled, (64 - 16 * g) % LANES, 1)
        rest = jnp.where((row32 >= 4 * g) & (row32 < 4 * g + 4), moved, rest)
    return jnp.where(lane32 < 64, top, rest)


def high_low(value):
    high = value.astype(BF16).astype(F32)
    return high, value - high


def valid_row(meta, i):
    lane = lax.broadcasted_iota(jnp.int32, (1, LANES), 1)
    return (meta[2] * PIECE + (i // 2) * LANES + lane < meta[i % 2]).astype(F32)


def masked(meta, rows):
    mask = jnp.concatenate([valid_row(meta, i) for i in range(4)] * 2, axis=0)
    return (rows.reshape(-1, 8, LANES) * mask[None]).reshape(-1, LANES)


CLIP_ROWS = 4 * CHANNELS
PADDED_ROWS = 4 * PADDED


def put_padded(padded, rows):
    padded[0:CLIP_ROWS, :] = rows
    padded[CLIP_ROWS:PADDED_ROWS, :] = jnp.zeros((PADDED_ROWS - CLIP_ROWS, LANES), F32)


def rows_to_message(padded, out, step, base):
    for m in range(12):
        out[pl.ds(base + m, DEVICES, stride=step), :] = padded[pl.ds(m, DEVICES, stride=12), :]


def rows_of_channels(padded, i):
    return padded[pl.ds(i, PADDED, stride=4), :]


def source_kernel(meta, x_ref, out_ref, padded, out):
    put_padded(padded, masked(meta, x_ref[...]))
    for b in range(2):
        length = meta[b]
        upper = lax.shift_right_logical(length, 7)
        out[pl.ds(12 + 2 * b, DEVICES, stride=16), :] = jnp.full((DEVICES, LANES), upper.astype(F32))
        out[pl.ds(13 + 2 * b, DEVICES, stride=16), :] = jnp.full(
            (DEVICES, LANES), (length - upper * 128).astype(F32)
        )
    rows_to_message(padded, out, 16, 0)
    out_ref[...] = out[...].reshape(DEVICES, 16, LANES).astype(BF16)


def make_lookup(lookup):
    row = lax.broadcasted_iota(jnp.int32, (DEVICES, PADDED), 0)
    column = lax.broadcasted_iota(jnp.int32, (DEVICES, PADDED), 1)
    for part in range(OWN):
        lookup[block(part), :] = (column == OWN * row + part).astype(F32).astype(BF16)


def make_weights(mix_w, mix_b, wide, lookup, weights, weights_back):
    make_lookup(lookup)
    wide[...] = jnp.zeros(wide.shape, BF16)
    row = lax.broadcasted_iota(jnp.int32, (LANES, CHANNELS), 0)
    lines = jnp.where(row == 0, mix_b[0:1, :], jnp.where(row == 1, mix_b[1:2, :], 0.0))
    turned = jnp.transpose(jnp.concatenate([lines, jnp.zeros((LANES, PADDED - CHANNELS), F32)], axis=1))
    lane = lax.broadcasted_iota(jnp.int32, (PADDED, PADDED), 1)
    for layer in range(2):
        wide[0:CHANNELS, 0:CHANNELS] = mix_w[:, layer, :]
        weights_back[layer] = dot_rows(lookup[...], wide[...]).astype(BF16)
        value = dot_rows(wide[...], lookup[...])
        rest = turned[:, layer : layer + 1]
        for spot in SPOTS:
            high, rest = high_low(rest)
            value = jnp.where(lane == spot, high, value)
        weights[layer] = value.astype(BF16)


def make_kernel(layer, meta, params, consts, bundle, tab, scratch):
    out_w, out_b, window, gain, bias, gabor, hidden_b, hidden_w = params
    first, second, _, twiddle = consts
    wide, tall, rows, pieces, x_ref, high, low = scratch
    own, columns = bundle.at[OWN_ROWS, :], bundle.at[COLUMN_ROWS, :]
    own_parameters(layer, meta[3], out_w, out_b, window, gain, bias, gabor, hidden_b, wide, tall, own, columns)
    generate(columns, hidden_w.at[layer], own, tab, rows)
    for n in range(64):
        for part in range(OWN):
            pieces[part * 64 + n : part * 64 + n + 1, :] = rows[part : part + 1, block(n)]
    for part in range(OWN):
        piece = pieces[block(part, 64), :].astype(BF16)
        x_ref[0:64, block(part)] = piece
        x_ref[64:128, block(part)] = piece
        x_ref[128:256, block(part)] = jnp.zeros((128, LANES), BF16)
    spec = transform(x_ref, high, low, first, second, twiddle, OWN)
    bundle[0:SPEC_IM, :] = spec[:, RE]
    bundle[SPEC_IM : 2 * SPEC_IM, :] = spec[:, IM]


def forward_kernel(
    meta, message_ref, out_w, out_b, window, gain, bias, gabor, hidden_b, hidden_w,
    first, second, last, twiddle,
    out_ref, spec_ref, normed_ref, slope_ref, inv_ref, len_ref, kernel_spec, tab,
    message, x_ref, high, low, e_high, e_low, y_ref, out, *make_scratch,
):
    own = kernel_spec.at[OWN_ROWS, :]
    params = (out_w, out_b, window, gain, bias, gabor, hidden_b, hidden_w)
    make_kernel(0, meta, params, (first, second, last, twiddle), kernel_spec, tab, make_scratch)
    message[...] = spread(message_ref[...])
    for y in range(4):
        for b in range(2):
            start = y * 16 + 12 + 2 * b
            len_ref[2 * y + b : 2 * y + b + 1, :] = (
                message[start : start + 1, :] * 128.0 + message[start + 1 : start + 2, :]
            )
    load_signals(message, 16, x_ref)
    convolve(x_ref, spec_ref, kernel_spec, high, low, e_high, e_low, (first, second, last, twiddle), y_ref)
    normalise_all(y_ref, own, len_ref, normed_ref, slope_ref, inv_ref)
    store_signals(out, 16, 0, lambda part, y: y_ref[:, block(part * 4 + y)])
    out_ref[...] = out[...].reshape(DEVICES, 16, LANES).astype(BF16)


def gather_active(message, step, rhs):
    row = lax.broadcasted_iota(jnp.int32, (DEVICES, LANES), 0)
    for i in range(4):
        for part in range(OWN):
            piece = message[pl.ds(part * 4 + i, DEVICES, stride=step), :]
            if part != 1:
                piece = jnp.where(row >= (126 if part == 2 else 127), 1.0, piece)
            rhs[block(part), block(i)] = piece.astype(BF16)


def store_rows(value, out, step, base):
    for i in range(4):
        for part in range(OWN):
            out[pl.ds(base + part * 4 + i, DEVICES, stride=step), :] = value[block(part), block(i)]


def mix_kernel(
    meta, message_ref, x_ref, cotangent, mix_w, mix_b,
    out_ref, next_ref, active_ref, weights, weights_back, message, padded, out, low, wide, lookup,
):
    make_weights(mix_w, mix_b, wide, lookup, weights, weights_back)
    message[...] = spread(message_ref[...])
    gather_active(message, 16, active_ref)
    mixed = dot(weights[0], active_ref[...])
    put_padded(padded, x_ref[...])
    for i in range(4):
        valid = valid_row(meta, i)
        value = rows_of_channels(padded, i) + mixed[:, block(i)] * valid
        next_ref[pl.ds(i, PADDED, stride=4), :] = value
        padded[pl.ds(i, PADDED, stride=4), :] = value * valid
    rows_to_message(padded, out, 24, 0)
    put_padded(padded, masked(meta, cotangent[...]))
    for i in range(4):
        low[:, block(i)] = rows_of_channels(padded, i).astype(BF16)
    store_rows(dot(weights_back[1], low[...]), out, 24, 12)
    out_ref[...] = out[...].reshape(DEVICES, 24, LANES).astype(BF16)


def forward_1_kernel(
    meta, message_ref, out_w, out_b, window, gain, bias, gabor, hidden_b, hidden_w,
    len_ref, first, second, last, twiddle,
    y_ref, spec_ref, normed_ref, slope_ref, inv_ref, kernel_spec, tab,
    message, x_ref, high, low, e_high, e_low, *make_scratch,
):
    own = kernel_spec.at[OWN_ROWS, :]
    consts = (first, second, last, twiddle)
    params = (out_w, out_b, window, gain, bias, gabor, hidden_b, hidden_w)
    make_kernel(1, meta, params, consts, kernel_spec, tab, make_scratch)
    message[...] = spread(message_ref[...])
    load_signals(message, 24, x_ref)
    convolve(x_ref, spec_ref, kernel_spec, high, low, e_high, e_low, consts, y_ref)
    normalise_all(y_ref, own, len_ref, normed_ref, slope_ref, inv_ref)


def backward_1_kernel(
    message_ref, active_ref, spec_ref, kernel_spec, normed_ref, slope_ref, inv_ref, len_ref,
    first, second, last, twiddle, hidden_w, tab,
    out_ref, hidden_out, outer_out,
    message, x_ref, high, low, e_high, e_low, out, grad_ref, returned_ref, rows, sums, mats,
):
    own, columns = kernel_spec.at[OWN_ROWS, :], kernel_spec.at[COLUMN_ROWS, :]
    message[...] = spread(message_ref[...])
    valid, tally = valid_of(len_ref), tally_of(len_ref)
    returned, norm_sums = conv_backward(
        message, 24, 12, lambda part: normed_ref[:, block(part, 512)], lambda part: slope_ref[:, block(part, 512)],
        lambda part: inv_ref[part : part + 1, 0:1], own, valid, tally, spec_ref, kernel_spec, x_ref, high, low,
        e_high, e_low, (first, second, last, twiddle), grad_ref,
    )
    returned_ref[...] = returned
    store_signals(out, 24, 0, lambda part, y: active_ref[:, block(part * 4 + y)])
    store_signals(out, 24, 12, lambda part, y: returned_ref[:, block(part * 4 + y)])
    out_ref[...] = out[...].reshape(DEVICES, 24, LANES).astype(BF16)
    hidden, outer = generate_back(
        lambda part: returned_ref[0:64, block(SIGNALS + part)], columns, hidden_w.at[1], own, tab, rows, sums, mats
    )
    hidden_out[...] = hidden
    outer_out[...] = with_norm_sums(outer, norm_sums)


def middle_kernel(
    meta, message_ref, x_ref, cotangent, weights, weights_back, active_0, hidden_1,
    output_ref, flow_ref, out_ref, message, padded, out, low_0, low_1, active_1,
):
    message[...] = spread(message_ref[...])
    gather_active(message, 24, active_1)
    mixed = dot(weights[1], active_1[...])
    for i in range(4):
        padded[pl.ds(i, PADDED, stride=4), :] = rows_of_channels(x_ref, i) + mixed[:, block(i)] * valid_row(meta, i)
    output_ref[...] = padded[0:CLIP_ROWS, :]
    put_padded(flow_ref, cotangent[...])
    for i in range(4):
        low_1[:, block(i)] = (rows_of_channels(flow_ref, i) * valid_row(meta, i)).astype(BF16)
    for m in range(12):
        padded[pl.ds(m, DEVICES, stride=12), :] = message[pl.ds(12 + m, DEVICES, stride=24), :]
    flow_ref[...] += masked(meta, padded[...])
    for i in range(4):
        low_0[:, block(i)] = (rows_of_channels(flow_ref, i) * valid_row(meta, i)).astype(BF16)
    store_rows(dot(weights_back[0], low_0[...]), out, 32, 0)
    for layer, (active, low) in enumerate(((active_0, low_0), (active_1, low_1))):
        part_sum = dot_rows(active[...], low[...])
        for part in range(OWN):
            for third in range(3):
                out[pl.ds(12 + layer * 9 + part * 3 + third, DEVICES, stride=32), :] = part_sum[
                    block(part), block(third)
                ]
    high, low = high_low(hidden_1[...])
    out[pl.ds(30, DEVICES, stride=32), :] = jnp.concatenate([high, jnp.zeros((96, LANES), F32)], axis=0)
    out[pl.ds(31, DEVICES, stride=32), :] = jnp.concatenate([low, jnp.zeros((96, LANES), F32)], axis=0)
    out_ref[...] = out[...].reshape(DEVICES, 32, LANES).astype(BF16)


LAST_ROWS = 56


def backward_0_kernel(
    message_ref, spec_ref, kernel_spec, normed_ref, slope_ref, inv_ref, len_ref,
    first, second, last, twiddle,
    returned_ref, gathered_ref, norm_out,
    message, x_ref, high, low, e_high, e_low, grad_ref,
):
    own = kernel_spec.at[OWN_ROWS, :]
    message[...] = spread(message_ref[...])
    valid, tally = valid_of(len_ref), tally_of(len_ref)
    returned, norm_sums = conv_backward(
        message, 32, 0, lambda part: normed_ref[:, block(part, 512)], lambda part: slope_ref[:, block(part, 512)],
        lambda part: inv_ref[part : part + 1, 0:1], own, valid, tally, spec_ref, kernel_spec, x_ref, high, low,
        e_high, e_low, (first, second, last, twiddle), grad_ref,
    )
    returned_ref[...] = returned
    gathered_ref[...] = jnp.sum(message[...].reshape(DEVICES, 32, LANES), axis=0)
    norm_out[...] = with_norm_sums(jnp.zeros((8, LANES), F32), norm_sums)


def pack_kernel(
    returned_ref, gathered_ref, norm_0, kernel_spec, hidden_w, tab, outer_1,
    out_ref,
    out, rows, sums, mats,
):
    columns, own = kernel_spec.at[COLUMN_ROWS, :], kernel_spec.at[OWN_ROWS, :]
    store_signals(out, 16, 0, lambda part, y: returned_ref[:, block(part * 4 + y)])
    hidden, outer = generate_back(
        lambda part: returned_ref[0:64, block(SIGNALS + part)], columns, hidden_w.at[0], own, tab, rows, sums, mats
    )
    gathered = gathered_ref[...]
    upper, lower = packed_hidden(hidden)
    hidden_1_high, hidden_1_low = high_low(gathered[30:31, :] + gathered[31:32, :])
    outer_0_high, outer_0_low = high_low(one_row(outer + norm_0[...]))
    outer_1_high, outer_1_low = high_low(one_row(outer_1[...]))
    shared = jnp.concatenate(
        [
            gathered[0:30, :], upper, lower, hidden_1_high, hidden_1_low,
            outer_0_high, outer_0_low, outer_1_high, outer_1_low,
        ],
        axis=0,
    )
    row = lax.broadcasted_iota(jnp.int32, (DEVICES, 16, LANES), 1)
    own_rows = jnp.where(row < 12, out[...].reshape(DEVICES, 16, LANES), shared[None, 0:16, :])
    rest = jnp.broadcast_to(shared[None, 16:LAST_ROWS, :], (DEVICES, LAST_ROWS - 16, LANES))
    out_ref[...] = jnp.concatenate([own_rows, rest], axis=1).astype(BF16)


def last_kernel(
    meta, message_ref, flow_ref,
    input_grad, gabor_grad, hidden_w_grad, hidden_b_grad, out_w_grad, out_b_grad, gain_grad, bias_grad,
    mix_w_grad, mix_b_grad, message, padded, owned, thirds, lookup,
):
    make_lookup(lookup)
    message[...] = spread(message_ref[...])

    def rows_of(k, count=DEVICES):
        return message[pl.ds(k, count, stride=LAST_ROWS), :]

    for m in range(12):
        padded[pl.ds(m, DEVICES, stride=12), :] = rows_of(m)
    input_grad[...] = flow_ref[0:CLIP_ROWS, :] + masked(meta, padded[0:CLIP_ROWS, :])
    shared = jnp.sum(message[...].reshape(DEVICES, LAST_ROWS, LANES)[:, 24:56, :], axis=0)
    hidden_0 = unpacked_hidden(shared[6:22, :], shared[22:26, :])
    hidden_1 = rows_of(50, 32) + rows_of(51, 32)
    lane = lax.broadcasted_iota(jnp.int32, (DEVICES, LANES), 1)
    for layer, hidden in enumerate((hidden_0, hidden_1)):
        hidden_w_grad[layer, 0] = hidden[:, 0:32]
        hidden_w_grad[layer, 1] = pltpu.roll(hidden, 96, 1)[:, 0:32]
        turned = jnp.transpose(jnp.concatenate([hidden, jnp.zeros((96, LANES), F32)], axis=0))
        hidden_b_grad[layer] = turned[64:66, 0:32]
        for j in range(3):
            gabor_grad[layer, j] = turned[66 + 4 * j : 70 + 4 * j, 0:32]
        value = rows_of(52 + 2 * layer) + rows_of(53 + 2 * layer)
        for part in range(OWN):
            wide = pltpu.roll(value, (LANES - 32 * part) % LANES, 1)
            small = pltpu.roll(value, 64 - 3 * part, 1)
            owned[pl.ds(part, DEVICES, stride=OWN), :] = jnp.where(lane < 32, wide, small)
        turned = jnp.transpose(owned[...])
        out_w_grad[layer] = turned[0:32, 0:CHANNELS]
        out_b_grad[layer : layer + 1, :] = turned[32:33, 0:CHANNELS]
        gain_grad[layer : layer + 1, :] = turned[33:34, 0:CHANNELS]
        bias_grad[layer : layer + 1, :] = turned[34:35, 0:CHANNELS]
        bias_rows = []
        for part in range(OWN):
            for third in range(3):
                piece = rows_of(12 + layer * 9 + part * 3 + third)
                thirds[block(part), block(third)] = piece.astype(BF16)
                if part == 2:
                    bias_rows.append(piece[SPOT - 2 * DEVICES : SPOT - 2 * DEVICES + 1, :])
        mix_w_grad[:, layer, :] = dot_columns(thirds[...], lookup[...])[0:CHANNELS, 0:CHANNELS]
        mix_b_grad[layer : layer + 1, :] = jnp.concatenate(bias_rows, axis=1)[:, 0:CHANNELS]


def exchange(message):
    return lax.all_to_all(message, AXES, split_axis=0, concat_axis=0, tiled=True)


def to_rows(clips):
    return clips.reshape(2, CHANNELS, 2, LANES).transpose(1, 2, 0, 3).reshape(CLIP_ROWS, LANES)


def from_rows(rows):
    return rows.reshape(CHANNELS, 2, 2, LANES).transpose(2, 0, 1, 3).reshape(2, CHANNELS, PIECE)


def shards(
    inputs, lengths, window, gabor_params, hidden_w, hidden_b, out_w, out_b, bn_gain, bn_bias, mix_w, mix_b, cotangent
):
    position = lax.axis_index("seq").astype(jnp.int32)
    number = position * 4 + lax.axis_index("clips").astype(jnp.int32)
    const = {name: jnp.asarray(value) for name, value in TABLES.items()}
    meta = jnp.concatenate([lengths, jnp.stack([position, number])])
    inputs, cotangent = to_rows(inputs), to_rows(cotangent)

    def rows(count):
        return ((count, LANES), F32)

    with jax.named_scope("source_0"):
        (message,) = run(
            source_kernel, [((DEVICES, 16, LANES), BF16)], [meta, inputs],
            [rows(PADDED_ROWS), rows(DEVICES * 16)], "source_0", 8, smem=(0,),
        )
        message = exchange(message)

    square = (PADDED, PADDED)
    generator = [
        jnp.swapaxes(out_w, 1, 2), out_b, jnp.swapaxes(window, 1, 2), bn_gain, bn_bias, gabor_params, hidden_b,
        hidden_w,
    ]
    shape_tab = ((8, HIDDEN, SAMPLES), F32)
    make_scratch = [
        ((LANES, PADDED), F32), rows(PADDED + 8), ((8, SAMPLES), F32), rows(192),
        ((256, OWN * LANES), BF16), ((OWN * LANES, 256), BF16), ((OWN * LANES, 256), BF16),
    ]
    mixers = ((2, *square), BF16)

    def scratch(signals):
        count = signals * LANES
        return [
            ((256, SIGNALS * LANES), BF16), ((count, 256), BF16), ((count, 256), BF16),
            ((256, count), BF16), ((256, count), BF16),
        ]

    shape_y = (LANES, SIGNALS * LANES)
    shape_s = (SIGNALS * LANES, 256)
    transforms = [const[name] for name in TABLE_NAMES]
    with jax.named_scope("conv_0"):
        message, spec_0, normed_0, slope_0, inv_0, lens, bundle_0, tab_0 = run(
            forward_kernel,
            [
                ((DEVICES, 16, LANES), BF16), (shape_s, F32), (shape_y, F32), (shape_y, F32), rows(8), rows(8),
                rows(BUNDLE), shape_tab,
            ],
            [meta, message, *generator, *transforms],
            [rows(DEVICES * 16), *scratch(SIGNALS), (shape_y, F32), rows(DEVICES * 16), *make_scratch],
            "conv_0", 16, smem=(0,),
        )
        message = exchange(message)

    with jax.named_scope("mix_0"):
        message, middle, active_0, weights, weights_back = run(
            mix_kernel,
            [((DEVICES, 24, LANES), BF16), rows(PADDED_ROWS), ((PADDED, 512), BF16), mixers, mixers],
            [meta, message, inputs, cotangent, jnp.swapaxes(mix_w, 0, 1), mix_b],
            [rows(DEVICES * 16), rows(PADDED_ROWS), rows(DEVICES * 24), ((PADDED, 512), BF16), (square, BF16), (square, BF16)],
            "mix_0", 12, smem=(0,),
        )
        message = exchange(message)

    back_scratch = [((8, SAMPLES), F32), rows(14 * 32 + 8), rows(72)]
    with jax.named_scope("conv_1"):
        active_1, spec_1, normed_1, slope_1, inv_1, bundle_1, tab_1 = run(
            forward_1_kernel,
            [
                (shape_y, F32), (shape_s, F32), (shape_y, F32), (shape_y, F32), rows(8), rows(BUNDLE), shape_tab,
            ],
            [meta, message, *generator, lens, *transforms],
            [rows(DEVICES * 24), *scratch(SIGNALS), *make_scratch],
            "conv_1", 16, smem=(0,),
        )
        message, hidden_1, outer_1 = run(
            backward_1_kernel,
            [((DEVICES, 24, LANES), BF16), rows(HIDDEN), rows(8)],
            [message, active_1, spec_1, bundle_1, normed_1, slope_1, inv_1, lens, *transforms, hidden_w, tab_1],
            [
                rows(DEVICES * 24), *scratch(SIGNALS + OWN), rows(DEVICES * 24), (shape_s, F32),
                ((LANES, (SIGNALS + OWN) * LANES), F32), *back_scratch,
            ],
            "conv_back_1", 18,
        )
        message = exchange(message)

    with jax.named_scope("mix_1"):
        outputs, flow, message = run(
            middle_kernel,
            [rows(CLIP_ROWS), rows(PADDED_ROWS), ((DEVICES, 32, LANES), BF16)],
            [meta, message, middle, cotangent, weights, weights_back, active_0, hidden_1],
            [
                rows(DEVICES * 24), rows(PADDED_ROWS), rows(DEVICES * 32),
                ((PADDED, 512), BF16), ((PADDED, 512), BF16), ((PADDED, 512), BF16),
            ],
            "mix_1", 12, smem=(0,),
        )
        message = exchange(message)

    shape_back = ((LANES, (SIGNALS + OWN) * LANES), F32)
    with jax.named_scope("conv_back_0"):
        returned, gathered, norm_0 = run(
            backward_0_kernel, [shape_back, rows(32), rows(8)],
            [message, spec_0, bundle_0, normed_0, slope_0, inv_0, lens, *transforms],
            [rows(DEVICES * 32), *scratch(SIGNALS + OWN), (shape_s, F32)],
            "conv_back_0", 14,
        )
    with jax.named_scope("generator_back_0"):
        (message,) = run(
            pack_kernel, [((DEVICES, LAST_ROWS, LANES), BF16)],
            [returned, gathered, norm_0, bundle_0, hidden_w, tab_0, outer_1],
            [rows(DEVICES * 16), *back_scratch], "generator_back_0", 10,
        )
        message = exchange(message)

    with jax.named_scope("gradients"):
        (
            input_grad, gabor_grad, hidden_w_grad, hidden_b_grad, out_w_grad, out_b_grad, gain_grad, bias_grad,
            mix_w_grad, mix_b_grad,
        ) = run(
            last_kernel,
            [
                rows(CLIP_ROWS), (gabor_params.shape, F32), (hidden_w.shape, F32), (hidden_b.shape, F32),
                ((2, HIDDEN, CHANNELS), F32), (out_b.shape, F32), (bn_gain.shape, F32), (bn_bias.shape, F32),
                ((CHANNELS, 2, CHANNELS), F32), (mix_b.shape, F32),
            ],
            [meta, message, flow],
            [rows(DEVICES * LAST_ROWS), rows(PADDED_ROWS), rows(PADDED), (square, BF16), (square, BF16)],
            "gradients", 14, smem=(0,),
        )
    return (
        from_rows(outputs), from_rows(input_grad), gabor_grad, hidden_w_grad, hidden_b_grad,
        jnp.swapaxes(out_w_grad, 1, 2), out_b_grad, gain_grad, bias_grad, jnp.swapaxes(mix_w_grad, 0, 1), mix_b_grad,
    )


def solution(mesh):
    clip = P("clips", None, "seq")
    in_specs = (clip, P("clips")) + (P(),) * 10 + (clip,)
    out_specs = (clip, clip) + (P(),) * 9
    return jax.shard_map(shards, mesh=mesh, in_specs=in_specs, out_specs=out_specs, check_vma=False)
```

```python
import math

import jax
import jax.numpy as jnp
import ml_dtypes
import numpy as np
from jax import lax
from jax.experimental import pallas as pl
from jax.experimental.pallas import tpu as pltpu
from jax.sharding import PartitionSpec as P

F32 = jnp.float32
BF16 = jnp.bfloat16
AXES = ("seq", "clips")
DEVICES = 128
OWN = 3
CHANNELS = 380
PADDED = DEVICES * OWN
SAMPLES = 8192
PIECE = 256
HIDDEN = 32
LANES = 128
SIGNALS = 12
TABLE_NAMES = ("first", "second", "last", "twiddle")
PERIOD = 2 * SAMPLES
EPSILON = 1e-05
MEGABYTE = 1024 * 1024
EXACT = lax.Precision.HIGHEST
SPOTS = (2 * DEVICES + 126, 2 * DEVICES + 127, 127)
SPOT = SPOTS[0]


def halves(table):
    high = table.astype(ml_dtypes.bfloat16)
    low = (table - high.astype(np.float64)).astype(ml_dtypes.bfloat16)
    return high, low


def tables():
    order = np.array([2 * j + r for r in range(2) for j in range(32)])
    k = np.arange(LANES)
    turn = 2 * np.pi * ((k[:, None] * order[None, :]) % LANES) / LANES
    c_high, c_low = halves(np.cos(turn))
    s_high, s_low = halves(np.sin(turn))
    first = np.concatenate(
        [
            np.concatenate([c_high, c_low, s_high, s_low], axis=1),
            np.concatenate([-s_high, -s_low, c_high, c_low], axis=1),
        ],
        axis=0,
    )
    turn = 2 * np.pi * ((k[:, None] * k[None, :]) % LANES) / LANES
    cosine, sine = np.cos(turn), np.sin(turn)
    second = halves(np.block([[cosine, -sine], [sine, cosine]]))
    turn = 2 * np.pi * ((order[:, None] * k[None, :]) % LANES) / LANES
    cosine, sine = np.cos(turn) / PERIOD, np.sin(turn) / PERIOD
    last = halves(np.block([[cosine, -sine], [sine, cosine]]))
    turn = 2 * np.pi * (k[:, None] * k[None, :]) / PERIOD
    twiddle = np.stack([np.cos(turn), np.sin(turn)]).astype(np.float32)
    return dict(
        first=first,
        second=np.stack(second),
        last=np.stack(last),
        twiddle=twiddle,
    )


TABLES = tables()


def run(body, outs, args, scratch, name, grant, smem=(), far=()):
    spaces = [pltpu.HBM if i in far else pltpu.SMEM if i in smem else pltpu.VMEM for i in range(len(args))]
    return pl.pallas_call(
        body,
        out_shape=[jax.ShapeDtypeStruct(shape, kind) for shape, kind in outs],
        in_specs=[pl.BlockSpec(memory_space=space) for space in spaces],
        out_specs=[pl.BlockSpec(memory_space=pltpu.VMEM)] * len(outs),
        scratch_shapes=[pltpu.VMEM(shape, kind) for shape, kind in scratch],
        compiler_params=pltpu.CompilerParams(vmem_limit_bytes=grant * MEGABYTE),
        name=name,
    )(*args)


def dot(a, b):
    return jnp.dot(a, b, preferred_element_type=F32)


def dot_rows(a, b, precision=None):
    return lax.dot_general(a, b, (((1,), (1,)), ((), ())), precision=precision, preferred_element_type=F32)


def dot_columns(a, b, precision=None):
    return lax.dot_general(a, b, (((0,), (0,)), ((), ())), precision=precision, preferred_element_type=F32)


def triple(a_high, a_low, b_high, b_low):
    left = jnp.concatenate([a_high, a_low, a_high], axis=1)
    return dot(left, jnp.concatenate([b_high, b_high, b_low], axis=0))


def triple_rows(a_high, a_low, b_high, b_low):
    left = jnp.concatenate([a_high, a_low, a_high], axis=1)
    return dot_rows(left, jnp.concatenate([b_high, b_high, b_low], axis=1))


def put_halves(high_ref, low_ref, rows, columns, value):
    high = value.astype(BF16)
    high_ref[rows, columns] = high
    low_ref[rows, columns] = (value - high.astype(F32)).astype(BF16)


def block(i, size=LANES):
    return slice(i * size, (i + 1) * size)


RE, IM = slice(0, LANES), slice(LANES, 2 * LANES)


def signal_row(b, part, r):
    return part * 4 + r * 2 + b


def spread(message):
    return message.astype(F32).reshape(-1, LANES)


def transform(x_ref, high_ref, low_ref, first, second, twiddle, count):
    part_a = dot(first[...], x_ref[:, : count * LANES])
    cosine, sine = twiddle[0], twiddle[1]
    for s in range(count):
        real, imag = part_a[:LANES, block(s)], part_a[LANES:, block(s)]
        put_halves(high_ref, low_ref, block(s), RE, real * cosine + imag * sine)
        put_halves(high_ref, low_ref, block(s), IM, imag * cosine - real * sine)
    rows = slice(0, count * LANES)
    return triple(high_ref[rows, :], low_ref[rows, :], second[0], second[1])


def transform_back(high_ref, low_ref, e_high, e_low, second, last, twiddle, count):
    rows = slice(0, count * LANES)
    part_d = triple_rows(high_ref[rows, :], low_ref[rows, :], second[0], second[1])
    cosine, sine = twiddle[0], twiddle[1]
    for s in range(count):
        real, imag = part_d[block(s), RE], part_d[block(s), IM]
        put_halves(e_high, e_low, RE, block(s), real * cosine - imag * sine)
        put_halves(e_high, e_low, IM, block(s), real * sine + imag * cosine)
    return triple(last[0], last[1], e_high[:, rows], e_low[:, rows])


def erf_parts(value):
    cdf = 0.5 * (1.0 + lax.erf(value * math.sqrt(0.5)))
    return cdf, jnp.exp(-0.5 * value * value) * (1.0 / math.sqrt(2.0 * math.pi))


def total(value):
    return jnp.sum(jnp.sum(value, axis=0, keepdims=True), axis=1, keepdims=True)


def times_of(row, lane):
    return (256 * (row & 31) + 128 * lax.shift_right_logical(row, 5 * jnp.ones_like(row)) + lane).astype(F32)


def valid_of(len_ref):
    row = lax.broadcasted_iota(jnp.int32, (LANES, LANES), 0) & 63
    times = times_of(row, lax.broadcasted_iota(jnp.int32, (LANES, LANES), 1))
    columns = []
    for y in range(4):
        upper = times[0:64, :] < len_ref[2 * y : 2 * y + 1, :]
        lower = times[64:128, :] < len_ref[2 * y + 1 : 2 * y + 2, :]
        columns.append(jnp.concatenate([upper, lower], axis=0).astype(F32))
    return jnp.concatenate(columns, axis=1)


def tally_of(len_ref):
    return jnp.sum(len_ref[:, 0:1], axis=0, keepdims=True)


def load_signals(message, step, x_ref):
    for part in range(OWN):
        for y in range(4):
            lanes = block(part * 4 + y)
            for b in range(2):
                for r in range(2):
                    start = y * step + signal_row(b, part, r)
                    piece = message[pl.ds(start, 32, stride=4 * step), :].astype(BF16)
                    x_ref[b * 128 + r * 32 : b * 128 + r * 32 + 32, lanes] = piece
                    x_ref[b * 128 + r * 32 + 64 : b * 128 + r * 32 + 96, lanes] = piece


def store_signals(out, step, base, get):
    for part in range(OWN):
        for y in range(4):
            value = get(part, y)
            for b in range(2):
                for r in range(2):
                    start = y * step + base + signal_row(b, part, r)
                    out[pl.ds(start, 32, stride=4 * step), :] = value[b * 64 + r * 32 : b * 64 + r * 32 + 32, :]


SPEC_IM = OWN * LANES
OWN_ROWS = slice(2 * SPEC_IM, 2 * SPEC_IM + 8)
COLUMN_ROWS = slice(2 * SPEC_IM + 8, 2 * SPEC_IM + 8 + HIDDEN)
BUNDLE = 2 * SPEC_IM + 8 + HIDDEN


def kernel_parts(bundle, part):
    return bundle[block(part), :], bundle[SPEC_IM + part * LANES : SPEC_IM + (part + 1) * LANES, :]


def convolve(x_ref, spec_ref, kernel_spec, high, low, e_high, e_low, consts, y_ref):
    first, second, last, twiddle = consts
    spec_ref[...] = transform(x_ref, high, low, first, second, twiddle, SIGNALS)
    for part in range(OWN):
        k_re, k_im = kernel_parts(kernel_spec, part)
        for y in range(4):
            rows = block(part * 4 + y)
            s_re, s_im = spec_ref[rows, RE], spec_ref[rows, IM]
            put_halves(high, low, rows, RE, s_re * k_re - s_im * k_im)
            put_halves(high, low, rows, IM, s_re * k_im + s_im * k_re)
    y_ref[...] = transform_back(high, low, e_high, e_low, second, last, twiddle, SIGNALS)


def normalise(y_ref, own, valid, tally, part):
    value = y_ref[:, block(part, 512)]
    mean = total(valid * value) / tally
    centred = value - mean
    var = total(valid * centred * centred) / tally
    inv_std = lax.rsqrt(var + EPSILON)
    normed = centred * inv_std
    pre_act = normed * own[part : part + 1, 35:36] + own[part : part + 1, 36:37]
    cdf, density = erf_parts(pre_act)
    return normed, inv_std, pre_act * cdf, cdf + pre_act * density


def conv_backward(
    message, step, base, normed_of, slope_of, inv_of, own, valid, tally, spec_ref, kernel_spec, x_ref, high, low,
    e_high, e_low, consts, grad_ref,
):
    first, second, last, twiddle = consts
    sums = []
    for part in range(OWN):
        columns = []
        for y in range(4):
            pieces = []
            for b in range(2):
                for r in range(2):
                    start = y * step + base + signal_row(b, part, r)
                    pieces.append(message[pl.ds(start, 32, stride=4 * step), :])
            columns.append(jnp.concatenate(pieces, axis=0))
        act_grad = jnp.concatenate(columns, axis=1)
        normed = normed_of(part)
        pre_grad = act_grad * slope_of(part)
        bias_total = total(pre_grad)
        gain_total = total(pre_grad * normed)
        gain = own[part : part + 1, 35:36]
        conv_grad = inv_of(part) * (
            gain * pre_grad - valid * (gain * bias_total + normed * (gain * gain_total)) / tally
        )
        conv_low = conv_grad.astype(BF16)
        for b in range(2):
            piece = conv_low[b * 64 : b * 64 + 64, :]
            x_ref[b * 128 : b * 128 + 64, block(part, 512)] = piece
            x_ref[b * 128 + 64 : b * 128 + 128, block(part, 512)] = piece
        sums.append((gain_total, bias_total))
    grad_ref[...] = transform(x_ref, high, low, first, second, twiddle, SIGNALS)
    for part in range(OWN):
        k_re, k_im = kernel_parts(kernel_spec, part)
        corr_re, corr_im = None, None
        for y in range(4):
            rows = block(part * 4 + y)
            g_re, g_im = grad_ref[rows, RE], grad_ref[rows, IM]
            s_re, s_im = spec_ref[rows, RE], spec_ref[rows, IM]
            put_halves(high, low, rows, RE, k_re * g_re + k_im * g_im)
            put_halves(high, low, rows, IM, k_re * g_im - k_im * g_re)
            now_re, now_im = s_re * g_re + s_im * g_im, s_re * g_im - s_im * g_re
            corr_re = now_re if corr_re is None else corr_re + now_re
            corr_im = now_im if corr_im is None else corr_im + now_im
        put_halves(high, low, block(SIGNALS + part), RE, corr_re)
        put_halves(high, low, block(SIGNALS + part), IM, corr_im)
    returned = transform_back(high, low, e_high, e_low, second, last, twiddle, SIGNALS + OWN)
    return returned, sums


def sin_cos(angle):
    turns = jnp.floor(angle * (2.0 / math.pi) + 0.5)
    rest = angle - turns * 1.5703125
    rest = rest - turns * 4.837512969970703125e-4
    rest = rest - turns * 7.549789948768648e-8
    square = rest * rest
    sine = rest + rest * square * (
        -1.6666654611e-1 + square * (8.3321608736e-3 + square * -1.9515295891e-4)
    )
    cosine = 1.0 - 0.5 * square + square * square * (
        4.166664568298827e-2 + square * (-1.388731625493765e-3 + square * 2.443315711809948e-5)
    )
    half = jnp.floor(turns * 0.5)
    odd = turns - 2.0 * half
    sign = 1.0 - 2.0 * (half - 2.0 * jnp.floor(half * 0.5))
    is_odd = odd > 0.5
    return sign * jnp.where(is_odd, cosine, sine), sign * jnp.where(is_odd, -sine, cosine)


CHUNK = 1024
F_TABLE = (0, 4, 7)
C_TABLE = (1, 3, 6)


def envelope_of(times, own):
    lower, upper = own[:, 33:34], own[:, 34:35]
    inside = (times >= lower) & (times < upper)
    offset = (times - lower) / (0.5 * (upper - lower))
    return jnp.where(inside, jnp.exp(-0.5 * offset * offset), 0.0)


def stacked_weight(weight):
    high, low = high_low(weight)
    return jnp.concatenate([high, high, low], axis=1).astype(BF16)


def stacked_dot(weight, value):
    high = value.astype(BF16)
    low = (value - high.astype(F32)).astype(BF16)
    return dot(weight, jnp.concatenate([high, low, high], axis=0))


def own_parameters(layer, number, out_w, out_b, window, gain, bias, gabor, hidden_b, wide, tall, own, columns):
    wide[...] = jnp.zeros(wide.shape, F32)
    wide[0:32, 0:CHANNELS] = out_w[layer]
    wide[32:33, 0:CHANNELS] = out_b[layer : layer + 1, :]
    wide[33:35, 0:CHANNELS] = window[layer].astype(F32)
    wide[35:36, 0:CHANNELS] = gain[layer : layer + 1, :]
    wide[36:37, 0:CHANNELS] = bias[layer : layer + 1, :]
    tall[0:PADDED, :] = jnp.transpose(wide[...])
    tall[PADDED : PADDED + 8, :] = jnp.zeros((8, LANES), F32)
    row = lax.broadcasted_iota(jnp.int32, (8, LANES), 0)
    lane = lax.broadcasted_iota(jnp.int32, (8, LANES), 1)
    mine = tall[pl.ds(number * OWN, 8), :]
    unused = (row >= OWN) | (number * OWN + row >= CHANNELS)
    own[...] = jnp.where(unused, jnp.where(lane == 34, float(SAMPLES), 0.0), mine)
    wide[:, 0:LANES] = jnp.zeros((LANES, LANES), F32)
    for j in range(3):
        wide[4 * j : 4 * j + 4, 0:HIDDEN] = gabor[layer, j]
    wide[12:14, 0:HIDDEN] = hidden_b[layer]
    columns[...] = jnp.transpose(wide[:, 0:LANES])[0:HIDDEN, :]


def sample_rows(first_lane, count):
    lane = first_lane + lax.broadcasted_iota(jnp.int32, (1, count), 1)
    times = times_of(lax.shift_right_logical(lane, 7 * jnp.ones_like(lane)), lane & 127)
    return times, times * (2.0 / (SAMPLES - 1)) - 1.0


def generate(columns, hidden_w, own, tab, rows):
    turns = []
    for j in range(3):
        turn = sin_cos(columns[:, 4 * j + 2 : 4 * j + 3] * (512.0 / (SAMPLES - 1)))
        turns.append([jnp.broadcast_to(value, (HIDDEN, LANES)) for value in turn])

    def step(i, carry):
        _, places = sample_rows(i * CHUNK, CHUNK)
        for j in range(3):
            sharpness, centre = columns[:, 4 * j : 4 * j + 1], columns[:, 4 * j + 1 : 4 * j + 2]
            frequency, phase = columns[:, 4 * j + 2 : 4 * j + 3], columns[:, 4 * j + 3 : 4 * j + 4]
            sine, cosine = sin_cos(frequency * places[:, 0:LANES] + phase)
            turn_sin, turn_cos = turns[j]
            for n in range(CHUNK // LANES):
                width = sharpness * (places[:, block(n)] - centre)
                bell = jnp.exp(-0.5 * width * width)
                here = pl.ds(pl.multiple_of(i * CHUNK + n * LANES, LANES), LANES)
                tab[F_TABLE[j], :, here] = bell * sine
                tab[C_TABLE[j], :, here] = bell * cosine
                sine, cosine = sine * turn_cos + cosine * turn_sin, cosine * turn_cos - sine * turn_sin
        return carry

    lax.fori_loop(0, SAMPLES // CHUNK, step, 0)
    weights = [stacked_weight(hidden_w[0]), stacked_weight(hidden_w[1]), stacked_weight(own[:, 0:32])]
    u_1 = stacked_dot(weights[0], tab[0]) + columns[:, 12:13]
    z_1 = u_1 * tab[4]
    tab[2] = z_1
    tab[3] = u_1 * tab[3]
    u_2 = stacked_dot(weights[1], z_1) + columns[:, 13:14]
    z_2 = u_2 * tab[7]
    tab[5] = z_2
    tab[6] = u_2 * tab[6]
    raw = stacked_dot(weights[2], z_2) + own[:, 32:33]
    times, _ = sample_rows(0, SAMPLES)
    rows[...] = raw * envelope_of(times, own)


def generate_back(kernel_grad, columns, hidden_w, own, tab, rows, sums, mats):
    rows[...] = jnp.zeros(rows.shape, F32)
    for part in range(OWN):
        grad = kernel_grad(part)
        for n in range(64):
            rows[part : part + 1, block(n)] = grad[n : n + 1, :]
    sums[...] = jnp.zeros(sums.shape, F32)
    mats[...] = jnp.zeros(mats.shape, F32)
    turned = jnp.transpose(jnp.concatenate([own[...], jnp.zeros((120, 128), F32)], axis=0))
    weight = [turned[0:32, part : part + 1] for part in range(OWN)]
    back = [stacked_weight(jnp.transpose(hidden_w[j])) for j in range(2)]

    def fold(value):
        acc = value[:, block(0)]
        for i in range(1, CHUNK // LANES):
            acc = acc + value[:, block(i)]
        return acc

    def add(k, value):
        sums[block(k, 32), :] += fold(value)

    def step(i, carry):
        span = pl.ds(pl.multiple_of(i * CHUNK, CHUNK), CHUNK)
        times, places = sample_rows(i * CHUNK, CHUNK)
        draw = rows[:, span] * envelope_of(times, own)
        dz_2 = weight[0] * draw[0:1, :] + weight[1] * draw[1:2, :] + weight[2] * draw[2:3, :]

        def level(j, e_value, g_value):
            centre = columns[:, 4 * j + 1 : 4 * j + 2]
            offset = places - centre
            moment = e_value * offset
            add(4 * j, moment * offset)
            add(4 * j + 1, moment)
            add(4 * j + 2, g_value * places)
            add(4 * j + 3, g_value)

        z_2 = tab[5, :, span]
        level(2, dz_2 * z_2, dz_2 * tab[6, :, span])
        du_2 = dz_2 * tab[7, :, span]
        add(13, du_2)
        dz_1 = stacked_dot(back[1], du_2)
        z_1 = tab[2, :, span]
        level(1, dz_1 * z_1, dz_1 * tab[3, :, span])
        du_1 = dz_1 * tab[4, :, span]
        add(12, du_1)
        dz_0 = stacked_dot(back[0], du_1)
        z_0 = tab[0, :, span]
        level(0, dz_0 * z_0, dz_0 * tab[1, :, span])
        sums[14 * 32 : 14 * 32 + 8, :] += fold(draw)
        left = jnp.concatenate([du_1, du_2, draw], axis=0)
        right = jnp.concatenate([z_0, z_1, z_2, jnp.zeros_like(z_0)], axis=0)
        left_high, right_high = left.astype(BF16), right.astype(BF16)
        left_low = (left - left_high.astype(F32)).astype(BF16)
        right_low = (right - right_high.astype(F32)).astype(BF16)
        mats[...] += (
            dot_rows(left_high, right_high) + dot_rows(left_low, right_high) + dot_rows(left_high, right_low)
        )
        return carry

    lax.fori_loop(0, SAMPLES // CHUNK, step, 0, unroll=2)
    lane = lax.broadcasted_iota(jnp.int32, (32, LANES), 1)
    hidden = jnp.where(lane < 32, mats[0:32, :], jnp.where(lane < 64, mats[32:64, :], 0.0))

    def column(k):
        return jnp.sum(sums[block(k, 32), :], axis=1, keepdims=True)

    hidden = jnp.where(lane == 64, column(12), hidden)
    hidden = jnp.where(lane == 65, column(13), hidden)
    for j in range(3):
        sharpness = columns[:, 4 * j : 4 * j + 1]
        hidden = jnp.where(lane == 66 + 4 * j, -sharpness * column(4 * j), hidden)
        hidden = jnp.where(lane == 67 + 4 * j, sharpness * sharpness * column(4 * j + 1), hidden)
        hidden = jnp.where(lane == 68 + 4 * j, column(4 * j + 2), hidden)
        hidden = jnp.where(lane == 69 + 4 * j, column(4 * j + 3), hidden)
    lane8 = lax.broadcasted_iota(jnp.int32, (8, LANES), 1)
    outer = pltpu.roll(mats[64:72, :], LANES - 64, 1)
    raw_total = jnp.sum(sums[14 * 32 : 14 * 32 + 8, :], axis=1, keepdims=True)
    outer = jnp.where(lane8 < 32, outer, 0.0)
    outer = jnp.where(lane8 == 32, raw_total, outer)
    return hidden, outer


def with_norm_sums(outer, sums):
    row = lax.broadcasted_iota(jnp.int32, (8, LANES), 0)
    lane = lax.broadcasted_iota(jnp.int32, (8, LANES), 1)
    for part in range(OWN):
        gain_total, bias_total = sums[part]
        outer = jnp.where((row == part) & (lane == 33), gain_total, outer)
        outer = jnp.where((row == part) & (lane == 34), bias_total, outer)
    return outer


def one_row(outer):
    lane = lax.broadcasted_iota(jnp.int32, (1, LANES), 1)
    result = jnp.zeros((1, LANES), F32)
    for part in range(OWN):
        row = outer[part : part + 1, :]
        moved = pltpu.roll(row, 32 * part, 1) if part else row
        result = jnp.where((lane >= 32 * part) & (lane < 32 * part + 32), moved, result)
        moved = pltpu.roll(row, 64 + 3 * part, 1)
        result = jnp.where((lane >= 96 + 3 * part) & (lane < 99 + 3 * part), moved, result)
    return result


def packed_hidden(hidden):
    lane16 = lax.broadcasted_iota(jnp.int32, (16, LANES), 1)
    upper = jnp.where(lane16 < 64, hidden[0:16, :], pltpu.roll(hidden[16:32, :], 64, 1))
    lane4 = lax.broadcasted_iota(jnp.int32, (4, LANES), 1)
    lower = jnp.zeros((4, LANES), F32)
    for g in range(8):
        moved = pltpu.roll(hidden, (64 + 16 * g) % LANES, 1)[4 * g : 4 * g + 4, :]
        lower = jnp.where((lane4 >= 16 * g) & (lane4 < 16 * g + 16), moved, lower)
    return upper, lower


def unpacked_hidden(upper, lower):
    lane16 = lax.broadcasted_iota(jnp.int32, (16, LANES), 1)
    lane32 = lax.broadcasted_iota(jnp.int32, (32, LANES), 1)
    top = jnp.concatenate([upper, pltpu.roll(upper, 64, 1)], axis=0)
    tiled = jnp.concatenate([lower] * 8, axis=0)
    row32 = lax.broadcasted_iota(jnp.int32, (32, LANES), 0)
    rest = jnp.zeros((32, LANES), F32)
    for g in range(8):
        moved = pltpu.roll(tiled, (64 - 16 * g) % LANES, 1)
        rest = jnp.where((row32 >= 4 * g) & (row32 < 4 * g + 4), moved, rest)
    return jnp.where(lane32 < 64, top, rest)


def high_low(value):
    high = value.astype(BF16).astype(F32)
    return high, value - high


def valid_row(meta, i):
    lane = lax.broadcasted_iota(jnp.int32, (1, LANES), 1)
    return (meta[2] * PIECE + (i // 2) * LANES + lane < meta[i % 2]).astype(F32)


def masked(meta, rows):
    mask = jnp.concatenate([valid_row(meta, i) for i in range(4)] * 2, axis=0)
    return (rows.reshape(-1, 8, LANES) * mask[None]).reshape(-1, LANES)


CLIP_ROWS = 4 * CHANNELS
PADDED_ROWS = 4 * PADDED


def put_padded(padded, rows):
    padded[0:CLIP_ROWS, :] = rows
    padded[CLIP_ROWS:PADDED_ROWS, :] = jnp.zeros((PADDED_ROWS - CLIP_ROWS, LANES), F32)


def rows_to_message(padded, out, step, base):
    for m in range(12):
        out[pl.ds(base + m, DEVICES, stride=step), :] = padded[pl.ds(m, DEVICES, stride=12), :]


def rows_of_channels(padded, i):
    return padded[pl.ds(i, PADDED, stride=4), :]


def source_kernel(meta, x_ref, mix_w, out_ref, padded, out):
    put_padded(padded, masked(meta, x_ref[...]))
    for b in range(2):
        length = meta[b]
        upper = lax.shift_right_logical(length, 7)
        out[pl.ds(12 + 2 * b, DEVICES, stride=16), :] = jnp.full((DEVICES, LANES), upper.astype(F32))
        out[pl.ds(13 + 2 * b, DEVICES, stride=16), :] = jnp.full(
            (DEVICES, LANES), (length - upper * 128).astype(F32)
        )
    rows_to_message(padded, out, 16, 0)
    out_ref[...] = out[...].reshape(DEVICES, 16, LANES).astype(BF16)


def make_lookup(lookup):
    row = lax.broadcasted_iota(jnp.int32, (DEVICES, PADDED), 0)
    column = lax.broadcasted_iota(jnp.int32, (DEVICES, PADDED), 1)
    for part in range(OWN):
        lookup[block(part), :] = (column == OWN * row + part).astype(F32).astype(BF16)


def make_weights(mix_w, mix_b, wide, lookup, weights, weights_back):
    make_lookup(lookup)
    wide[...] = jnp.zeros(wide.shape, BF16)
    row = lax.broadcasted_iota(jnp.int32, (LANES, CHANNELS), 0)
    lines = jnp.where(row == 0, mix_b[0:1, :], jnp.where(row == 1, mix_b[1:2, :], 0.0))
    turned = jnp.transpose(jnp.concatenate([lines, jnp.zeros((LANES, PADDED - CHANNELS), F32)], axis=1))
    lane = lax.broadcasted_iota(jnp.int32, (PADDED, PADDED), 1)
    for layer in range(2):
        wide[0:CHANNELS, 0:CHANNELS] = mix_w[layer]
        weights_back[layer] = dot_rows(lookup[...], wide[...]).astype(BF16)
        value = dot_rows(wide[...], lookup[...])
        rest = turned[:, layer : layer + 1]
        for spot in SPOTS:
            high, rest = high_low(rest)
            value = jnp.where(lane == spot, high, value)
        weights[layer] = value.astype(BF16)


def make_kernel(layer, meta, params, consts, bundle, tab, scratch):
    out_w, out_b, window, gain, bias, gabor, hidden_b, hidden_w = params
    first, second, _, twiddle = consts
    wide, tall, rows, pieces, x_ref, high, low = scratch
    own, columns = bundle.at[OWN_ROWS, :], bundle.at[COLUMN_ROWS, :]
    own_parameters(layer, meta[3], out_w, out_b, window, gain, bias, gabor, hidden_b, wide, tall, own, columns)
    generate(columns, hidden_w.at[layer], own, tab, rows)
    for n in range(64):
        for part in range(OWN):
            pieces[part * 64 + n : part * 64 + n + 1, :] = rows[part : part + 1, block(n)]
    for part in range(OWN):
        piece = pieces[block(part, 64), :].astype(BF16)
        x_ref[0:64, block(part)] = piece
        x_ref[64:128, block(part)] = piece
        x_ref[128:256, block(part)] = jnp.zeros((128, LANES), BF16)
    spec = transform(x_ref, high, low, first, second, twiddle, OWN)
    bundle[0:SPEC_IM, :] = spec[:, RE]
    bundle[SPEC_IM : 2 * SPEC_IM, :] = spec[:, IM]


def forward_kernel(
    meta, message_ref, out_w, out_b, window, gain, bias, gabor, hidden_b, hidden_w,
    first, second, last, twiddle,
    out_ref, spec_ref, normed_ref, slope_ref, inv_ref, len_ref, kernel_spec, tab,
    message, x_ref, high, low, e_high, e_low, y_ref, out, *make_scratch,
):
    own = kernel_spec.at[OWN_ROWS, :]
    params = (out_w, out_b, window, gain, bias, gabor, hidden_b, hidden_w)
    make_kernel(0, meta, params, (first, second, last, twiddle), kernel_spec, tab, make_scratch)
    message[...] = spread(message_ref[...])
    for y in range(4):
        for b in range(2):
            start = y * 16 + 12 + 2 * b
            len_ref[2 * y + b : 2 * y + b + 1, :] = (
                message[start : start + 1, :] * 128.0 + message[start + 1 : start + 2, :]
            )
    load_signals(message, 16, x_ref)
    convolve(x_ref, spec_ref, kernel_spec, high, low, e_high, e_low, (first, second, last, twiddle), y_ref)
    valid, tally = valid_of(len_ref), tally_of(len_ref)
    inv_ref[...] = jnp.zeros((8, LANES), F32)
    for part in range(OWN):
        normed, inv_std, active, slope = normalise(y_ref, own, valid, tally, part)
        normed_ref[:, block(part, 512)] = normed
        slope_ref[:, block(part, 512)] = slope
        inv_ref[part : part + 1, :] = jnp.broadcast_to(inv_std, (1, LANES))
        y_ref[:, block(part, 512)] = active
    store_signals(out, 16, 0, lambda part, y: y_ref[:, block(part * 4 + y)])
    out_ref[...] = out[...].reshape(DEVICES, 16, LANES).astype(BF16)


def gather_active(message, step, rhs):
    row = lax.broadcasted_iota(jnp.int32, (DEVICES, LANES), 0)
    for i in range(4):
        for part in range(OWN):
            piece = message[pl.ds(part * 4 + i, DEVICES, stride=step), :]
            if part != 1:
                piece = jnp.where(row >= (126 if part == 2 else 127), 1.0, piece)
            rhs[block(part), block(i)] = piece.astype(BF16)


def store_rows(value, out, step, base):
    for i in range(4):
        for part in range(OWN):
            out[pl.ds(base + part * 4 + i, DEVICES, stride=step), :] = value[block(part), block(i)]


def mix_kernel(
    meta, message_ref, x_ref, cotangent, mix_w, mix_b,
    out_ref, next_ref, active_ref, weights, weights_back, message, padded, out, low, wide, lookup,
):
    make_weights(mix_w, mix_b, wide, lookup, weights, weights_back)
    message[...] = spread(message_ref[...])
    gather_active(message, 16, active_ref)
    mixed = dot(weights[0], active_ref[...])
    put_padded(padded, x_ref[...])
    for i in range(4):
        valid = valid_row(meta, i)
        value = rows_of_channels(padded, i) + mixed[:, block(i)] * valid
        next_ref[pl.ds(i, PADDED, stride=4), :] = value
        padded[pl.ds(i, PADDED, stride=4), :] = value * valid
    rows_to_message(padded, out, 24, 0)
    put_padded(padded, masked(meta, cotangent[...]))
    for i in range(4):
        low[:, block(i)] = rows_of_channels(padded, i).astype(BF16)
    store_rows(dot(weights_back[1], low[...]), out, 24, 12)
    out_ref[...] = out[...].reshape(DEVICES, 24, LANES).astype(BF16)


def forward_backward_kernel(
    meta, message_ref, out_w, out_b, window, gain, bias, gabor, hidden_b, hidden_w,
    len_ref, first, second, last, twiddle,
    out_ref, hidden_out, outer_out,
    message, x_ref, high, low, e_high, e_low, y_ref, out, spec_ref, grad_ref, normed_ref, slope_ref, returned_ref,
    rows, sums, mats, kernel_spec, tab, *make_scratch,
):
    own, columns = kernel_spec.at[OWN_ROWS, :], kernel_spec.at[COLUMN_ROWS, :]
    consts = (first, second, last, twiddle)
    params = (out_w, out_b, window, gain, bias, gabor, hidden_b, hidden_w)
    make_kernel(1, meta, params, consts, kernel_spec, tab, make_scratch)
    message[...] = spread(message_ref[...])
    load_signals(message, 24, x_ref)
    convolve(x_ref, spec_ref, kernel_spec, high, low, e_high, e_low, consts, y_ref)
    valid, tally = valid_of(len_ref), tally_of(len_ref)
    inv = []
    for part in range(OWN):
        normed, inv_std, active, slope = normalise(y_ref, own, valid, tally, part)
        normed_ref[:, block(part, 512)] = normed
        slope_ref[:, block(part, 512)] = slope
        inv.append(inv_std)
        y_ref[:, block(part, 512)] = active
    store_signals(out, 24, 0, lambda part, y: y_ref[:, block(part * 4 + y)])
    returned, norm_sums = conv_backward(
        message, 24, 12, lambda part: normed_ref[:, block(part, 512)], lambda part: slope_ref[:, block(part, 512)],
        lambda part: inv[part], own, valid, tally, spec_ref, kernel_spec, x_ref, high, low, e_high, e_low, consts, grad_ref,
    )
    returned_ref[...] = returned
    store_signals(out, 24, 12, lambda part, y: returned_ref[:, block(part * 4 + y)])
    out_ref[...] = out[...].reshape(DEVICES, 24, LANES).astype(BF16)
    hidden, outer = generate_back(
        lambda part: returned_ref[0:64, block(SIGNALS + part)], columns, hidden_w.at[1], own, tab,
        rows, sums, mats,
    )
    hidden_out[...] = hidden
    outer_out[...] = with_norm_sums(outer, norm_sums)


def middle_kernel(
    meta, message_ref, x_ref, cotangent, weights, weights_back, active_0, hidden_1,
    output_ref, flow_ref, out_ref, message, padded, out, low_0, low_1, active_1,
):
    message[...] = spread(message_ref[...])
    gather_active(message, 24, active_1)
    mixed = dot(weights[1], active_1[...])
    for i in range(4):
        padded[pl.ds(i, PADDED, stride=4), :] = rows_of_channels(x_ref, i) + mixed[:, block(i)] * valid_row(meta, i)
    output_ref[...] = padded[0:CLIP_ROWS, :]
    put_padded(flow_ref, cotangent[...])
    for i in range(4):
        low_1[:, block(i)] = (rows_of_channels(flow_ref, i) * valid_row(meta, i)).astype(BF16)
    for m in range(12):
        padded[pl.ds(m, DEVICES, stride=12), :] = message[pl.ds(12 + m, DEVICES, stride=24), :]
    flow_ref[...] += masked(meta, padded[...])
    for i in range(4):
        low_0[:, block(i)] = (rows_of_channels(flow_ref, i) * valid_row(meta, i)).astype(BF16)
    store_rows(dot(weights_back[0], low_0[...]), out, 32, 0)
    for layer, (active, low) in enumerate(((active_0, low_0), (active_1, low_1))):
        part_sum = dot_rows(active[...], low[...])
        for part in range(OWN):
            for third in range(3):
                out[pl.ds(12 + layer * 9 + part * 3 + third, DEVICES, stride=32), :] = part_sum[
                    block(part), block(third)
                ]
    high, low = high_low(hidden_1[...])
    out[pl.ds(30, DEVICES, stride=32), :] = jnp.concatenate([high, jnp.zeros((96, LANES), F32)], axis=0)
    out[pl.ds(31, DEVICES, stride=32), :] = jnp.concatenate([low, jnp.zeros((96, LANES), F32)], axis=0)
    out_ref[...] = out[...].reshape(DEVICES, 32, LANES).astype(BF16)


LAST_ROWS = 56


def backward_kernel(
    message_ref, spec_ref, kernel_spec, normed_ref, slope_ref, inv_ref, len_ref,
    first, second, last, twiddle, hidden_w, tab, outer_1,
    out_ref,
    message, x_ref, high, low, e_high, e_low, out, grad_ref, returned_ref, rows, sums, mats,
):
    own, columns = kernel_spec.at[OWN_ROWS, :], kernel_spec.at[COLUMN_ROWS, :]
    consts = (first, second, last, twiddle)
    message[...] = spread(message_ref[...])
    valid, tally = valid_of(len_ref), tally_of(len_ref)
    returned, norm_sums = conv_backward(
        message, 32, 0, lambda part: normed_ref[:, block(part, 512)], lambda part: slope_ref[:, block(part, 512)],
        lambda part: inv_ref[part : part + 1, 0:1], own, valid, tally, spec_ref, kernel_spec, x_ref, high, low,
        e_high, e_low, consts, grad_ref,
    )
    returned_ref[...] = returned
    store_signals(out, 16, 0, lambda part, y: returned_ref[:, block(part * 4 + y)])
    hidden, outer = generate_back(
        lambda part: returned_ref[0:64, block(SIGNALS + part)], columns, hidden_w.at[0], own, tab,
        rows, sums, mats,
    )
    outer = with_norm_sums(outer, norm_sums)
    gathered = jnp.sum(message[...].reshape(DEVICES, 32, LANES), axis=0)
    upper, lower = packed_hidden(hidden)
    hidden_1_high, hidden_1_low = high_low(gathered[30:31, :] + gathered[31:32, :])
    outer_0_high, outer_0_low = high_low(one_row(outer))
    outer_1_high, outer_1_low = high_low(one_row(outer_1[...]))
    shared = jnp.concatenate(
        [
            gathered[0:30, :], upper, lower, hidden_1_high, hidden_1_low,
            outer_0_high, outer_0_low, outer_1_high, outer_1_low,
        ],
        axis=0,
    )
    row = lax.broadcasted_iota(jnp.int32, (DEVICES, 16, LANES), 1)
    own_rows = jnp.where(row < 12, out[...].reshape(DEVICES, 16, LANES), shared[None, 0:16, :])
    rest = jnp.broadcast_to(shared[None, 16:LAST_ROWS, :], (DEVICES, LAST_ROWS - 16, LANES))
    out_ref[...] = jnp.concatenate([own_rows, rest], axis=1).astype(BF16)


def last_kernel(
    meta, message_ref, flow_ref,
    input_grad, gabor_grad, hidden_w_grad, hidden_b_grad, out_w_grad, out_b_grad, gain_grad, bias_grad,
    mix_w_grad, mix_b_grad, message, padded, owned, thirds, lookup,
):
    make_lookup(lookup)
    message[...] = spread(message_ref[...])

    def rows_of(k, count=DEVICES):
        return message[pl.ds(k, count, stride=LAST_ROWS), :]

    for m in range(12):
        padded[pl.ds(m, DEVICES, stride=12), :] = rows_of(m)
    input_grad[...] = flow_ref[0:CLIP_ROWS, :] + masked(meta, padded[0:CLIP_ROWS, :])
    shared = jnp.sum(message[...].reshape(DEVICES, LAST_ROWS, LANES)[:, 24:56, :], axis=0)
    hidden_0 = unpacked_hidden(shared[6:22, :], shared[22:26, :])
    hidden_1 = rows_of(50, 32) + rows_of(51, 32)
    lane = lax.broadcasted_iota(jnp.int32, (DEVICES, LANES), 1)
    for layer, hidden in enumerate((hidden_0, hidden_1)):
        hidden_w_grad[layer, 0] = hidden[:, 0:32]
        hidden_w_grad[layer, 1] = pltpu.roll(hidden, 96, 1)[:, 0:32]
        turned = jnp.transpose(jnp.concatenate([hidden, jnp.zeros((96, LANES), F32)], axis=0))
        hidden_b_grad[layer] = turned[64:66, 0:32]
        for j in range(3):
            gabor_grad[layer, j] = turned[66 + 4 * j : 70 + 4 * j, 0:32]
        value = rows_of(52 + 2 * layer) + rows_of(53 + 2 * layer)
        for part in range(OWN):
            wide = pltpu.roll(value, (LANES - 32 * part) % LANES, 1)
            small = pltpu.roll(value, 64 - 3 * part, 1)
            owned[pl.ds(part, DEVICES, stride=OWN), :] = jnp.where(lane < 32, wide, small)
        turned = jnp.transpose(owned[...])
        out_w_grad[layer] = turned[0:32, 0:CHANNELS]
        out_b_grad[layer : layer + 1, :] = turned[32:33, 0:CHANNELS]
        gain_grad[layer : layer + 1, :] = turned[33:34, 0:CHANNELS]
        bias_grad[layer : layer + 1, :] = turned[34:35, 0:CHANNELS]
        bias_rows = []
        for part in range(OWN):
            for third in range(3):
                piece = rows_of(12 + layer * 9 + part * 3 + third)
                thirds[block(part), block(third)] = piece.astype(BF16)
                if part == 2:
                    bias_rows.append(piece[SPOT - 2 * DEVICES : SPOT - 2 * DEVICES + 1, :])
        mix_w_grad[:, layer, :] = dot_columns(thirds[...], lookup[...])[0:CHANNELS, 0:CHANNELS]
        mix_b_grad[layer : layer + 1, :] = jnp.concatenate(bias_rows, axis=1)[:, 0:CHANNELS]


def exchange(message):
    return lax.all_to_all(message, AXES, split_axis=0, concat_axis=0, tiled=True)


def to_rows(clips):
    return clips.reshape(2, CHANNELS, 2, LANES).transpose(1, 2, 0, 3).reshape(CLIP_ROWS, LANES)


def from_rows(rows):
    return rows.reshape(CHANNELS, 2, 2, LANES).transpose(2, 0, 1, 3).reshape(2, CHANNELS, PIECE)


def shards(
    inputs, lengths, window, gabor_params, hidden_w, hidden_b, out_w, out_b, bn_gain, bn_bias, mix_w, mix_b, cotangent
):
    position = lax.axis_index("seq").astype(jnp.int32)
    number = position * 4 + lax.axis_index("clips").astype(jnp.int32)
    const = {name: jnp.asarray(value) for name, value in TABLES.items()}
    meta = jnp.concatenate([lengths, jnp.stack([position, number])])
    inputs, cotangent = to_rows(inputs), to_rows(cotangent)

    def rows(count):
        return ((count, LANES), F32)

    with jax.named_scope("source_0"):
        (message,) = run(
            source_kernel, [((DEVICES, 16, LANES), BF16)], [meta, inputs, mix_w],
            [rows(PADDED_ROWS), rows(DEVICES * 16)], "source_0", 8, smem=(0,), far=(2,),
        )
        message = exchange(message)

    square = (PADDED, PADDED)
    generator = [
        jnp.swapaxes(out_w, 1, 2), out_b, jnp.swapaxes(window, 1, 2), bn_gain, bn_bias, gabor_params, hidden_b,
        hidden_w,
    ]
    shape_tab = ((8, HIDDEN, SAMPLES), F32)
    make_scratch = [
        ((LANES, PADDED), F32), rows(PADDED + 8), ((8, SAMPLES), F32), rows(192),
        ((256, OWN * LANES), BF16), ((OWN * LANES, 256), BF16), ((OWN * LANES, 256), BF16),
    ]
    mixers = ((2, *square), BF16)

    def scratch(signals):
        count = signals * LANES
        return [
            ((256, SIGNALS * LANES), BF16), ((count, 256), BF16), ((count, 256), BF16),
            ((256, count), BF16), ((256, count), BF16),
        ]

    shape_y = (LANES, SIGNALS * LANES)
    shape_s = (SIGNALS * LANES, 256)
    transforms = [const[name] for name in TABLE_NAMES]
    with jax.named_scope("conv_0"):
        message, spec_0, normed_0, slope_0, inv_0, lens, bundle_0, tab_0 = run(
            forward_kernel,
            [
                ((DEVICES, 16, LANES), BF16), (shape_s, F32), (shape_y, F32), (shape_y, F32), rows(8), rows(8),
                rows(BUNDLE), shape_tab,
            ],
            [meta, message, *generator, *transforms],
            [rows(DEVICES * 16), *scratch(SIGNALS), (shape_y, F32), rows(DEVICES * 16), *make_scratch],
            "conv_0", 16, smem=(0,),
        )
        message = exchange(message)

    with jax.named_scope("mix_0"):
        message, middle, active_0, weights, weights_back = run(
            mix_kernel,
            [((DEVICES, 24, LANES), BF16), rows(PADDED_ROWS), ((PADDED, 512), BF16), mixers, mixers],
            [meta, message, inputs, cotangent, mix_w, mix_b],
            [rows(DEVICES * 16), rows(PADDED_ROWS), rows(DEVICES * 24), ((PADDED, 512), BF16), (square, BF16), (square, BF16)],
            "mix_0", 12, smem=(0,),
        )
        message = exchange(message)

    back_scratch = [((8, SAMPLES), F32), rows(14 * 32 + 8), rows(72)]
    with jax.named_scope("conv_1"):
        message, hidden_1, outer_1 = run(
            forward_backward_kernel,
            [((DEVICES, 24, LANES), BF16), rows(HIDDEN), rows(8)],
            [
                meta, message, *generator, lens, *transforms,
            ],
            [
                rows(DEVICES * 24), *scratch(SIGNALS + OWN), (shape_y, F32), rows(DEVICES * 24),
                (shape_s, F32), (shape_s, F32), (shape_y, F32), (shape_y, F32),
                ((LANES, (SIGNALS + OWN) * LANES), F32), *back_scratch, rows(BUNDLE), shape_tab, *make_scratch,
            ],
            "conv_1", 26, smem=(0,),
        )
        message = exchange(message)

    with jax.named_scope("mix_1"):
        outputs, flow, message = run(
            middle_kernel,
            [rows(CLIP_ROWS), rows(PADDED_ROWS), ((DEVICES, 32, LANES), BF16)],
            [meta, message, middle, cotangent, weights, weights_back, active_0, hidden_1],
            [
                rows(DEVICES * 24), rows(PADDED_ROWS), rows(DEVICES * 32),
                ((PADDED, 512), BF16), ((PADDED, 512), BF16), ((PADDED, 512), BF16),
            ],
            "mix_1", 12, smem=(0,),
        )
        message = exchange(message)

    with jax.named_scope("conv_back_0"):
        (message,) = run(
            backward_kernel,
            [((DEVICES, LAST_ROWS, LANES), BF16)],
            [
                message, spec_0, bundle_0, normed_0, slope_0, inv_0, lens, *transforms,
                hidden_w, tab_0, outer_1,
            ],
            [
                rows(DEVICES * 32), *scratch(SIGNALS + OWN), rows(DEVICES * 16), (shape_s, F32),
                ((LANES, (SIGNALS + OWN) * LANES), F32), *back_scratch,
            ],
            "conv_back_0", 16,
        )
        message = exchange(message)

    with jax.named_scope("gradients"):
        (
            input_grad, gabor_grad, hidden_w_grad, hidden_b_grad, out_w_grad, out_b_grad, gain_grad, bias_grad,
            mix_w_grad, mix_b_grad,
        ) = run(
            last_kernel,
            [
                rows(CLIP_ROWS), (gabor_params.shape, F32), (hidden_w.shape, F32), (hidden_b.shape, F32),
                ((2, HIDDEN, CHANNELS), F32), (out_b.shape, F32), (bn_gain.shape, F32), (bn_bias.shape, F32),
                ((CHANNELS, 2, CHANNELS), F32), (mix_b.shape, F32),
            ],
            [meta, message, flow],
            [rows(DEVICES * LAST_ROWS), rows(PADDED_ROWS), rows(PADDED), (square, BF16), (square, BF16)],
            "gradients", 14, smem=(0,),
        )
    return (
        from_rows(outputs), from_rows(input_grad), gabor_grad, hidden_w_grad, hidden_b_grad,
        jnp.swapaxes(out_w_grad, 1, 2), out_b_grad, gain_grad, bias_grad, jnp.swapaxes(mix_w_grad, 0, 1), mix_b_grad,
    )


def solution(mesh):
    clip = P("clips", None, "seq")
    in_specs = (clip, P("clips")) + (P(),) * 10 + (clip,)
    out_specs = (clip, clip) + (P(),) * 9
    return jax.shard_map(shards, mesh=mesh, in_specs=in_specs, out_specs=out_specs, check_vma=False)
```

```python
import math

import jax
import jax.numpy as jnp
import ml_dtypes
import numpy as np
from jax import lax
from jax.experimental import pallas as pl
from jax.experimental.pallas import tpu as pltpu
from jax.sharding import PartitionSpec as P

F32 = jnp.float32
BF16 = jnp.bfloat16
AXES = ("seq", "clips")
DEVICES = 128
OWN = 3
CHANNELS = 380
PADDED = DEVICES * OWN
SAMPLES = 8192
PIECE = 256
HIDDEN = 32
LANES = 128
SIGNALS = 12
TABLE_NAMES = ("first", "second", "last", "twiddle")
PERIOD = 2 * SAMPLES
EPSILON = 1e-05
MEGABYTE = 1024 * 1024
EXACT = lax.Precision.HIGHEST
SPOTS = (2 * DEVICES + 126, 2 * DEVICES + 127, 127)
SPOT = SPOTS[0]


def halves(table):
    high = table.astype(ml_dtypes.bfloat16)
    low = (table - high.astype(np.float64)).astype(ml_dtypes.bfloat16)
    return high, low


def tables():
    order = np.array([2 * j + r for r in range(2) for j in range(32)])
    k = np.arange(LANES)
    turn = 2 * np.pi * ((k[:, None] * order[None, :]) % LANES) / LANES
    c_high, c_low = halves(np.cos(turn))
    s_high, s_low = halves(np.sin(turn))
    first = np.concatenate(
        [
            np.concatenate([c_high, c_low, s_high, s_low], axis=1),
            np.concatenate([-s_high, -s_low, c_high, c_low], axis=1),
        ],
        axis=0,
    )
    turn = 2 * np.pi * ((k[:, None] * k[None, :]) % LANES) / LANES
    cosine, sine = np.cos(turn), np.sin(turn)
    second = halves(np.block([[cosine, -sine], [sine, cosine]]))
    turn = 2 * np.pi * ((order[:, None] * k[None, :]) % LANES) / LANES
    cosine, sine = np.cos(turn) / PERIOD, np.sin(turn) / PERIOD
    last = halves(np.block([[cosine, -sine], [sine, cosine]]))
    turn = 2 * np.pi * (k[:, None] * k[None, :]) / PERIOD
    twiddle = np.stack([np.cos(turn), np.sin(turn)]).astype(np.float32)
    return dict(
        first=first,
        second=np.stack(second),
        last=np.stack(last),
        twiddle=twiddle,
    )


TABLES = tables()


def run(body, outs, args, scratch, name, grant, smem=(), far=(), far_outs=(), copies=0):
    spaces = [pltpu.HBM if i in far else pltpu.SMEM if i in smem else pltpu.VMEM for i in range(len(args))]
    return pl.pallas_call(
        body,
        out_shape=[jax.ShapeDtypeStruct(shape, kind) for shape, kind in outs],
        in_specs=[pl.BlockSpec(memory_space=space) for space in spaces],
        out_specs=[
            pl.BlockSpec(memory_space=pltpu.HBM if i in far_outs else pltpu.VMEM) for i in range(len(outs))
        ],
        scratch_shapes=[pltpu.VMEM(shape, kind) for shape, kind in scratch]
        + ([pltpu.SemaphoreType.DMA((copies,))] if copies else []),
        compiler_params=pltpu.CompilerParams(vmem_limit_bytes=grant * MEGABYTE),
        name=name,
    )(*args)


def dot(a, b):
    return jnp.dot(a, b, preferred_element_type=F32)


def dot_rows(a, b, precision=None):
    return lax.dot_general(a, b, (((1,), (1,)), ((), ())), precision=precision, preferred_element_type=F32)


def dot_columns(a, b, precision=None):
    return lax.dot_general(a, b, (((0,), (0,)), ((), ())), precision=precision, preferred_element_type=F32)


def triple(a_high, a_low, b_high, b_low):
    left = jnp.concatenate([a_high, a_low, a_high], axis=1)
    return dot(left, jnp.concatenate([b_high, b_high, b_low], axis=0))


def triple_rows(a_high, a_low, b_high, b_low):
    left = jnp.concatenate([a_high, a_low, a_high], axis=1)
    return dot_rows(left, jnp.concatenate([b_high, b_high, b_low], axis=1))


def put_halves(high_ref, low_ref, rows, columns, value):
    high = value.astype(BF16)
    high_ref[rows, columns] = high
    low_ref[rows, columns] = (value - high.astype(F32)).astype(BF16)


def block(i, size=LANES):
    return slice(i * size, (i + 1) * size)


RE, IM = slice(0, LANES), slice(LANES, 2 * LANES)


def signal_row(b, part, r):
    return part * 4 + r * 2 + b


def spread(message):
    return message.astype(F32).reshape(-1, LANES)


def transform(x_ref, high_ref, low_ref, first, second, twiddle, count):
    part_a = dot(first[...], x_ref[:, : count * LANES])
    cosine, sine = twiddle[0], twiddle[1]
    for s in range(count):
        real, imag = part_a[:LANES, block(s)], part_a[LANES:, block(s)]
        put_halves(high_ref, low_ref, block(s), RE, real * cosine + imag * sine)
        put_halves(high_ref, low_ref, block(s), IM, imag * cosine - real * sine)
    rows = slice(0, count * LANES)
    return triple(high_ref[rows, :], low_ref[rows, :], second[0], second[1])


def transform_back(high_ref, low_ref, e_high, e_low, second, last, twiddle, count):
    rows = slice(0, count * LANES)
    part_d = triple_rows(high_ref[rows, :], low_ref[rows, :], second[0], second[1])
    cosine, sine = twiddle[0], twiddle[1]
    for s in range(count):
        real, imag = part_d[block(s), RE], part_d[block(s), IM]
        put_halves(e_high, e_low, RE, block(s), real * cosine - imag * sine)
        put_halves(e_high, e_low, IM, block(s), real * sine + imag * cosine)
    return triple(last[0], last[1], e_high[:, rows], e_low[:, rows])


def erf_parts(value):
    cdf = 0.5 * (1.0 + lax.erf(value * math.sqrt(0.5)))
    return cdf, jnp.exp(-0.5 * value * value) * (1.0 / math.sqrt(2.0 * math.pi))


def total(value):
    return jnp.sum(jnp.sum(value, axis=0, keepdims=True), axis=1, keepdims=True)


def times_of(row, lane):
    return (256 * (row & 31) + 128 * lax.shift_right_logical(row, 5 * jnp.ones_like(row)) + lane).astype(F32)


def valid_of(len_ref):
    row = lax.broadcasted_iota(jnp.int32, (LANES, LANES), 0) & 63
    times = times_of(row, lax.broadcasted_iota(jnp.int32, (LANES, LANES), 1))
    columns = []
    for y in range(4):
        upper = times[0:64, :] < len_ref[2 * y : 2 * y + 1, :]
        lower = times[64:128, :] < len_ref[2 * y + 1 : 2 * y + 2, :]
        columns.append(jnp.concatenate([upper, lower], axis=0).astype(F32))
    return jnp.concatenate(columns, axis=1)


def tally_of(len_ref):
    return jnp.sum(len_ref[:, 0:1], axis=0, keepdims=True)


def load_signals(message, step, x_ref):
    for part in range(OWN):
        for y in range(4):
            lanes = block(part * 4 + y)
            for b in range(2):
                for r in range(2):
                    start = y * step + signal_row(b, part, r)
                    piece = message[pl.ds(start, 32, stride=4 * step), :].astype(BF16)
                    x_ref[b * 128 + r * 32 : b * 128 + r * 32 + 32, lanes] = piece
                    x_ref[b * 128 + r * 32 + 64 : b * 128 + r * 32 + 96, lanes] = piece


def store_signals(out, step, base, get):
    for part in range(OWN):
        for y in range(4):
            value = get(part, y)
            for b in range(2):
                for r in range(2):
                    start = y * step + base + signal_row(b, part, r)
                    out[pl.ds(start, 32, stride=4 * step), :] = value[b * 64 + r * 32 : b * 64 + r * 32 + 32, :]


SPEC_IM = OWN * LANES
OWN_ROWS = slice(2 * SPEC_IM, 2 * SPEC_IM + 8)
COLUMN_ROWS = slice(2 * SPEC_IM + 8, 2 * SPEC_IM + 8 + HIDDEN)
BUNDLE = 2 * SPEC_IM + 8 + HIDDEN


def kernel_parts(bundle, part):
    return bundle[block(part), :], bundle[SPEC_IM + part * LANES : SPEC_IM + (part + 1) * LANES, :]


def convolve(x_ref, spec_ref, kernel_spec, high, low, e_high, e_low, consts, y_ref):
    first, second, last, twiddle = consts
    spec_ref[...] = transform(x_ref, high, low, first, second, twiddle, SIGNALS)
    for part in range(OWN):
        k_re, k_im = kernel_parts(kernel_spec, part)
        for y in range(4):
            rows = block(part * 4 + y)
            s_re, s_im = spec_ref[rows, RE], spec_ref[rows, IM]
            put_halves(high, low, rows, RE, s_re * k_re - s_im * k_im)
            put_halves(high, low, rows, IM, s_re * k_im + s_im * k_re)
    y_ref[...] = transform_back(high, low, e_high, e_low, second, last, twiddle, SIGNALS)


def normalise(y_ref, own, valid, tally, part):
    value = y_ref[:, block(part, 512)]
    mean = total(valid * value) / tally
    centred = value - mean
    var = total(valid * centred * centred) / tally
    inv_std = lax.rsqrt(var + EPSILON)
    normed = centred * inv_std
    pre_act = normed * own[part : part + 1, 35:36] + own[part : part + 1, 36:37]
    cdf, density = erf_parts(pre_act)
    return normed, inv_std, pre_act * cdf, cdf + pre_act * density


def conv_backward(
    message, step, base, normed_of, slope_of, inv_of, own, valid, tally, spec_ref, kernel_spec, x_ref, high, low,
    e_high, e_low, consts, grad_ref,
):
    first, second, last, twiddle = consts
    sums = []
    for part in range(OWN):
        columns = []
        for y in range(4):
            pieces = []
            for b in range(2):
                for r in range(2):
                    start = y * step + base + signal_row(b, part, r)
                    pieces.append(message[pl.ds(start, 32, stride=4 * step), :])
            columns.append(jnp.concatenate(pieces, axis=0))
        act_grad = jnp.concatenate(columns, axis=1)
        normed = normed_of(part)
        pre_grad = act_grad * slope_of(part)
        bias_total = total(pre_grad)
        gain_total = total(pre_grad * normed)
        gain = own[part : part + 1, 35:36]
        conv_grad = inv_of(part) * (
            gain * pre_grad - valid * (gain * bias_total + normed * (gain * gain_total)) / tally
        )
        conv_low = conv_grad.astype(BF16)
        for b in range(2):
            piece = conv_low[b * 64 : b * 64 + 64, :]
            x_ref[b * 128 : b * 128 + 64, block(part, 512)] = piece
            x_ref[b * 128 + 64 : b * 128 + 128, block(part, 512)] = piece
        sums.append((gain_total, bias_total))
    grad_ref[...] = transform(x_ref, high, low, first, second, twiddle, SIGNALS)
    for part in range(OWN):
        k_re, k_im = kernel_parts(kernel_spec, part)
        corr_re, corr_im = None, None
        for y in range(4):
            rows = block(part * 4 + y)
            g_re, g_im = grad_ref[rows, RE], grad_ref[rows, IM]
            s_re, s_im = spec_ref[rows, RE], spec_ref[rows, IM]
            put_halves(high, low, rows, RE, k_re * g_re + k_im * g_im)
            put_halves(high, low, rows, IM, k_re * g_im - k_im * g_re)
            now_re, now_im = s_re * g_re + s_im * g_im, s_re * g_im - s_im * g_re
            corr_re = now_re if corr_re is None else corr_re + now_re
            corr_im = now_im if corr_im is None else corr_im + now_im
        put_halves(high, low, block(SIGNALS + part), RE, corr_re)
        put_halves(high, low, block(SIGNALS + part), IM, corr_im)
    returned = transform_back(high, low, e_high, e_low, second, last, twiddle, SIGNALS + OWN)
    return returned, sums


def sin_cos(angle):
    turns = jnp.floor(angle * (2.0 / math.pi) + 0.5)
    rest = angle - turns * 1.5703125
    rest = rest - turns * 4.837512969970703125e-4
    rest = rest - turns * 7.549789948768648e-8
    square = rest * rest
    sine = rest + rest * square * (
        -1.6666654611e-1 + square * (8.3321608736e-3 + square * -1.9515295891e-4)
    )
    cosine = 1.0 - 0.5 * square + square * square * (
        4.166664568298827e-2 + square * (-1.388731625493765e-3 + square * 2.443315711809948e-5)
    )
    half = jnp.floor(turns * 0.5)
    odd = turns - 2.0 * half
    sign = 1.0 - 2.0 * (half - 2.0 * jnp.floor(half * 0.5))
    is_odd = odd > 0.5
    return sign * jnp.where(is_odd, cosine, sine), sign * jnp.where(is_odd, -sine, cosine)


CHUNK = 1024
F_TABLE = (0, 4, 7)
C_TABLE = (1, 3, 6)


def envelope_of(times, own):
    lower, upper = own[:, 33:34], own[:, 34:35]
    inside = (times >= lower) & (times < upper)
    offset = (times - lower) / (0.5 * (upper - lower))
    return jnp.where(inside, jnp.exp(-0.5 * offset * offset), 0.0)


def stacked_weight(weight):
    high, low = high_low(weight)
    return jnp.concatenate([high, high, low], axis=1).astype(BF16)


def stacked_dot(weight, value):
    high = value.astype(BF16)
    low = (value - high.astype(F32)).astype(BF16)
    return dot(weight, jnp.concatenate([high, low, high], axis=0))


def own_parameters(layer, number, out_w, out_b, window, gain, bias, gabor, hidden_b, wide, tall, own, columns):
    wide[...] = jnp.zeros(wide.shape, F32)
    wide[0:32, 0:CHANNELS] = out_w[layer]
    wide[32:33, 0:CHANNELS] = out_b[layer : layer + 1, :]
    wide[33:35, 0:CHANNELS] = window[layer].astype(F32)
    wide[35:36, 0:CHANNELS] = gain[layer : layer + 1, :]
    wide[36:37, 0:CHANNELS] = bias[layer : layer + 1, :]
    tall[0:PADDED, :] = jnp.transpose(wide[...])
    tall[PADDED : PADDED + 8, :] = jnp.zeros((8, LANES), F32)
    row = lax.broadcasted_iota(jnp.int32, (8, LANES), 0)
    lane = lax.broadcasted_iota(jnp.int32, (8, LANES), 1)
    mine = tall[pl.ds(number * OWN, 8), :]
    unused = (row >= OWN) | (number * OWN + row >= CHANNELS)
    own[...] = jnp.where(unused, jnp.where(lane == 34, float(SAMPLES), 0.0), mine)
    wide[:, 0:LANES] = jnp.zeros((LANES, LANES), F32)
    for j in range(3):
        wide[4 * j : 4 * j + 4, 0:HIDDEN] = gabor[layer, j]
    wide[12:14, 0:HIDDEN] = hidden_b[layer]
    columns[...] = jnp.transpose(wide[:, 0:LANES])[0:HIDDEN, :]


def sample_rows(first_lane, count):
    lane = first_lane + lax.broadcasted_iota(jnp.int32, (1, count), 1)
    times = times_of(lax.shift_right_logical(lane, 7 * jnp.ones_like(lane)), lane & 127)
    return times, times * (2.0 / (SAMPLES - 1)) - 1.0


def generate(columns, hidden_w, own, tab, rows):
    turns = []
    for j in range(3):
        turn = sin_cos(columns[:, 4 * j + 2 : 4 * j + 3] * (512.0 / (SAMPLES - 1)))
        turns.append([jnp.broadcast_to(value, (HIDDEN, LANES)) for value in turn])

    def step(i, carry):
        _, places = sample_rows(i * CHUNK, CHUNK)
        for j in range(3):
            sharpness, centre = columns[:, 4 * j : 4 * j + 1], columns[:, 4 * j + 1 : 4 * j + 2]
            frequency, phase = columns[:, 4 * j + 2 : 4 * j + 3], columns[:, 4 * j + 3 : 4 * j + 4]
            sine, cosine = sin_cos(frequency * places[:, 0:LANES] + phase)
            turn_sin, turn_cos = turns[j]
            for n in range(CHUNK // LANES):
                width = sharpness * (places[:, block(n)] - centre)
                bell = jnp.exp(-0.5 * width * width)
                here = pl.ds(pl.multiple_of(i * CHUNK + n * LANES, LANES), LANES)
                tab[F_TABLE[j], :, here] = bell * sine
                tab[C_TABLE[j], :, here] = bell * cosine
                sine, cosine = sine * turn_cos + cosine * turn_sin, cosine * turn_cos - sine * turn_sin
        return carry

    lax.fori_loop(0, SAMPLES // CHUNK, step, 0, unroll=2)
    weights = [stacked_weight(hidden_w[0]), stacked_weight(hidden_w[1]), stacked_weight(own[:, 0:32])]
    u_1 = stacked_dot(weights[0], tab[0]) + columns[:, 12:13]
    z_1 = u_1 * tab[4]
    tab[2] = z_1
    tab[3] = u_1 * tab[3]
    u_2 = stacked_dot(weights[1], z_1) + columns[:, 13:14]
    z_2 = u_2 * tab[7]
    tab[5] = z_2
    tab[6] = u_2 * tab[6]
    raw = stacked_dot(weights[2], z_2) + own[:, 32:33]
    times, _ = sample_rows(0, SAMPLES)
    rows[...] = raw * envelope_of(times, own)


def generate_back(kernel_grad, columns, hidden_w, own, tab, rows, sums, mats):
    rows[...] = jnp.zeros(rows.shape, F32)
    for part in range(OWN):
        grad = kernel_grad(part)
        for n in range(64):
            rows[part : part + 1, block(n)] = grad[n : n + 1, :]
    sums[...] = jnp.zeros(sums.shape, F32)
    mats[...] = jnp.zeros(mats.shape, F32)
    turned = jnp.transpose(jnp.concatenate([own[...], jnp.zeros((120, 128), F32)], axis=0))
    weight = [turned[0:32, part : part + 1] for part in range(OWN)]
    back = [stacked_weight(jnp.transpose(hidden_w[j])) for j in range(2)]

    def fold(value):
        acc = value[:, block(0)]
        for i in range(1, CHUNK // LANES):
            acc = acc + value[:, block(i)]
        return acc

    def add(k, value):
        sums[block(k, 32), :] += fold(value)

    def step(i, carry):
        span = pl.ds(pl.multiple_of(i * CHUNK, CHUNK), CHUNK)
        times, places = sample_rows(i * CHUNK, CHUNK)
        draw = rows[:, span] * envelope_of(times, own)
        dz_2 = weight[0] * draw[0:1, :] + weight[1] * draw[1:2, :] + weight[2] * draw[2:3, :]

        def level(j, e_value, g_value):
            centre = columns[:, 4 * j + 1 : 4 * j + 2]
            offset = places - centre
            moment = e_value * offset
            add(4 * j, moment * offset)
            add(4 * j + 1, moment)
            add(4 * j + 2, g_value * places)
            add(4 * j + 3, g_value)

        z_2 = tab[5, :, span]
        level(2, dz_2 * z_2, dz_2 * tab[6, :, span])
        du_2 = dz_2 * tab[7, :, span]
        add(13, du_2)
        dz_1 = stacked_dot(back[1], du_2)
        z_1 = tab[2, :, span]
        level(1, dz_1 * z_1, dz_1 * tab[3, :, span])
        du_1 = dz_1 * tab[4, :, span]
        add(12, du_1)
        dz_0 = stacked_dot(back[0], du_1)
        z_0 = tab[0, :, span]
        level(0, dz_0 * z_0, dz_0 * tab[1, :, span])
        sums[14 * 32 : 14 * 32 + 8, :] += fold(draw)
        left = jnp.concatenate([du_1, du_2, draw], axis=0)
        right = jnp.concatenate([z_0, z_1, z_2, jnp.zeros_like(z_0)], axis=0)
        left_high, right_high = left.astype(BF16), right.astype(BF16)
        left_low = (left - left_high.astype(F32)).astype(BF16)
        right_low = (right - right_high.astype(F32)).astype(BF16)
        mats[...] += (
            dot_rows(left_high, right_high) + dot_rows(left_low, right_high) + dot_rows(left_high, right_low)
        )
        return carry

    lax.fori_loop(0, SAMPLES // CHUNK, step, 0, unroll=2)
    lane = lax.broadcasted_iota(jnp.int32, (32, LANES), 1)
    hidden = jnp.where(lane < 32, mats[0:32, :], jnp.where(lane < 64, mats[32:64, :], 0.0))

    def column(k):
        return jnp.sum(sums[block(k, 32), :], axis=1, keepdims=True)

    hidden = jnp.where(lane == 64, column(12), hidden)
    hidden = jnp.where(lane == 65, column(13), hidden)
    for j in range(3):
        sharpness = columns[:, 4 * j : 4 * j + 1]
        hidden = jnp.where(lane == 66 + 4 * j, -sharpness * column(4 * j), hidden)
        hidden = jnp.where(lane == 67 + 4 * j, sharpness * sharpness * column(4 * j + 1), hidden)
        hidden = jnp.where(lane == 68 + 4 * j, column(4 * j + 2), hidden)
        hidden = jnp.where(lane == 69 + 4 * j, column(4 * j + 3), hidden)
    lane8 = lax.broadcasted_iota(jnp.int32, (8, LANES), 1)
    outer = pltpu.roll(mats[64:72, :], LANES - 64, 1)
    raw_total = jnp.sum(sums[14 * 32 : 14 * 32 + 8, :], axis=1, keepdims=True)
    outer = jnp.where(lane8 < 32, outer, 0.0)
    outer = jnp.where(lane8 == 32, raw_total, outer)
    return hidden, outer


def with_norm_sums(outer, sums):
    row = lax.broadcasted_iota(jnp.int32, (8, LANES), 0)
    lane = lax.broadcasted_iota(jnp.int32, (8, LANES), 1)
    for part in range(OWN):
        gain_total, bias_total = sums[part]
        outer = jnp.where((row == part) & (lane == 33), gain_total, outer)
        outer = jnp.where((row == part) & (lane == 34), bias_total, outer)
    return outer


def one_row(outer):
    lane = lax.broadcasted_iota(jnp.int32, (1, LANES), 1)
    result = jnp.zeros((1, LANES), F32)
    for part in range(OWN):
        row = outer[part : part + 1, :]
        moved = pltpu.roll(row, 32 * part, 1) if part else row
        result = jnp.where((lane >= 32 * part) & (lane < 32 * part + 32), moved, result)
        moved = pltpu.roll(row, 64 + 3 * part, 1)
        result = jnp.where((lane >= 96 + 3 * part) & (lane < 99 + 3 * part), moved, result)
    return result


def packed_hidden(hidden):
    lane16 = lax.broadcasted_iota(jnp.int32, (16, LANES), 1)
    upper = jnp.where(lane16 < 64, hidden[0:16, :], pltpu.roll(hidden[16:32, :], 64, 1))
    lane4 = lax.broadcasted_iota(jnp.int32, (4, LANES), 1)
    lower = jnp.zeros((4, LANES), F32)
    for g in range(8):
        moved = pltpu.roll(hidden, (64 + 16 * g) % LANES, 1)[4 * g : 4 * g + 4, :]
        lower = jnp.where((lane4 >= 16 * g) & (lane4 < 16 * g + 16), moved, lower)
    return upper, lower


def unpacked_hidden(upper, lower):
    lane16 = lax.broadcasted_iota(jnp.int32, (16, LANES), 1)
    lane32 = lax.broadcasted_iota(jnp.int32, (32, LANES), 1)
    top = jnp.concatenate([upper, pltpu.roll(upper, 64, 1)], axis=0)
    tiled = jnp.concatenate([lower] * 8, axis=0)
    row32 = lax.broadcasted_iota(jnp.int32, (32, LANES), 0)
    rest = jnp.zeros((32, LANES), F32)
    for g in range(8):
        moved = pltpu.roll(tiled, (64 - 16 * g) % LANES, 1)
        rest = jnp.where((row32 >= 4 * g) & (row32 < 4 * g + 4), moved, rest)
    return jnp.where(lane32 < 64, top, rest)


def high_low(value):
    high = value.astype(BF16).astype(F32)
    return high, value - high


def valid_row(meta, i):
    lane = lax.broadcasted_iota(jnp.int32, (1, LANES), 1)
    return (lax.axis_index("seq") * PIECE + (i // 2) * LANES + lane < meta[i % 2]).astype(F32)


def masked(meta, rows):
    mask = jnp.concatenate([valid_row(meta, i) for i in range(4)] * 2, axis=0)
    return (rows.reshape(-1, 8, LANES) * mask[None]).reshape(-1, LANES)


CLIP_ROWS = 4 * CHANNELS
PADDED_ROWS = 4 * PADDED


def put_padded(padded, rows):
    padded[0:CLIP_ROWS, :] = rows
    padded[CLIP_ROWS:PADDED_ROWS, :] = jnp.zeros((PADDED_ROWS - CLIP_ROWS, LANES), F32)


def rows_to_message(padded, out, step, base):
    for m in range(12):
        out[pl.ds(base + m, DEVICES, stride=step), :] = padded[pl.ds(m, DEVICES, stride=12), :]


def rows_of_channels(padded, i):
    return padded[pl.ds(i, PADDED, stride=4), :]


def source_kernel(meta, x_ref, mix_w, out_ref, padded, out):
    put_padded(padded, masked(meta, x_ref[...]))
    for b in range(2):
        length = meta[b]
        upper = lax.shift_right_logical(length, 7)
        out[pl.ds(12 + 2 * b, DEVICES, stride=16), :] = jnp.full((DEVICES, LANES), upper.astype(F32))
        out[pl.ds(13 + 2 * b, DEVICES, stride=16), :] = jnp.full(
            (DEVICES, LANES), (length - upper * 128).astype(F32)
        )
    rows_to_message(padded, out, 16, 0)
    out_ref[...] = out[...].reshape(DEVICES, 16, LANES).astype(BF16)


def make_lookup(lookup):
    row = lax.broadcasted_iota(jnp.int32, (DEVICES, PADDED), 0)
    column = lax.broadcasted_iota(jnp.int32, (DEVICES, PADDED), 1)
    for part in range(OWN):
        lookup[block(part), :] = (column == OWN * row + part).astype(F32).astype(BF16)


def make_weights(mix_w, mix_b, wide, lookup, weights, weights_back):
    make_lookup(lookup)
    wide[...] = jnp.zeros(wide.shape, BF16)
    row = lax.broadcasted_iota(jnp.int32, (LANES, CHANNELS), 0)
    lines = jnp.where(row == 0, mix_b[0:1, :], jnp.where(row == 1, mix_b[1:2, :], 0.0))
    turned = jnp.transpose(jnp.concatenate([lines, jnp.zeros((LANES, PADDED - CHANNELS), F32)], axis=1))
    lane = lax.broadcasted_iota(jnp.int32, (PADDED, PADDED), 1)
    for layer in range(2):
        wide[0:CHANNELS, 0:CHANNELS] = mix_w[layer]
        weights_back[layer] = dot_rows(lookup[...], wide[...]).astype(BF16)
        value = dot_rows(wide[...], lookup[...])
        rest = turned[:, layer : layer + 1]
        for spot in SPOTS:
            high, rest = high_low(rest)
            value = jnp.where(lane == spot, high, value)
        weights[layer] = value.astype(BF16)


def make_kernel(layer, meta, params, consts, bundle, tab, scratch):
    out_w, out_b, window, gain, bias, gabor, hidden_b, hidden_w = params
    first, second, _, twiddle = consts
    wide, tall, rows, pieces, x_ref, high, low = scratch
    own, columns = bundle.at[OWN_ROWS, :], bundle.at[COLUMN_ROWS, :]
    own_parameters(layer, lax.axis_index("seq") * 4 + lax.axis_index("clips"), out_w, out_b, window, gain, bias, gabor, hidden_b, wide, tall, own, columns)
    generate(columns, hidden_w.at[layer], own, tab, rows)
    for n in range(64):
        for part in range(OWN):
            pieces[part * 64 + n : part * 64 + n + 1, :] = rows[part : part + 1, block(n)]
    for part in range(OWN):
        piece = pieces[block(part, 64), :].astype(BF16)
        x_ref[0:64, block(part)] = piece
        x_ref[64:128, block(part)] = piece
        x_ref[128:256, block(part)] = jnp.zeros((128, LANES), BF16)
    spec = transform(x_ref, high, low, first, second, twiddle, OWN)
    bundle[0:SPEC_IM, :] = spec[:, RE]
    bundle[SPEC_IM : 2 * SPEC_IM, :] = spec[:, IM]


def forward_kernel(
    meta, message_ref, out_w, out_b, window, gain, bias, gabor, hidden_b, hidden_w,
    first, second, last, twiddle,
    out_ref, spec_ref, normed_ref, slope_ref, inv_ref, len_ref, kernel_spec, tab,
    message, x_ref, high, low, e_high, e_low, y_ref, out, *make_scratch,
):
    own = kernel_spec.at[OWN_ROWS, :]
    params = (out_w, out_b, window, gain, bias, gabor, hidden_b, hidden_w)
    make_kernel(0, meta, params, (first, second, last, twiddle), kernel_spec, tab, make_scratch)
    message[...] = spread(message_ref[...])
    for y in range(4):
        for b in range(2):
            start = y * 16 + 12 + 2 * b
            len_ref[2 * y + b : 2 * y + b + 1, :] = (
                message[start : start + 1, :] * 128.0 + message[start + 1 : start + 2, :]
            )
    load_signals(message, 16, x_ref)
    convolve(x_ref, spec_ref, kernel_spec, high, low, e_high, e_low, (first, second, last, twiddle), y_ref)
    valid, tally = valid_of(len_ref), tally_of(len_ref)
    inv_ref[...] = jnp.zeros((8, LANES), F32)
    for part in range(OWN):
        normed, inv_std, active, slope = normalise(y_ref, own, valid, tally, part)
        normed_ref[:, block(part, 512)] = normed
        slope_ref[:, block(part, 512)] = slope
        inv_ref[part : part + 1, :] = jnp.broadcast_to(inv_std, (1, LANES))
        y_ref[:, block(part, 512)] = active
    store_signals(out, 16, 0, lambda part, y: y_ref[:, block(part * 4 + y)])
    out_ref[...] = out[...].reshape(DEVICES, 16, LANES).astype(BF16)


def gather_active(message, step, rhs):
    row = lax.broadcasted_iota(jnp.int32, (DEVICES, LANES), 0)
    for i in range(4):
        for part in range(OWN):
            piece = message[pl.ds(part * 4 + i, DEVICES, stride=step), :]
            if part != 1:
                piece = jnp.where(row >= (126 if part == 2 else 127), 1.0, piece)
            rhs[block(part), block(i)] = piece.astype(BF16)


def store_rows(value, out, step, base):
    for i in range(4):
        for part in range(OWN):
            out[pl.ds(base + part * 4 + i, DEVICES, stride=step), :] = value[block(part), block(i)]


def mix_kernel(
    meta, message_ref, x_ref, cotangent, mix_w, mix_b,
    out_ref, next_ref, active_ref, weights, weights_back, message, padded, out, low, wide, lookup,
):
    make_weights(mix_w, mix_b, wide, lookup, weights, weights_back)
    message[...] = spread(message_ref[...])
    gather_active(message, 16, active_ref)
    mixed = dot(weights[0], active_ref[...])
    put_padded(padded, x_ref[...])
    for i in range(4):
        valid = valid_row(meta, i)
        value = rows_of_channels(padded, i) + mixed[:, block(i)] * valid
        next_ref[pl.ds(i, PADDED, stride=4), :] = value
        padded[pl.ds(i, PADDED, stride=4), :] = value * valid
    rows_to_message(padded, out, 24, 0)
    put_padded(padded, masked(meta, cotangent[...]))
    for i in range(4):
        low[:, block(i)] = rows_of_channels(padded, i).astype(BF16)
    store_rows(dot(weights_back[1], low[...]), out, 24, 12)
    out_ref[...] = out[...].reshape(DEVICES, 24, LANES).astype(BF16)


def forward_backward_kernel(
    meta, message_ref, out_w, out_b, window, gain, bias, gabor, hidden_b, hidden_w,
    len_ref, first, second, last, twiddle,
    out_ref, hidden_out, outer_out,
    message, x_ref, high, low, e_high, e_low, y_ref, out, spec_ref, grad_ref, normed_ref, slope_ref, returned_ref,
    rows, sums, mats, kernel_spec, tab, *make_scratch,
):
    own, columns = kernel_spec.at[OWN_ROWS, :], kernel_spec.at[COLUMN_ROWS, :]
    consts = (first, second, last, twiddle)
    params = (out_w, out_b, window, gain, bias, gabor, hidden_b, hidden_w)
    make_kernel(1, meta, params, consts, kernel_spec, tab, make_scratch)
    message[...] = spread(message_ref[...])
    load_signals(message, 24, x_ref)
    convolve(x_ref, spec_ref, kernel_spec, high, low, e_high, e_low, consts, y_ref)
    valid, tally = valid_of(len_ref), tally_of(len_ref)
    inv = []
    for part in range(OWN):
        normed, inv_std, active, slope = normalise(y_ref, own, valid, tally, part)
        normed_ref[:, block(part, 512)] = normed
        slope_ref[:, block(part, 512)] = slope
        inv.append(inv_std)
        y_ref[:, block(part, 512)] = active
    store_signals(out, 24, 0, lambda part, y: y_ref[:, block(part * 4 + y)])
    returned, norm_sums = conv_backward(
        message, 24, 12, lambda part: normed_ref[:, block(part, 512)], lambda part: slope_ref[:, block(part, 512)],
        lambda part: inv[part], own, valid, tally, spec_ref, kernel_spec, x_ref, high, low, e_high, e_low, consts, grad_ref,
    )
    returned_ref[...] = returned
    store_signals(out, 24, 12, lambda part, y: returned_ref[:, block(part * 4 + y)])
    out_ref[...] = out[...].reshape(DEVICES, 24, LANES).astype(BF16)
    hidden, outer = generate_back(
        lambda part: returned_ref[0:64, block(SIGNALS + part)], columns, hidden_w.at[1], own, tab,
        rows, sums, mats,
    )
    hidden_out[...] = hidden
    outer_out[...] = with_norm_sums(outer, norm_sums)


def middle_kernel(
    meta, message_ref, x_ref, cotangent, weights, weights_back, active_0, hidden_1,
    output_far, flow_ref, out_ref, message, padded, out, low_0, low_1, active_1, output, sent,
):
    message[...] = spread(message_ref[...])
    gather_active(message, 24, active_1)
    mixed = dot(weights[1], active_1[...])
    for i in range(4):
        padded[pl.ds(i, PADDED, stride=4), :] = rows_of_channels(x_ref, i) + mixed[:, block(i)] * valid_row(meta, i)
    output[...] = padded[0:CLIP_ROWS, :]
    leaving = pltpu.make_async_copy(output, output_far, sent.at[0])
    leaving.start()
    put_padded(flow_ref, cotangent[...])
    for i in range(4):
        low_1[:, block(i)] = (rows_of_channels(flow_ref, i) * valid_row(meta, i)).astype(BF16)
    for m in range(12):
        padded[pl.ds(m, DEVICES, stride=12), :] = message[pl.ds(12 + m, DEVICES, stride=24), :]
    flow_ref[...] += masked(meta, padded[...])
    for i in range(4):
        low_0[:, block(i)] = (rows_of_channels(flow_ref, i) * valid_row(meta, i)).astype(BF16)
    store_rows(dot(weights_back[0], low_0[...]), out, 32, 0)
    for layer, (active, low) in enumerate(((active_0, low_0), (active_1, low_1))):
        part_sum = dot_rows(active[...], low[...])
        for part in range(OWN):
            for third in range(3):
                out[pl.ds(12 + layer * 9 + part * 3 + third, DEVICES, stride=32), :] = part_sum[
                    block(part), block(third)
                ]
    high, low = high_low(hidden_1[...])
    out[pl.ds(30, DEVICES, stride=32), :] = jnp.concatenate([high, jnp.zeros((96, LANES), F32)], axis=0)
    out[pl.ds(31, DEVICES, stride=32), :] = jnp.concatenate([low, jnp.zeros((96, LANES), F32)], axis=0)
    out_ref[...] = out[...].reshape(DEVICES, 32, LANES).astype(BF16)
    leaving.wait()


LAST_ROWS = 56


def backward_kernel(
    message_ref, spec_ref, kernel_spec, normed_ref, slope_ref, inv_ref, len_ref,
    first, second, last, twiddle, hidden_w, tab, outer_1,
    out_ref,
    message, x_ref, high, low, e_high, e_low, out, grad_ref, returned_ref, rows, sums, mats,
):
    own, columns = kernel_spec.at[OWN_ROWS, :], kernel_spec.at[COLUMN_ROWS, :]
    consts = (first, second, last, twiddle)
    message[...] = spread(message_ref[...])
    valid, tally = valid_of(len_ref), tally_of(len_ref)
    returned, norm_sums = conv_backward(
        message, 32, 0, lambda part: normed_ref[:, block(part, 512)], lambda part: slope_ref[:, block(part, 512)],
        lambda part: inv_ref[part : part + 1, 0:1], own, valid, tally, spec_ref, kernel_spec, x_ref, high, low,
        e_high, e_low, consts, grad_ref,
    )
    returned_ref[...] = returned
    store_signals(out, 16, 0, lambda part, y: returned_ref[:, block(part * 4 + y)])
    hidden, outer = generate_back(
        lambda part: returned_ref[0:64, block(SIGNALS + part)], columns, hidden_w.at[0], own, tab,
        rows, sums, mats,
    )
    outer = with_norm_sums(outer, norm_sums)
    gathered = jnp.sum(message[...].reshape(DEVICES, 32, LANES), axis=0)
    upper, lower = packed_hidden(hidden)
    hidden_1_high, hidden_1_low = high_low(gathered[30:31, :] + gathered[31:32, :])
    outer_0_high, outer_0_low = high_low(one_row(outer))
    outer_1_high, outer_1_low = high_low(one_row(outer_1[...]))
    shared = jnp.concatenate(
        [
            gathered[0:30, :], upper, lower, hidden_1_high, hidden_1_low,
            outer_0_high, outer_0_low, outer_1_high, outer_1_low,
        ],
        axis=0,
    )
    row = lax.broadcasted_iota(jnp.int32, (DEVICES, 16, LANES), 1)
    own_rows = jnp.where(row < 12, out[...].reshape(DEVICES, 16, LANES), shared[None, 0:16, :])
    rest = jnp.broadcast_to(shared[None, 16:LAST_ROWS, :], (DEVICES, LAST_ROWS - 16, LANES))
    out_ref[...] = jnp.concatenate([own_rows, rest], axis=1).astype(BF16)


def last_kernel(
    meta, message_ref, flow_ref,
    input_far, gabor_grad, hidden_w_grad, hidden_b_grad, out_w_grad, out_b_grad, gain_grad, bias_grad,
    mix_w_far, mix_b_grad, message, padded, owned, thirds, lookup, input_grad, mix_w_grad, sent,
):
    make_lookup(lookup)
    message[...] = spread(message_ref[...])

    def rows_of(k, count=DEVICES):
        return message[pl.ds(k, count, stride=LAST_ROWS), :]

    for m in range(12):
        padded[pl.ds(m, DEVICES, stride=12), :] = rows_of(m)
    input_grad[...] = flow_ref[0:CLIP_ROWS, :] + masked(meta, padded[0:CLIP_ROWS, :])
    input_leaves = pltpu.make_async_copy(input_grad, input_far, sent.at[0])
    input_leaves.start()
    for layer in range(2):
        bias_rows = []
        for part in range(OWN):
            for third in range(3):
                piece = rows_of(12 + layer * 9 + part * 3 + third)
                thirds[block(part), block(third)] = piece.astype(BF16)
                if part == 2:
                    bias_rows.append(piece[SPOT - 2 * DEVICES : SPOT - 2 * DEVICES + 1, :])
        mix_w_grad[:, layer, :] = dot_columns(thirds[...], lookup[...])[0:CHANNELS, 0:CHANNELS]
        mix_b_grad[layer : layer + 1, :] = jnp.concatenate(bias_rows, axis=1)[:, 0:CHANNELS]
    mix_leaves = pltpu.make_async_copy(mix_w_grad, mix_w_far, sent.at[1])
    mix_leaves.start()
    shared = jnp.sum(message[...].reshape(DEVICES, LAST_ROWS, LANES)[:, 24:56, :], axis=0)
    hidden_0 = unpacked_hidden(shared[6:22, :], shared[22:26, :])
    hidden_1 = rows_of(50, 32) + rows_of(51, 32)
    lane = lax.broadcasted_iota(jnp.int32, (DEVICES, LANES), 1)
    for layer, hidden in enumerate((hidden_0, hidden_1)):
        hidden_w_grad[layer, 0] = hidden[:, 0:32]
        hidden_w_grad[layer, 1] = pltpu.roll(hidden, 96, 1)[:, 0:32]
        turned = jnp.transpose(jnp.concatenate([hidden, jnp.zeros((96, LANES), F32)], axis=0))
        hidden_b_grad[layer] = turned[64:66, 0:32]
        for j in range(3):
            gabor_grad[layer, j] = turned[66 + 4 * j : 70 + 4 * j, 0:32]
        value = rows_of(52 + 2 * layer) + rows_of(53 + 2 * layer)
        for part in range(OWN):
            wide = pltpu.roll(value, (LANES - 32 * part) % LANES, 1)
            small = pltpu.roll(value, 64 - 3 * part, 1)
            owned[pl.ds(part, DEVICES, stride=OWN), :] = jnp.where(lane < 32, wide, small)
        turned = jnp.transpose(owned[...])
        out_w_grad[layer] = turned[0:32, 0:CHANNELS]
        out_b_grad[layer : layer + 1, :] = turned[32:33, 0:CHANNELS]
        gain_grad[layer : layer + 1, :] = turned[33:34, 0:CHANNELS]
        bias_grad[layer : layer + 1, :] = turned[34:35, 0:CHANNELS]
    input_leaves.wait()
    mix_leaves.wait()


def exchange(message):
    return lax.all_to_all(message, AXES, split_axis=0, concat_axis=0, tiled=True)


def to_rows(clips):
    return clips.reshape(2, CHANNELS, 2, LANES).transpose(1, 2, 0, 3).reshape(CLIP_ROWS, LANES)


def from_rows(rows):
    return rows.reshape(CHANNELS, 2, 2, LANES).transpose(2, 0, 1, 3).reshape(2, CHANNELS, PIECE)


def shards(
    inputs, lengths, window, gabor_params, hidden_w, hidden_b, out_w, out_b, bn_gain, bn_bias, mix_w, mix_b, cotangent
):
    const = {name: jnp.asarray(value) for name, value in TABLES.items()}
    meta = lengths
    inputs, cotangent = to_rows(inputs), to_rows(cotangent)

    def rows(count):
        return ((count, LANES), F32)

    with jax.named_scope("source_0"):
        (message,) = run(
            source_kernel, [((DEVICES, 16, LANES), BF16)], [meta, inputs, mix_w],
            [rows(PADDED_ROWS), rows(DEVICES * 16)], "source_0", 8, smem=(0,), far=(2,),
        )
        message = exchange(message)

    square = (PADDED, PADDED)
    generator = [
        jnp.swapaxes(out_w, 1, 2), out_b, jnp.swapaxes(window, 1, 2), bn_gain, bn_bias, gabor_params, hidden_b,
        hidden_w,
    ]
    shape_tab = ((8, HIDDEN, SAMPLES), F32)
    make_scratch = [
        ((LANES, PADDED), F32), rows(PADDED + 8), ((8, SAMPLES), F32), rows(192),
        ((256, OWN * LANES), BF16), ((OWN * LANES, 256), BF16), ((OWN * LANES, 256), BF16),
    ]
    mixers = ((2, *square), BF16)

    def scratch(signals):
        count = signals * LANES
        return [
            ((256, SIGNALS * LANES), BF16), ((count, 256), BF16), ((count, 256), BF16),
            ((256, count), BF16), ((256, count), BF16),
        ]

    shape_y = (LANES, SIGNALS * LANES)
    shape_s = (SIGNALS * LANES, 256)
    transforms = [const[name] for name in TABLE_NAMES]
    with jax.named_scope("conv_0"):
        message, spec_0, normed_0, slope_0, inv_0, lens, bundle_0, tab_0 = run(
            forward_kernel,
            [
                ((DEVICES, 16, LANES), BF16), (shape_s, F32), (shape_y, F32), (shape_y, F32), rows(8), rows(8),
                rows(BUNDLE), shape_tab,
            ],
            [meta, message, *generator, *transforms],
            [rows(DEVICES * 16), *scratch(SIGNALS), (shape_y, F32), rows(DEVICES * 16), *make_scratch],
            "conv_0", 16, smem=(0,),
        )
        message = exchange(message)

    with jax.named_scope("mix_0"):
        message, middle, active_0, weights, weights_back = run(
            mix_kernel,
            [((DEVICES, 24, LANES), BF16), rows(PADDED_ROWS), ((PADDED, 512), BF16), mixers, mixers],
            [meta, message, inputs, cotangent, mix_w, mix_b],
            [rows(DEVICES * 16), rows(PADDED_ROWS), rows(DEVICES * 24), ((PADDED, 512), BF16), (square, BF16), (square, BF16)],
            "mix_0", 12, smem=(0,),
        )
        message = exchange(message)

    back_scratch = [((8, SAMPLES), F32), rows(14 * 32 + 8), rows(72)]
    with jax.named_scope("conv_1"):
        message, hidden_1, outer_1 = run(
            forward_backward_kernel,
            [((DEVICES, 24, LANES), BF16), rows(HIDDEN), rows(8)],
            [
                meta, message, *generator, lens, *transforms,
            ],
            [
                rows(DEVICES * 24), *scratch(SIGNALS + OWN), (shape_y, F32), rows(DEVICES * 24),
                (shape_s, F32), (shape_s, F32), (shape_y, F32), (shape_y, F32),
                ((LANES, (SIGNALS + OWN) * LANES), F32), *back_scratch, rows(BUNDLE), shape_tab, *make_scratch,
            ],
            "conv_1", 26, smem=(0,),
        )
        message = exchange(message)

    with jax.named_scope("mix_1"):
        outputs, flow, message = run(
            middle_kernel,
            [rows(CLIP_ROWS), rows(PADDED_ROWS), ((DEVICES, 32, LANES), BF16)],
            [meta, message, middle, cotangent, weights, weights_back, active_0, hidden_1],
            [
                rows(DEVICES * 24), rows(PADDED_ROWS), rows(DEVICES * 32),
                ((PADDED, 512), BF16), ((PADDED, 512), BF16), ((PADDED, 512), BF16),
                rows(CLIP_ROWS),
            ],
            "mix_1", 12, smem=(0,), far_outs=(0,), copies=1,
        )
        message = exchange(message)

    with jax.named_scope("conv_back_0"):
        (message,) = run(
            backward_kernel,
            [((DEVICES, LAST_ROWS, LANES), BF16)],
            [
                message, spec_0, bundle_0, normed_0, slope_0, inv_0, lens, *transforms,
                hidden_w, tab_0, outer_1,
            ],
            [
                rows(DEVICES * 32), *scratch(SIGNALS + OWN), rows(DEVICES * 16), (shape_s, F32),
                ((LANES, (SIGNALS + OWN) * LANES), F32), *back_scratch,
            ],
            "conv_back_0", 16,
        )
        message = exchange(message)

    with jax.named_scope("gradients"):
        (
            input_grad, gabor_grad, hidden_w_grad, hidden_b_grad, out_w_grad, out_b_grad, gain_grad, bias_grad,
            mix_w_grad, mix_b_grad,
        ) = run(
            last_kernel,
            [
                rows(CLIP_ROWS), (gabor_params.shape, F32), (hidden_w.shape, F32), (hidden_b.shape, F32),
                ((2, HIDDEN, CHANNELS), F32), (out_b.shape, F32), (bn_gain.shape, F32), (bn_bias.shape, F32),
                ((CHANNELS, 2, CHANNELS), F32), (mix_b.shape, F32),
            ],
            [meta, message, flow],
            [
                rows(DEVICES * LAST_ROWS), rows(PADDED_ROWS), rows(PADDED), (square, BF16), (square, BF16),
                rows(CLIP_ROWS), ((CHANNELS, 2, CHANNELS), F32),
            ],
            "gradients", 20, smem=(0,), far_outs=(0, 8), copies=2,
        )
    return (
        from_rows(outputs), from_rows(input_grad), gabor_grad, hidden_w_grad, hidden_b_grad,
        jnp.swapaxes(out_w_grad, 1, 2), out_b_grad, gain_grad, bias_grad, jnp.swapaxes(mix_w_grad, 0, 1), mix_b_grad,
    )


def solution(mesh):
    clip = P("clips", None, "seq")
    in_specs = (clip, P("clips")) + (P(),) * 10 + (clip,)
    out_specs = (clip, clip) + (P(),) * 9
    return jax.shard_map(shards, mesh=mesh, in_specs=in_specs, out_specs=out_specs, check_vma=False)
```

```python
import math

import jax
import jax.numpy as jnp
import ml_dtypes
import numpy as np
from jax import lax
from jax.experimental import pallas as pl
from jax.experimental.pallas import tpu as pltpu
from jax.sharding import PartitionSpec as P

F32 = jnp.float32
BF16 = jnp.bfloat16
AXES = ("seq", "clips")
DEVICES = 128
OWN = 3
CHANNELS = 380
PADDED = DEVICES * OWN
SAMPLES = 8192
PIECE = 256
HIDDEN = 32
LANES = 128
SIGNALS = 12
TABLE_NAMES = ("first", "second", "last", "twiddle")
PERIOD = 2 * SAMPLES
EPSILON = 1e-05
MEGABYTE = 1024 * 1024
EXACT = lax.Precision.HIGHEST
SPOTS = (2 * DEVICES + 126, 2 * DEVICES + 127, 127)
SPOT = SPOTS[0]


def halves(table):
    high = table.astype(ml_dtypes.bfloat16)
    low = (table - high.astype(np.float64)).astype(ml_dtypes.bfloat16)
    return high, low


def tables():
    order = np.array([2 * j + r for r in range(2) for j in range(32)])
    k = np.arange(LANES)
    turn = 2 * np.pi * ((k[:, None] * order[None, :]) % LANES) / LANES
    c_high, c_low = halves(np.cos(turn))
    s_high, s_low = halves(np.sin(turn))
    first = np.concatenate(
        [
            np.concatenate([c_high, c_low, s_high, s_low], axis=1),
            np.concatenate([-s_high, -s_low, c_high, c_low], axis=1),
        ],
        axis=0,
    )
    turn = 2 * np.pi * ((k[:, None] * k[None, :]) % LANES) / LANES
    cosine, sine = np.cos(turn), np.sin(turn)
    second = halves(np.block([[cosine, -sine], [sine, cosine]]))
    turn = 2 * np.pi * ((order[:, None] * k[None, :]) % LANES) / LANES
    cosine, sine = np.cos(turn) / PERIOD, np.sin(turn) / PERIOD
    last = halves(np.block([[cosine, -sine], [sine, cosine]]))
    turn = 2 * np.pi * (k[:, None] * k[None, :]) / PERIOD
    twiddle = np.stack([np.cos(turn), np.sin(turn)]).astype(np.float32)
    return dict(
        first=first,
        second=np.stack(second),
        last=np.stack(last),
        twiddle=twiddle,
    )


TABLES = tables()


def run(body, outs, args, scratch, name, grant, smem=(), far=()):
    spaces = [pltpu.HBM if i in far else pltpu.SMEM if i in smem else pltpu.VMEM for i in range(len(args))]
    return pl.pallas_call(
        body,
        out_shape=[jax.ShapeDtypeStruct(shape, kind) for shape, kind in outs],
        in_specs=[pl.BlockSpec(memory_space=space) for space in spaces],
        out_specs=[pl.BlockSpec(memory_space=pltpu.VMEM)] * len(outs),
        scratch_shapes=[pltpu.VMEM(shape, kind) for shape, kind in scratch],
        compiler_params=pltpu.CompilerParams(vmem_limit_bytes=grant * MEGABYTE),
        name=name,
    )(*args)


def dot(a, b):
    return jnp.dot(a, b, preferred_element_type=F32)


def dot_rows(a, b, precision=None):
    return lax.dot_general(a, b, (((1,), (1,)), ((), ())), precision=precision, preferred_element_type=F32)


def dot_columns(a, b, precision=None):
    return lax.dot_general(a, b, (((0,), (0,)), ((), ())), precision=precision, preferred_element_type=F32)


def triple(a_high, a_low, b_high, b_low):
    left = jnp.concatenate([a_high, a_low, a_high], axis=1)
    return dot(left, jnp.concatenate([b_high, b_high, b_low], axis=0))


def triple_rows(a_high, a_low, b_high, b_low):
    left = jnp.concatenate([a_high, a_low, a_high], axis=1)
    return dot_rows(left, jnp.concatenate([b_high, b_high, b_low], axis=1))


def put_halves(high_ref, low_ref, rows, columns, value):
    high = value.astype(BF16)
    high_ref[rows, columns] = high
    low_ref[rows, columns] = (value - high.astype(F32)).astype(BF16)


def block(i, size=LANES):
    return slice(i * size, (i + 1) * size)


RE, IM = slice(0, LANES), slice(LANES, 2 * LANES)


def signal_row(b, part, r):
    return part * 4 + r * 2 + b


def spread(message):
    return message.astype(F32).reshape(-1, LANES)


def transform(x_ref, high_ref, low_ref, first, second, twiddle, count):
    part_a = dot(first[...], x_ref[:, : count * LANES])
    cosine, sine = twiddle[0], twiddle[1]
    for s in range(count):
        real, imag = part_a[:LANES, block(s)], part_a[LANES:, block(s)]
        put_halves(high_ref, low_ref, block(s), RE, real * cosine + imag * sine)
        put_halves(high_ref, low_ref, block(s), IM, imag * cosine - real * sine)
    rows = slice(0, count * LANES)
    return triple(high_ref[rows, :], low_ref[rows, :], second[0], second[1])


def transform_back(high_ref, low_ref, e_high, e_low, second, last, twiddle, count):
    rows = slice(0, count * LANES)
    part_d = triple_rows(high_ref[rows, :], low_ref[rows, :], second[0], second[1])
    cosine, sine = twiddle[0], twiddle[1]
    for s in range(count):
        real, imag = part_d[block(s), RE], part_d[block(s), IM]
        put_halves(e_high, e_low, RE, block(s), real * cosine - imag * sine)
        put_halves(e_high, e_low, IM, block(s), real * sine + imag * cosine)
    return triple(last[0], last[1], e_high[:, rows], e_low[:, rows])


def erf_parts(value):
    cdf = 0.5 * (1.0 + lax.erf(value * math.sqrt(0.5)))
    return cdf, jnp.exp(-0.5 * value * value) * (1.0 / math.sqrt(2.0 * math.pi))


def total(value):
    return jnp.sum(jnp.sum(value, axis=0, keepdims=True), axis=1, keepdims=True)


def times_of(row, lane):
    return (256 * (row & 31) + 128 * lax.shift_right_logical(row, 5 * jnp.ones_like(row)) + lane).astype(F32)


def valid_of(len_ref):
    row = lax.broadcasted_iota(jnp.int32, (LANES, LANES), 0) & 63
    times = times_of(row, lax.broadcasted_iota(jnp.int32, (LANES, LANES), 1))
    columns = []
    for y in range(4):
        upper = times[0:64, :] < len_ref[2 * y : 2 * y + 1, :]
        lower = times[64:128, :] < len_ref[2 * y + 1 : 2 * y + 2, :]
        columns.append(jnp.concatenate([upper, lower], axis=0).astype(F32))
    return jnp.concatenate(columns, axis=1)


def tally_of(len_ref):
    return jnp.sum(len_ref[:, 0:1], axis=0, keepdims=True)


def load_signals(message, step, x_ref):
    for part in range(OWN):
        for y in range(4):
            lanes = block(part * 4 + y)
            for b in range(2):
                for r in range(2):
                    start = y * step + signal_row(b, part, r)
                    piece = message[pl.ds(start, 32, stride=4 * step), :].astype(BF16)
                    x_ref[b * 128 + r * 32 : b * 128 + r * 32 + 32, lanes] = piece
                    x_ref[b * 128 + r * 32 + 64 : b * 128 + r * 32 + 96, lanes] = piece


def store_signals(out, step, base, get):
    for part in range(OWN):
        for y in range(4):
            value = get(part, y)
            for b in range(2):
                for r in range(2):
                    start = y * step + base + signal_row(b, part, r)
                    out[pl.ds(start, 32, stride=4 * step), :] = value[b * 64 + r * 32 : b * 64 + r * 32 + 32, :]


SPEC_IM = OWN * LANES
OWN_ROWS = slice(2 * SPEC_IM, 2 * SPEC_IM + 8)
COLUMN_ROWS = slice(2 * SPEC_IM + 8, 2 * SPEC_IM + 8 + HIDDEN)
BUNDLE = 2 * SPEC_IM + 8 + HIDDEN


def kernel_parts(bundle, part):
    return bundle[block(part), :], bundle[SPEC_IM + part * LANES : SPEC_IM + (part + 1) * LANES, :]


def convolve(x_ref, spec_ref, kernel_spec, high, low, e_high, e_low, consts, y_ref):
    first, second, last, twiddle = consts
    spec_ref[...] = transform(x_ref, high, low, first, second, twiddle, SIGNALS)
    for part in range(OWN):
        k_re, k_im = kernel_parts(kernel_spec, part)
        for y in range(4):
            rows = block(part * 4 + y)
            s_re, s_im = spec_ref[rows, RE], spec_ref[rows, IM]
            put_halves(high, low, rows, RE, s_re * k_re - s_im * k_im)
            put_halves(high, low, rows, IM, s_re * k_im + s_im * k_re)
    y_ref[...] = transform_back(high, low, e_high, e_low, second, last, twiddle, SIGNALS)


def normalise(y_ref, own, valid, tally, part):
    value = y_ref[:, block(part, 512)]
    mean = total(valid * value) / tally
    centred = value - mean
    var = total(valid * centred * centred) / tally
    inv_std = lax.rsqrt(var + EPSILON)
    normed = centred * inv_std
    pre_act = normed * own[part : part + 1, 35:36] + own[part : part + 1, 36:37]
    cdf, density = erf_parts(pre_act)
    return normed, inv_std, pre_act * cdf, cdf + pre_act * density


def conv_backward(
    message, step, base, normed_of, slope_of, inv_of, own, valid, tally, spec_ref, kernel_spec, x_ref, high, low,
    e_high, e_low, consts, grad_ref,
):
    first, second, last, twiddle = consts
    sums = []
    for part in range(OWN):
        columns = []
        for y in range(4):
            pieces = []
            for b in range(2):
                for r in range(2):
                    start = y * step + base + signal_row(b, part, r)
                    pieces.append(message[pl.ds(start, 32, stride=4 * step), :])
            columns.append(jnp.concatenate(pieces, axis=0))
        act_grad = jnp.concatenate(columns, axis=1)
        normed = normed_of(part)
        pre_grad = act_grad * slope_of(part)
        bias_total = total(pre_grad)
        gain_total = total(pre_grad * normed)
        gain = own[part : part + 1, 35:36]
        conv_grad = inv_of(part) * (
            gain * pre_grad - valid * (gain * bias_total + normed * (gain * gain_total)) / tally
        )
        conv_low = conv_grad.astype(BF16)
        for b in range(2):
            piece = conv_low[b * 64 : b * 64 + 64, :]
            x_ref[b * 128 : b * 128 + 64, block(part, 512)] = piece
            x_ref[b * 128 + 64 : b * 128 + 128, block(part, 512)] = piece
        sums.append((gain_total, bias_total))
    grad_ref[...] = transform(x_ref, high, low, first, second, twiddle, SIGNALS)
    for part in range(OWN):
        k_re, k_im = kernel_parts(kernel_spec, part)
        corr_re, corr_im = None, None
        for y in range(4):
            rows = block(part * 4 + y)
            g_re, g_im = grad_ref[rows, RE], grad_ref[rows, IM]
            s_re, s_im = spec_ref[rows, RE], spec_ref[rows, IM]
            put_halves(high, low, rows, RE, k_re * g_re + k_im * g_im)
            put_halves(high, low, rows, IM, k_re * g_im - k_im * g_re)
            now_re, now_im = s_re * g_re + s_im * g_im, s_re * g_im - s_im * g_re
            corr_re = now_re if corr_re is None else corr_re + now_re
            corr_im = now_im if corr_im is None else corr_im + now_im
        put_halves(high, low, block(SIGNALS + part), RE, corr_re)
        put_halves(high, low, block(SIGNALS + part), IM, corr_im)
    returned = transform_back(high, low, e_high, e_low, second, last, twiddle, SIGNALS + OWN)
    return returned, sums


def sin_cos(angle):
    turns = jnp.floor(angle * (2.0 / math.pi) + 0.5)
    rest = angle - turns * 1.5703125
    rest = rest - turns * 4.837512969970703125e-4
    rest = rest - turns * 7.549789948768648e-8
    square = rest * rest
    sine = rest + rest * square * (
        -1.6666654611e-1 + square * (8.3321608736e-3 + square * -1.9515295891e-4)
    )
    cosine = 1.0 - 0.5 * square + square * square * (
        4.166664568298827e-2 + square * (-1.388731625493765e-3 + square * 2.443315711809948e-5)
    )
    half = jnp.floor(turns * 0.5)
    odd = turns - 2.0 * half
    sign = 1.0 - 2.0 * (half - 2.0 * jnp.floor(half * 0.5))
    is_odd = odd > 0.5
    return sign * jnp.where(is_odd, cosine, sine), sign * jnp.where(is_odd, -sine, cosine)


CHUNK = 1024
F_TABLE = (0, 4, 7)
C_TABLE = (1, 3, 6)


def envelope_of(times, own):
    lower, upper = own[:, 33:34], own[:, 34:35]
    inside = (times >= lower) & (times < upper)
    offset = (times - lower) / (0.5 * (upper - lower))
    return jnp.where(inside, jnp.exp(-0.5 * offset * offset), 0.0)


def stacked_weight(weight):
    high, low = high_low(weight)
    return jnp.concatenate([high, high, low], axis=1).astype(BF16)


def stacked_dot(weight, value):
    high = value.astype(BF16)
    low = (value - high.astype(F32)).astype(BF16)
    return dot(weight, jnp.concatenate([high, low, high], axis=0))


def own_parameters(layer, number, out_w, out_b, window, gain, bias, gabor, hidden_b, wide, tall, own, columns):
    wide[...] = jnp.zeros(wide.shape, F32)
    wide[0:32, 0:CHANNELS] = out_w[layer]
    wide[32:33, 0:CHANNELS] = out_b[layer : layer + 1, :]
    wide[33:35, 0:CHANNELS] = window[layer].astype(F32)
    wide[35:36, 0:CHANNELS] = gain[layer : layer + 1, :]
    wide[36:37, 0:CHANNELS] = bias[layer : layer + 1, :]
    tall[0:PADDED, :] = jnp.transpose(wide[...])
    tall[PADDED : PADDED + 8, :] = jnp.zeros((8, LANES), F32)
    row = lax.broadcasted_iota(jnp.int32, (8, LANES), 0)
    lane = lax.broadcasted_iota(jnp.int32, (8, LANES), 1)
    mine = tall[pl.ds(number * OWN, 8), :]
    unused = (row >= OWN) | (number * OWN + row >= CHANNELS)
    own[...] = jnp.where(unused, jnp.where(lane == 34, float(SAMPLES), 0.0), mine)
    wide[:, 0:LANES] = jnp.zeros((LANES, LANES), F32)
    for j in range(3):
        wide[4 * j : 4 * j + 4, 0:HIDDEN] = gabor[layer, j]
    wide[12:14, 0:HIDDEN] = hidden_b[layer]
    columns[...] = jnp.transpose(wide[:, 0:LANES])[0:HIDDEN, :]


def sample_rows(first_lane, count):
    lane = first_lane + lax.broadcasted_iota(jnp.int32, (1, count), 1)
    times = times_of(lax.shift_right_logical(lane, 7 * jnp.ones_like(lane)), lane & 127)
    return times, times * (2.0 / (SAMPLES - 1)) - 1.0


def generate(columns, hidden_w, own, tab, rows):
    turns = []
    for j in range(3):
        turn = sin_cos(columns[:, 4 * j + 2 : 4 * j + 3] * (512.0 / (SAMPLES - 1)))
        turns.append([jnp.broadcast_to(value, (HIDDEN, LANES)) for value in turn])

    def step(i, carry):
        _, places = sample_rows(i * CHUNK, CHUNK)
        for j in range(3):
            sharpness, centre = columns[:, 4 * j : 4 * j + 1], columns[:, 4 * j + 1 : 4 * j + 2]
            frequency, phase = columns[:, 4 * j + 2 : 4 * j + 3], columns[:, 4 * j + 3 : 4 * j + 4]
            sine, cosine = sin_cos(frequency * places[:, 0:LANES] + phase)
            turn_sin, turn_cos = turns[j]
            for n in range(CHUNK // LANES):
                width = sharpness * (places[:, block(n)] - centre)
                bell = jnp.exp(-0.5 * width * width)
                here = pl.ds(pl.multiple_of(i * CHUNK + n * LANES, LANES), LANES)
                tab[F_TABLE[j], :, here] = bell * sine
                tab[C_TABLE[j], :, here] = bell * cosine
                sine, cosine = sine * turn_cos + cosine * turn_sin, cosine * turn_cos - sine * turn_sin
        return carry

    lax.fori_loop(0, SAMPLES // CHUNK, step, 0, unroll=2)
    weights = [stacked_weight(hidden_w[0]), stacked_weight(hidden_w[1]), stacked_weight(own[:, 0:32])]
    u_1 = stacked_dot(weights[0], tab[0]) + columns[:, 12:13]
    z_1 = u_1 * tab[4]
    tab[2] = z_1
    tab[3] = u_1 * tab[3]
    u_2 = stacked_dot(weights[1], z_1) + columns[:, 13:14]
    z_2 = u_2 * tab[7]
    tab[5] = z_2
    tab[6] = u_2 * tab[6]
    raw = stacked_dot(weights[2], z_2) + own[:, 32:33]
    times, _ = sample_rows(0, SAMPLES)
    rows[...] = raw * envelope_of(times, own)


def generate_back(kernel_grad, columns, hidden_w, own, tab, rows, sums, mats):
    rows[...] = jnp.zeros(rows.shape, F32)
    for part in range(OWN):
        grad = kernel_grad(part)
        for n in range(64):
            rows[part : part + 1, block(n)] = grad[n : n + 1, :]
    sums[...] = jnp.zeros(sums.shape, F32)
    mats[...] = jnp.zeros(mats.shape, F32)
    turned = jnp.transpose(jnp.concatenate([own[...], jnp.zeros((120, 128), F32)], axis=0))
    weight = [turned[0:32, part : part + 1] for part in range(OWN)]
    back = [stacked_weight(jnp.transpose(hidden_w[j])) for j in range(2)]

    def fold(value):
        acc = value[:, block(0)]
        for i in range(1, CHUNK // LANES):
            acc = acc + value[:, block(i)]
        return acc

    def add(k, value):
        sums[block(k, 32), :] += fold(value)

    def step(i, carry):
        span = pl.ds(pl.multiple_of(i * CHUNK, CHUNK), CHUNK)
        times, places = sample_rows(i * CHUNK, CHUNK)
        draw = rows[:, span] * envelope_of(times, own)
        dz_2 = weight[0] * draw[0:1, :] + weight[1] * draw[1:2, :] + weight[2] * draw[2:3, :]

        def level(j, e_value, g_value):
            centre = columns[:, 4 * j + 1 : 4 * j + 2]
            offset = places - centre
            moment = e_value * offset
            add(4 * j, moment * offset)
            add(4 * j + 1, moment)
            add(4 * j + 2, g_value * places)
            add(4 * j + 3, g_value)

        z_2 = tab[5, :, span]
        level(2, dz_2 * z_2, dz_2 * tab[6, :, span])
        du_2 = dz_2 * tab[7, :, span]
        add(13, du_2)
        dz_1 = stacked_dot(back[1], du_2)
        z_1 = tab[2, :, span]
        level(1, dz_1 * z_1, dz_1 * tab[3, :, span])
        du_1 = dz_1 * tab[4, :, span]
        add(12, du_1)
        dz_0 = stacked_dot(back[0], du_1)
        z_0 = tab[0, :, span]
        level(0, dz_0 * z_0, dz_0 * tab[1, :, span])
        sums[14 * 32 : 14 * 32 + 8, :] += fold(draw)
        left = jnp.concatenate([du_1, du_2, draw], axis=0)
        right = jnp.concatenate([z_0, z_1, z_2, jnp.zeros_like(z_0)], axis=0)
        left_high, right_high = left.astype(BF16), right.astype(BF16)
        left_low = (left - left_high.astype(F32)).astype(BF16)
        right_low = (right - right_high.astype(F32)).astype(BF16)
        mats[...] += (
            dot_rows(left_high, right_high) + dot_rows(left_low, right_high) + dot_rows(left_high, right_low)
        )
        return carry

    lax.fori_loop(0, SAMPLES // CHUNK, step, 0, unroll=2)
    lane = lax.broadcasted_iota(jnp.int32, (32, LANES), 1)
    hidden = jnp.where(lane < 32, mats[0:32, :], jnp.where(lane < 64, mats[32:64, :], 0.0))

    def column(k):
        return jnp.sum(sums[block(k, 32), :], axis=1, keepdims=True)

    hidden = jnp.where(lane == 64, column(12), hidden)
    hidden = jnp.where(lane == 65, column(13), hidden)
    for j in range(3):
        sharpness = columns[:, 4 * j : 4 * j + 1]
        hidden = jnp.where(lane == 66 + 4 * j, -sharpness * column(4 * j), hidden)
        hidden = jnp.where(lane == 67 + 4 * j, sharpness * sharpness * column(4 * j + 1), hidden)
        hidden = jnp.where(lane == 68 + 4 * j, column(4 * j + 2), hidden)
        hidden = jnp.where(lane == 69 + 4 * j, column(4 * j + 3), hidden)
    lane8 = lax.broadcasted_iota(jnp.int32, (8, LANES), 1)
    outer = pltpu.roll(mats[64:72, :], LANES - 64, 1)
    raw_total = jnp.sum(sums[14 * 32 : 14 * 32 + 8, :], axis=1, keepdims=True)
    outer = jnp.where(lane8 < 32, outer, 0.0)
    outer = jnp.where(lane8 == 32, raw_total, outer)
    return hidden, outer


def with_norm_sums(outer, sums):
    row = lax.broadcasted_iota(jnp.int32, (8, LANES), 0)
    lane = lax.broadcasted_iota(jnp.int32, (8, LANES), 1)
    for part in range(OWN):
        gain_total, bias_total = sums[part]
        outer = jnp.where((row == part) & (lane == 33), gain_total, outer)
        outer = jnp.where((row == part) & (lane == 34), bias_total, outer)
    return outer


def one_row(outer):
    lane = lax.broadcasted_iota(jnp.int32, (1, LANES), 1)
    result = jnp.zeros((1, LANES), F32)
    for part in range(OWN):
        row = outer[part : part + 1, :]
        moved = pltpu.roll(row, 32 * part, 1) if part else row
        result = jnp.where((lane >= 32 * part) & (lane < 32 * part + 32), moved, result)
        moved = pltpu.roll(row, 64 + 3 * part, 1)
        result = jnp.where((lane >= 96 + 3 * part) & (lane < 99 + 3 * part), moved, result)
    return result


def packed_hidden(hidden):
    lane16 = lax.broadcasted_iota(jnp.int32, (16, LANES), 1)
    upper = jnp.where(lane16 < 64, hidden[0:16, :], pltpu.roll(hidden[16:32, :], 64, 1))
    lane4 = lax.broadcasted_iota(jnp.int32, (4, LANES), 1)
    lower = jnp.zeros((4, LANES), F32)
    for g in range(8):
        moved = pltpu.roll(hidden, (64 + 16 * g) % LANES, 1)[4 * g : 4 * g + 4, :]
        lower = jnp.where((lane4 >= 16 * g) & (lane4 < 16 * g + 16), moved, lower)
    return upper, lower


def unpacked_hidden(upper, lower):
    lane16 = lax.broadcasted_iota(jnp.int32, (16, LANES), 1)
    lane32 = lax.broadcasted_iota(jnp.int32, (32, LANES), 1)
    top = jnp.concatenate([upper, pltpu.roll(upper, 64, 1)], axis=0)
    tiled = jnp.concatenate([lower] * 8, axis=0)
    row32 = lax.broadcasted_iota(jnp.int32, (32, LANES), 0)
    rest = jnp.zeros((32, LANES), F32)
    for g in range(8):
        moved = pltpu.roll(tiled, (64 - 16 * g) % LANES, 1)
        rest = jnp.where((row32 >= 4 * g) & (row32 < 4 * g + 4), moved, rest)
    return jnp.where(lane32 < 64, top, rest)


def high_low(value):
    high = value.astype(BF16).astype(F32)
    return high, value - high


def valid_row(meta, i):
    lane = lax.broadcasted_iota(jnp.int32, (1, LANES), 1)
    return (meta[2] * PIECE + (i // 2) * LANES + lane < meta[i % 2]).astype(F32)


def masked(meta, rows):
    mask = jnp.concatenate([valid_row(meta, i) for i in range(4)] * 2, axis=0)
    return (rows.reshape(-1, 8, LANES) * mask[None]).reshape(-1, LANES)


CLIP_ROWS = 4 * CHANNELS
PADDED_ROWS = 4 * PADDED


def put_padded(padded, rows):
    padded[0:CLIP_ROWS, :] = rows
    padded[CLIP_ROWS:PADDED_ROWS, :] = jnp.zeros((PADDED_ROWS - CLIP_ROWS, LANES), F32)


def rows_to_message(padded, out, step, base):
    for m in range(12):
        out[pl.ds(base + m, DEVICES, stride=step), :] = padded[pl.ds(m, DEVICES, stride=12), :]


def rows_of_channels(padded, i):
    return padded[pl.ds(i, PADDED, stride=4), :]


def source_kernel(meta, x_ref, mix_w, out_ref, padded, out):
    put_padded(padded, masked(meta, x_ref[...]))
    for b in range(2):
        length = meta[b]
        upper = lax.shift_right_logical(length, 7)
        out[pl.ds(12 + 2 * b, DEVICES, stride=16), :] = jnp.full((DEVICES, LANES), upper.astype(F32))
        out[pl.ds(13 + 2 * b, DEVICES, stride=16), :] = jnp.full(
            (DEVICES, LANES), (length - upper * 128).astype(F32)
        )
    rows_to_message(padded, out, 16, 0)
    out_ref[...] = out[...].reshape(DEVICES, 16, LANES).astype(BF16)


def make_lookup(lookup):
    row = lax.broadcasted_iota(jnp.int32, (DEVICES, PADDED), 0)
    column = lax.broadcasted_iota(jnp.int32, (DEVICES, PADDED), 1)
    for part in range(OWN):
        lookup[block(part), :] = (column == OWN * row + part).astype(F32).astype(BF16)


def make_weights(mix_w, mix_b, wide, lookup, weights, weights_back):
    make_lookup(lookup)
    wide[...] = jnp.zeros(wide.shape, BF16)
    row = lax.broadcasted_iota(jnp.int32, (LANES, CHANNELS), 0)
    lines = jnp.where(row == 0, mix_b[0:1, :], jnp.where(row == 1, mix_b[1:2, :], 0.0))
    turned = jnp.transpose(jnp.concatenate([lines, jnp.zeros((LANES, PADDED - CHANNELS), F32)], axis=1))
    lane = lax.broadcasted_iota(jnp.int32, (PADDED, PADDED), 1)
    for layer in range(2):
        wide[0:CHANNELS, 0:CHANNELS] = mix_w[layer]
        weights_back[layer] = dot_rows(lookup[...], wide[...]).astype(BF16)
        value = dot_rows(wide[...], lookup[...])
        rest = turned[:, layer : layer + 1]
        for spot in SPOTS:
            high, rest = high_low(rest)
            value = jnp.where(lane == spot, high, value)
        weights[layer] = value.astype(BF16)


def make_kernel(layer, meta, params, consts, bundle, tab, scratch):
    out_w, out_b, window, gain, bias, gabor, hidden_b, hidden_w = params
    first, second, _, twiddle = consts
    wide, tall, rows, pieces, x_ref, high, low = scratch
    own, columns = bundle.at[OWN_ROWS, :], bundle.at[COLUMN_ROWS, :]
    own_parameters(layer, meta[3], out_w, out_b, window, gain, bias, gabor, hidden_b, wide, tall, own, columns)
    generate(columns, hidden_w.at[layer], own, tab, rows)
    for n in range(64):
        for part in range(OWN):
            pieces[part * 64 + n : part * 64 + n + 1, :] = rows[part : part + 1, block(n)]
    for part in range(OWN):
        piece = pieces[block(part, 64), :].astype(BF16)
        x_ref[0:64, block(part)] = piece
        x_ref[64:128, block(part)] = piece
        x_ref[128:256, block(part)] = jnp.zeros((128, LANES), BF16)
    spec = transform(x_ref, high, low, first, second, twiddle, OWN)
    bundle[0:SPEC_IM, :] = spec[:, RE]
    bundle[SPEC_IM : 2 * SPEC_IM, :] = spec[:, IM]


def forward_kernel(
    meta, message_ref, out_w, out_b, window, gain, bias, gabor, hidden_b, hidden_w,
    first, second, last, twiddle,
    out_ref, spec_ref, normed_ref, slope_ref, inv_ref, len_ref, kernel_spec, tab,
    message, x_ref, high, low, e_high, e_low, y_ref, out, *make_scratch,
):
    own = kernel_spec.at[OWN_ROWS, :]
    params = (out_w, out_b, window, gain, bias, gabor, hidden_b, hidden_w)
    make_kernel(0, meta, params, (first, second, last, twiddle), kernel_spec, tab, make_scratch)
    message[...] = spread(message_ref[...])
    for y in range(4):
        for b in range(2):
            start = y * 16 + 12 + 2 * b
            len_ref[2 * y + b : 2 * y + b + 1, :] = (
                message[start : start + 1, :] * 128.0 + message[start + 1 : start + 2, :]
            )
    load_signals(message, 16, x_ref)
    convolve(x_ref, spec_ref, kernel_spec, high, low, e_high, e_low, (first, second, last, twiddle), y_ref)
    valid, tally = valid_of(len_ref), tally_of(len_ref)
    inv_ref[...] = jnp.zeros((8, LANES), F32)
    for part in range(OWN):
        normed, inv_std, active, slope = normalise(y_ref, own, valid, tally, part)
        normed_ref[:, block(part, 512)] = normed
        slope_ref[:, block(part, 512)] = slope
        inv_ref[part : part + 1, :] = jnp.broadcast_to(inv_std, (1, LANES))
        y_ref[:, block(part, 512)] = active
    store_signals(out, 12, 0, lambda part, y: y_ref[:, block(part * 4 + y)])
    out_ref[...] = out[...].reshape(DEVICES, 3, 4, LANES).astype(BF16)


def gather_active(message, step, rhs):
    row = lax.broadcasted_iota(jnp.int32, (DEVICES, LANES), 0)
    for i in range(4):
        for part in range(OWN):
            piece = message[pl.ds(part * 4 + i, DEVICES, stride=step), :]
            if part != 1:
                piece = jnp.where(row >= (126 if part == 2 else 127), 1.0, piece)
            rhs[block(part), block(i)] = piece.astype(BF16)


def store_rows(value, out, step, base):
    for i in range(4):
        for part in range(OWN):
            out[pl.ds(base + part * 4 + i, DEVICES, stride=step), :] = value[block(part), block(i)]


def mix_kernel(
    meta, message_ref, x_ref, cotangent, mix_w, mix_b,
    out_ref, next_ref, active_ref, weights, weights_back, message, padded, out, low, wide, lookup,
):
    make_weights(mix_w, mix_b, wide, lookup, weights, weights_back)
    message[...] = spread(message_ref[...])
    gather_active(message, 12, active_ref)
    mixed = dot(weights[0], active_ref[...])
    put_padded(padded, x_ref[...])
    for i in range(4):
        valid = valid_row(meta, i)
        value = rows_of_channels(padded, i) + mixed[:, block(i)] * valid
        next_ref[pl.ds(i, PADDED, stride=4), :] = value
        padded[pl.ds(i, PADDED, stride=4), :] = value * valid
    rows_to_message(padded, out, 24, 0)
    put_padded(padded, masked(meta, cotangent[...]))
    for i in range(4):
        low[:, block(i)] = rows_of_channels(padded, i).astype(BF16)
    store_rows(dot(weights_back[1], low[...]), out, 24, 12)
    out_ref[...] = out[...].reshape(DEVICES, 24, LANES).astype(BF16)


def forward_backward_kernel(
    meta, message_ref, out_w, out_b, window, gain, bias, gabor, hidden_b, hidden_w,
    len_ref, first, second, last, twiddle,
    out_ref, hidden_out, outer_out,
    message, x_ref, high, low, e_high, e_low, y_ref, out, spec_ref, grad_ref, normed_ref, slope_ref, returned_ref,
    rows, sums, mats, kernel_spec, tab, *make_scratch,
):
    own, columns = kernel_spec.at[OWN_ROWS, :], kernel_spec.at[COLUMN_ROWS, :]
    consts = (first, second, last, twiddle)
    params = (out_w, out_b, window, gain, bias, gabor, hidden_b, hidden_w)
    make_kernel(1, meta, params, consts, kernel_spec, tab, make_scratch)
    message[...] = spread(message_ref[...])
    load_signals(message, 24, x_ref)
    convolve(x_ref, spec_ref, kernel_spec, high, low, e_high, e_low, consts, y_ref)
    valid, tally = valid_of(len_ref), tally_of(len_ref)
    inv = []
    for part in range(OWN):
        normed, inv_std, active, slope = normalise(y_ref, own, valid, tally, part)
        normed_ref[:, block(part, 512)] = normed
        slope_ref[:, block(part, 512)] = slope
        inv.append(inv_std)
        y_ref[:, block(part, 512)] = active
    store_signals(out, 24, 0, lambda part, y: y_ref[:, block(part * 4 + y)])
    returned, norm_sums = conv_backward(
        message, 24, 12, lambda part: normed_ref[:, block(part, 512)], lambda part: slope_ref[:, block(part, 512)],
        lambda part: inv[part], own, valid, tally, spec_ref, kernel_spec, x_ref, high, low, e_high, e_low, consts, grad_ref,
    )
    returned_ref[...] = returned
    store_signals(out, 24, 12, lambda part, y: returned_ref[:, block(part * 4 + y)])
    out_ref[...] = out[...].reshape(DEVICES, 24, LANES).astype(BF16)
    hidden, outer = generate_back(
        lambda part: returned_ref[0:64, block(SIGNALS + part)], columns, hidden_w.at[1], own, tab,
        rows, sums, mats,
    )
    hidden_out[...] = hidden
    outer_out[...] = with_norm_sums(outer, norm_sums)


def middle_kernel(
    meta, message_ref, x_ref, cotangent, weights, weights_back, active_0, hidden_1,
    output_ref, flow_ref, out_ref, message, padded, out, low_0, low_1, active_1,
):
    message[...] = spread(message_ref[...])
    gather_active(message, 24, active_1)
    mixed = dot(weights[1], active_1[...])
    for i in range(4):
        padded[pl.ds(i, PADDED, stride=4), :] = rows_of_channels(x_ref, i) + mixed[:, block(i)] * valid_row(meta, i)
    output_ref[...] = padded[0:CLIP_ROWS, :]
    put_padded(flow_ref, cotangent[...])
    for i in range(4):
        low_1[:, block(i)] = (rows_of_channels(flow_ref, i) * valid_row(meta, i)).astype(BF16)
    for m in range(12):
        padded[pl.ds(m, DEVICES, stride=12), :] = message[pl.ds(12 + m, DEVICES, stride=24), :]
    flow_ref[...] += masked(meta, padded[...])
    for i in range(4):
        low_0[:, block(i)] = (rows_of_channels(flow_ref, i) * valid_row(meta, i)).astype(BF16)
    store_rows(dot(weights_back[0], low_0[...]), out, 32, 0)
    for layer, (active, low) in enumerate(((active_0, low_0), (active_1, low_1))):
        part_sum = dot_rows(active[...], low[...])
        for part in range(OWN):
            for third in range(3):
                out[pl.ds(12 + layer * 9 + part * 3 + third, DEVICES, stride=32), :] = part_sum[
                    block(part), block(third)
                ]
    high, low = high_low(hidden_1[...])
    out[pl.ds(30, DEVICES, stride=32), :] = jnp.concatenate([high, jnp.zeros((96, LANES), F32)], axis=0)
    out[pl.ds(31, DEVICES, stride=32), :] = jnp.concatenate([low, jnp.zeros((96, LANES), F32)], axis=0)
    out_ref[...] = out[...].reshape(DEVICES, 32, LANES).astype(BF16)


LAST_ROWS = 56


def backward_kernel(
    message_ref, spec_ref, kernel_spec, normed_ref, slope_ref, inv_ref, len_ref,
    first, second, last, twiddle, hidden_w, tab, outer_1,
    out_ref,
    message, x_ref, high, low, e_high, e_low, out, grad_ref, returned_ref, rows, sums, mats,
):
    own, columns = kernel_spec.at[OWN_ROWS, :], kernel_spec.at[COLUMN_ROWS, :]
    consts = (first, second, last, twiddle)
    message[...] = spread(message_ref[...])
    valid, tally = valid_of(len_ref), tally_of(len_ref)
    returned, norm_sums = conv_backward(
        message, 32, 0, lambda part: normed_ref[:, block(part, 512)], lambda part: slope_ref[:, block(part, 512)],
        lambda part: inv_ref[part : part + 1, 0:1], own, valid, tally, spec_ref, kernel_spec, x_ref, high, low,
        e_high, e_low, consts, grad_ref,
    )
    returned_ref[...] = returned
    store_signals(out, 16, 0, lambda part, y: returned_ref[:, block(part * 4 + y)])
    hidden, outer = generate_back(
        lambda part: returned_ref[0:64, block(SIGNALS + part)], columns, hidden_w.at[0], own, tab,
        rows, sums, mats,
    )
    outer = with_norm_sums(outer, norm_sums)
    gathered = jnp.sum(message[...].reshape(DEVICES, 32, LANES), axis=0)
    upper, lower = packed_hidden(hidden)
    hidden_1_high, hidden_1_low = high_low(gathered[30:31, :] + gathered[31:32, :])
    outer_0_high, outer_0_low = high_low(one_row(outer))
    outer_1_high, outer_1_low = high_low(one_row(outer_1[...]))
    shared = jnp.concatenate(
        [
            gathered[0:30, :], upper, lower, hidden_1_high, hidden_1_low,
            outer_0_high, outer_0_low, outer_1_high, outer_1_low,
        ],
        axis=0,
    )
    row = lax.broadcasted_iota(jnp.int32, (DEVICES, 16, LANES), 1)
    own_rows = jnp.where(row < 12, out[...].reshape(DEVICES, 16, LANES), shared[None, 0:16, :])
    rest = jnp.broadcast_to(shared[None, 16:LAST_ROWS, :], (DEVICES, LAST_ROWS - 16, LANES))
    out_ref[...] = jnp.concatenate([own_rows, rest], axis=1).astype(BF16)


def last_kernel(
    meta, message_ref, flow_ref,
    input_grad, gabor_grad, hidden_w_grad, hidden_b_grad, out_w_grad, out_b_grad, gain_grad, bias_grad,
    mix_w_grad, mix_b_grad, message, padded, owned, thirds, lookup,
):
    make_lookup(lookup)
    message[...] = spread(message_ref[...])

    def rows_of(k, count=DEVICES):
        return message[pl.ds(k, count, stride=LAST_ROWS), :]

    for m in range(12):
        padded[pl.ds(m, DEVICES, stride=12), :] = rows_of(m)
    input_grad[...] = flow_ref[0:CLIP_ROWS, :] + masked(meta, padded[0:CLIP_ROWS, :])
    shared = jnp.sum(message[...].reshape(DEVICES, LAST_ROWS, LANES)[:, 24:56, :], axis=0)
    hidden_0 = unpacked_hidden(shared[6:22, :], shared[22:26, :])
    hidden_1 = rows_of(50, 32) + rows_of(51, 32)
    lane = lax.broadcasted_iota(jnp.int32, (DEVICES, LANES), 1)
    for layer, hidden in enumerate((hidden_0, hidden_1)):
        hidden_w_grad[layer, 0] = hidden[:, 0:32]
        hidden_w_grad[layer, 1] = pltpu.roll(hidden, 96, 1)[:, 0:32]
        turned = jnp.transpose(jnp.concatenate([hidden, jnp.zeros((96, LANES), F32)], axis=0))
        hidden_b_grad[layer] = turned[64:66, 0:32]
        for j in range(3):
            gabor_grad[layer, j] = turned[66 + 4 * j : 70 + 4 * j, 0:32]
        value = rows_of(52 + 2 * layer) + rows_of(53 + 2 * layer)
        for part in range(OWN):
            wide = pltpu.roll(value, (LANES - 32 * part) % LANES, 1)
            small = pltpu.roll(value, 64 - 3 * part, 1)
            owned[pl.ds(part, DEVICES, stride=OWN), :] = jnp.where(lane < 32, wide, small)
        turned = jnp.transpose(owned[...])
        out_w_grad[layer] = turned[0:32, 0:CHANNELS]
        out_b_grad[layer : layer + 1, :] = turned[32:33, 0:CHANNELS]
        gain_grad[layer : layer + 1, :] = turned[33:34, 0:CHANNELS]
        bias_grad[layer : layer + 1, :] = turned[34:35, 0:CHANNELS]
        bias_rows = []
        for part in range(OWN):
            for third in range(3):
                piece = rows_of(12 + layer * 9 + part * 3 + third)
                thirds[block(part), block(third)] = piece.astype(BF16)
                if part == 2:
                    bias_rows.append(piece[SPOT - 2 * DEVICES : SPOT - 2 * DEVICES + 1, :])
        mix_w_grad[:, layer, :] = dot_columns(thirds[...], lookup[...])[0:CHANNELS, 0:CHANNELS]
        mix_b_grad[layer : layer + 1, :] = jnp.concatenate(bias_rows, axis=1)[:, 0:CHANNELS]


def exchange(message):
    return lax.all_to_all(message, AXES, split_axis=0, concat_axis=0, tiled=True)


def to_rows(clips):
    return clips.reshape(2, CHANNELS, 2, LANES).transpose(1, 2, 0, 3).reshape(CLIP_ROWS, LANES)


def from_rows(rows):
    return rows.reshape(CHANNELS, 2, 2, LANES).transpose(2, 0, 1, 3).reshape(2, CHANNELS, PIECE)


def shards(
    inputs, lengths, window, gabor_params, hidden_w, hidden_b, out_w, out_b, bn_gain, bn_bias, mix_w, mix_b, cotangent
):
    position = lax.axis_index("seq").astype(jnp.int32)
    number = position * 4 + lax.axis_index("clips").astype(jnp.int32)
    const = {name: jnp.asarray(value) for name, value in TABLES.items()}
    meta = jnp.concatenate([lengths, jnp.stack([position, number])])
    inputs, cotangent = to_rows(inputs), to_rows(cotangent)

    def rows(count):
        return ((count, LANES), F32)

    with jax.named_scope("source_0"):
        (message,) = run(
            source_kernel, [((DEVICES, 16, LANES), BF16)], [meta, inputs, mix_w],
            [rows(PADDED_ROWS), rows(DEVICES * 16)], "source_0", 8, smem=(0,), far=(2,),
        )
        message = exchange(message)

    square = (PADDED, PADDED)
    generator = [
        jnp.swapaxes(out_w, 1, 2), out_b, jnp.swapaxes(window, 1, 2), bn_gain, bn_bias, gabor_params, hidden_b,
        hidden_w,
    ]
    shape_tab = ((8, HIDDEN, SAMPLES), F32)
    make_scratch = [
        ((LANES, PADDED), F32), rows(PADDED + 8), ((8, SAMPLES), F32), rows(192),
        ((256, OWN * LANES), BF16), ((OWN * LANES, 256), BF16), ((OWN * LANES, 256), BF16),
    ]
    mixers = ((2, *square), BF16)

    def scratch(signals):
        count = signals * LANES
        return [
            ((256, SIGNALS * LANES), BF16), ((count, 256), BF16), ((count, 256), BF16),
            ((256, count), BF16), ((256, count), BF16),
        ]

    shape_y = (LANES, SIGNALS * LANES)
    shape_s = (SIGNALS * LANES, 256)
    transforms = [const[name] for name in TABLE_NAMES]
    with jax.named_scope("conv_0"):
        message, spec_0, normed_0, slope_0, inv_0, lens, bundle_0, tab_0 = run(
            forward_kernel,
            [
                ((DEVICES, 3, 4, LANES), BF16), (shape_s, F32), (shape_y, F32), (shape_y, F32), rows(8), rows(8),
                rows(BUNDLE), shape_tab,
            ],
            [meta, message, *generator, *transforms],
            [rows(DEVICES * 16), *scratch(SIGNALS), (shape_y, F32), rows(DEVICES * 12), *make_scratch],
            "conv_0", 16, smem=(0,),
        )
        message = exchange(message)

    with jax.named_scope("mix_0"):
        message, middle, active_0, weights, weights_back = run(
            mix_kernel,
            [((DEVICES, 24, LANES), BF16), rows(PADDED_ROWS), ((PADDED, 512), BF16), mixers, mixers],
            [meta, message, inputs, cotangent, mix_w, mix_b],
            [rows(DEVICES * 12), rows(PADDED_ROWS), rows(DEVICES * 24), ((PADDED, 512), BF16), (square, BF16), (square, BF16)],
            "mix_0", 12, smem=(0,),
        )
        message = exchange(message)

    back_scratch = [((8, SAMPLES), F32), rows(14 * 32 + 8), rows(72)]
    with jax.named_scope("conv_1"):
        message, hidden_1, outer_1 = run(
            forward_backward_kernel,
            [((DEVICES, 24, LANES), BF16), rows(HIDDEN), rows(8)],
            [
                meta, message, *generator, lens, *transforms,
            ],
            [
                rows(DEVICES * 24), *scratch(SIGNALS + OWN), (shape_y, F32), rows(DEVICES * 24),
                (shape_s, F32), (shape_s, F32), (shape_y, F32), (shape_y, F32),
                ((LANES, (SIGNALS + OWN) * LANES), F32), *back_scratch, rows(BUNDLE), shape_tab, *make_scratch,
            ],
            "conv_1", 26, smem=(0,),
        )
        message = exchange(message)

    with jax.named_scope("mix_1"):
        outputs, flow, message = run(
            middle_kernel,
            [rows(CLIP_ROWS), rows(PADDED_ROWS), ((DEVICES, 32, LANES), BF16)],
            [meta, message, middle, cotangent, weights, weights_back, active_0, hidden_1],
            [
                rows(DEVICES * 24), rows(PADDED_ROWS), rows(DEVICES * 32),
                ((PADDED, 512), BF16), ((PADDED, 512), BF16), ((PADDED, 512), BF16),
            ],
            "mix_1", 12, smem=(0,),
        )
        message = exchange(message)

    with jax.named_scope("conv_back_0"):
        (message,) = run(
            backward_kernel,
            [((DEVICES, LAST_ROWS, LANES), BF16)],
            [
                message, spec_0, bundle_0, normed_0, slope_0, inv_0, lens, *transforms,
                hidden_w, tab_0, outer_1,
            ],
            [
                rows(DEVICES * 32), *scratch(SIGNALS + OWN), rows(DEVICES * 16), (shape_s, F32),
                ((LANES, (SIGNALS + OWN) * LANES), F32), *back_scratch,
            ],
            "conv_back_0", 16,
        )
        message = exchange(message)

    with jax.named_scope("gradients"):
        (
            input_grad, gabor_grad, hidden_w_grad, hidden_b_grad, out_w_grad, out_b_grad, gain_grad, bias_grad,
            mix_w_grad, mix_b_grad,
        ) = run(
            last_kernel,
            [
                rows(CLIP_ROWS), (gabor_params.shape, F32), (hidden_w.shape, F32), (hidden_b.shape, F32),
                ((2, HIDDEN, CHANNELS), F32), (out_b.shape, F32), (bn_gain.shape, F32), (bn_bias.shape, F32),
                ((CHANNELS, 2, CHANNELS), F32), (mix_b.shape, F32),
            ],
            [meta, message, flow],
            [rows(DEVICES * LAST_ROWS), rows(PADDED_ROWS), rows(PADDED), (square, BF16), (square, BF16)],
            "gradients", 14, smem=(0,),
        )
    return (
        from_rows(outputs), from_rows(input_grad), gabor_grad, hidden_w_grad, hidden_b_grad,
        jnp.swapaxes(out_w_grad, 1, 2), out_b_grad, gain_grad, bias_grad, jnp.swapaxes(mix_w_grad, 0, 1), mix_b_grad,
    )


def solution(mesh):
    clip = P("clips", None, "seq")
    in_specs = (clip, P("clips")) + (P(),) * 10 + (clip,)
    out_specs = (clip, clip) + (P(),) * 9
    return jax.shard_map(shards, mesh=mesh, in_specs=in_specs, out_specs=out_specs, check_vma=False)
```

```python
import math

import jax
import jax.numpy as jnp
import ml_dtypes
import numpy as np
from jax import lax
from jax.experimental import pallas as pl
from jax.experimental.pallas import tpu as pltpu
from jax.sharding import PartitionSpec as P

F32 = jnp.float32
BF16 = jnp.bfloat16
AXES = ("seq", "clips")
DEVICES = 128
OWN = 3
CHANNELS = 380
PADDED = DEVICES * OWN
SAMPLES = 8192
PIECE = 256
HIDDEN = 32
LANES = 128
SIGNALS = 12
TABLE_NAMES = ("first", "second", "last", "twiddle")
PERIOD = 2 * SAMPLES
EPSILON = 1e-05
MEGABYTE = 1024 * 1024
EXACT = lax.Precision.HIGHEST
SPOTS = (2 * DEVICES + 126, 2 * DEVICES + 127, 127)
SPOT = SPOTS[0]


def halves(table):
    high = table.astype(ml_dtypes.bfloat16)
    low = (table - high.astype(np.float64)).astype(ml_dtypes.bfloat16)
    return high, low


def tables():
    order = np.array([2 * j + r for r in range(2) for j in range(32)])
    k = np.arange(LANES)
    turn = 2 * np.pi * ((k[:, None] * order[None, :]) % LANES) / LANES
    c_high, c_low = halves(np.cos(turn))
    s_high, s_low = halves(np.sin(turn))
    first = np.concatenate(
        [
            np.concatenate([c_high, c_low, s_high, s_low], axis=1),
            np.concatenate([-s_high, -s_low, c_high, c_low], axis=1),
        ],
        axis=0,
    )
    turn = 2 * np.pi * ((k[:, None] * k[None, :]) % LANES) / LANES
    cosine, sine = np.cos(turn), np.sin(turn)
    second = halves(np.block([[cosine, -sine], [sine, cosine]]))
    turn = 2 * np.pi * ((order[:, None] * k[None, :]) % LANES) / LANES
    cosine, sine = np.cos(turn) / PERIOD, np.sin(turn) / PERIOD
    last = halves(np.block([[cosine, -sine], [sine, cosine]]))
    turn = 2 * np.pi * (k[:, None] * k[None, :]) / PERIOD
    twiddle = np.stack([np.cos(turn), np.sin(turn)]).astype(np.float32)
    return dict(
        first=first,
        second=np.stack(second),
        last=np.stack(last),
        twiddle=twiddle,
    )


TABLES = tables()


def run(body, outs, args, scratch, name, grant, smem=(), far=()):
    spaces = [pltpu.HBM if i in far else pltpu.SMEM if i in smem else pltpu.VMEM for i in range(len(args))]
    return pl.pallas_call(
        body,
        out_shape=[jax.ShapeDtypeStruct(shape, kind) for shape, kind in outs],
        in_specs=[pl.BlockSpec(memory_space=space) for space in spaces],
        out_specs=[pl.BlockSpec(memory_space=pltpu.VMEM)] * len(outs),
        scratch_shapes=[pltpu.VMEM(shape, kind) for shape, kind in scratch],
        compiler_params=pltpu.CompilerParams(vmem_limit_bytes=grant * MEGABYTE),
        name=name,
    )(*args)


def dot(a, b):
    return jnp.dot(a, b, preferred_element_type=F32)


def dot_rows(a, b, precision=None):
    return lax.dot_general(a, b, (((1,), (1,)), ((), ())), precision=precision, preferred_element_type=F32)


def dot_columns(a, b, precision=None):
    return lax.dot_general(a, b, (((0,), (0,)), ((), ())), precision=precision, preferred_element_type=F32)


def triple(a_high, a_low, b_high, b_low):
    left = jnp.concatenate([a_high, a_low, a_high], axis=1)
    return dot(left, jnp.concatenate([b_high, b_high, b_low], axis=0))


def triple_rows(a_high, a_low, b_high, b_low):
    left = jnp.concatenate([a_high, a_low, a_high], axis=1)
    return dot_rows(left, jnp.concatenate([b_high, b_high, b_low], axis=1))


def put_halves(high_ref, low_ref, rows, columns, value):
    high = value.astype(BF16)
    high_ref[rows, columns] = high
    low_ref[rows, columns] = (value - high.astype(F32)).astype(BF16)


def block(i, size=LANES):
    return slice(i * size, (i + 1) * size)


RE, IM = slice(0, LANES), slice(LANES, 2 * LANES)


def signal_row(b, part, r):
    return part * 4 + r * 2 + b


def spread(message):
    return message.astype(F32).reshape(-1, LANES)


def transform(x_ref, high_ref, low_ref, first, second, twiddle, count):
    part_a = dot(first[...], x_ref[:, : count * LANES])
    cosine, sine = twiddle[0], twiddle[1]
    for s in range(count):
        real, imag = part_a[:LANES, block(s)], part_a[LANES:, block(s)]
        put_halves(high_ref, low_ref, block(s), RE, real * cosine + imag * sine)
        put_halves(high_ref, low_ref, block(s), IM, imag * cosine - real * sine)
    rows = slice(0, count * LANES)
    return triple(high_ref[rows, :], low_ref[rows, :], second[0], second[1])


def transform_back(high_ref, low_ref, e_high, e_low, second, last, twiddle, count):
    rows = slice(0, count * LANES)
    part_d = triple_rows(high_ref[rows, :], low_ref[rows, :], second[0], second[1])
    cosine, sine = twiddle[0], twiddle[1]
    for s in range(count):
        real, imag = part_d[block(s), RE], part_d[block(s), IM]
        put_halves(e_high, e_low, RE, block(s), real * cosine - imag * sine)
        put_halves(e_high, e_low, IM, block(s), real * sine + imag * cosine)
    return triple(last[0], last[1], e_high[:, rows], e_low[:, rows])


def erf_parts(value):
    cdf = 0.5 * (1.0 + lax.erf(value * math.sqrt(0.5)))
    return cdf, jnp.exp(-0.5 * value * value) * (1.0 / math.sqrt(2.0 * math.pi))


def total(value):
    return jnp.sum(jnp.sum(value, axis=0, keepdims=True), axis=1, keepdims=True)


def times_of(row, lane):
    return (256 * (row & 31) + 128 * lax.shift_right_logical(row, 5 * jnp.ones_like(row)) + lane).astype(F32)


def valid_of(len_ref):
    row = lax.broadcasted_iota(jnp.int32, (LANES, LANES), 0) & 63
    times = times_of(row, lax.broadcasted_iota(jnp.int32, (LANES, LANES), 1))
    columns = []
    for y in range(4):
        upper = times[0:64, :] < len_ref[2 * y : 2 * y + 1, :]
        lower = times[64:128, :] < len_ref[2 * y + 1 : 2 * y + 2, :]
        columns.append(jnp.concatenate([upper, lower], axis=0).astype(F32))
    return jnp.concatenate(columns, axis=1)


def tally_of(len_ref):
    return jnp.sum(len_ref[:, 0:1], axis=0, keepdims=True)


def load_signals(message, step, x_ref):
    for part in range(OWN):
        for y in range(4):
            lanes = block(part * 4 + y)
            for b in range(2):
                for r in range(2):
                    start = y * step + signal_row(b, part, r)
                    piece = message[pl.ds(start, 32, stride=4 * step), :].astype(BF16)
                    x_ref[b * 128 + r * 32 : b * 128 + r * 32 + 32, lanes] = piece
                    x_ref[b * 128 + r * 32 + 64 : b * 128 + r * 32 + 96, lanes] = piece


def store_signals(out, step, base, get):
    for part in range(OWN):
        for y in range(4):
            value = get(part, y)
            for b in range(2):
                for r in range(2):
                    start = y * step + base + signal_row(b, part, r)
                    out[pl.ds(start, 32, stride=4 * step), :] = value[b * 64 + r * 32 : b * 64 + r * 32 + 32, :]


SPEC_IM = OWN * LANES
OWN_ROWS = slice(2 * SPEC_IM, 2 * SPEC_IM + 8)
COLUMN_ROWS = slice(2 * SPEC_IM + 8, 2 * SPEC_IM + 8 + HIDDEN)
BUNDLE = 2 * SPEC_IM + 8 + HIDDEN


def kernel_parts(bundle, part):
    return bundle[block(part), :], bundle[SPEC_IM + part * LANES : SPEC_IM + (part + 1) * LANES, :]


def convolve(x_ref, spec_ref, kernel_spec, high, low, e_high, e_low, consts, y_ref):
    first, second, last, twiddle = consts
    spec_ref[...] = transform(x_ref, high, low, first, second, twiddle, SIGNALS)
    for part in range(OWN):
        k_re, k_im = kernel_parts(kernel_spec, part)
        for y in range(4):
            rows = block(part * 4 + y)
            s_re, s_im = spec_ref[rows, RE], spec_ref[rows, IM]
            put_halves(high, low, rows, RE, s_re * k_re - s_im * k_im)
            put_halves(high, low, rows, IM, s_re * k_im + s_im * k_re)
    y_ref[...] = transform_back(high, low, e_high, e_low, second, last, twiddle, SIGNALS)


def normalise(y_ref, own, valid, tally, part):
    value = y_ref[:, block(part, 512)]
    mean = total(valid * value) / tally
    centred = value - mean
    var = total(valid * centred * centred) / tally
    inv_std = lax.rsqrt(var + EPSILON)
    normed = centred * inv_std
    pre_act = normed * own[part : part + 1, 35:36] + own[part : part + 1, 36:37]
    cdf, density = erf_parts(pre_act)
    return normed, inv_std, pre_act * cdf, cdf + pre_act * density


def conv_backward(
    message, step, base, normed_of, slope_of, inv_of, own, valid, tally, spec_ref, kernel_spec, x_ref, high, low,
    e_high, e_low, consts, grad_ref,
):
    first, second, last, twiddle = consts
    sums = []
    for part in range(OWN):
        columns = []
        for y in range(4):
            pieces = []
            for b in range(2):
                for r in range(2):
                    start = y * step + base + signal_row(b, part, r)
                    pieces.append(message[pl.ds(start, 32, stride=4 * step), :])
            columns.append(jnp.concatenate(pieces, axis=0))
        act_grad = jnp.concatenate(columns, axis=1)
        normed = normed_of(part)
        pre_grad = act_grad * slope_of(part)
        bias_total = total(pre_grad)
        gain_total = total(pre_grad * normed)
        gain = own[part : part + 1, 35:36]
        conv_grad = inv_of(part) * (
            gain * pre_grad - valid * (gain * bias_total + normed * (gain * gain_total)) / tally
        )
        conv_low = conv_grad.astype(BF16)
        for b in range(2):
            piece = conv_low[b * 64 : b * 64 + 64, :]
            x_ref[b * 128 : b * 128 + 64, block(part, 512)] = piece
            x_ref[b * 128 + 64 : b * 128 + 128, block(part, 512)] = piece
        sums.append((gain_total, bias_total))
    grad_ref[...] = transform(x_ref, high, low, first, second, twiddle, SIGNALS)
    for part in range(OWN):
        k_re, k_im = kernel_parts(kernel_spec, part)
        corr_re, corr_im = None, None
        for y in range(4):
            rows = block(part * 4 + y)
            g_re, g_im = grad_ref[rows, RE], grad_ref[rows, IM]
            s_re, s_im = spec_ref[rows, RE], spec_ref[rows, IM]
            put_halves(high, low, rows, RE, k_re * g_re + k_im * g_im)
            put_halves(high, low, rows, IM, k_re * g_im - k_im * g_re)
            now_re, now_im = s_re * g_re + s_im * g_im, s_re * g_im - s_im * g_re
            corr_re = now_re if corr_re is None else corr_re + now_re
            corr_im = now_im if corr_im is None else corr_im + now_im
        put_halves(high, low, block(SIGNALS + part), RE, corr_re)
        put_halves(high, low, block(SIGNALS + part), IM, corr_im)
    returned = transform_back(high, low, e_high, e_low, second, last, twiddle, SIGNALS + OWN)
    return returned, sums


def sin_cos(angle):
    turns = jnp.floor(angle * (2.0 / math.pi) + 0.5)
    rest = angle - turns * 1.5703125
    rest = rest - turns * 4.837512969970703125e-4
    rest = rest - turns * 7.549789948768648e-8
    square = rest * rest
    sine = rest + rest * square * (
        -1.6666654611e-1 + square * (8.3321608736e-3 + square * -1.9515295891e-4)
    )
    cosine = 1.0 - 0.5 * square + square * square * (
        4.166664568298827e-2 + square * (-1.388731625493765e-3 + square * 2.443315711809948e-5)
    )
    half = jnp.floor(turns * 0.5)
    odd = turns - 2.0 * half
    sign = 1.0 - 2.0 * (half - 2.0 * jnp.floor(half * 0.5))
    is_odd = odd > 0.5
    return sign * jnp.where(is_odd, cosine, sine), sign * jnp.where(is_odd, -sine, cosine)


CHUNK = 1024
F_TABLE = (0, 4, 7)
C_TABLE = (1, 3, 6)


def envelope_of(times, own):
    lower, upper = own[:, 33:34], own[:, 34:35]
    inside = (times >= lower) & (times < upper)
    offset = (times - lower) / (0.5 * (upper - lower))
    return jnp.where(inside, jnp.exp(-0.5 * offset * offset), 0.0)


def stacked_weight(weight):
    high, low = high_low(weight)
    return jnp.concatenate([high, high, low], axis=1).astype(BF16)


def stacked_dot(weight, value):
    high = value.astype(BF16)
    low = (value - high.astype(F32)).astype(BF16)
    return dot(weight, jnp.concatenate([high, low, high], axis=0))


def own_parameters(layer, number, out_w, out_b, window, gain, bias, gabor, hidden_b, wide, tall, own, columns):
    wide[...] = jnp.zeros(wide.shape, F32)
    wide[0:32, 0:CHANNELS] = out_w[layer]
    wide[32:33, 0:CHANNELS] = out_b[layer : layer + 1, :]
    wide[33:35, 0:CHANNELS] = window[layer].astype(F32)
    wide[35:36, 0:CHANNELS] = gain[layer : layer + 1, :]
    wide[36:37, 0:CHANNELS] = bias[layer : layer + 1, :]
    tall[0:PADDED, :] = jnp.transpose(wide[...])
    tall[PADDED : PADDED + 8, :] = jnp.zeros((8, LANES), F32)
    row = lax.broadcasted_iota(jnp.int32, (8, LANES), 0)
    lane = lax.broadcasted_iota(jnp.int32, (8, LANES), 1)
    mine = tall[pl.ds(number * OWN, 8), :]
    unused = (row >= OWN) | (number * OWN + row >= CHANNELS)
    own[...] = jnp.where(unused, jnp.where(lane == 34, float(SAMPLES), 0.0), mine)
    wide[:, 0:LANES] = jnp.zeros((LANES, LANES), F32)
    for j in range(3):
        wide[4 * j : 4 * j + 4, 0:HIDDEN] = gabor[layer, j]
    wide[12:14, 0:HIDDEN] = hidden_b[layer]
    columns[...] = jnp.transpose(wide[:, 0:LANES])[0:HIDDEN, :]


def sample_rows(first_lane, count):
    lane = first_lane + lax.broadcasted_iota(jnp.int32, (1, count), 1)
    times = times_of(lax.shift_right_logical(lane, 7 * jnp.ones_like(lane)), lane & 127)
    return times, times * (2.0 / (SAMPLES - 1)) - 1.0


def generate(columns, hidden_w, own, tab, rows):
    turns = []
    for j in range(3):
        turn = sin_cos(columns[:, 4 * j + 2 : 4 * j + 3] * (512.0 / (SAMPLES - 1)))
        turns.append([jnp.broadcast_to(value, (HIDDEN, LANES)) for value in turn])

    def step(i, carry):
        _, places = sample_rows(i * CHUNK, CHUNK)
        for j in range(3):
            sharpness, centre = columns[:, 4 * j : 4 * j + 1], columns[:, 4 * j + 1 : 4 * j + 2]
            frequency, phase = columns[:, 4 * j + 2 : 4 * j + 3], columns[:, 4 * j + 3 : 4 * j + 4]
            sine, cosine = sin_cos(frequency * places[:, 0:LANES] + phase)
            turn_sin, turn_cos = turns[j]
            for n in range(CHUNK // LANES):
                width = sharpness * (places[:, block(n)] - centre)
                bell = jnp.exp(-0.5 * width * width)
                here = pl.ds(pl.multiple_of(i * CHUNK + n * LANES, LANES), LANES)
                tab[F_TABLE[j], :, here] = bell * sine
                tab[C_TABLE[j], :, here] = bell * cosine
                sine, cosine = sine * turn_cos + cosine * turn_sin, cosine * turn_cos - sine * turn_sin
        return carry

    lax.fori_loop(0, SAMPLES // CHUNK, step, 0, unroll=2)
    weights = [stacked_weight(hidden_w[0]), stacked_weight(hidden_w[1]), stacked_weight(own[:, 0:32])]
    u_1 = stacked_dot(weights[0], tab[0]) + columns[:, 12:13]
    z_1 = u_1 * tab[4]
    tab[2] = z_1
    tab[3] = u_1 * tab[3]
    u_2 = stacked_dot(weights[1], z_1) + columns[:, 13:14]
    z_2 = u_2 * tab[7]
    tab[5] = z_2
    tab[6] = u_2 * tab[6]
    raw = stacked_dot(weights[2], z_2) + own[:, 32:33]
    times, _ = sample_rows(0, SAMPLES)
    rows[...] = raw * envelope_of(times, own)


def generate_back(kernel_grad, columns, hidden_w, own, tab, rows, sums, mats):
    rows[...] = jnp.zeros(rows.shape, F32)
    for part in range(OWN):
        grad = kernel_grad(part)
        for n in range(64):
            rows[part : part + 1, block(n)] = grad[n : n + 1, :]
    sums[...] = jnp.zeros(sums.shape, F32)
    mats[...] = jnp.zeros(mats.shape, F32)
    turned = jnp.transpose(jnp.concatenate([own[...], jnp.zeros((120, 128), F32)], axis=0))
    weight = [turned[0:32, part : part + 1] for part in range(OWN)]
    back = [stacked_weight(jnp.transpose(hidden_w[j])) for j in range(2)]

    def fold(value):
        acc = value[:, block(0)]
        for i in range(1, CHUNK // LANES):
            acc = acc + value[:, block(i)]
        return acc

    def add(k, value):
        sums[block(k, 32), :] += fold(value)

    def step(i, carry):
        span = pl.ds(pl.multiple_of(i * CHUNK, CHUNK), CHUNK)
        times, places = sample_rows(i * CHUNK, CHUNK)
        draw = rows[:, span] * envelope_of(times, own)
        dz_2 = weight[0] * draw[0:1, :] + weight[1] * draw[1:2, :] + weight[2] * draw[2:3, :]

        def level(j, e_value, g_value):
            centre = columns[:, 4 * j + 1 : 4 * j + 2]
            offset = places - centre
            moment = e_value * offset
            add(4 * j, moment * offset)
            add(4 * j + 1, moment)
            add(4 * j + 2, g_value * places)
            add(4 * j + 3, g_value)

        z_2 = tab[5, :, span]
        level(2, dz_2 * z_2, dz_2 * tab[6, :, span])
        du_2 = dz_2 * tab[7, :, span]
        add(13, du_2)
        dz_1 = stacked_dot(back[1], du_2)
        z_1 = tab[2, :, span]
        level(1, dz_1 * z_1, dz_1 * tab[3, :, span])
        du_1 = dz_1 * tab[4, :, span]
        add(12, du_1)
        dz_0 = stacked_dot(back[0], du_1)
        z_0 = tab[0, :, span]
        level(0, dz_0 * z_0, dz_0 * tab[1, :, span])
        sums[14 * 32 : 14 * 32 + 8, :] += fold(draw)
        left = jnp.concatenate([du_1, du_2, draw], axis=0).astype(BF16)
        right = jnp.concatenate([z_0, z_1, z_2, jnp.zeros_like(z_0)], axis=0).astype(BF16)
        mats[...] += dot_rows(left, right)
        return carry

    lax.fori_loop(0, SAMPLES // CHUNK, step, 0, unroll=4)
    lane = lax.broadcasted_iota(jnp.int32, (32, LANES), 1)
    hidden = jnp.where(lane < 32, mats[0:32, :], jnp.where(lane < 64, mats[32:64, :], 0.0))

    def column(k):
        return jnp.sum(sums[block(k, 32), :], axis=1, keepdims=True)

    hidden = jnp.where(lane == 64, column(12), hidden)
    hidden = jnp.where(lane == 65, column(13), hidden)
    for j in range(3):
        sharpness = columns[:, 4 * j : 4 * j + 1]
        hidden = jnp.where(lane == 66 + 4 * j, -sharpness * column(4 * j), hidden)
        hidden = jnp.where(lane == 67 + 4 * j, sharpness * sharpness * column(4 * j + 1), hidden)
        hidden = jnp.where(lane == 68 + 4 * j, column(4 * j + 2), hidden)
        hidden = jnp.where(lane == 69 + 4 * j, column(4 * j + 3), hidden)
    lane8 = lax.broadcasted_iota(jnp.int32, (8, LANES), 1)
    outer = pltpu.roll(mats[64:72, :], LANES - 64, 1)
    raw_total = jnp.sum(sums[14 * 32 : 14 * 32 + 8, :], axis=1, keepdims=True)
    outer = jnp.where(lane8 < 32, outer, 0.0)
    outer = jnp.where(lane8 == 32, raw_total, outer)
    return hidden, outer


def with_norm_sums(outer, sums):
    row = lax.broadcasted_iota(jnp.int32, (8, LANES), 0)
    lane = lax.broadcasted_iota(jnp.int32, (8, LANES), 1)
    for part in range(OWN):
        gain_total, bias_total = sums[part]
        outer = jnp.where((row == part) & (lane == 33), gain_total, outer)
        outer = jnp.where((row == part) & (lane == 34), bias_total, outer)
    return outer


def one_row(outer):
    lane = lax.broadcasted_iota(jnp.int32, (1, LANES), 1)
    result = jnp.zeros((1, LANES), F32)
    for part in range(OWN):
        row = outer[part : part + 1, :]
        moved = pltpu.roll(row, 32 * part, 1) if part else row
        result = jnp.where((lane >= 32 * part) & (lane < 32 * part + 32), moved, result)
        moved = pltpu.roll(row, 64 + 3 * part, 1)
        result = jnp.where((lane >= 96 + 3 * part) & (lane < 99 + 3 * part), moved, result)
    return result


def packed_hidden(hidden):
    lane16 = lax.broadcasted_iota(jnp.int32, (16, LANES), 1)
    upper = jnp.where(lane16 < 64, hidden[0:16, :], pltpu.roll(hidden[16:32, :], 64, 1))
    lane4 = lax.broadcasted_iota(jnp.int32, (4, LANES), 1)
    lower = jnp.zeros((4, LANES), F32)
    for g in range(8):
        moved = pltpu.roll(hidden, (64 + 16 * g) % LANES, 1)[4 * g : 4 * g + 4, :]
        lower = jnp.where((lane4 >= 16 * g) & (lane4 < 16 * g + 16), moved, lower)
    return upper, lower


def unpacked_hidden(upper, lower):
    lane16 = lax.broadcasted_iota(jnp.int32, (16, LANES), 1)
    lane32 = lax.broadcasted_iota(jnp.int32, (32, LANES), 1)
    top = jnp.concatenate([upper, pltpu.roll(upper, 64, 1)], axis=0)
    tiled = jnp.concatenate([lower] * 8, axis=0)
    row32 = lax.broadcasted_iota(jnp.int32, (32, LANES), 0)
    rest = jnp.zeros((32, LANES), F32)
    for g in range(8):
        moved = pltpu.roll(tiled, (64 - 16 * g) % LANES, 1)
        rest = jnp.where((row32 >= 4 * g) & (row32 < 4 * g + 4), moved, rest)
    return jnp.where(lane32 < 64, top, rest)


def high_low(value):
    high = value.astype(BF16).astype(F32)
    return high, value - high


def valid_row(meta, i):
    lane = lax.broadcasted_iota(jnp.int32, (1, LANES), 1)
    return (meta[2] * PIECE + (i // 2) * LANES + lane < meta[i % 2]).astype(F32)


def masked(meta, rows):
    mask = jnp.concatenate([valid_row(meta, i) for i in range(4)] * 2, axis=0)
    return (rows.reshape(-1, 8, LANES) * mask[None]).reshape(-1, LANES)


CLIP_ROWS = 4 * CHANNELS
PADDED_ROWS = 4 * PADDED


def put_padded(padded, rows):
    padded[0:CLIP_ROWS, :] = rows
    padded[CLIP_ROWS:PADDED_ROWS, :] = jnp.zeros((PADDED_ROWS - CLIP_ROWS, LANES), F32)


def rows_to_message(padded, out, step, base):
    for m in range(12):
        out[pl.ds(base + m, DEVICES, stride=step), :] = padded[pl.ds(m, DEVICES, stride=12), :]


def rows_of_channels(padded, i):
    return padded[pl.ds(i, PADDED, stride=4), :]


def source_kernel(meta, x_ref, mix_w, out_ref, padded, out):
    put_padded(padded, masked(meta, x_ref[...]))
    for b in range(2):
        length = meta[b]
        upper = lax.shift_right_logical(length, 7)
        out[pl.ds(12 + 2 * b, DEVICES, stride=16), :] = jnp.full((DEVICES, LANES), upper.astype(F32))
        out[pl.ds(13 + 2 * b, DEVICES, stride=16), :] = jnp.full(
            (DEVICES, LANES), (length - upper * 128).astype(F32)
        )
    rows_to_message(padded, out, 16, 0)
    out_ref[...] = out[...].reshape(DEVICES, 16, LANES).astype(BF16)


def make_lookup(lookup):
    row = lax.broadcasted_iota(jnp.int32, (DEVICES, PADDED), 0)
    column = lax.broadcasted_iota(jnp.int32, (DEVICES, PADDED), 1)
    for part in range(OWN):
        lookup[block(part), :] = (column == OWN * row + part).astype(F32).astype(BF16)


def make_weights(mix_w, mix_b, wide, lookup, weights, weights_back):
    make_lookup(lookup)
    wide[...] = jnp.zeros(wide.shape, BF16)
    row = lax.broadcasted_iota(jnp.int32, (LANES, CHANNELS), 0)
    lines = jnp.where(row == 0, mix_b[0:1, :], jnp.where(row == 1, mix_b[1:2, :], 0.0))
    turned = jnp.transpose(jnp.concatenate([lines, jnp.zeros((LANES, PADDED - CHANNELS), F32)], axis=1))
    lane = lax.broadcasted_iota(jnp.int32, (PADDED, PADDED), 1)
    for layer in range(2):
        wide[0:CHANNELS, 0:CHANNELS] = mix_w[layer]
        weights_back[layer] = dot_rows(lookup[...], wide[...]).astype(BF16)
        value = dot_rows(wide[...], lookup[...])
        rest = turned[:, layer : layer + 1]
        for spot in SPOTS:
            high, rest = high_low(rest)
            value = jnp.where(lane == spot, high, value)
        weights[layer] = value.astype(BF16)


def make_kernel(layer, meta, params, consts, bundle, tab, scratch):
    out_w, out_b, window, gain, bias, gabor, hidden_b, hidden_w = params
    first, second, _, twiddle = consts
    wide, tall, rows, pieces, x_ref, high, low = scratch
    own, columns = bundle.at[OWN_ROWS, :], bundle.at[COLUMN_ROWS, :]
    own_parameters(layer, meta[3], out_w, out_b, window, gain, bias, gabor, hidden_b, wide, tall, own, columns)
    generate(columns, hidden_w.at[layer], own, tab, rows)
    for n in range(64):
        for part in range(OWN):
            pieces[part * 64 + n : part * 64 + n + 1, :] = rows[part : part + 1, block(n)]
    for part in range(OWN):
        piece = pieces[block(part, 64), :].astype(BF16)
        x_ref[0:64, block(part)] = piece
        x_ref[64:128, block(part)] = piece
        x_ref[128:256, block(part)] = jnp.zeros((128, LANES), BF16)
    spec = transform(x_ref, high, low, first, second, twiddle, OWN)
    bundle[0:SPEC_IM, :] = spec[:, RE]
    bundle[SPEC_IM : 2 * SPEC_IM, :] = spec[:, IM]


def forward_kernel(
    meta, message_ref, out_w, out_b, window, gain, bias, gabor, hidden_b, hidden_w,
    first, second, last, twiddle,
    out_ref, spec_ref, normed_ref, slope_ref, inv_ref, len_ref, kernel_spec, tab,
    message, x_ref, high, low, e_high, e_low, y_ref, out, *make_scratch,
):
    own = kernel_spec.at[OWN_ROWS, :]
    params = (out_w, out_b, window, gain, bias, gabor, hidden_b, hidden_w)
    make_kernel(0, meta, params, (first, second, last, twiddle), kernel_spec, tab, make_scratch)
    message[...] = spread(message_ref[...])
    for y in range(4):
        for b in range(2):
            start = y * 16 + 12 + 2 * b
            len_ref[2 * y + b : 2 * y + b + 1, :] = (
                message[start : start + 1, :] * 128.0 + message[start + 1 : start + 2, :]
            )
    load_signals(message, 16, x_ref)
    convolve(x_ref, spec_ref, kernel_spec, high, low, e_high, e_low, (first, second, last, twiddle), y_ref)
    valid, tally = valid_of(len_ref), tally_of(len_ref)
    inv_ref[...] = jnp.zeros((8, LANES), F32)
    for part in range(OWN):
        normed, inv_std, active, slope = normalise(y_ref, own, valid, tally, part)
        normed_ref[:, block(part, 512)] = normed
        slope_ref[:, block(part, 512)] = slope
        inv_ref[part : part + 1, :] = jnp.broadcast_to(inv_std, (1, LANES))
        y_ref[:, block(part, 512)] = active
    store_signals(out, 12, 0, lambda part, y: y_ref[:, block(part * 4 + y)])
    out_ref[...] = out[...].reshape(DEVICES, 3, 4, LANES).astype(BF16)


def gather_active(message, step, rhs):
    row = lax.broadcasted_iota(jnp.int32, (DEVICES, LANES), 0)
    for i in range(4):
        for part in range(OWN):
            piece = message[pl.ds(part * 4 + i, DEVICES, stride=step), :]
            if part != 1:
                piece = jnp.where(row >= (126 if part == 2 else 127), 1.0, piece)
            rhs[block(part), block(i)] = piece.astype(BF16)


def store_rows(value, out, step, base):
    for i in range(4):
        for part in range(OWN):
            out[pl.ds(base + part * 4 + i, DEVICES, stride=step), :] = value[block(part), block(i)]


def mix_kernel(
    meta, message_ref, x_ref, cotangent, mix_w, mix_b,
    out_ref, next_ref, active_ref, weights, weights_back, message, padded, out, low, wide, lookup,
):
    make_weights(mix_w, mix_b, wide, lookup, weights, weights_back)
    message[...] = spread(message_ref[...])
    gather_active(message, 12, active_ref)
    mixed = dot(weights[0], active_ref[...])
    put_padded(padded, x_ref[...])
    for i in range(4):
        valid = valid_row(meta, i)
        value = rows_of_channels(padded, i) + mixed[:, block(i)] * valid
        next_ref[pl.ds(i, PADDED, stride=4), :] = value
        padded[pl.ds(i, PADDED, stride=4), :] = value * valid
    rows_to_message(padded, out, 24, 0)
    put_padded(padded, masked(meta, cotangent[...]))
    for i in range(4):
        low[:, block(i)] = rows_of_channels(padded, i).astype(BF16)
    store_rows(dot(weights_back[1], low[...]), out, 24, 12)
    out_ref[...] = out[...].reshape(DEVICES, 24, LANES).astype(BF16)


def forward_backward_kernel(
    meta, message_ref, out_w, out_b, window, gain, bias, gabor, hidden_b, hidden_w,
    len_ref, first, second, last, twiddle,
    out_ref, hidden_out, outer_out,
    message, x_ref, high, low, e_high, e_low, y_ref, out, spec_ref, grad_ref, normed_ref, slope_ref, returned_ref,
    rows, sums, mats, kernel_spec, tab, *make_scratch,
):
    own, columns = kernel_spec.at[OWN_ROWS, :], kernel_spec.at[COLUMN_ROWS, :]
    consts = (first, second, last, twiddle)
    params = (out_w, out_b, window, gain, bias, gabor, hidden_b, hidden_w)
    make_kernel(1, meta, params, consts, kernel_spec, tab, make_scratch)
    message[...] = spread(message_ref[...])
    load_signals(message, 24, x_ref)
    convolve(x_ref, spec_ref, kernel_spec, high, low, e_high, e_low, consts, y_ref)
    valid, tally = valid_of(len_ref), tally_of(len_ref)
    inv = []
    for part in range(OWN):
        normed, inv_std, active, slope = normalise(y_ref, own, valid, tally, part)
        normed_ref[:, block(part, 512)] = normed
        slope_ref[:, block(part, 512)] = slope
        inv.append(inv_std)
        y_ref[:, block(part, 512)] = active
    store_signals(out, 24, 0, lambda part, y: y_ref[:, block(part * 4 + y)])
    returned, norm_sums = conv_backward(
        message, 24, 12, lambda part: normed_ref[:, block(part, 512)], lambda part: slope_ref[:, block(part, 512)],
        lambda part: inv[part], own, valid, tally, spec_ref, kernel_spec, x_ref, high, low, e_high, e_low, consts, grad_ref,
    )
    returned_ref[...] = returned
    store_signals(out, 24, 12, lambda part, y: returned_ref[:, block(part * 4 + y)])
    out_ref[...] = out[...].reshape(DEVICES, 24, LANES).astype(BF16)
    hidden, outer = generate_back(
        lambda part: returned_ref[0:64, block(SIGNALS + part)], columns, hidden_w.at[1], own, tab,
        rows, sums, mats,
    )
    hidden_out[...] = hidden
    outer_out[...] = with_norm_sums(outer, norm_sums)


def middle_kernel(
    meta, message_ref, x_ref, cotangent, weights, weights_back, active_0, hidden_1,
    output_ref, flow_ref, out_ref, message, padded, out, low_0, low_1, active_1,
):
    message[...] = spread(message_ref[...])
    gather_active(message, 24, active_1)
    mixed = dot(weights[1], active_1[...])
    for i in range(4):
        padded[pl.ds(i, PADDED, stride=4), :] = rows_of_channels(x_ref, i) + mixed[:, block(i)] * valid_row(meta, i)
    output_ref[...] = padded[0:CLIP_ROWS, :]
    put_padded(flow_ref, cotangent[...])
    for i in range(4):
        low_1[:, block(i)] = (rows_of_channels(flow_ref, i) * valid_row(meta, i)).astype(BF16)
    for m in range(12):
        padded[pl.ds(m, DEVICES, stride=12), :] = message[pl.ds(12 + m, DEVICES, stride=24), :]
    flow_ref[...] += masked(meta, padded[...])
    for i in range(4):
        low_0[:, block(i)] = (rows_of_channels(flow_ref, i) * valid_row(meta, i)).astype(BF16)
    store_rows(dot(weights_back[0], low_0[...]), out, 32, 0)
    for layer, (active, low) in enumerate(((active_0, low_0), (active_1, low_1))):
        part_sum = dot_rows(active[...], low[...])
        for part in range(OWN):
            for third in range(3):
                out[pl.ds(12 + layer * 9 + part * 3 + third, DEVICES, stride=32), :] = part_sum[
                    block(part), block(third)
                ]
    high, low = high_low(hidden_1[...])
    out[pl.ds(30, DEVICES, stride=32), :] = jnp.concatenate([high, jnp.zeros((96, LANES), F32)], axis=0)
    out[pl.ds(31, DEVICES, stride=32), :] = jnp.concatenate([low, jnp.zeros((96, LANES), F32)], axis=0)
    out_ref[...] = out[...].reshape(DEVICES, 32, LANES).astype(BF16)


LAST_ROWS = 56


def backward_kernel(
    message_ref, spec_ref, kernel_spec, normed_ref, slope_ref, inv_ref, len_ref,
    first, second, last, twiddle, hidden_w, tab, outer_1,
    out_ref,
    message, x_ref, high, low, e_high, e_low, out, grad_ref, returned_ref, rows, sums, mats,
):
    own, columns = kernel_spec.at[OWN_ROWS, :], kernel_spec.at[COLUMN_ROWS, :]
    consts = (first, second, last, twiddle)
    message[...] = spread(message_ref[...])
    valid, tally = valid_of(len_ref), tally_of(len_ref)
    returned, norm_sums = conv_backward(
        message, 32, 0, lambda part: normed_ref[:, block(part, 512)], lambda part: slope_ref[:, block(part, 512)],
        lambda part: inv_ref[part : part + 1, 0:1], own, valid, tally, spec_ref, kernel_spec, x_ref, high, low,
        e_high, e_low, consts, grad_ref,
    )
    returned_ref[...] = returned
    store_signals(out, 16, 0, lambda part, y: returned_ref[:, block(part * 4 + y)])
    hidden, outer = generate_back(
        lambda part: returned_ref[0:64, block(SIGNALS + part)], columns, hidden_w.at[0], own, tab,
        rows, sums, mats,
    )
    outer = with_norm_sums(outer, norm_sums)
    gathered = jnp.sum(message[...].reshape(DEVICES, 32, LANES), axis=0)
    upper, lower = packed_hidden(hidden)
    hidden_1_high, hidden_1_low = high_low(gathered[30:31, :] + gathered[31:32, :])
    outer_0_high, outer_0_low = high_low(one_row(outer))
    outer_1_high, outer_1_low = high_low(one_row(outer_1[...]))
    shared = jnp.concatenate(
        [
            gathered[0:30, :], upper, lower, hidden_1_high, hidden_1_low,
            outer_0_high, outer_0_low, outer_1_high, outer_1_low,
        ],
        axis=0,
    )
    row = lax.broadcasted_iota(jnp.int32, (DEVICES, 16, LANES), 1)
    own_rows = jnp.where(row < 12, out[...].reshape(DEVICES, 16, LANES), shared[None, 0:16, :])
    rest = jnp.broadcast_to(shared[None, 16:LAST_ROWS, :], (DEVICES, LAST_ROWS - 16, LANES))
    out_ref[...] = jnp.concatenate([own_rows, rest], axis=1).astype(BF16)


def last_kernel(
    meta, message_ref, flow_ref,
    input_grad, gabor_grad, hidden_w_grad, hidden_b_grad, out_w_grad, out_b_grad, gain_grad, bias_grad,
    mix_w_grad, mix_b_grad, message, padded, owned, thirds, lookup,
):
    make_lookup(lookup)
    message[...] = spread(message_ref[...])

    def rows_of(k, count=DEVICES):
        return message[pl.ds(k, count, stride=LAST_ROWS), :]

    for m in range(12):
        padded[pl.ds(m, DEVICES, stride=12), :] = rows_of(m)
    input_grad[...] = flow_ref[0:CLIP_ROWS, :] + masked(meta, padded[0:CLIP_ROWS, :])
    shared = jnp.sum(message[...].reshape(DEVICES, LAST_ROWS, LANES)[:, 24:56, :], axis=0)
    hidden_0 = unpacked_hidden(shared[6:22, :], shared[22:26, :])
    hidden_1 = rows_of(50, 32) + rows_of(51, 32)
    lane = lax.broadcasted_iota(jnp.int32, (DEVICES, LANES), 1)
    for layer, hidden in enumerate((hidden_0, hidden_1)):
        hidden_w_grad[layer, 0] = hidden[:, 0:32]
        hidden_w_grad[layer, 1] = pltpu.roll(hidden, 96, 1)[:, 0:32]
        turned = jnp.transpose(jnp.concatenate([hidden, jnp.zeros((96, LANES), F32)], axis=0))
        hidden_b_grad[layer] = turned[64:66, 0:32]
        for j in range(3):
            gabor_grad[layer, j] = turned[66 + 4 * j : 70 + 4 * j, 0:32]
        value = rows_of(52 + 2 * layer) + rows_of(53 + 2 * layer)
        for part in range(OWN):
            wide = pltpu.roll(value, (LANES - 32 * part) % LANES, 1)
            small = pltpu.roll(value, 64 - 3 * part, 1)
            owned[pl.ds(part, DEVICES, stride=OWN), :] = jnp.where(lane < 32, wide, small)
        turned = jnp.transpose(owned[...])
        out_w_grad[layer] = turned[0:32, 0:CHANNELS]
        out_b_grad[layer : layer + 1, :] = turned[32:33, 0:CHANNELS]
        gain_grad[layer : layer + 1, :] = turned[33:34, 0:CHANNELS]
        bias_grad[layer : layer + 1, :] = turned[34:35, 0:CHANNELS]
        bias_rows = []
        for part in range(OWN):
            for third in range(3):
                piece = rows_of(12 + layer * 9 + part * 3 + third)
                thirds[block(part), block(third)] = piece.astype(BF16)
                if part == 2:
                    bias_rows.append(piece[SPOT - 2 * DEVICES : SPOT - 2 * DEVICES + 1, :])
        mix_w_grad[:, layer, :] = dot_columns(thirds[...], lookup[...])[0:CHANNELS, 0:CHANNELS]
        mix_b_grad[layer : layer + 1, :] = jnp.concatenate(bias_rows, axis=1)[:, 0:CHANNELS]


def exchange(message):
    return lax.all_to_all(message, AXES, split_axis=0, concat_axis=0, tiled=True)


def to_rows(clips):
    return clips.reshape(2, CHANNELS, 2, LANES).transpose(1, 2, 0, 3).reshape(CLIP_ROWS, LANES)


def from_rows(rows):
    return rows.reshape(CHANNELS, 2, 2, LANES).transpose(2, 0, 1, 3).reshape(2, CHANNELS, PIECE)


def shards(
    inputs, lengths, window, gabor_params, hidden_w, hidden_b, out_w, out_b, bn_gain, bn_bias, mix_w, mix_b, cotangent
):
    position = lax.axis_index("seq").astype(jnp.int32)
    number = position * 4 + lax.axis_index("clips").astype(jnp.int32)
    const = {name: jnp.asarray(value) for name, value in TABLES.items()}
    meta = jnp.concatenate([lengths, jnp.stack([position, number])])
    inputs, cotangent = to_rows(inputs), to_rows(cotangent)

    def rows(count):
        return ((count, LANES), F32)

    with jax.named_scope("source_0"):
        (message,) = run(
            source_kernel, [((DEVICES, 16, LANES), BF16)], [meta, inputs, mix_w],
            [rows(PADDED_ROWS), rows(DEVICES * 16)], "source_0", 8, smem=(0,), far=(2,),
        )
        message = exchange(message)

    square = (PADDED, PADDED)
    generator = [
        jnp.swapaxes(out_w, 1, 2), out_b, jnp.swapaxes(window, 1, 2), bn_gain, bn_bias, gabor_params, hidden_b,
        hidden_w,
    ]
    shape_tab = ((8, HIDDEN, SAMPLES), F32)
    make_scratch = [
        ((LANES, PADDED), F32), rows(PADDED + 8), ((8, SAMPLES), F32), rows(192),
        ((256, OWN * LANES), BF16), ((OWN * LANES, 256), BF16), ((OWN * LANES, 256), BF16),
    ]
    mixers = ((2, *square), BF16)

    def scratch(signals):
        count = signals * LANES
        return [
            ((256, SIGNALS * LANES), BF16), ((count, 256), BF16), ((count, 256), BF16),
            ((256, count), BF16), ((256, count), BF16),
        ]

    shape_y = (LANES, SIGNALS * LANES)
    shape_s = (SIGNALS * LANES, 256)
    transforms = [const[name] for name in TABLE_NAMES]
    with jax.named_scope("conv_0"):
        message, spec_0, normed_0, slope_0, inv_0, lens, bundle_0, tab_0 = run(
            forward_kernel,
            [
                ((DEVICES, 3, 4, LANES), BF16), (shape_s, F32), (shape_y, F32), (shape_y, F32), rows(8), rows(8),
                rows(BUNDLE), shape_tab,
            ],
            [meta, message, *generator, *transforms],
            [rows(DEVICES * 16), *scratch(SIGNALS), (shape_y, F32), rows(DEVICES * 12), *make_scratch],
            "conv_0", 16, smem=(0,),
        )
        message = exchange(message)

    with jax.named_scope("mix_0"):
        message, middle, active_0, weights, weights_back = run(
            mix_kernel,
            [((DEVICES, 24, LANES), BF16), rows(PADDED_ROWS), ((PADDED, 512), BF16), mixers, mixers],
            [meta, message, inputs, cotangent, mix_w, mix_b],
            [rows(DEVICES * 12), rows(PADDED_ROWS), rows(DEVICES * 24), ((PADDED, 512), BF16), (square, BF16), (square, BF16)],
            "mix_0", 12, smem=(0,),
        )
        message = exchange(message)

    back_scratch = [((8, SAMPLES), F32), rows(14 * 32 + 8), rows(72)]
    with jax.named_scope("conv_1"):
        message, hidden_1, outer_1 = run(
            forward_backward_kernel,
            [((DEVICES, 24, LANES), BF16), rows(HIDDEN), rows(8)],
            [
                meta, message, *generator, lens, *transforms,
            ],
            [
                rows(DEVICES * 24), *scratch(SIGNALS + OWN), (shape_y, F32), rows(DEVICES * 24),
                (shape_s, F32), (shape_s, F32), (shape_y, F32), (shape_y, F32),
                ((LANES, (SIGNALS + OWN) * LANES), F32), *back_scratch, rows(BUNDLE), shape_tab, *make_scratch,
            ],
            "conv_1", 26, smem=(0,),
        )
        message = exchange(message)

    with jax.named_scope("mix_1"):
        outputs, flow, message = run(
            middle_kernel,
            [rows(CLIP_ROWS), rows(PADDED_ROWS), ((DEVICES, 32, LANES), BF16)],
            [meta, message, middle, cotangent, weights, weights_back, active_0, hidden_1],
            [
                rows(DEVICES * 24), rows(PADDED_ROWS), rows(DEVICES * 32),
                ((PADDED, 512), BF16), ((PADDED, 512), BF16), ((PADDED, 512), BF16),
            ],
            "mix_1", 12, smem=(0,),
        )
        message = exchange(message)

    with jax.named_scope("conv_back_0"):
        (message,) = run(
            backward_kernel,
            [((DEVICES, LAST_ROWS, LANES), BF16)],
            [
                message, spec_0, bundle_0, normed_0, slope_0, inv_0, lens, *transforms,
                hidden_w, tab_0, outer_1,
            ],
            [
                rows(DEVICES * 32), *scratch(SIGNALS + OWN), rows(DEVICES * 16), (shape_s, F32),
                ((LANES, (SIGNALS + OWN) * LANES), F32), *back_scratch,
            ],
            "conv_back_0", 16,
        )
        message = exchange(message)

    with jax.named_scope("gradients"):
        (
            input_grad, gabor_grad, hidden_w_grad, hidden_b_grad, out_w_grad, out_b_grad, gain_grad, bias_grad,
            mix_w_grad, mix_b_grad,
        ) = run(
            last_kernel,
            [
                rows(CLIP_ROWS), (gabor_params.shape, F32), (hidden_w.shape, F32), (hidden_b.shape, F32),
                ((2, HIDDEN, CHANNELS), F32), (out_b.shape, F32), (bn_gain.shape, F32), (bn_bias.shape, F32),
                ((CHANNELS, 2, CHANNELS), F32), (mix_b.shape, F32),
            ],
            [meta, message, flow],
            [rows(DEVICES * LAST_ROWS), rows(PADDED_ROWS), rows(PADDED), (square, BF16), (square, BF16)],
            "gradients", 14, smem=(0,),
        )
    return (
        from_rows(outputs), from_rows(input_grad), gabor_grad, hidden_w_grad, hidden_b_grad,
        jnp.swapaxes(out_w_grad, 1, 2), out_b_grad, gain_grad, bias_grad, jnp.swapaxes(mix_w_grad, 0, 1), mix_b_grad,
    )


def solution(mesh):
    clip = P("clips", None, "seq")
    in_specs = (clip, P("clips")) + (P(),) * 10 + (clip,)
    out_specs = (clip, clip) + (P(),) * 9
    return jax.shard_map(shards, mesh=mesh, in_specs=in_specs, out_specs=out_specs, check_vma=False)
```

```python
import math

import jax
import jax.numpy as jnp
import ml_dtypes
import numpy as np
from jax import lax
from jax.experimental import pallas as pl
from jax.experimental.pallas import tpu as pltpu
from jax.sharding import PartitionSpec as P

F32 = jnp.float32
BF16 = jnp.bfloat16
AXES = ("seq", "clips")
DEVICES = 128
OWN = 3
CHANNELS = 380
PADDED = DEVICES * OWN
SAMPLES = 8192
PIECE = 256
HIDDEN = 32
LANES = 128
SIGNALS = 12
TABLE_NAMES = ("first", "second", "last", "twiddle")
PERIOD = 2 * SAMPLES
EPSILON = 1e-05
MEGABYTE = 1024 * 1024
EXACT = lax.Precision.HIGHEST
SPOTS = (2 * DEVICES + 126, 2 * DEVICES + 127, 127)
SPOT = SPOTS[0]


def halves(table):
    high = table.astype(ml_dtypes.bfloat16)
    low = (table - high.astype(np.float64)).astype(ml_dtypes.bfloat16)
    return high, low


def tables():
    order = np.array([2 * j + r for r in range(2) for j in range(32)])
    k = np.arange(LANES)
    turn = 2 * np.pi * ((k[:, None] * order[None, :]) % LANES) / LANES
    c_high, c_low = halves(np.cos(turn))
    s_high, s_low = halves(np.sin(turn))
    first = np.concatenate(
        [
            np.concatenate([c_high, c_low, s_high, s_low], axis=1),
            np.concatenate([-s_high, -s_low, c_high, c_low], axis=1),
        ],
        axis=0,
    )
    turn = 2 * np.pi * ((k[:, None] * k[None, :]) % LANES) / LANES
    cosine, sine = np.cos(turn), np.sin(turn)
    second = halves(np.block([[cosine, -sine], [sine, cosine]]))
    turn = 2 * np.pi * ((order[:, None] * k[None, :]) % LANES) / LANES
    cosine, sine = np.cos(turn) / PERIOD, np.sin(turn) / PERIOD
    last = halves(np.block([[cosine, -sine], [sine, cosine]]))
    turn = 2 * np.pi * (k[:, None] * k[None, :]) / PERIOD
    twiddle = np.stack([np.cos(turn), np.sin(turn)]).astype(np.float32)
    return dict(
        first=first,
        second=np.stack(second),
        last=np.stack(last),
        twiddle=twiddle,
    )


TABLES = tables()


def run(body, outs, args, scratch, name, grant, smem=(), far=()):
    spaces = [pltpu.HBM if i in far else pltpu.SMEM if i in smem else pltpu.VMEM for i in range(len(args))]
    return pl.pallas_call(
        body,
        out_shape=[jax.ShapeDtypeStruct(shape, kind) for shape, kind in outs],
        in_specs=[pl.BlockSpec(memory_space=space) for space in spaces],
        out_specs=[pl.BlockSpec(memory_space=pltpu.VMEM)] * len(outs),
        scratch_shapes=[pltpu.VMEM(shape, kind) for shape, kind in scratch],
        compiler_params=pltpu.CompilerParams(vmem_limit_bytes=grant * MEGABYTE),
        name=name,
    )(*args)


def dot(a, b):
    return jnp.dot(a, b, preferred_element_type=F32)


def dot_rows(a, b, precision=None):
    return lax.dot_general(a, b, (((1,), (1,)), ((), ())), precision=precision, preferred_element_type=F32)


def dot_columns(a, b, precision=None):
    return lax.dot_general(a, b, (((0,), (0,)), ((), ())), precision=precision, preferred_element_type=F32)


def triple(a_high, a_low, b_high, b_low):
    left = jnp.concatenate([a_high, a_low, a_high], axis=1)
    return dot(left, jnp.concatenate([b_high, b_high, b_low], axis=0))


def triple_rows(a_high, a_low, b_high, b_low):
    left = jnp.concatenate([a_high, a_low, a_high], axis=1)
    return dot_rows(left, jnp.concatenate([b_high, b_high, b_low], axis=1))


def put_halves(high_ref, low_ref, rows, columns, value):
    high = value.astype(BF16)
    high_ref[rows, columns] = high
    low_ref[rows, columns] = (value - high.astype(F32)).astype(BF16)


def block(i, size=LANES):
    return slice(i * size, (i + 1) * size)


RE, IM = slice(0, LANES), slice(LANES, 2 * LANES)


def signal_row(b, part, r):
    return part * 4 + r * 2 + b


def spread(message):
    return message.astype(F32).reshape(-1, LANES)


def transform(x_ref, high_ref, low_ref, first, second, twiddle, count):
    part_a = dot(first[...], x_ref[:, : count * LANES])
    cosine, sine = twiddle[0], twiddle[1]
    for s in range(count):
        real, imag = part_a[:LANES, block(s)], part_a[LANES:, block(s)]
        put_halves(high_ref, low_ref, block(s), RE, real * cosine + imag * sine)
        put_halves(high_ref, low_ref, block(s), IM, imag * cosine - real * sine)
    rows = slice(0, count * LANES)
    return triple(high_ref[rows, :], low_ref[rows, :], second[0], second[1])


def transform_back(high_ref, low_ref, e_high, e_low, second, last, twiddle, count):
    rows = slice(0, count * LANES)
    part_d = triple_rows(high_ref[rows, :], low_ref[rows, :], second[0], second[1])
    cosine, sine = twiddle[0], twiddle[1]
    for s in range(count):
        real, imag = part_d[block(s), RE], part_d[block(s), IM]
        put_halves(e_high, e_low, RE, block(s), real * cosine - imag * sine)
        put_halves(e_high, e_low, IM, block(s), real * sine + imag * cosine)
    return triple(last[0], last[1], e_high[:, rows], e_low[:, rows])


def erf_parts(value):
    cdf = 0.5 * (1.0 + lax.erf(value * math.sqrt(0.5)))
    return cdf, jnp.exp(-0.5 * value * value) * (1.0 / math.sqrt(2.0 * math.pi))


def total(value):
    return jnp.sum(jnp.sum(value, axis=0, keepdims=True), axis=1, keepdims=True)


def times_of(row, lane):
    return (256 * (row & 31) + 128 * lax.shift_right_logical(row, 5 * jnp.ones_like(row)) + lane).astype(F32)


def valid_of(len_ref):
    row = lax.broadcasted_iota(jnp.int32, (LANES, LANES), 0) & 63
    times = times_of(row, lax.broadcasted_iota(jnp.int32, (LANES, LANES), 1))
    columns = []
    for y in range(4):
        upper = times[0:64, :] < len_ref[2 * y : 2 * y + 1, :]
        lower = times[64:128, :] < len_ref[2 * y + 1 : 2 * y + 2, :]
        columns.append(jnp.concatenate([upper, lower], axis=0).astype(F32))
    return jnp.concatenate(columns, axis=1)


def tally_of(len_ref):
    return jnp.sum(len_ref[:, 0:1], axis=0, keepdims=True)


def load_signals(message, step, x_ref):
    for part in range(OWN):
        for y in range(4):
            lanes = block(part * 4 + y)
            for b in range(2):
                for r in range(2):
                    start = y * step + signal_row(b, part, r)
                    piece = message[pl.ds(start, 32, stride=4 * step), :].astype(BF16)
                    x_ref[b * 128 + r * 32 : b * 128 + r * 32 + 32, lanes] = piece
                    x_ref[b * 128 + r * 32 + 64 : b * 128 + r * 32 + 96, lanes] = piece


def store_signals(out, step, base, get):
    for part in range(OWN):
        for y in range(4):
            value = get(part, y)
            for b in range(2):
                for r in range(2):
                    start = y * step + base + signal_row(b, part, r)
                    out[pl.ds(start, 32, stride=4 * step), :] = value[b * 64 + r * 32 : b * 64 + r * 32 + 32, :]


SPEC_IM = OWN * LANES
OWN_ROWS = slice(2 * SPEC_IM, 2 * SPEC_IM + 8)
COLUMN_ROWS = slice(2 * SPEC_IM + 8, 2 * SPEC_IM + 8 + HIDDEN)
BUNDLE = 2 * SPEC_IM + 8 + HIDDEN


def kernel_parts(bundle, part):
    return bundle[block(part), :], bundle[SPEC_IM + part * LANES : SPEC_IM + (part + 1) * LANES, :]


def convolve(x_ref, spec_ref, kernel_spec, high, low, e_high, e_low, consts, y_ref):
    first, second, last, twiddle = consts
    spec_ref[...] = transform(x_ref, high, low, first, second, twiddle, SIGNALS)
    for part in range(OWN):
        k_re, k_im = kernel_parts(kernel_spec, part)
        for y in range(4):
            rows = block(part * 4 + y)
            s_re, s_im = spec_ref[rows, RE], spec_ref[rows, IM]
            put_halves(high, low, rows, RE, s_re * k_re - s_im * k_im)
            put_halves(high, low, rows, IM, s_re * k_im + s_im * k_re)
    y_ref[...] = transform_back(high, low, e_high, e_low, second, last, twiddle, SIGNALS)


def normalise_all(y_ref, own, len_ref, normed_ref, slope_ref, inv_ref):
    valid, tally = valid_of(len_ref), tally_of(len_ref)
    inv_ref[...] = jnp.zeros((8, LANES), F32)
    means = [total(valid * y_ref[:, block(part, 512)]) / tally for part in range(OWN)]
    spreads = []
    for part in range(OWN):
        centred = y_ref[:, block(part, 512)] - means[part]
        spreads.append(total(valid * centred * centred) / tally)
    for part in range(OWN):
        inv_std = lax.rsqrt(spreads[part] + EPSILON)
        normed = (y_ref[:, block(part, 512)] - means[part]) * inv_std
        pre_act = normed * own[part : part + 1, 35:36] + own[part : part + 1, 36:37]
        cdf, density = erf_parts(pre_act)
        normed_ref[:, block(part, 512)] = normed
        slope_ref[:, block(part, 512)] = cdf + pre_act * density
        inv_ref[part : part + 1, :] = jnp.broadcast_to(inv_std, (1, LANES))
        y_ref[:, block(part, 512)] = pre_act * cdf


def conv_backward(
    message, step, base, normed_of, slope_of, inv_of, own, valid, tally, spec_ref, kernel_spec, x_ref, high, low,
    e_high, e_low, consts, grad_ref,
):
    first, second, last, twiddle = consts
    sums = []
    for part in range(OWN):
        columns = []
        for y in range(4):
            pieces = []
            for b in range(2):
                for r in range(2):
                    start = y * step + base + signal_row(b, part, r)
                    pieces.append(message[pl.ds(start, 32, stride=4 * step), :])
            columns.append(jnp.concatenate(pieces, axis=0))
        act_grad = jnp.concatenate(columns, axis=1)
        normed = normed_of(part)
        pre_grad = act_grad * slope_of(part)
        bias_total = total(pre_grad)
        gain_total = total(pre_grad * normed)
        gain = own[part : part + 1, 35:36]
        conv_grad = inv_of(part) * (
            gain * pre_grad - valid * (gain * bias_total + normed * (gain * gain_total)) / tally
        )
        conv_low = conv_grad.astype(BF16)
        for b in range(2):
            piece = conv_low[b * 64 : b * 64 + 64, :]
            x_ref[b * 128 : b * 128 + 64, block(part, 512)] = piece
            x_ref[b * 128 + 64 : b * 128 + 128, block(part, 512)] = piece
        sums.append((gain_total, bias_total))
    grad_ref[...] = transform(x_ref, high, low, first, second, twiddle, SIGNALS)
    for part in range(OWN):
        k_re, k_im = kernel_parts(kernel_spec, part)
        corr_re, corr_im = None, None
        for y in range(4):
            rows = block(part * 4 + y)
            g_re, g_im = grad_ref[rows, RE], grad_ref[rows, IM]
            s_re, s_im = spec_ref[rows, RE], spec_ref[rows, IM]
            put_halves(high, low, rows, RE, k_re * g_re + k_im * g_im)
            put_halves(high, low, rows, IM, k_re * g_im - k_im * g_re)
            now_re, now_im = s_re * g_re + s_im * g_im, s_re * g_im - s_im * g_re
            corr_re = now_re if corr_re is None else corr_re + now_re
            corr_im = now_im if corr_im is None else corr_im + now_im
        put_halves(high, low, block(SIGNALS + part), RE, corr_re)
        put_halves(high, low, block(SIGNALS + part), IM, corr_im)
    returned = transform_back(high, low, e_high, e_low, second, last, twiddle, SIGNALS + OWN)
    return returned, sums


def sin_cos(angle):
    turns = jnp.floor(angle * (2.0 / math.pi) + 0.5)
    rest = angle - turns * 1.5703125
    rest = rest - turns * 4.837512969970703125e-4
    rest = rest - turns * 7.549789948768648e-8
    square = rest * rest
    sine = rest + rest * square * (
        -1.6666654611e-1 + square * (8.3321608736e-3 + square * -1.9515295891e-4)
    )
    cosine = 1.0 - 0.5 * square + square * square * (
        4.166664568298827e-2 + square * (-1.388731625493765e-3 + square * 2.443315711809948e-5)
    )
    half = jnp.floor(turns * 0.5)
    odd = turns - 2.0 * half
    sign = 1.0 - 2.0 * (half - 2.0 * jnp.floor(half * 0.5))
    is_odd = odd > 0.5
    return sign * jnp.where(is_odd, cosine, sine), sign * jnp.where(is_odd, -sine, cosine)


CHUNK = 1024
F_TABLE = (0, 4, 7)
C_TABLE = (1, 3, 6)


def envelope_of(times, own):
    lower, upper = own[:, 33:34], own[:, 34:35]
    inside = (times >= lower) & (times < upper)
    offset = (times - lower) / (0.5 * (upper - lower))
    return jnp.where(inside, jnp.exp(-0.5 * offset * offset), 0.0)


def stacked_weight(weight):
    high, low = high_low(weight)
    return jnp.concatenate([high, high, low], axis=1).astype(BF16)


def stacked_dot(weight, value):
    high = value.astype(BF16)
    low = (value - high.astype(F32)).astype(BF16)
    return dot(weight, jnp.concatenate([high, low, high], axis=0))


def own_parameters(layer, number, out_w, out_b, window, gain, bias, gabor, hidden_b, wide, tall, own, columns):
    wide[...] = jnp.zeros(wide.shape, F32)
    wide[0:32, 0:CHANNELS] = out_w[layer]
    wide[32:33, 0:CHANNELS] = out_b[layer : layer + 1, :]
    wide[33:35, 0:CHANNELS] = window[layer].astype(F32)
    wide[35:36, 0:CHANNELS] = gain[layer : layer + 1, :]
    wide[36:37, 0:CHANNELS] = bias[layer : layer + 1, :]
    tall[0:PADDED, :] = jnp.transpose(wide[...])
    tall[PADDED : PADDED + 8, :] = jnp.zeros((8, LANES), F32)
    row = lax.broadcasted_iota(jnp.int32, (8, LANES), 0)
    lane = lax.broadcasted_iota(jnp.int32, (8, LANES), 1)
    mine = tall[pl.ds(number * OWN, 8), :]
    unused = (row >= OWN) | (number * OWN + row >= CHANNELS)
    own[...] = jnp.where(unused, jnp.where(lane == 34, float(SAMPLES), 0.0), mine)
    wide[:, 0:LANES] = jnp.zeros((LANES, LANES), F32)
    for j in range(3):
        wide[4 * j : 4 * j + 4, 0:HIDDEN] = gabor[layer, j]
    wide[12:14, 0:HIDDEN] = hidden_b[layer]
    columns[...] = jnp.transpose(wide[:, 0:LANES])[0:HIDDEN, :]


def sample_rows(first_lane, count):
    lane = first_lane + lax.broadcasted_iota(jnp.int32, (1, count), 1)
    times = times_of(lax.shift_right_logical(lane, 7 * jnp.ones_like(lane)), lane & 127)
    return times, times * (2.0 / (SAMPLES - 1)) - 1.0


def generate(columns, hidden_w, own, tab, rows):
    turns = []
    for j in range(3):
        turn = sin_cos(columns[:, 4 * j + 2 : 4 * j + 3] * (512.0 / (SAMPLES - 1)))
        turns.append([jnp.broadcast_to(value, (HIDDEN, LANES)) for value in turn])

    def step(i, carry):
        _, places = sample_rows(i * CHUNK, CHUNK)
        for j in range(3):
            sharpness, centre = columns[:, 4 * j : 4 * j + 1], columns[:, 4 * j + 1 : 4 * j + 2]
            frequency, phase = columns[:, 4 * j + 2 : 4 * j + 3], columns[:, 4 * j + 3 : 4 * j + 4]
            sine, cosine = sin_cos(frequency * places[:, 0:LANES] + phase)
            turn_sin, turn_cos = turns[j]
            for n in range(CHUNK // LANES):
                width = sharpness * (places[:, block(n)] - centre)
                bell = jnp.exp(-0.5 * width * width)
                here = pl.ds(pl.multiple_of(i * CHUNK + n * LANES, LANES), LANES)
                tab[F_TABLE[j], :, here] = bell * sine
                tab[C_TABLE[j], :, here] = bell * cosine
                sine, cosine = sine * turn_cos + cosine * turn_sin, cosine * turn_cos - sine * turn_sin
        return carry

    lax.fori_loop(0, SAMPLES // CHUNK, step, 0, unroll=2)
    weights = [stacked_weight(hidden_w[0]), stacked_weight(hidden_w[1]), stacked_weight(own[:, 0:32])]
    u_1 = stacked_dot(weights[0], tab[0]) + columns[:, 12:13]
    z_1 = u_1 * tab[4]
    tab[2] = z_1
    tab[3] = u_1 * tab[3]
    u_2 = stacked_dot(weights[1], z_1) + columns[:, 13:14]
    z_2 = u_2 * tab[7]
    tab[5] = z_2
    tab[6] = u_2 * tab[6]
    raw = stacked_dot(weights[2], z_2) + own[:, 32:33]
    times, _ = sample_rows(0, SAMPLES)
    rows[...] = raw * envelope_of(times, own)


def generate_back(kernel_grad, columns, hidden_w, own, tab, rows, sums, mats):
    rows[...] = jnp.zeros(rows.shape, F32)
    for part in range(OWN):
        grad = kernel_grad(part)
        for n in range(64):
            rows[part : part + 1, block(n)] = grad[n : n + 1, :]
    sums[...] = jnp.zeros(sums.shape, F32)
    mats[...] = jnp.zeros(mats.shape, F32)
    turned = jnp.transpose(jnp.concatenate([own[...], jnp.zeros((120, 128), F32)], axis=0))
    weight = [turned[0:32, part : part + 1] for part in range(OWN)]
    back = [stacked_weight(jnp.transpose(hidden_w[j])) for j in range(2)]

    def fold(value):
        acc = value[:, block(0)]
        for i in range(1, CHUNK // LANES):
            acc = acc + value[:, block(i)]
        return acc

    def add(k, value):
        sums[block(k, 32), :] += fold(value)

    def step(i, carry):
        span = pl.ds(pl.multiple_of(i * CHUNK, CHUNK), CHUNK)
        times, places = sample_rows(i * CHUNK, CHUNK)
        draw = rows[:, span] * envelope_of(times, own)
        dz_2 = weight[0] * draw[0:1, :] + weight[1] * draw[1:2, :] + weight[2] * draw[2:3, :]

        def level(j, e_value, g_value):
            centre = columns[:, 4 * j + 1 : 4 * j + 2]
            offset = places - centre
            moment = e_value * offset
            add(4 * j, moment * offset)
            add(4 * j + 1, moment)
            add(4 * j + 2, g_value * places)
            add(4 * j + 3, g_value)

        z_2 = tab[5, :, span]
        level(2, dz_2 * z_2, dz_2 * tab[6, :, span])
        du_2 = dz_2 * tab[7, :, span]
        add(13, du_2)
        dz_1 = stacked_dot(back[1], du_2)
        z_1 = tab[2, :, span]
        level(1, dz_1 * z_1, dz_1 * tab[3, :, span])
        du_1 = dz_1 * tab[4, :, span]
        add(12, du_1)
        dz_0 = stacked_dot(back[0], du_1)
        z_0 = tab[0, :, span]
        level(0, dz_0 * z_0, dz_0 * tab[1, :, span])
        sums[14 * 32 : 14 * 32 + 8, :] += fold(draw)
        left = jnp.concatenate([du_1, du_2, draw], axis=0).astype(BF16)
        right = jnp.concatenate([z_0, z_1, z_2, jnp.zeros_like(z_0)], axis=0).astype(BF16)
        mats[...] += dot_rows(left, right)
        return carry

    lax.fori_loop(0, SAMPLES // CHUNK, step, 0, unroll=4)
    lane = lax.broadcasted_iota(jnp.int32, (32, LANES), 1)
    hidden = jnp.where(lane < 32, mats[0:32, :], jnp.where(lane < 64, mats[32:64, :], 0.0))

    def column(k):
        return jnp.sum(sums[block(k, 32), :], axis=1, keepdims=True)

    hidden = jnp.where(lane == 64, column(12), hidden)
    hidden = jnp.where(lane == 65, column(13), hidden)
    for j in range(3):
        sharpness = columns[:, 4 * j : 4 * j + 1]
        hidden = jnp.where(lane == 66 + 4 * j, -sharpness * column(4 * j), hidden)
        hidden = jnp.where(lane == 67 + 4 * j, sharpness * sharpness * column(4 * j + 1), hidden)
        hidden = jnp.where(lane == 68 + 4 * j, column(4 * j + 2), hidden)
        hidden = jnp.where(lane == 69 + 4 * j, column(4 * j + 3), hidden)
    lane8 = lax.broadcasted_iota(jnp.int32, (8, LANES), 1)
    outer = pltpu.roll(mats[64:72, :], LANES - 64, 1)
    raw_total = jnp.sum(sums[14 * 32 : 14 * 32 + 8, :], axis=1, keepdims=True)
    outer = jnp.where(lane8 < 32, outer, 0.0)
    outer = jnp.where(lane8 == 32, raw_total, outer)
    return hidden, outer


def with_norm_sums(outer, sums):
    row = lax.broadcasted_iota(jnp.int32, (8, LANES), 0)
    lane = lax.broadcasted_iota(jnp.int32, (8, LANES), 1)
    for part in range(OWN):
        gain_total, bias_total = sums[part]
        outer = jnp.where((row == part) & (lane == 33), gain_total, outer)
        outer = jnp.where((row == part) & (lane == 34), bias_total, outer)
    return outer


def one_row(outer):
    lane = lax.broadcasted_iota(jnp.int32, (1, LANES), 1)
    result = jnp.zeros((1, LANES), F32)
    for part in range(OWN):
        row = outer[part : part + 1, :]
        moved = pltpu.roll(row, 32 * part, 1) if part else row
        result = jnp.where((lane >= 32 * part) & (lane < 32 * part + 32), moved, result)
        moved = pltpu.roll(row, 64 + 3 * part, 1)
        result = jnp.where((lane >= 96 + 3 * part) & (lane < 99 + 3 * part), moved, result)
    return result


def packed_hidden(hidden):
    lane16 = lax.broadcasted_iota(jnp.int32, (16, LANES), 1)
    upper = jnp.where(lane16 < 64, hidden[0:16, :], pltpu.roll(hidden[16:32, :], 64, 1))
    lane4 = lax.broadcasted_iota(jnp.int32, (4, LANES), 1)
    lower = jnp.zeros((4, LANES), F32)
    for g in range(8):
        moved = pltpu.roll(hidden, (64 + 16 * g) % LANES, 1)[4 * g : 4 * g + 4, :]
        lower = jnp.where((lane4 >= 16 * g) & (lane4 < 16 * g + 16), moved, lower)
    return upper, lower


def unpacked_hidden(upper, lower):
    lane16 = lax.broadcasted_iota(jnp.int32, (16, LANES), 1)
    lane32 = lax.broadcasted_iota(jnp.int32, (32, LANES), 1)
    top = jnp.concatenate([upper, pltpu.roll(upper, 64, 1)], axis=0)
    tiled = jnp.concatenate([lower] * 8, axis=0)
    row32 = lax.broadcasted_iota(jnp.int32, (32, LANES), 0)
    rest = jnp.zeros((32, LANES), F32)
    for g in range(8):
        moved = pltpu.roll(tiled, (64 - 16 * g) % LANES, 1)
        rest = jnp.where((row32 >= 4 * g) & (row32 < 4 * g + 4), moved, rest)
    return jnp.where(lane32 < 64, top, rest)


def high_low(value):
    high = value.astype(BF16).astype(F32)
    return high, value - high


def valid_row(meta, i):
    lane = lax.broadcasted_iota(jnp.int32, (1, LANES), 1)
    return (meta[2] * PIECE + (i // 2) * LANES + lane < meta[i % 2]).astype(F32)


def masked(meta, rows):
    mask = jnp.concatenate([valid_row(meta, i) for i in range(4)] * 2, axis=0)
    return (rows.reshape(-1, 8, LANES) * mask[None]).reshape(-1, LANES)


CLIP_ROWS = 4 * CHANNELS
PADDED_ROWS = 4 * PADDED


def put_padded(padded, rows):
    padded[0:CLIP_ROWS, :] = rows
    padded[CLIP_ROWS:PADDED_ROWS, :] = jnp.zeros((PADDED_ROWS - CLIP_ROWS, LANES), F32)


def rows_to_message(padded, out, step, base):
    for m in range(12):
        out[pl.ds(base + m, DEVICES, stride=step), :] = padded[pl.ds(m, DEVICES, stride=12), :]


def rows_of_channels(padded, i):
    return padded[pl.ds(i, PADDED, stride=4), :]


def source_kernel(meta, x_ref, mix_w, out_ref, padded, out):
    put_padded(padded, masked(meta, x_ref[...]))
    for b in range(2):
        length = meta[b]
        upper = lax.shift_right_logical(length, 7)
        out[pl.ds(12 + 2 * b, DEVICES, stride=16), :] = jnp.full((DEVICES, LANES), upper.astype(F32))
        out[pl.ds(13 + 2 * b, DEVICES, stride=16), :] = jnp.full(
            (DEVICES, LANES), (length - upper * 128).astype(F32)
        )
    rows_to_message(padded, out, 16, 0)
    out_ref[...] = out[...].reshape(DEVICES, 16, LANES).astype(BF16)


def make_lookup(lookup):
    row = lax.broadcasted_iota(jnp.int32, (DEVICES, PADDED), 0)
    column = lax.broadcasted_iota(jnp.int32, (DEVICES, PADDED), 1)
    for part in range(OWN):
        lookup[block(part), :] = (column == OWN * row + part).astype(F32).astype(BF16)


def make_weights(mix_w, mix_b, wide, lookup, weights, weights_back):
    make_lookup(lookup)
    wide[...] = jnp.zeros(wide.shape, BF16)
    row = lax.broadcasted_iota(jnp.int32, (LANES, CHANNELS), 0)
    lines = jnp.where(row == 0, mix_b[0:1, :], jnp.where(row == 1, mix_b[1:2, :], 0.0))
    turned = jnp.transpose(jnp.concatenate([lines, jnp.zeros((LANES, PADDED - CHANNELS), F32)], axis=1))
    lane = lax.broadcasted_iota(jnp.int32, (PADDED, PADDED), 1)
    for layer in range(2):
        wide[0:CHANNELS, 0:CHANNELS] = mix_w[layer]
        weights_back[layer] = dot_rows(lookup[...], wide[...]).astype(BF16)
        value = dot_rows(wide[...], lookup[...])
        rest = turned[:, layer : layer + 1]
        for spot in SPOTS:
            high, rest = high_low(rest)
            value = jnp.where(lane == spot, high, value)
        weights[layer] = value.astype(BF16)


def make_kernel(layer, meta, params, consts, bundle, tab, scratch):
    out_w, out_b, window, gain, bias, gabor, hidden_b, hidden_w = params
    first, second, _, twiddle = consts
    wide, tall, rows, pieces, x_ref, high, low = scratch
    own, columns = bundle.at[OWN_ROWS, :], bundle.at[COLUMN_ROWS, :]
    own_parameters(layer, meta[3], out_w, out_b, window, gain, bias, gabor, hidden_b, wide, tall, own, columns)
    generate(columns, hidden_w.at[layer], own, tab, rows)
    for n in range(64):
        for part in range(OWN):
            pieces[part * 64 + n : part * 64 + n + 1, :] = rows[part : part + 1, block(n)]
    for part in range(OWN):
        piece = pieces[block(part, 64), :].astype(BF16)
        x_ref[0:64, block(part)] = piece
        x_ref[64:128, block(part)] = piece
        x_ref[128:256, block(part)] = jnp.zeros((128, LANES), BF16)
    spec = transform(x_ref, high, low, first, second, twiddle, OWN)
    bundle[0:SPEC_IM, :] = spec[:, RE]
    bundle[SPEC_IM : 2 * SPEC_IM, :] = spec[:, IM]


def forward_kernel(
    meta, message_ref, out_w, out_b, window, gain, bias, gabor, hidden_b, hidden_w,
    first, second, last, twiddle,
    out_ref, spec_ref, normed_ref, slope_ref, inv_ref, len_ref, kernel_spec, tab,
    message, x_ref, high, low, e_high, e_low, y_ref, out, *make_scratch,
):
    own = kernel_spec.at[OWN_ROWS, :]
    params = (out_w, out_b, window, gain, bias, gabor, hidden_b, hidden_w)
    make_kernel(0, meta, params, (first, second, last, twiddle), kernel_spec, tab, make_scratch)
    message[...] = spread(message_ref[...])
    for y in range(4):
        for b in range(2):
            start = y * 16 + 12 + 2 * b
            len_ref[2 * y + b : 2 * y + b + 1, :] = (
                message[start : start + 1, :] * 128.0 + message[start + 1 : start + 2, :]
            )
    load_signals(message, 16, x_ref)
    convolve(x_ref, spec_ref, kernel_spec, high, low, e_high, e_low, (first, second, last, twiddle), y_ref)
    normalise_all(y_ref, own, len_ref, normed_ref, slope_ref, inv_ref)
    store_signals(out, 12, 0, lambda part, y: y_ref[:, block(part * 4 + y)])
    out_ref[...] = out[...].reshape(DEVICES, 3, 4, LANES).astype(BF16)


def gather_active(message, step, rhs):
    row = lax.broadcasted_iota(jnp.int32, (DEVICES, LANES), 0)
    for i in range(4):
        for part in range(OWN):
            piece = message[pl.ds(part * 4 + i, DEVICES, stride=step), :]
            if part != 1:
                piece = jnp.where(row >= (126 if part == 2 else 127), 1.0, piece)
            rhs[block(part), block(i)] = piece.astype(BF16)


def store_rows(value, out, step, base):
    for i in range(4):
        for part in range(OWN):
            out[pl.ds(base + part * 4 + i, DEVICES, stride=step), :] = value[block(part), block(i)]


def mix_kernel(
    meta, message_ref, x_ref, cotangent, mix_w, mix_b,
    out_ref, next_ref, active_ref, weights, weights_back, message, padded, out, low, wide, lookup,
):
    make_weights(mix_w, mix_b, wide, lookup, weights, weights_back)
    message[...] = spread(message_ref[...])
    gather_active(message, 12, active_ref)
    mixed = dot(weights[0], active_ref[...])
    put_padded(padded, x_ref[...])
    for i in range(4):
        valid = valid_row(meta, i)
        value = rows_of_channels(padded, i) + mixed[:, block(i)] * valid
        next_ref[pl.ds(i, PADDED, stride=4), :] = value
        padded[pl.ds(i, PADDED, stride=4), :] = value * valid
    rows_to_message(padded, out, 24, 0)
    put_padded(padded, masked(meta, cotangent[...]))
    for i in range(4):
        low[:, block(i)] = rows_of_channels(padded, i).astype(BF16)
    store_rows(dot(weights_back[1], low[...]), out, 24, 12)
    out_ref[...] = out[...].reshape(DEVICES, 24, LANES).astype(BF16)


def forward_backward_kernel(
    meta, message_ref, out_w, out_b, window, gain, bias, gabor, hidden_b, hidden_w,
    len_ref, first, second, last, twiddle,
    out_ref, hidden_out, outer_out,
    message, x_ref, high, low, e_high, e_low, y_ref, out, spec_ref, grad_ref, normed_ref, slope_ref, returned_ref,
    rows, sums, mats, kernel_spec, tab, inv_ref, *make_scratch,
):
    own, columns = kernel_spec.at[OWN_ROWS, :], kernel_spec.at[COLUMN_ROWS, :]
    consts = (first, second, last, twiddle)
    params = (out_w, out_b, window, gain, bias, gabor, hidden_b, hidden_w)
    make_kernel(1, meta, params, consts, kernel_spec, tab, make_scratch)
    message[...] = spread(message_ref[...])
    load_signals(message, 24, x_ref)
    convolve(x_ref, spec_ref, kernel_spec, high, low, e_high, e_low, consts, y_ref)
    valid, tally = valid_of(len_ref), tally_of(len_ref)
    normalise_all(y_ref, own, len_ref, normed_ref, slope_ref, inv_ref)
    store_signals(out, 24, 0, lambda part, y: y_ref[:, block(part * 4 + y)])
    returned, norm_sums = conv_backward(
        message, 24, 12, lambda part: normed_ref[:, block(part, 512)], lambda part: slope_ref[:, block(part, 512)],
        lambda part: inv_ref[part : part + 1, 0:1], own, valid, tally, spec_ref, kernel_spec, x_ref, high, low, e_high, e_low, consts, grad_ref,
    )
    returned_ref[...] = returned
    store_signals(out, 24, 12, lambda part, y: returned_ref[:, block(part * 4 + y)])
    out_ref[...] = out[...].reshape(DEVICES, 24, LANES).astype(BF16)
    hidden, outer = generate_back(
        lambda part: returned_ref[0:64, block(SIGNALS + part)], columns, hidden_w.at[1], own, tab,
        rows, sums, mats,
    )
    hidden_out[...] = hidden
    outer_out[...] = with_norm_sums(outer, norm_sums)


def middle_kernel(
    meta, message_ref, x_ref, cotangent, weights, weights_back, active_0, hidden_1,
    output_ref, flow_ref, out_ref, message, padded, out, low_0, low_1, active_1,
):
    message[...] = spread(message_ref[...])
    gather_active(message, 24, active_1)
    mixed = dot(weights[1], active_1[...])
    for i in range(4):
        padded[pl.ds(i, PADDED, stride=4), :] = rows_of_channels(x_ref, i) + mixed[:, block(i)] * valid_row(meta, i)
    output_ref[...] = padded[0:CLIP_ROWS, :]
    put_padded(flow_ref, cotangent[...])
    for i in range(4):
        low_1[:, block(i)] = (rows_of_channels(flow_ref, i) * valid_row(meta, i)).astype(BF16)
    for m in range(12):
        padded[pl.ds(m, DEVICES, stride=12), :] = message[pl.ds(12 + m, DEVICES, stride=24), :]
    flow_ref[...] += masked(meta, padded[...])
    for i in range(4):
        low_0[:, block(i)] = (rows_of_channels(flow_ref, i) * valid_row(meta, i)).astype(BF16)
    store_rows(dot(weights_back[0], low_0[...]), out, 32, 0)
    for layer, (active, low) in enumerate(((active_0, low_0), (active_1, low_1))):
        part_sum = dot_rows(active[...], low[...])
        for part in range(OWN):
            for third in range(3):
                out[pl.ds(12 + layer * 9 + part * 3 + third, DEVICES, stride=32), :] = part_sum[
                    block(part), block(third)
                ]
    high, low = high_low(hidden_1[...])
    out[pl.ds(30, DEVICES, stride=32), :] = jnp.concatenate([high, jnp.zeros((96, LANES), F32)], axis=0)
    out[pl.ds(31, DEVICES, stride=32), :] = jnp.concatenate([low, jnp.zeros((96, LANES), F32)], axis=0)
    out_ref[...] = out[...].reshape(DEVICES, 32, LANES).astype(BF16)


LAST_ROWS = 56


def backward_kernel(
    message_ref, spec_ref, kernel_spec, normed_ref, slope_ref, inv_ref, len_ref,
    first, second, last, twiddle, hidden_w, tab, outer_1,
    out_ref,
    message, x_ref, high, low, e_high, e_low, out, grad_ref, returned_ref, rows, sums, mats,
):
    own, columns = kernel_spec.at[OWN_ROWS, :], kernel_spec.at[COLUMN_ROWS, :]
    consts = (first, second, last, twiddle)
    message[...] = spread(message_ref[...])
    valid, tally = valid_of(len_ref), tally_of(len_ref)
    returned, norm_sums = conv_backward(
        message, 32, 0, lambda part: normed_ref[:, block(part, 512)], lambda part: slope_ref[:, block(part, 512)],
        lambda part: inv_ref[part : part + 1, 0:1], own, valid, tally, spec_ref, kernel_spec, x_ref, high, low,
        e_high, e_low, consts, grad_ref,
    )
    returned_ref[...] = returned
    store_signals(out, 16, 0, lambda part, y: returned_ref[:, block(part * 4 + y)])
    hidden, outer = generate_back(
        lambda part: returned_ref[0:64, block(SIGNALS + part)], columns, hidden_w.at[0], own, tab,
        rows, sums, mats,
    )
    outer = with_norm_sums(outer, norm_sums)
    gathered = jnp.sum(message[...].reshape(DEVICES, 32, LANES), axis=0)
    upper, lower = packed_hidden(hidden)
    hidden_1_high, hidden_1_low = high_low(gathered[30:31, :] + gathered[31:32, :])
    outer_0_high, outer_0_low = high_low(one_row(outer))
    outer_1_high, outer_1_low = high_low(one_row(outer_1[...]))
    shared = jnp.concatenate(
        [
            gathered[0:30, :], upper, lower, hidden_1_high, hidden_1_low,
            outer_0_high, outer_0_low, outer_1_high, outer_1_low,
        ],
        axis=0,
    )
    row = lax.broadcasted_iota(jnp.int32, (DEVICES, 16, LANES), 1)
    own_rows = jnp.where(row < 12, out[...].reshape(DEVICES, 16, LANES), shared[None, 0:16, :])
    rest = jnp.broadcast_to(shared[None, 16:LAST_ROWS, :], (DEVICES, LAST_ROWS - 16, LANES))
    out_ref[...] = jnp.concatenate([own_rows, rest], axis=1).astype(BF16)


def last_kernel(
    meta, message_ref, flow_ref,
    input_grad, gabor_grad, hidden_w_grad, hidden_b_grad, out_w_grad, out_b_grad, gain_grad, bias_grad,
    mix_w_grad, mix_b_grad, message, padded, owned, thirds, lookup,
):
    make_lookup(lookup)
    message[...] = spread(message_ref[...])

    def rows_of(k, count=DEVICES):
        return message[pl.ds(k, count, stride=LAST_ROWS), :]

    for m in range(12):
        padded[pl.ds(m, DEVICES, stride=12), :] = rows_of(m)
    input_grad[...] = flow_ref[0:CLIP_ROWS, :] + masked(meta, padded[0:CLIP_ROWS, :])
    shared = jnp.sum(message[...].reshape(DEVICES, LAST_ROWS, LANES)[:, 24:56, :], axis=0)
    hidden_0 = unpacked_hidden(shared[6:22, :], shared[22:26, :])
    hidden_1 = rows_of(50, 32) + rows_of(51, 32)
    lane = lax.broadcasted_iota(jnp.int32, (DEVICES, LANES), 1)
    for layer, hidden in enumerate((hidden_0, hidden_1)):
        hidden_w_grad[layer, 0] = hidden[:, 0:32]
        hidden_w_grad[layer, 1] = pltpu.roll(hidden, 96, 1)[:, 0:32]
        turned = jnp.transpose(jnp.concatenate([hidden, jnp.zeros((96, LANES), F32)], axis=0))
        hidden_b_grad[layer] = turned[64:66, 0:32]
        for j in range(3):
            gabor_grad[layer, j] = turned[66 + 4 * j : 70 + 4 * j, 0:32]
        value = rows_of(52 + 2 * layer) + rows_of(53 + 2 * layer)
        for part in range(OWN):
            wide = pltpu.roll(value, (LANES - 32 * part) % LANES, 1)
            small = pltpu.roll(value, 64 - 3 * part, 1)
            owned[pl.ds(part, DEVICES, stride=OWN), :] = jnp.where(lane < 32, wide, small)
        turned = jnp.transpose(owned[...])
        out_w_grad[layer] = turned[0:32, 0:CHANNELS]
        out_b_grad[layer : layer + 1, :] = turned[32:33, 0:CHANNELS]
        gain_grad[layer : layer + 1, :] = turned[33:34, 0:CHANNELS]
        bias_grad[layer : layer + 1, :] = turned[34:35, 0:CHANNELS]
        bias_rows = []
        for part in range(OWN):
            for third in range(3):
                piece = rows_of(12 + layer * 9 + part * 3 + third)
                thirds[block(part), block(third)] = piece.astype(BF16)
                if part == 2:
                    bias_rows.append(piece[SPOT - 2 * DEVICES : SPOT - 2 * DEVICES + 1, :])
        mix_w_grad[:, layer, :] = dot_columns(thirds[...], lookup[...])[0:CHANNELS, 0:CHANNELS]
        mix_b_grad[layer : layer + 1, :] = jnp.concatenate(bias_rows, axis=1)[:, 0:CHANNELS]


def exchange(message):
    return lax.all_to_all(message, AXES, split_axis=0, concat_axis=0, tiled=True)


def to_rows(clips):
    return clips.reshape(2, CHANNELS, 2, LANES).transpose(1, 2, 0, 3).reshape(CLIP_ROWS, LANES)


def from_rows(rows):
    return rows.reshape(CHANNELS, 2, 2, LANES).transpose(2, 0, 1, 3).reshape(2, CHANNELS, PIECE)


def shards(
    inputs, lengths, window, gabor_params, hidden_w, hidden_b, out_w, out_b, bn_gain, bn_bias, mix_w, mix_b, cotangent
):
    position = lax.axis_index("seq").astype(jnp.int32)
    number = position * 4 + lax.axis_index("clips").astype(jnp.int32)
    const = {name: jnp.asarray(value) for name, value in TABLES.items()}
    meta = jnp.concatenate([lengths, jnp.stack([position, number])])
    inputs, cotangent = to_rows(inputs), to_rows(cotangent)

    def rows(count):
        return ((count, LANES), F32)

    with jax.named_scope("source_0"):
        (message,) = run(
            source_kernel, [((DEVICES, 16, LANES), BF16)], [meta, inputs, mix_w],
            [rows(PADDED_ROWS), rows(DEVICES * 16)], "source_0", 8, smem=(0,), far=(2,),
        )
        message = exchange(message)

    square = (PADDED, PADDED)
    generator = [
        jnp.swapaxes(out_w, 1, 2), out_b, jnp.swapaxes(window, 1, 2), bn_gain, bn_bias, gabor_params, hidden_b,
        hidden_w,
    ]
    shape_tab = ((8, HIDDEN, SAMPLES), F32)
    make_scratch = [
        ((LANES, PADDED), F32), rows(PADDED + 8), ((8, SAMPLES), F32), rows(192),
        ((256, OWN * LANES), BF16), ((OWN * LANES, 256), BF16), ((OWN * LANES, 256), BF16),
    ]
    mixers = ((2, *square), BF16)

    def scratch(signals):
        count = signals * LANES
        return [
            ((256, SIGNALS * LANES), BF16), ((count, 256), BF16), ((count, 256), BF16),
            ((256, count), BF16), ((256, count), BF16),
        ]

    shape_y = (LANES, SIGNALS * LANES)
    shape_s = (SIGNALS * LANES, 256)
    transforms = [const[name] for name in TABLE_NAMES]
    with jax.named_scope("conv_0"):
        message, spec_0, normed_0, slope_0, inv_0, lens, bundle_0, tab_0 = run(
            forward_kernel,
            [
                ((DEVICES, 3, 4, LANES), BF16), (shape_s, F32), (shape_y, F32), (shape_y, F32), rows(8), rows(8),
                rows(BUNDLE), shape_tab,
            ],
            [meta, message, *generator, *transforms],
            [rows(DEVICES * 16), *scratch(SIGNALS), (shape_y, F32), rows(DEVICES * 12), *make_scratch],
            "conv_0", 16, smem=(0,),
        )
        message = exchange(message)

    with jax.named_scope("mix_0"):
        message, middle, active_0, weights, weights_back = run(
            mix_kernel,
            [((DEVICES, 24, LANES), BF16), rows(PADDED_ROWS), ((PADDED, 512), BF16), mixers, mixers],
            [meta, message, inputs, cotangent, mix_w, mix_b],
            [rows(DEVICES * 12), rows(PADDED_ROWS), rows(DEVICES * 24), ((PADDED, 512), BF16), (square, BF16), (square, BF16)],
            "mix_0", 12, smem=(0,),
        )
        message = exchange(message)

    back_scratch = [((8, SAMPLES), F32), rows(14 * 32 + 8), rows(72)]
    with jax.named_scope("conv_1"):
        message, hidden_1, outer_1 = run(
            forward_backward_kernel,
            [((DEVICES, 24, LANES), BF16), rows(HIDDEN), rows(8)],
            [
                meta, message, *generator, lens, *transforms,
            ],
            [
                rows(DEVICES * 24), *scratch(SIGNALS + OWN), (shape_y, F32), rows(DEVICES * 24),
                (shape_s, F32), (shape_s, F32), (shape_y, F32), (shape_y, F32),
                ((LANES, (SIGNALS + OWN) * LANES), F32), *back_scratch, rows(BUNDLE), shape_tab, rows(8), *make_scratch,
            ],
            "conv_1", 26, smem=(0,),
        )
        message = exchange(message)

    with jax.named_scope("mix_1"):
        outputs, flow, message = run(
            middle_kernel,
            [rows(CLIP_ROWS), rows(PADDED_ROWS), ((DEVICES, 32, LANES), BF16)],
            [meta, message, middle, cotangent, weights, weights_back, active_0, hidden_1],
            [
                rows(DEVICES * 24), rows(PADDED_ROWS), rows(DEVICES * 32),
                ((PADDED, 512), BF16), ((PADDED, 512), BF16), ((PADDED, 512), BF16),
            ],
            "mix_1", 12, smem=(0,),
        )
        message = exchange(message)

    with jax.named_scope("conv_back_0"):
        (message,) = run(
            backward_kernel,
            [((DEVICES, LAST_ROWS, LANES), BF16)],
            [
                message, spec_0, bundle_0, normed_0, slope_0, inv_0, lens, *transforms,
                hidden_w, tab_0, outer_1,
            ],
            [
                rows(DEVICES * 32), *scratch(SIGNALS + OWN), rows(DEVICES * 16), (shape_s, F32),
                ((LANES, (SIGNALS + OWN) * LANES), F32), *back_scratch,
            ],
            "conv_back_0", 16,
        )
        message = exchange(message)

    with jax.named_scope("gradients"):
        (
            input_grad, gabor_grad, hidden_w_grad, hidden_b_grad, out_w_grad, out_b_grad, gain_grad, bias_grad,
            mix_w_grad, mix_b_grad,
        ) = run(
            last_kernel,
            [
                rows(CLIP_ROWS), (gabor_params.shape, F32), (hidden_w.shape, F32), (hidden_b.shape, F32),
                ((2, HIDDEN, CHANNELS), F32), (out_b.shape, F32), (bn_gain.shape, F32), (bn_bias.shape, F32),
                ((CHANNELS, 2, CHANNELS), F32), (mix_b.shape, F32),
            ],
            [meta, message, flow],
            [rows(DEVICES * LAST_ROWS), rows(PADDED_ROWS), rows(PADDED), (square, BF16), (square, BF16)],
            "gradients", 14, smem=(0,),
        )
    return (
        from_rows(outputs), from_rows(input_grad), gabor_grad, hidden_w_grad, hidden_b_grad,
        jnp.swapaxes(out_w_grad, 1, 2), out_b_grad, gain_grad, bias_grad, jnp.swapaxes(mix_w_grad, 0, 1), mix_b_grad,
    )


def solution(mesh):
    clip = P("clips", None, "seq")
    in_specs = (clip, P("clips")) + (P(),) * 10 + (clip,)
    out_specs = (clip, clip) + (P(),) * 9
    return jax.shard_map(shards, mesh=mesh, in_specs=in_specs, out_specs=out_specs, check_vma=False)
```
